32 devices in a mesh: dp: 16 (over z, y, core), tensor: 2 (over x).
Axes of the slice: x: 2, y: 2, z: 4, core: 2. Of those that a mesh axis runs over, the one named last changes fastest.
Arguments:
- source: bfloat16 [32, 1024, 512], P('dp', 'tensor'), may hold values from -6 to 6
- target: bfloat16 [32, 1024, 512], P('dp', 'tensor'), may hold values from -6 to 6
- cotangent: bfloat16 [32, 1024, 512], P('dp', 'tensor'), may hold values from -6 to 6
- lengths: int32 [32], P('dp'), may hold values from 128 to 1024, as said below
- timesteps: int32 [32], P('dp'), may hold values from 1 to 50
- masked: int32 [32, 1024], P('dp', 'tensor'), may hold values 0 or 1
- loss_mask: int32 [32, 1024], P('dp', 'tensor'), may hold values 0 or 1
- enc_query: bfloat16 [512, 512], P('dp', 'tensor'), may hold values from -0.25 to 0.25
- enc_key: bfloat16 [512, 512], P('dp', 'tensor'), may hold values from -0.25 to 0.25
- enc_value: bfloat16 [512, 512], P('dp', 'tensor'), may hold values from -0.25 to 0.25
- enc_out: bfloat16 [512, 512], P('tensor', 'dp'), may hold values from -3 to 3
- enc_up: bfloat16 [512, 2048], P('dp', 'tensor'), may hold values from -0.25 to 0.25
- enc_down: bfloat16 [2048, 512], P('tensor', 'dp'), may hold values from -0.125 to 0.125
- self_query: bfloat16 [512, 512], P('dp', 'tensor'), may hold values from -0.25 to 0.25
- self_key: bfloat16 [512, 512], P('dp', 'tensor'), may hold values from -0.25 to 0.25
- self_value: bfloat16 [512, 512], P('dp', 'tensor'), may hold values from -0.25 to 0.25
- self_out: bfloat16 [512, 512], P('tensor', 'dp'), may hold values from -3 to 3
- cross_query: bfloat16 [512, 512], P('dp', 'tensor'), may hold values from -0.25 to 0.25
- cross_key: bfloat16 [512, 512], P('dp', 'tensor'), may hold values from -0.25 to 0.25
- cross_value: bfloat16 [512, 512], P('dp', 'tensor'), may hold values from -0.25 to 0.25
- cross_out: bfloat16 [512, 512], P('tensor', 'dp'), may hold values from -3 to 3
- dec_up: bfloat16 [512, 2048], P('dp', 'tensor'), may hold values from -0.25 to 0.25
- dec_down: bfloat16 [2048, 512], P('tensor', 'dp'), may hold values from -0.125 to 0.125
- norm_gains: float32 [6, 512], replicated, may hold values from 0.1 to 1.9
- norm_shifts: float32 [6, 512], replicated, may hold values from -1.5 to 1.5
- mask_vector: float32 [512], replicated, may hold values from -4 to 4
Outputs:
- decoded: bfloat16 [32, 1024, 512], P('dp', 'tensor')
- source_grad: bfloat16 [32, 1024, 512], P('dp', 'tensor')
- target_grad: bfloat16 [32, 1024, 512], P('dp', 'tensor')
- enc_query_grad: float32 [512, 512], P('dp', 'tensor')
- enc_key_grad: float32 [512, 512], P('dp', 'tensor')
- enc_value_grad: float32 [512, 512], P('dp', 'tensor')
- enc_out_grad: float32 [512, 512], P('tensor', 'dp')
- enc_up_grad: float32 [512, 2048], P('dp', 'tensor')
- enc_down_grad: float32 [2048, 512], P('tensor', 'dp')
- self_query_grad: float32 [512, 512], P('dp', 'tensor')
- self_key_grad: float32 [512, 512], P('dp', 'tensor')
- self_value_grad: float32 [512, 512], P('dp', 'tensor')
- self_out_grad: float32 [512, 512], P('tensor', 'dp')
- cross_query_grad: float32 [512, 512], P('dp', 'tensor')
- cross_key_grad: float32 [512, 512], P('dp', 'tensor')
- cross_value_grad: float32 [512, 512], P('dp', 'tensor')
- cross_out_grad: float32 [512, 512], P('tensor', 'dp')
- dec_up_grad: float32 [512, 2048], P('dp', 'tensor')
- dec_down_grad: float32 [2048, 512], P('tensor', 'dp')
- gains_grad: float32 [6, 512], replicated
- shifts_grad: float32 [6, 512], replicated
- mask_grad: float32 [512], replicated
The draws below stay inside these ranges and needn't reach their ends.
Inputs may be any that keep to these rules, and one draw needn't show every extreme that they name: `lengths`: among the 2 x 1 pairs of each index of dp one has all 1024 source tokens live.
All inputs are finite; a program needn't handle non-finite values. No bound on the sum of `masked` or of `loss_mask` on one device may be relied on, other than what follows from the above.
Results may differ from the reference program's by a relative error of at most 0.029.
Values may be sent and summed in bfloat16 or wider, within the bound.
A program may use at most 448 MiB of HBM per device.

```python
import jax
import jax.numpy as jnp
from jax import lax

D = 512
HEADS = 8
HD = 64
FF = 2048
SEQ = 1024
PAIR_MB = 1
MICRO = 2
STEPS = 50
PAIRS = 32


def draw_lengths(key, part):
    key = jax.random.fold_in(key, 7)
    first_key, second_key = jax.random.split(key)
    span = MICRO * PAIR_MB
    groups = PAIRS // span
    drawn = jax.random.randint(first_key, (groups, span), max(1, SEQ // 8), SEQ + 1)
    chosen = jax.random.randint(second_key, (groups, 1), 0, span)
    slots = jnp.arange(span)[None, :]
    return jnp.where(slots == chosen, SEQ, drawn).reshape(PAIRS).astype(jnp.int32)


def set_ends(result, key, least, largest):
    index_at = [jax.random.randint(jax.random.fold_in(key, axis), (), 0, length) for axis, length in enumerate(result.shape)]
    main_axis = result.shape.index(max(result.shape))
    next_to = index_at[:main_axis] + [(index_at[main_axis] + 1) % result.shape[main_axis]] + index_at[main_axis + 1:]
    return result.at[tuple(index_at)].set(least).at[tuple(next_to)].set(largest)


def block_levels(key, extent, pieces, low, top_value):
    level, own = 1.0, jax.random.fold_in(key, 6)
    for axis_at, parts in pieces:
        steps = jnp.exp(jax.random.uniform(jax.random.fold_in(own, axis_at), (parts,), jnp.float32, low / len(pieces), top_value / len(pieces)))
        level = level * jnp.repeat(steps, extent[axis_at] // parts).reshape([-1 if axis == axis_at else 1 for axis in range(len(extent))])
    return level


def scatter_about(key, dims, deviation, limit, pieces=(), kind=jnp.bfloat16):
    loudness = block_levels(key, dims, pieces, -0.22, 0.18) if pieces else 1.0
    values = jax.random.normal(key, dims, jnp.float32) * deviation * loudness
    return jnp.minimum(jnp.maximum(values, -limit), limit).astype(kind)


def setup_inputs(seed: int = 0) -> dict:
    splits = jax.random.split(jax.random.key(seed), 27)
    source = scatter_about(splits[0], (PAIRS, SEQ, D), 1.0, 6.0, ((0, 16), (1, 2)))
    target = scatter_about(splits[1], (PAIRS, SEQ, D), 1.0, 6.0, ((0, 16), (1, 2)))
    cotangent = scatter_about(splits[2], (PAIRS, SEQ, D), 1.0, 6.0, ((0, 16), (1, 2)))
    lengths = draw_lengths(jax.random.fold_in(splits[26], 71), 0)
    timesteps = set_ends(jax.random.randint(splits[4], (PAIRS,), 1, STEPS + 1), jax.random.fold_in(splits[4], 1), 1, STEPS).astype(jnp.int32)
    masked = set_ends((jax.random.randint(splits[5], (PAIRS, SEQ), 0, 2) < 1).astype(jnp.int32), jax.random.fold_in(splits[5], 1), 0, 1)
    loss_mask = set_ends((jax.random.randint(splits[6], (PAIRS, SEQ), 0, 4) < 3).astype(jnp.int32), jax.random.fold_in(splits[6], 1), 0, 1)
    enc_query = scatter_about(splits[7], (D, HEADS * HD), D ** -0.5, 0.25, ((0, 16), (1, 2)))
    enc_key = scatter_about(splits[8], (D, HEADS * HD), D ** -0.5, 0.25, ((0, 16), (1, 2)))
    enc_value = scatter_about(splits[9], (D, HEADS * HD), D ** -0.5, 0.25, ((0, 16), (1, 2)))
    enc_out = scatter_about(splits[10], (HEADS * HD, D), (max(1, HEADS * HD * 8 // SEQ)) ** -0.5, 3.0, ((0, 2), (1, 16)))
    enc_up = scatter_about(splits[11], (D, FF), D ** -0.5, 0.25, ((0, 16), (1, 2)))
    enc_down = scatter_about(splits[12], (FF, D), FF ** -0.5, 0.125, ((0, 2), (1, 16)))
    self_query = scatter_about(splits[13], (D, HEADS * HD), D ** -0.5, 0.25, ((0, 16), (1, 2)))
    self_key = scatter_about(splits[14], (D, HEADS * HD), D ** -0.5, 0.25, ((0, 16), (1, 2)))
    self_value = scatter_about(splits[15], (D, HEADS * HD), D ** -0.5, 0.25, ((0, 16), (1, 2)))
    self_out = scatter_about(splits[16], (HEADS * HD, D), (max(1, HEADS * HD * 8 // SEQ)) ** -0.5, 3.0, ((0, 2), (1, 16)))
    cross_query = scatter_about(splits[17], (D, HEADS * HD), D ** -0.5, 0.25, ((0, 16), (1, 2)))
    cross_key = scatter_about(splits[18], (D, HEADS * HD), D ** -0.5, 0.25, ((0, 16), (1, 2)))
    cross_value = scatter_about(splits[19], (D, HEADS * HD), D ** -0.5, 0.25, ((0, 16), (1, 2)))
    cross_out = scatter_about(splits[20], (HEADS * HD, D), (max(1, HEADS * HD * 8 // SEQ)) ** -0.5, 3.0, ((0, 2), (1, 16)))
    dec_up = scatter_about(splits[21], (D, FF), D ** -0.5, 0.25, ((0, 16), (1, 2)))
    dec_down = scatter_about(splits[22], (FF, D), FF ** -0.5, 0.125, ((0, 2), (1, 16)))
    norm_gains = jnp.clip(1.0 + 0.18 * jax.random.normal(splits[23], (6, D), jnp.float32), 0.1, 1.9)
    norm_shifts = scatter_about(splits[24], (6, D), 0.3, 1.5, (), jnp.float32)
    mask_vector = scatter_about(splits[25], (D,), 1.0, 4.0, (), jnp.float32)
    return dict(source=source, target=target, cotangent=cotangent, lengths=lengths, timesteps=timesteps, masked=masked, loss_mask=loss_mask, enc_query=enc_query, enc_key=enc_key, enc_value=enc_value, enc_out=enc_out, enc_up=enc_up, enc_down=enc_down, self_query=self_query, self_key=self_key, self_value=self_value, self_out=self_out, cross_query=cross_query, cross_key=cross_key, cross_value=cross_value, cross_out=cross_out, dec_up=dec_up, dec_down=dec_down, norm_gains=norm_gains, norm_shifts=norm_shifts, mask_vector=mask_vector)


@jax.custom_vjp
def low(v):
    return lax.optimization_barrier(v.astype(jnp.bfloat16)).astype(jnp.float32)

@jax.custom_vjp
def low_back(v):
    return v

def low_keep(v):
    return (low(v), None)

def low_pass(kept, grad):
    return (grad,)

def back_keep(v):
    return (v, None)

def back_low(kept, grad):
    return (low(grad),)
low.defvjp(low_keep, low_pass)
low_back.defvjp(back_keep, back_low)
eps = 1e-05

def hdot(left, right):
    return jnp.dot(left, right, preferred_element_type=jnp.float32, precision=lax.Precision.HIGHEST)

def norm_rows(inputs, gain, shift):
    average = lax.optimization_barrier(jnp.mean(inputs, axis=-1, keepdims=True))
    centred = inputs - average
    second = lax.optimization_barrier(jnp.mean(centred * centred, axis=-1, keepdims=True))
    return centred * lax.rsqrt(second + eps) * gain + shift

def attend(query_in, keys_in, w_query, w_key, w_value, w_out, live):
    queries = low_back(low(hdot(query_in, w_query))).reshape(SEQ, HEADS, HD)
    key_rows = low_back(low(hdot(keys_in, w_key))).reshape(SEQ, HEADS, HD)
    value_rows = low_back(low(hdot(keys_in, w_value))).reshape(SEQ, HEADS, HD)
    block_rows = min(512, SEQ)
    scale_score = HD ** (-0.5)

    def one_block(query_part):
        scores = jnp.einsum('qhd,khd->hqk', query_part, key_rows, precision=lax.Precision.HIGHEST) * scale_score
        scores = low_back(scores)
        scores = jnp.where(live[None, None, :], scores, -1e+30)
        highest = lax.optimization_barrier(jnp.max(scores, axis=-1, keepdims=True))
        exponent = jnp.exp(scores - highest)
        softmax = low(exponent / lax.optimization_barrier(jnp.sum(exponent, axis=-1, keepdims=True)))
        return jnp.einsum('hqk,khd->qhd', softmax, value_rows, precision=lax.Precision.HIGHEST)
    attended = lax.map(jax.checkpoint(one_block), queries.reshape(SEQ // block_rows, block_rows, HEADS, HD))
    attended = low_back(low(attended.reshape(SEQ, HEADS * HD)))
    return low_back(hdot(attended, w_out))

def feed(inputs, w_up, w_down):
    lifted = low_back(hdot(inputs, w_up))
    active = low(jax.nn.gelu(lifted, approximate=False))
    return low_back(hdot(active, w_down))

def forward_pair(source_row, target_row, weights, gains, shifts, mask_vec, chosen, live):
    every = jnp.ones((SEQ,), bool)
    rows0 = low(norm_rows(source_row, gains[0], shifts[0]))
    stream1 = source_row + attend(rows0, rows0, weights[0], weights[1], weights[2], weights[3], live)
    rows1 = low(norm_rows(stream1, gains[1], shifts[1]))
    stream2 = stream1 + feed(rows1, weights[4], weights[5])
    memory_rows = low(norm_rows(stream2, gains[2], shifts[2]))
    start_y = jnp.where(chosen[:, None], mask_vec[None, :], target_row)
    rows3 = low(norm_rows(start_y, gains[3], shifts[3]))
    stream4 = start_y + attend(rows3, rows3, weights[6], weights[7], weights[8], weights[9], every)
    rows4 = low(norm_rows(stream4, gains[4], shifts[4]))
    stream5 = stream4 + attend(rows4, memory_rows, weights[10], weights[11], weights[12], weights[13], live)
    rows5 = low(norm_rows(stream5, gains[5], shifts[5]))
    return stream5 + feed(rows5, weights[14], weights[15])

def reference(source, target, cotangent, lengths, timesteps, masked, loss_mask, enc_query, enc_key, enc_value, enc_out, enc_up, enc_down, self_query, self_key, self_value, self_out, cross_query, cross_key, cross_value, cross_out, dec_up, dec_down, norm_gains, norm_shifts, mask_vector):
    weights = tuple((matrix.astype(jnp.float32) for matrix in (enc_query, enc_key, enc_value, enc_out, enc_up, enc_down, self_query, self_key, self_value, self_out, cross_query, cross_key, cross_value, cross_out, dec_up, dec_down)))
    positions = jnp.arange(SEQ, dtype=jnp.int32)

    def one_pair(running, pair_items):
        source_row, target_row, cotangent_row, length, timestep, masked_row, loss_row = pair_items
        live = positions < length
        chosen = masked_row == 1

        def forward(source_f, target_f, weight_set, gains, shifts, mask_vec):
            return forward_pair(source_f, target_f, weight_set, gains, shifts, mask_vec, chosen, live)
        decoded, pullback = jax.vjp(forward, source_row.astype(jnp.float32), target_row.astype(jnp.float32), weights, norm_gains, norm_shifts, mask_vector)
        factor = (STEPS + 1 - timestep).astype(jnp.float32) / STEPS
        grad_out = cotangent_row.astype(jnp.float32) * (factor * loss_row.astype(jnp.float32))[:, None]
        source_g, target_g, weight_g, gain_g, shift_g, mask_g = pullback(grad_out)
        running = jax.tree.map(jnp.add, running, (weight_g, gain_g, shift_g, mask_g))
        return (running, (decoded.astype(jnp.bfloat16), source_g.astype(jnp.bfloat16), target_g.astype(jnp.bfloat16)))
    start = jax.tree.map(jnp.zeros_like, (weights, norm_gains, norm_shifts, mask_vector))
    totals, stacked = lax.scan(one_pair, start, (source, target, cotangent, lengths, timesteps, masked, loss_mask))
    wsum = totals[0]
    return (stacked[0], stacked[1], stacked[2], wsum[0], wsum[1], wsum[2], wsum[3], wsum[4], wsum[5], wsum[6], wsum[7], wsum[8], wsum[9], wsum[10], wsum[11], wsum[12], wsum[13], wsum[14], wsum[15], totals[1], totals[2], totals[3])
```

```python
import jax
import jax.numpy as jnp
from jax import lax
from jax.experimental import pallas as pl
from jax.experimental.pallas import tpu as pltpu
from jax.sharding import PartitionSpec as P

HD = 64
MICRO = 2
STEPS = 50


eps = 1e-05
floor_score = -1e30


def norm_rows(inputs, gain, shift):
    average = jnp.mean(inputs, axis=-1, keepdims=True)
    centred = inputs - average
    second = jnp.mean(centred * centred, axis=-1, keepdims=True)
    return centred * lax.rsqrt(second + eps) * gain + shift


def norm_back(inputs, gain, shift, gradient):
    unused, pullback = jax.vjp(norm_rows, inputs, gain, shift)
    return pullback(gradient)


def smooth(values):
    return jax.nn.gelu(values, approximate=False)


def spread(inputs):
    return lax.all_gather(inputs.astype(jnp.bfloat16), "tensor", axis=1, tiled=True)


def collect(partial_value):
    return lax.psum_scatter(partial_value, "tensor", scatter_dimension=1, tiled=True)


def spread_grad(gradient):
    return lax.all_gather(gradient.astype(jnp.bfloat16), "tensor", axis=1, tiled=True)


def collect_grad(partial_value):
    return lax.psum_scatter(partial_value, "tensor", scatter_dimension=1, tiled=True)


def project(inputs, weight):
    return jnp.einsum("bsk,kn->bsn", inputs, weight, preferred_element_type=jnp.float32)


def weight_grad(inputs, gradient):
    return jnp.einsum("bsk,bsn->kn", inputs, gradient, preferred_element_type=jnp.float32)


def back_project(gradient, weight):
    return jnp.einsum("bsn,kn->bsk", gradient, weight, preferred_element_type=jnp.float32)


def masked_scores(query_part, key_rows, live):
    scores = jnp.einsum(
        "bqhd,bkhd->bhqk", query_part, key_rows, preferred_element_type=jnp.float32
    ) * HD ** (-0.5)
    return jnp.where(live[:, None, None, :], scores, floor_score)


def attend_forward(query_in, keys_in, w_query, w_key, w_value, live):
    pair_count, length = (query_in.shape[0], query_in.shape[1])
    head_count = w_query.shape[1] // HD
    queries = (
        project(query_in, w_query).astype(jnp.bfloat16).reshape(pair_count, length, head_count, HD)
    )
    key_rows = (
        project(keys_in, w_key).astype(jnp.bfloat16).reshape(pair_count, length, head_count, HD)
    )
    value_rows = (
        project(keys_in, w_value).astype(jnp.bfloat16).reshape(pair_count, length, head_count, HD)
    )
    block_rows = min(512, length)
    pieces = []
    totals = []
    for offset in range(0, length, block_rows):
        scores = masked_scores(queries[:, offset : offset + block_rows], key_rows, live)
        highest = jnp.max(scores, axis=-1, keepdims=True)
        exponent = jnp.exp(scores - highest)
        summed = jnp.sum(exponent, axis=-1, keepdims=True)
        softmax = (exponent / summed).astype(jnp.bfloat16)
        pieces.append(
            jnp.einsum("bhqk,bkhd->bqhd", softmax, value_rows, preferred_element_type=jnp.float32)
        )
        totals.append(highest + jnp.log(summed))
    attended = (
        jnp.concatenate(pieces, axis=1)
        .astype(jnp.bfloat16)
        .reshape(pair_count, length, head_count * HD)
    )
    return (queries, key_rows, value_rows, attended, jnp.concatenate(totals, axis=2))


def attend_backward(whole_grad, query_in, keys_in, w_query, w_key, w_value, w_out, saved, live):
    queries, key_rows, value_rows, attended, totals = saved
    pair_count, length, head_count = (queries.shape[0], queries.shape[1], queries.shape[2])
    scale_score = HD ** (-0.5)
    out_grad = weight_grad(attended, whole_grad)
    head_grad = (
        back_project(whole_grad, w_out)
        .astype(jnp.bfloat16)
        .reshape(pair_count, length, head_count, HD)
    )
    block_rows = min(512, length)
    key_total = jnp.zeros(key_rows.shape, jnp.float32)
    value_total = jnp.zeros(value_rows.shape, jnp.float32)
    query_parts = []
    for offset in range(0, length, block_rows):
        query_part = queries[:, offset : offset + block_rows]
        grad_part = head_grad[:, offset : offset + block_rows]
        scores = masked_scores(query_part, key_rows, live)
        softmax = jnp.exp(scores - totals[:, :, offset : offset + block_rows])
        value_total = value_total + jnp.einsum(
            "bhqk,bqhd->bkhd",
            softmax.astype(jnp.bfloat16),
            grad_part,
            preferred_element_type=jnp.float32,
        )
        soft_grad = jnp.einsum(
            "bqhd,bkhd->bhqk", grad_part, value_rows, preferred_element_type=jnp.float32
        )
        inner = jnp.sum(softmax * soft_grad, axis=-1, keepdims=True)
        score_grad = (softmax * (soft_grad - inner)).astype(jnp.bfloat16)
        query_parts.append(
            jnp.einsum("bhqk,bkhd->bqhd", score_grad, key_rows, preferred_element_type=jnp.float32)
            * scale_score
        )
        key_total = (
            key_total
            + jnp.einsum(
                "bhqk,bqhd->bkhd", score_grad, query_part, preferred_element_type=jnp.float32
            )
            * scale_score
        )
    query_grad = (
        jnp.concatenate(query_parts, axis=1)
        .astype(jnp.bfloat16)
        .reshape(pair_count, length, head_count * HD)
    )
    key_grad = key_total.astype(jnp.bfloat16).reshape(
        pair_count, key_rows.shape[1], head_count * HD
    )
    value_grad = value_total.astype(jnp.bfloat16).reshape(
        pair_count, value_rows.shape[1], head_count * HD
    )
    grads = (
        weight_grad(query_in, query_grad),
        weight_grad(keys_in, key_grad),
        weight_grad(keys_in, value_grad),
        out_grad,
    )
    into_keys = back_project(key_grad, w_key) + back_project(value_grad, w_value)
    return (grads, back_project(query_grad, w_query), into_keys)


def feed_forward(inputs, w_up, w_down):
    lifted = project(inputs, w_up)
    active = smooth(lifted).astype(jnp.bfloat16)
    return (lifted, active, project(active, w_down))


def feed_backward(gradient, inputs, w_up, w_down, lifted, active):
    down_grad = weight_grad(active, gradient)
    active_grad = back_project(gradient, w_down)
    unused, smooth_back = jax.vjp(smooth, lifted)
    lifted_grad = smooth_back(active_grad)[0].astype(jnp.bfloat16)
    return ((weight_grad(inputs, lifted_grad), down_grad), back_project(lifted_grad, w_up))


def body(
    source,
    target,
    cotangent,
    lengths,
    timesteps,
    masked,
    loss_mask,
    enc_query,
    enc_key,
    enc_value,
    enc_out,
    enc_up,
    enc_down,
    self_query,
    self_key,
    self_value,
    self_out,
    cross_query,
    cross_key,
    cross_value,
    cross_out,
    dec_up,
    dec_down,
    norm_gains,
    norm_shifts,
    mask_vector,
):
    pairs_dev, rows_dev = (source.shape[0], source.shape[1])
    per_micro = pairs_dev // MICRO
    seq_len = rows_dev * lax.axis_size("tensor")
    positions = jnp.arange(seq_len)
    gains, shifts = (norm_gains, norm_shifts)
    gain_total = jnp.zeros(norm_gains.shape, jnp.float32)
    shift_total = jnp.zeros(norm_shifts.shape, jnp.float32)
    mask_total = jnp.zeros(mask_vector.shape, jnp.float32)
    decoded_parts = []
    source_parts = []
    target_parts = []
    running = None
    for micro in range(MICRO):
        weights = (
            lax.all_gather(enc_query, "dp", axis=0, tiled=True),
            lax.all_gather(enc_key, "dp", axis=0, tiled=True),
            lax.all_gather(enc_value, "dp", axis=0, tiled=True),
            lax.all_gather(enc_out, "dp", axis=1, tiled=True),
            lax.all_gather(enc_up, "dp", axis=0, tiled=True),
            lax.all_gather(enc_down, "dp", axis=1, tiled=True),
            lax.all_gather(self_query, "dp", axis=0, tiled=True),
            lax.all_gather(self_key, "dp", axis=0, tiled=True),
            lax.all_gather(self_value, "dp", axis=0, tiled=True),
            lax.all_gather(self_out, "dp", axis=1, tiled=True),
            lax.all_gather(cross_query, "dp", axis=0, tiled=True),
            lax.all_gather(cross_key, "dp", axis=0, tiled=True),
            lax.all_gather(cross_value, "dp", axis=0, tiled=True),
            lax.all_gather(cross_out, "dp", axis=1, tiled=True),
            lax.all_gather(dec_up, "dp", axis=0, tiled=True),
            lax.all_gather(dec_down, "dp", axis=1, tiled=True),
        )
        wide = (
            lax.all_gather(weights[4], "tensor", axis=1, tiled=True),
            lax.all_gather(weights[5], "tensor", axis=0, tiled=True),
            lax.all_gather(weights[14], "tensor", axis=1, tiled=True),
            lax.all_gather(weights[15], "tensor", axis=0, tiled=True),
        )
        lower = micro * per_micro
        upper = lower + per_micro
        live = positions[None, :] < lengths[lower:upper][:, None]
        every = jnp.ones((per_micro, seq_len), bool)
        inputs_x = source[lower:upper].astype(jnp.float32)
        rows0 = spread(norm_rows(inputs_x, gains[0], shifts[0]))
        saved0 = attend_forward(rows0, rows0, weights[0], weights[1], weights[2], live)
        stream1 = inputs_x + collect(project(saved0[3], weights[3]))
        normed1 = norm_rows(stream1, gains[1], shifts[1])
        rows1 = normed1.astype(jnp.bfloat16)
        lifted1, active1, partial1 = feed_forward(rows1, wide[0], wide[1])
        stream2 = stream1 + partial1
        memory_rows = spread(norm_rows(stream2, gains[2], shifts[2]))
        chosen = masked[lower:upper][:, :, None] == 1
        start_y = jnp.where(chosen, mask_vector, target[lower:upper].astype(jnp.float32))
        rows3 = spread(norm_rows(start_y, gains[3], shifts[3]))
        saved3 = attend_forward(rows3, rows3, weights[6], weights[7], weights[8], every)
        stream4 = start_y + collect(project(saved3[3], weights[9]))
        rows4 = spread(norm_rows(stream4, gains[4], shifts[4]))
        saved4 = attend_forward(rows4, memory_rows, weights[10], weights[11], weights[12], live)
        stream5 = stream4 + collect(project(saved4[3], weights[13]))
        normed5 = norm_rows(stream5, gains[5], shifts[5])
        rows5 = normed5.astype(jnp.bfloat16)
        lifted5, active5, partial5 = feed_forward(rows5, wide[2], wide[3])
        stream6 = stream5 + partial5
        decoded_parts.append(stream6.astype(jnp.bfloat16))
        factor = (STEPS + 1 - timesteps[lower:upper]).astype(jnp.float32) / STEPS
        grad6 = (
            cotangent[lower:upper].astype(jnp.float32)
            * (factor[:, None] * loss_mask[lower:upper].astype(jnp.float32))[:, :, None]
        )
        (up5, down5), into5 = feed_backward(
            grad6.astype(jnp.bfloat16), rows5, wide[2], wide[3], lifted5, active5
        )
        back5 = norm_back(stream5, gains[5], shifts[5], into5)
        grad5 = grad6 + back5[0]
        grads4, query_term4, memory_term = attend_backward(
            spread_grad(grad5),
            rows4,
            memory_rows,
            weights[10],
            weights[11],
            weights[12],
            weights[13],
            saved4,
            live,
        )
        back4 = norm_back(stream4, gains[4], shifts[4], collect_grad(query_term4))
        grad4 = grad5 + back4[0]
        memory_grad = collect_grad(memory_term)
        grads3, query_term3, keys_term3 = attend_backward(
            spread_grad(grad4),
            rows3,
            rows3,
            weights[6],
            weights[7],
            weights[8],
            weights[9],
            saved3,
            every,
        )
        back3 = norm_back(start_y, gains[3], shifts[3], collect_grad(query_term3 + keys_term3))
        grad_y = grad4 + back3[0]
        target_parts.append(jnp.where(chosen, 0.0, grad_y).astype(jnp.bfloat16))
        mask_total = mask_total + jnp.sum(jnp.where(chosen, grad_y, 0.0), axis=(0, 1))
        back2 = norm_back(stream2, gains[2], shifts[2], memory_grad)
        grad2 = back2[0]
        (up1, down1), into1 = feed_backward(
            grad2.astype(jnp.bfloat16), rows1, wide[0], wide[1], lifted1, active1
        )
        back1 = norm_back(stream1, gains[1], shifts[1], into1)
        grad1 = grad2 + back1[0]
        grads0, query_term0, keys_term0 = attend_backward(
            spread_grad(grad1),
            rows0,
            rows0,
            weights[0],
            weights[1],
            weights[2],
            weights[3],
            saved0,
            live,
        )
        back0 = norm_back(inputs_x, gains[0], shifts[0], collect_grad(query_term0 + keys_term0))
        source_parts.append((grad1 + back0[0]).astype(jnp.bfloat16))
        gain_total = gain_total + jnp.stack(
            [back0[1], back1[1], back2[1], back3[1], back4[1], back5[1]]
        )
        shift_total = shift_total + jnp.stack(
            [back0[2], back1[2], back2[2], back3[2], back4[2], back5[2]]
        )
        up1, down1, up5, down5 = (
            lax.psum_scatter(
                up1.astype(jnp.bfloat16), "tensor", scatter_dimension=1, tiled=True
            ).astype(jnp.float32),
            lax.psum_scatter(
                down1.astype(jnp.bfloat16), "tensor", scatter_dimension=0, tiled=True
            ).astype(jnp.float32),
            lax.psum_scatter(
                up5.astype(jnp.bfloat16), "tensor", scatter_dimension=1, tiled=True
            ).astype(jnp.float32),
            lax.psum_scatter(
                down5.astype(jnp.bfloat16), "tensor", scatter_dimension=0, tiled=True
            ).astype(jnp.float32),
        )
        fresh = (
            grads0[0],
            grads0[1],
            grads0[2],
            grads0[3],
            up1,
            down1,
            grads3[0],
            grads3[1],
            grads3[2],
            grads3[3],
            grads4[0],
            grads4[1],
            grads4[2],
            grads4[3],
            up5,
            down5,
        )
        running = fresh if micro == 0 else jax.tree.map(jnp.add, running, tuple(fresh))
    running = (
        lax.psum_scatter(
            running[0].astype(jnp.bfloat16), "dp", scatter_dimension=0, tiled=True
        ).astype(jnp.float32),
        lax.psum_scatter(
            running[1].astype(jnp.bfloat16), "dp", scatter_dimension=0, tiled=True
        ).astype(jnp.float32),
        lax.psum_scatter(
            running[2].astype(jnp.bfloat16), "dp", scatter_dimension=0, tiled=True
        ).astype(jnp.float32),
        lax.psum_scatter(
            running[3].astype(jnp.bfloat16), "dp", scatter_dimension=1, tiled=True
        ).astype(jnp.float32),
        lax.psum_scatter(
            running[4].astype(jnp.bfloat16), "dp", scatter_dimension=0, tiled=True
        ).astype(jnp.float32),
        lax.psum_scatter(
            running[5].astype(jnp.bfloat16), "dp", scatter_dimension=1, tiled=True
        ).astype(jnp.float32),
        lax.psum_scatter(
            running[6].astype(jnp.bfloat16), "dp", scatter_dimension=0, tiled=True
        ).astype(jnp.float32),
        lax.psum_scatter(
            running[7].astype(jnp.bfloat16), "dp", scatter_dimension=0, tiled=True
        ).astype(jnp.float32),
        lax.psum_scatter(
            running[8].astype(jnp.bfloat16), "dp", scatter_dimension=0, tiled=True
        ).astype(jnp.float32),
        lax.psum_scatter(
            running[9].astype(jnp.bfloat16), "dp", scatter_dimension=1, tiled=True
        ).astype(jnp.float32),
        lax.psum_scatter(
            running[10].astype(jnp.bfloat16), "dp", scatter_dimension=0, tiled=True
        ).astype(jnp.float32),
        lax.psum_scatter(
            running[11].astype(jnp.bfloat16), "dp", scatter_dimension=0, tiled=True
        ).astype(jnp.float32),
        lax.psum_scatter(
            running[12].astype(jnp.bfloat16), "dp", scatter_dimension=0, tiled=True
        ).astype(jnp.float32),
        lax.psum_scatter(
            running[13].astype(jnp.bfloat16), "dp", scatter_dimension=1, tiled=True
        ).astype(jnp.float32),
        lax.psum_scatter(
            running[14].astype(jnp.bfloat16), "dp", scatter_dimension=0, tiled=True
        ).astype(jnp.float32),
        lax.psum_scatter(
            running[15].astype(jnp.bfloat16), "dp", scatter_dimension=1, tiled=True
        ).astype(jnp.float32),
    )
    vectors = lax.psum((gain_total, shift_total, mask_total), ("dp", "tensor"))
    return (
        jnp.concatenate(decoded_parts, axis=0),
        jnp.concatenate(source_parts, axis=0),
        jnp.concatenate(target_parts, axis=0),
        running[0],
        running[1],
        running[2],
        running[3],
        running[4],
        running[5],
        running[6],
        running[7],
        running[8],
        running[9],
        running[10],
        running[11],
        running[12],
        running[13],
        running[14],
        running[15],
        vectors[0],
        vectors[1],
        vectors[2],
    )


F32 = jnp.float32
BF = jnp.bfloat16
LOG2E = 1.4426950408889634
LN2 = 0.6931471805599453
NN = (((1,), (0,)), ((), ()))
NT = (((1,), (1,)), ((), ()))
MESH = pl.DeviceIdType.MESH
RB = 256
VMEM_LIMIT = 62 * 2**20


def dg(left, right, dims=NN):
    return lax.dot_general(left, right, dims, preferred_element_type=F32)


def ln_hat(x):
    centred = x - jnp.mean(x, axis=-1, keepdims=True)
    rstd = lax.rsqrt(jnp.mean(centred * centred, axis=-1, keepdims=True) + eps)
    return centred * rstd, rstd


def ln_back(x, gain, gradient):
    hat, rstd = ln_hat(x)
    scaled = gradient * gain
    first = jnp.mean(scaled, axis=-1, keepdims=True)
    second = jnp.mean(scaled * hat, axis=-1, keepdims=True)
    dx = rstd * (scaled - first - hat * second)
    dgain = jnp.sum(gradient * hat, axis=0, keepdims=True)
    dshift = jnp.sum(gradient, axis=0, keepdims=True)
    return dx, dgain, dshift


def gelu_both(u):
    size = jnp.abs(u)
    t = 1.0 / (1.0 + (0.3275911 * 0.7071067811865476) * size)
    ex = jnp.exp2(u * u * (-0.5 * LOG2E))
    poly = t * (
        0.127414796
        + t * (-0.142248368 + t * (0.7107068705 + t * (-0.7265760135 + t * 0.5307027145)))
    )
    tail = poly * ex
    phi = jnp.where(u > 0, 1.0 - tail, tail)
    return u * phi, phi + u * ex * 0.3989422804014327


def rows_loop(total, step, run):
    def once(i, carry):
        run(pl.ds(pl.multiple_of(i * step, step), step))
        return carry

    lax.fori_loop(0, total // step, once, 0)


def load_weight(w_hbm, offset, width, dst, sems, base):
    copies = []
    for t in range(2):
        cp = pltpu.make_async_copy(
            w_hbm.at[t, :, pl.ds(offset, width)],
            dst.at[:, pl.ds(t * width, width)],
            sems.at[base + t],
        )
        cp.start()
        copies.append(cp)
    return copies


def store_grad(src, g_hbm, offset, width, sems, base):
    copies = []
    for t in range(2):
        cp = pltpu.make_async_copy(
            src.at[:, pl.ds(t * width, width)],
            g_hbm.at[t, :, pl.ds(offset, width)],
            sems.at[base + t],
        )
        cp.start()
        copies.append(cp)
    return copies


def wait_all(copies):
    for cp in copies:
        cp.wait()


def attn_project(x, gain, shift, kv, wq, wk, wv, a, q, k, v):
    def run(sl):
        hat, unused = ln_hat(x[sl, :].astype(F32))
        rows = (hat * gain + shift).astype(BF)
        a[sl, :] = rows
        q[sl, :] = (dg(rows, wq[...]) * (LOG2E * HD**-0.5)).astype(BF)
        keys_in = rows if kv is None else kv[sl, :]
        k[sl, :] = dg(keys_in, wk[...]).astype(BF)
        v[sl, :] = dg(keys_in, wv[...]).astype(BF)

    rows_loop(x.shape[0], RB, run)


def attn_core(length, q, k, v, o, ol, r, e_hbm, ebuf, esem):
    seq = q.shape[0]
    pairs = q.shape[1] // 128
    block = 512
    lane = lax.broadcasted_iota(jnp.int32, (1, 128), 1)
    low = lane < 64
    one = jnp.ones((), BF)
    key = lax.broadcasted_iota(jnp.int32, (seq, 1), 0)
    bias = jnp.where(key < length, 0.0, floor_score).astype(F32)

    def out(head, h, b):
        sl = pl.ds(b * block, block)
        return pltpu.make_async_copy(ebuf.at[h, sl, :], e_hbm.at[head, sl, :], esem.at[h, b])

    def pair(p, carry):
        cols = pl.ds(pl.multiple_of(p * 128, 128), 128)
        kp = k[:, cols].astype(F32)
        vp = v[:, cols]
        parts = []
        for h in range(2):
            if h == 0:
                ka = jnp.where(low, kp, jnp.where(lane == 64, bias, 0.0)).astype(BF)
                va = jnp.where(low, vp, one)
            else:
                ka = jnp.where(low, jnp.where(lane == 0, bias, 0.0), kp).astype(BF)
                va = jnp.where(low, one, vp)
            for b in range(seq // block):
                sl = pl.ds(b * block, block)

                @pl.when(p > 0)
                def unused_wait():
                    out(2 * p - 2 + h, h, b).wait()

                qp = q[sl, cols]
                qm = jnp.where(low, qp, one) if h == 0 else jnp.where(low, one, qp)
                s = dg(qm, ka, NT)
                e = jnp.exp2(s - jnp.max(s, axis=-1, keepdims=True)).astype(BF)
                ebuf[h, sl, :] = e
                out(2 * p + h, h, b).start()
                parts.append(dg(e, va))
        for b in range(seq // block):
            sl = pl.ds(b * block, block)
            first, second = parts[b], parts[seq // block + b]
            un = jnp.where(low, first, second)
            sums = pltpu.roll(jnp.where(low, second, first), 64, 1)
            inverse = 1.0 / sums
            r[sl, cols] = inverse.astype(BF)
            joined = un * inverse
            rounded = joined.astype(BF)
            o[sl, cols] = rounded
            ol[sl, cols] = (joined - rounded.astype(F32)).astype(BF)
        return carry

    lax.fori_loop(0, pairs, pair, 0)
    for h in range(2):
        for b in range(seq // block):
            out(2 * pairs - 2 + h, h, b).wait()


def attn_join(x, o, wo, y):
    def run(sl):
        y[sl, :] = x[sl, :].astype(F32) + dg(o[sl, :], wo[...], NT)

    rows_loop(x.shape[0], RB, run)


def attn_back_core(q, k, v, do, o, ol, e_hbm, ebuf, esem, ds, dq, dk, dv):
    seq = q.shape[0]
    heads = e_hbm.shape[0]
    block = 512
    lane = lax.broadcasted_iota(jnp.int32, (1, 128), 1)
    low = lane < 64
    zero = jnp.zeros((), BF)
    one = jnp.ones((), BF)
    row2 = lax.broadcasted_iota(jnp.int32, (256, 128), 0)
    col2 = lax.broadcasted_iota(jnp.int32, (256, 128), 1)
    swap = jnp.where(((row2 // 64) % 2) != (col2 // 64), 1.0, 0.0).astype(BF)

    def fetch(head, h):
        copies = []
        for b in range(seq // block):
            sl = pl.ds(b * block, block)
            copies.append(
                pltpu.make_async_copy(e_hbm.at[head, sl, :], ebuf.at[h, sl, :], esem.at[h, b])
            )
        return copies

    for cp in fetch(0, 0):
        cp.start()

    def pair(p, carry):
        cols = pl.ds(pl.multiple_of(p * 128, 128), 128)
        qp, kp, vp, dop = q[:, cols], k[:, cols], v[:, cols], do[:, cols]
        product = dop.astype(F32) * (o[:, cols].astype(F32) + ol[:, cols].astype(F32))
        high = product.astype(BF)
        rest = (product - high.astype(F32)).astype(BF)
        inner = -dg(jnp.concatenate([high, rest], axis=1), swap)
        inner_high = inner.astype(BF)
        inner_rest = (inner - inner_high.astype(F32)).astype(BF)
        do_t, q_t = dop.T, qp.T
        dq_sum = None
        dks, dvs = [], []
        for h in range(2):
            head = 2 * p + h

            @pl.when(head + 1 < heads)
            def unused_fetch():
                for cp in fetch(head + 1, 1 - h):
                    cp.start()

            if h == 0:
                lhs = jnp.where(low, dop, jnp.where(lane == 64, inner_high, inner_rest))
                va = jnp.where(low, vp, jnp.where(lane < 66, one, zero))
                km = jnp.where(low, kp, zero)
            else:
                lhs = jnp.where(low, jnp.where(lane == 0, inner_high, inner_rest), dop)
                va = jnp.where(low, jnp.where(lane < 2, one, zero), vp)
                km = jnp.where(low, zero, kp)
            for cp in fetch(head, h):
                cp.wait()
            for b in range(seq // block):
                sl = pl.ds(b * block, block)
                t = dg(lhs[b * block : (b + 1) * block], va, NT)
                ds[h, sl, :] = ebuf[h, sl, :] * t.astype(BF)
            part = dg(ds[h], km)
            dq_sum = part if dq_sum is None else dq_sum + part
            dks.append(dg(q_t[64 * h : 64 * h + 64], ds[h]))
            dvs.append(dg(do_t[64 * h : 64 * h + 64], ebuf[h]))
        dq[:, cols] = (dq_sum * HD**-0.5).astype(BF)
        dk[:, cols] = (jnp.concatenate(dks, axis=0) * LN2).astype(BF).T
        dv[:, cols] = jnp.concatenate(dvs, axis=0).astype(BF).T
        return carry

    lax.fori_loop(0, heads // 2, pair, 0)


def enc_forward(
    len_ref, gains, shifts, x_hbm, w_hbm,
    a0_o, q0_o, k0_o, v0_o, o0_o, ol0_o, r0_o, e0_o, x1_o, a1_o, h1_o, gp1_o, x2_o, mem_o,
    x, wq, wk, wv, wo, wu, wd, a0, q, k, v, o, ol, r, x1, a1, h, gp, x2, mem, ebuf,
    xsem, wsem, esem, osem,
):
    n1, n2 = wq.shape[1] // 2, wu.shape[1] // 2
    cx = pltpu.make_async_copy(x_hbm, x, xsem.at[0])
    cx.start()
    loads = []
    offset = 0
    for i, (w, n) in enumerate(((wq, n1), (wk, n1), (wv, n1), (wo, n1), (wu, n2), (wd, n2))):
        loads.append(load_weight(w_hbm, offset, n, w, wsem, 2 * i))
        offset += n
    cx.wait()
    for i in range(3):
        wait_all(loads[i])
    saved = []

    def save(src, dst):
        cp = pltpu.make_async_copy(src, dst, osem.at[len(saved)])
        cp.start()
        saved.append(cp)

    attn_project(x, gains[0:1, :], shifts[0:1, :], None, wq, wk, wv, a0, q, k, v)
    save(a0, a0_o)
    save(q, q0_o)
    save(k, k0_o)
    save(v, v0_o)
    attn_core(len_ref[0], q, k, v, o, ol, r, e0_o, ebuf, esem)
    save(o, o0_o)
    save(ol, ol0_o)
    save(r, r0_o)
    wait_all(loads[3])
    attn_join(x, o, wo, x1)
    save(x1, x1_o)
    wait_all(loads[4])
    wait_all(loads[5])

    def run(sl):
        stream = x1[sl, :]
        hat, unused = ln_hat(stream)
        rows = (hat * gains[1:2, :] + shifts[1:2, :]).astype(BF)
        a1[sl, :] = rows
        active, slope = gelu_both(dg(rows, wu[...]))
        active = active.astype(BF)
        h[sl, :] = active
        gp[sl, :] = slope.astype(BF)
        out = stream + dg(active, wd[...], NT)
        x2[sl, :] = out
        hat, unused = ln_hat(out)
        mem[sl, :] = (hat * gains[2:3, :] + shifts[2:3, :]).astype(BF)

    rows_loop(x.shape[0], RB, run)
    save(a1, a1_o)
    save(h, h1_o)
    save(gp, gp1_o)
    save(x2, x2_o)
    save(mem, mem_o)
    wait_all(saved)


def attn_backward(
    g, x, gain, ng, index, a_t, kv_t, g_t, wq, wk, wv, wo, q, k, v, o, ol, r, e_hbm, ebuf, esem, ds,
    do, dq, dk, dv, stage, slot, free, emit, into_keys, finish,
):
    seq = x.shape[0]

    def before(sl):
        rows = g[sl, :].astype(BF)
        g_t[:, sl] = rows.T
        do[sl, :] = (dg(rows, wo[...]) * r[sl, :].astype(F32)).astype(BF)

    rows_loop(seq, RB, before)
    free(slot + 3)
    stage[slot + 3] = dg(g_t[...], o[...]).astype(BF)
    emit(slot + 3)
    attn_back_core(q, k, v, do, o, ol, e_hbm, ebuf, esem, ds, dq, dk, dv)
    free(slot)
    stage[slot] = dg(a_t[...], dq[...]).astype(BF)
    emit(slot)
    free(slot + 1)
    stage[slot + 1] = dg(kv_t[...], dk[...]).astype(BF)
    emit(slot + 1)
    free(slot + 2)
    stage[slot + 2] = dg(kv_t[...], dv[...]).astype(BF)
    emit(slot + 2)

    def after(sl):
        into = dg(dq[sl, :], wq[...], NT)
        keys = dg(dk[sl, :], wk[...], NT) + dg(dv[sl, :], wv[...], NT)
        if into_keys is None:
            into = into + keys
        else:
            into_keys[sl, :] = keys
        dx, dgain, dshift = ln_back(x[sl, :].astype(F32), gain, into)
        ng[index : index + 1, :] += dgain
        ng[8 + index : 9 + index, :] += dshift
        finish(sl, g[sl, :] + dx)

    rows_loop(seq, RB, after)


def dec_both(
    len_ref, gains, shifts, y0_hbm, g3_hbm, mem_hbm, w_hbm,
    dec_o, gy_o, ge_o, grad_o, ng, e3_o, e4_o,
    y0, g3, mem, sq, sk, sv, so, cq, ck, cv, co, wu, wd, a3, q3, k3, v3, o3, ol3, r3, y1, a4, q4, k4, v4,
    o4, ol4, r4, y2, a5, big, gs, do, a_t, kv_t, g_t, dec, stage, ebuf,
    xsem, wsem, esem, osem,
):
    seq, width = y0.shape
    n1, n2 = sq.shape[1] // 2, wu.shape[1] // 2
    ins = []
    for i, (src, dst) in enumerate(((y0_hbm, y0), (mem_hbm, mem), (g3_hbm, g3))):
        cp = pltpu.make_async_copy(src, dst, xsem.at[i])
        cp.start()
        ins.append(cp)
    loads = []
    start = 4 * n1 + 2 * n2
    offset = start
    for i, (w, n) in enumerate(
        ((sq, n1), (sk, n1), (sv, n1), (so, n1), (cq, n1), (ck, n1), (cv, n1), (co, n1), (wu, n2), (wd, n2))
    ):
        loads.append(load_weight(w_hbm, offset, n, w, wsem, 2 * i))
        offset += n
    ng[...] = jnp.zeros_like(ng)
    ins[0].wait()
    for i in range(3):
        wait_all(loads[i])
    attn_project(y0, gains[3:4, :], shifts[3:4, :], None, sq, sk, sv, a3, q3, k3, v3)
    attn_core(seq, q3, k3, v3, o3, ol3, r3, e3_o, ebuf, esem)
    wait_all(loads[3])
    attn_join(y0, o3, so, y1)
    ins[1].wait()
    for i in range(4, 7):
        wait_all(loads[i])
    attn_project(y1, gains[4:5, :], shifts[4:5, :], mem, cq, ck, cv, a4, q4, k4, v4)
    attn_core(len_ref[0], q4, k4, v4, o4, ol4, r4, e4_o, ebuf, esem)
    wait_all(loads[7])
    attn_join(y1, o4, co, y2)
    ins[2].wait()
    wait_all(loads[8])
    wait_all(loads[9])
    save = Saver(osem)
    h, du = big.at[0], big.at[1]

    def feed(sl):
        stream = y2[sl, :]
        hat, unused = ln_hat(stream)
        rows = (hat * gains[5:6, :] + shifts[5:6, :]).astype(BF)
        a_t[:, sl] = rows.T
        active, slope = gelu_both(dg(rows, wu[...]))
        active = active.astype(BF)
        h[sl, :] = active
        dec[sl, :] = (stream + dg(active, wd[...], NT)).astype(BF)
        grad = g3[sl, :]
        g_t[:, sl] = grad.T
        lifted = (dg(grad, wd[...]) * slope).astype(BF)
        du[sl, :] = lifted
        into = dg(lifted, wu[...], NT)
        dx, dgain, dshift = ln_back(stream, gains[5:6, :], into)
        ng[5:6, :] += dgain
        ng[13:14, :] += dshift
        gs[sl, :] = grad.astype(F32) + dx

    rows_loop(seq, RB, feed)
    save(dec, dec_o, "dec")
    parts = 2 * n2 // width

    def emit_part(src_slot, offset, n, lower):
        done = 0
        while done < width:
            t = (lower + done) // n
            at = (lower + done) % n
            take = min(width - done, n - at)
            save(
                stage.at[src_slot, :, pl.ds(done, take)],
                grad_o.at[t, :, pl.ds(offset + at, take)],
                src_slot,
            )
            done += take

    ff_offset = 8 * n1
    for j in range(parts):
        cols = pl.ds(j * width, width)
        stage[j] = dg(a_t[...], du[:, cols]).astype(BF)
        emit_part(j, ff_offset, n2, j * width)
        stage[parts + j] = dg(g_t[...], h[:, cols]).astype(BF)
        emit_part(parts + j, ff_offset + n2, n2, j * width)

    def emit(slot):
        emit_part(slot, slot * n1, n1, 0)

    ds = big.at[0]
    ds_view = big.at[0]
    dq, dk, dv = (big.at[1, :, pl.ds(i * width, width)] for i in range(3))
    a_t[...] = a4[...].T
    kv_t[...] = mem[...].T

    def keep(sl, gradient):
        gs[sl, :] = gradient

    attn_backward(
        gs, y1, gains[4:5, :], ng, 4, a_t, kv_t, g_t, cq, ck, cv, co, q4, k4, v4, o4, ol4, r4, e4_o,
        ebuf, esem, SplitColumns(ds_view, seq), do, dq, dk, dv, stage, 4, save.free, emit, y2, keep,
    )
    save(y2, ge_o)
    a_t[...] = a3[...].T

    def last(sl, gradient):
        dec[sl, :] = gradient.astype(BF)

    save.free("dec")
    attn_backward(
        gs, y0, gains[3:4, :], ng, 3, a_t, a_t, g_t, sq, sk, sv, so, q3, k3, v3, o3, ol3, r3, e3_o,
        ebuf, esem, SplitColumns(ds_view, seq), do, dq, dk, dv, stage, 0, save.free, emit, None, last,
    )
    save(dec, gy_o)
    save.finish()


class Saver:
    def __init__(self, sems):
        self.sems, self.count, self.live = sems, 0, []

    def __call__(self, src, dst, slot=None):
        cp = pltpu.make_async_copy(src, dst, self.sems.at[self.count])
        cp.start()
        self.count += 1
        self.live.append((slot, cp))

    def free(self, slot):
        for name, cp in self.live:
            if name == slot:
                cp.wait()
        self.live = [entry for entry in self.live if entry[0] != slot]

    def finish(self):
        for name, cp in self.live:
            cp.wait()
        self.live = []


class SplitColumns:
    def __init__(self, ref, n):
        self.ref, self.n = ref, n

    def cols(self, h):
        return pl.ds(h * self.n, self.n)

    def __getitem__(self, h):
        return self.ref[:, self.cols(h)]

    def __setitem__(self, key, value):
        h, sl, unused = key
        self.ref[sl, self.cols(h)] = value


def enc_backward(
    gains, shifts, ge_hbm, x_hbm, x1_hbm, x2_hbm, a0_hbm, q0_hbm, k0_hbm, v0_hbm, o0_hbm, ol0_hbm, r0_hbm,
    a1_hbm, h1_hbm, gp1_hbm, e0_hbm, w_hbm,
    sg_o, grad_o, ng,
    ge, x, x1, x2, a0, q, k, v, o, ol, r, a1, big, wq, wk, wv, wo, wu, wd, gs, do, a_t, g_t, sg, stage, ebuf,
    xsem, wsem, esem, osem,
):
    seq, width = x.shape
    n1, n2 = wq.shape[1] // 2, wu.shape[1] // 2
    ins = {}
    order = (
        ("ge", ge_hbm, ge), ("x2", x2_hbm, x2), ("gp", gp1_hbm, big.at[1]), ("x1", x1_hbm, x1),
        ("a1", a1_hbm, a1), ("h", h1_hbm, big.at[0]), ("o", o0_hbm, o), ("ol", ol0_hbm, ol), ("r", r0_hbm, r),
        ("q", q0_hbm, q), ("k", k0_hbm, k), ("v", v0_hbm, v), ("a0", a0_hbm, a0), ("x", x_hbm, x),
    )
    loads = {}

    def begin(names):
        for i, (name, src, dst) in enumerate(order):
            if name in names:
                cp = pltpu.make_async_copy(src, dst, xsem.at[i])
                cp.start()
                ins[name] = cp

    begin(("ge", "x2", "gp", "x1"))
    offsets = (0, n1, 2 * n1, 3 * n1, 4 * n1, 4 * n1 + n2)
    for i, w in ((5, wd), (4, wu)):
        loads[i] = load_weight(w_hbm, offsets[i], n2, w, wsem, 2 * i)
    begin(("a1", "h", "o", "ol", "r", "q", "k", "v", "a0", "x"))
    for i, w in ((3, wo), (0, wq), (1, wk), (2, wv)):
        loads[i] = load_weight(w_hbm, offsets[i], n1, w, wsem, 2 * i)
    ng[...] = jnp.zeros_like(ng)
    for name in ("ge", "x2", "gp", "x1"):
        ins[name].wait()
    wait_all(loads[5])
    wait_all(loads[4])
    h, du = big.at[0], big.at[1]
    save = Saver(osem)

    def feed(sl):
        dx, dgain, dshift = ln_back(x2[sl, :], gains[2:3, :], ge[sl, :])
        ng[2:3, :] += dgain
        ng[10:11, :] += dshift
        grad = dx.astype(BF)
        g_t[:, sl] = grad.T
        lifted = (dg(grad, wd[...]) * du[sl, :].astype(F32)).astype(BF)
        du[sl, :] = lifted
        into = dg(lifted, wu[...], NT)
        dx1, dgain, dshift = ln_back(x1[sl, :], gains[1:2, :], into)
        ng[1:2, :] += dgain
        ng[9:10, :] += dshift
        gs[sl, :] = dx + dx1

    rows_loop(seq, RB, feed)
    parts = 2 * n2 // width

    def emit_part(src_slot, offset, n, lower):
        done = 0
        while done < width:
            t = (lower + done) // n
            at = (lower + done) % n
            take = min(width - done, n - at)
            save(
                stage.at[src_slot, :, pl.ds(done, take)],
                grad_o.at[t, :, pl.ds(offset + at, take)],
            )
            done += take

    ins["a1"].wait()
    ins["h"].wait()
    a_t[...] = a1[...].T
    for j in range(parts):
        cols = pl.ds(j * width, width)
        stage[4 + j] = dg(a_t[...], du[:, cols]).astype(BF)
        emit_part(4 + j, 4 * n1, n2, j * width)
        stage[4 + parts + j] = dg(g_t[...], h[:, cols]).astype(BF)
        emit_part(4 + parts + j, 4 * n1 + n2, n2, j * width)
    for name in ("o", "ol", "r", "q", "k", "v", "a0", "x"):
        ins[name].wait()
    for i in range(4):
        wait_all(loads[i])
    a_t[...] = a0[...].T

    def emit(slot):
        emit_part(slot, slot * n1, n1, 0)

    def last(sl, gradient):
        sg[sl, :] = gradient.astype(BF)

    dq, dk, dv = (big.at[1, :, pl.ds(i * width, width)] for i in range(3))
    attn_backward(
        gs, x, gains[0:1, :], ng, 0, a_t, a_t, g_t, wq, wk, wv, wo, q, k, v, o, ol, r, e0_hbm,
        ebuf, esem, SplitColumns(big.at[0], seq), do, dq, dk, dv, stage, 0, save.free, emit, None, last,
    )
    save(sg, sg_o)
    save.finish()


def compute_all(length, gains, shifts, x, y0, g3, weights):
    seq, width = x.shape
    total = weights.shape[2]
    n1 = width // 2
    n2 = (total - 12 * n1) // 4
    hidden = 2 * n2
    heads = width // HD
    sd = jax.ShapeDtypeStruct
    any_spec = pl.BlockSpec(memory_space=pl.ANY)
    vmem = pl.BlockSpec(memory_space=pltpu.VMEM)
    smem = pl.BlockSpec(memory_space=pltpu.SMEM)
    dma = pltpu.SemaphoreType.DMA
    row = lambda kind: sd((seq, width), kind)
    tall = lambda kind: sd((seq, hidden), kind)
    escores = sd((heads, seq, seq), BF)
    vrow = lambda kind: pltpu.VMEM((seq, width), kind)
    vsq = pltpu.VMEM((width, width), BF)
    vwide = pltpu.VMEM((width, hidden), BF)
    vtall = pltpu.VMEM((seq, hidden), BF)
    params = pltpu.CompilerParams(vmem_limit_bytes=VMEM_LIMIT)
    (a0, q0, k0, v0, o0, ol0, r0, e0, x1, a1, h1, gp1, x2, mem) = pl.pallas_call(
        enc_forward,
        in_specs=[smem, vmem, vmem, any_spec, any_spec],
        out_specs=[any_spec] * 14,
        out_shape=[row(BF)] * 7 + [escores, row(F32), row(BF), tall(BF), tall(BF), row(F32), row(BF)],
        scratch_shapes=[vrow(BF)] + [vsq] * 4 + [vwide] * 2 + [vrow(BF)] * 7
        + [vrow(F32), vrow(BF), vtall, vtall, vrow(F32), vrow(BF), pltpu.VMEM((2, seq, seq), BF)]
        + [dma((1,)), dma((12,)), dma((2, 2)), dma((13,))],
        compiler_params=params,
        name="enc_forward",
    )(length, gains, shifts, x, weights)
    slots = max(8, 2 * (hidden // width))
    dec, gy, ge, gdec, ng_dec, unused3, unused4 = pl.pallas_call(
        dec_both,
        in_specs=[smem, vmem, vmem] + [any_spec] * 4,
        out_specs=[any_spec] * 4 + [vmem, any_spec, any_spec],
        out_shape=[row(BF), row(BF), row(F32), sd((2, width, 8 * n1 + 2 * n2), BF), sd((16, width), F32)]
        + [escores] * 2,
        scratch_shapes=[vrow(BF)] * 3 + [vsq] * 8 + [vwide] * 2 + [vrow(BF)] * 7 + [vrow(F32)]
        + [vrow(BF)] * 7 + [vrow(F32), vrow(BF), pltpu.VMEM((2, seq, hidden), BF), vrow(F32), vrow(BF)]
        + [pltpu.VMEM((width, seq), BF)] * 3 + [vrow(BF), pltpu.VMEM((slots, width, width), BF)]
        + [pltpu.VMEM((2, seq, seq), BF)]
        + [dma((3,)), dma((20,)), dma((2, 2)), dma((3 + 4 * slots,))],
        compiler_params=params,
        name="dec_both",
    )(length, gains, shifts, y0, g3, mem, weights)
    slots = 4 + 2 * (hidden // width)
    sg, genc, ng_enc = pl.pallas_call(
        enc_backward,
        in_specs=[vmem, vmem] + [any_spec] * 16,
        out_specs=[any_spec] * 2 + [vmem],
        out_shape=[row(BF), sd((2, width, 4 * n1 + 2 * n2), BF), sd((16, width), F32)],
        scratch_shapes=[vrow(F32), vrow(BF), vrow(F32), vrow(F32)] + [vrow(BF)] * 8
        + [pltpu.VMEM((2, seq, hidden), BF)] + [vsq] * 4 + [vwide] * 2 + [vrow(F32), vrow(BF)]
        + [pltpu.VMEM((width, seq), BF)] * 2 + [vrow(BF), pltpu.VMEM((slots, width, width), BF)]
        + [pltpu.VMEM((2, seq, seq), BF)]
        + [dma((14,)), dma((12,)), dma((2, 2)), dma((3 + 4 * slots,))],
        compiler_params=params,
        name="enc_backward",
    )(gains, shifts, ge, x, x1, x2, a0, q0, k0, v0, o0, ol0, r0, a1, h1, gp1, e0, weights)
    return dec, sg, gy, genc, gdec, ng_enc + ng_dec


def places():
    d = lax.axis_index("dp")
    return lax.axis_index("tensor"), d // 4, (d // 2) % 2, d % 2


def at(t, z, y, c):
    return (z * 4 + y * 2 + c, t)


def greet(partners):
    barrier = pltpu.get_barrier_semaphore()
    for device in partners:
        pl.semaphore_signal(barrier, inc=1, device_id=device, device_id_type=MESH)
    pl.semaphore_wait(barrier, len(partners))


def all_partners(t, z, y, c):
    others = [at(t, lax.rem(z + j, 4), y, c) for j in range(1, 4)]
    return [at(t, z, y, 1 - c), at(1 - t, z, y, c), at(t, z, 1 - y, c)] + others


CHUNK = 1024


def gather_weights(own, out, send, recv, local):
    t, z, y, c = places()
    greet(all_partners(t, z, y, c))
    cp = pltpu.make_async_copy(own, out.at[t, z, y, c], local.at[0])
    cp.start()
    chunks = own.shape[1] // CHUNK
    half = CHUNK // 2
    sends = []

    def push(src, dst, k, i, device):
        copy = pltpu.make_async_remote_copy(
            src_ref=src, dst_ref=dst, send_sem=send.at[k, i], recv_sem=recv.at[k, i],
            device_id=device, device_id_type=MESH,
        )
        copy.start()
        sends.append(copy)
        return copy

    pending = {}

    def stage(k, s):
        full = pl.ds(k * CHUNK, CHUNK)
        left = pl.ds(k * CHUNK, half)
        right = pl.ds(k * CHUNK + half, half)
        if s == 0:
            pending[k] = [
                push(own.at[:, full], out.at[t, z, y, c, :, full], k, j - 1, at(t, lax.rem(z + j, 4), y, c))
                for j in range(1, 4)
            ]
            return
        for copy in pending[k]:
            copy.wait_recv()
        if s == 1:
            a = out.at[t, :, y, c, :, left]
            b = out.at[t, :, y, c, :, right]
            pending[k] = [push(a, a, k, 3, at(1 - t, z, y, c)), push(b, b, k, 4, at(t, z, 1 - y, c))]
        elif s == 2:
            a = out.at[:, :, y, c, :, left]
            b = out.at[t, :, :, c, :, right]
            pending[k] = [push(a, a, k, 5, at(t, z, 1 - y, c)), push(b, b, k, 6, at(1 - t, z, y, c))]
        elif s == 3:
            a = out.at[:, :, :, c, :, full]
            pending[k] = [push(a, a, k, 7, at(t, z, y, 1 - c))]

    for tick in range(chunks + 4):
        if tick == 1:
            cp.wait()
        for s in (4, 3, 2, 1, 0):
            k = tick - s
            if 0 <= k < chunks:
                stage(k, s)
    for copy in sends:
        copy.wait_send()


def sum_grads(genc, gdec, vec, out, vec_out, r1, s1, r2a, r2b, s2a, s2b, r3a, r3b, s3, r4, v1, vr, send, recv, local, vsend, vrecv):
    t, z, y, c = places()
    greet(all_partners(t, z, y, c))
    enc_chunks = genc.shape[-1] // CHUNK
    chunks = enc_chunks + gdec.shape[-1] // CHUNK
    half = CHUNK // 2
    sends = []

    def push(src, dst, ssem, rsem, device):
        copy = pltpu.make_async_remote_copy(
            src_ref=src, dst_ref=dst, send_sem=ssem, recv_sem=rsem, device_id=device, device_id_type=MESH,
        )
        copy.start()
        sends.append(copy)
        return copy

    def big(k):
        if k < enc_chunks:
            return genc, pl.ds(k * CHUNK, CHUNK)
        return gdec, pl.ds((k - enc_chunks) * CHUNK, CHUNK)

    pending, own = {}, {}
    left, right = pl.ds(0, half), pl.ds(half, half)

    def stage(k, s):
        if s == 0:
            g, cols = big(k)
            own[k] = pltpu.make_async_copy(g.at[:, :, :, c, :, cols], s1.at[k], local.at[k])
            own[k].start()
            pending[k] = [push(g.at[:, :, :, 1 - c, :, cols], r1.at[k], send.at[k, 0], recv.at[k, 0], at(t, z, y, 1 - c))]
            return
        for copy in pending[k]:
            copy.wait_recv()
        if s == 1:
            own[k].wait()
            s1[k] = (s1[k].astype(F32) + r1[k].astype(F32)).astype(BF)
            pending[k] = [
                push(s1.at[k, 1 - t, :, :, :, left], r2a.at[k], send.at[k, 1], recv.at[k, 1], at(1 - t, z, y, c)),
                push(s1.at[k, :, :, 1 - y, :, right], r2b.at[k], send.at[k, 2], recv.at[k, 2], at(t, z, 1 - y, c)),
            ]
        elif s == 2:
            s2a[k] = (s1[k, t, :, :, :, left].astype(F32) + r2a[k].astype(F32)).astype(BF)
            s2b[k] = (s1[k, :, :, y, :, right].astype(F32) + r2b[k].astype(F32)).astype(BF)
            pending[k] = [
                push(s2a.at[k, :, 1 - y], r3a.at[k], send.at[k, 3], recv.at[k, 3], at(t, z, 1 - y, c)),
                push(s2b.at[k, 1 - t], r3b.at[k], send.at[k, 4], recv.at[k, 4], at(1 - t, z, y, c)),
            ]
        elif s == 3:
            s3[k, :, :, left] = (s2a[k, :, y].astype(F32) + r3a[k].astype(F32)).astype(BF)
            s3[k, :, :, right] = (s2b[k, t].astype(F32) + r3b[k].astype(F32)).astype(BF)
            pending[k] = []
            for j in range(1, 4):
                zz = lax.rem(z + j, 4)
                pending[k].append(push(s3.at[k, zz], r4.at[k, j - 1], send.at[k, 4 + j], recv.at[k, 4 + j], at(t, zz, y, c)))
        elif s == 4:
            out[:, pl.ds(k * CHUNK, CHUNK)] = (s3[k, z].astype(F32) + r4[k, 0].astype(F32)) + (
                r4[k, 1].astype(F32) + r4[k, 2].astype(F32)
            )

    vpending = []

    def vector_stage(s):
        for copy in vpending:
            copy.wait_recv()
        vpending.clear()
        if s == 0:
            v1[0] = vec[...]
        elif s < 4:
            v1[s] = v1[s - 1] + vr[s - 1]
        if s < 3:
            device = (at(t, z, y, 1 - c), at(1 - t, z, y, c), at(t, z, 1 - y, c))[s]
            vpending.append(push(v1.at[s], vr.at[s], vsend.at[s], vrecv.at[s], device))
        elif s == 3:
            for j in range(1, 4):
                vpending.append(
                    push(v1.at[3], vr.at[2 + j], vsend.at[2 + j], vrecv.at[2 + j], at(t, lax.rem(z + j, 4), y, c))
                )
        else:
            vec_out[...] = (v1[3] + vr[3]) + (vr[4] + vr[5])

    for tick in range(chunks + 4):
        for s in (4, 3, 2, 1, 0):
            k = tick - s
            if 0 <= k < chunks:
                stage(k, s)
        if tick < 5:
            vector_stage(tick)
    for copy in sends:
        copy.wait_send()


def call_gather(own):
    rows, n = own.shape
    chunks = n // CHUNK
    any_spec = pl.BlockSpec(memory_space=pl.ANY)
    dma = pltpu.SemaphoreType.DMA
    return pl.pallas_call(
        gather_weights,
        in_specs=[any_spec],
        out_specs=any_spec,
        out_shape=jax.ShapeDtypeStruct((2, 4, 2, 2, rows, n), BF),
        scratch_shapes=[dma((chunks, 8)), dma((chunks, 8)), dma((1,))],
        compiler_params=pltpu.CompilerParams(collective_id=0, has_side_effects=True),
        name="gather_weights",
    )(own)


def call_sum(genc, gdec, vec):
    rows = genc.shape[1] // 16
    split = lambda g: g.reshape(2, 4, 2, 2, rows, g.shape[2])
    n = genc.shape[2] + gdec.shape[2]
    chunks = n // CHUNK
    half = CHUNK // 2
    any_spec = pl.BlockSpec(memory_space=pl.ANY)
    vmem = pl.BlockSpec(memory_space=pltpu.VMEM)
    dma = pltpu.SemaphoreType.DMA
    buf = lambda *dims: pltpu.VMEM((chunks,) + dims, BF)
    return pl.pallas_call(
        sum_grads,
        in_specs=[any_spec, any_spec, vmem],
        out_specs=[vmem, vmem],
        out_shape=[jax.ShapeDtypeStruct((rows, n), F32), jax.ShapeDtypeStruct(vec.shape, F32)],
        scratch_shapes=[
            buf(2, 4, 2, rows, CHUNK), buf(2, 4, 2, rows, CHUNK),
            buf(4, 2, rows, half), buf(2, 4, rows, half), buf(4, 2, rows, half), buf(2, 4, rows, half),
            buf(4, rows, half), buf(4, rows, half), buf(4, rows, CHUNK), buf(3, rows, CHUNK),
            pltpu.VMEM((4,) + vec.shape, F32), pltpu.VMEM((6,) + vec.shape, F32),
            dma((chunks, 8)), dma((chunks, 8)), dma((chunks,)), dma((6,)), dma((6,)),
        ],
        compiler_params=pltpu.CompilerParams(
            collective_id=1, has_side_effects=True, vmem_limit_bytes=VMEM_LIMIT
        ),
        name="sum_grads",
    )(split(genc), split(gdec), vec)


def swap_halves(arrays):
    t = lax.axis_index("tensor")
    results = []
    for mine in arrays:
        sent = lax.dynamic_index_in_dim(mine, 1 - t, 0, keepdims=False)
        kept = lax.dynamic_index_in_dim(mine, t, 0, keepdims=False)
        got = lax.ppermute(sent, "tensor", [(0, 1), (1, 0)])
        low = jnp.where(t == 0, kept, got)
        high = jnp.where(t == 0, got, kept)
        results.append(jnp.concatenate([low, high], axis=0))
    return results


def return_halves(whole):
    t = lax.axis_index("tensor")
    rows = whole.shape[0] // 2
    parts = whole.reshape(2, rows, whole.shape[1])
    sent = lax.dynamic_index_in_dim(parts, 1 - t, 0, keepdims=False)
    kept = lax.dynamic_index_in_dim(parts, t, 0, keepdims=False)
    got = lax.ppermute(sent, "tensor", [(0, 1), (1, 0)])
    return jnp.stack([jnp.where(t == 0, kept, got), jnp.where(t == 0, got, kept)])


def pair_body(*arguments):
    source, target, cotangent, lengths, timesteps, masked, loss_mask = arguments[:7]
    matrices = arguments[7:23]
    norm_gains, norm_shifts, mask_vector = arguments[23:]
    t = lax.axis_index("tensor")
    turned = (3, 5, 9, 13, 15)
    own = jnp.concatenate([m.T if i in turned else m for i, m in enumerate(matrices)], axis=1)
    gathered = call_gather(own)
    weights = gathered.reshape(2, 16 * own.shape[0], own.shape[1])
    chosen = masked[:, :, None] == 1
    start_y = jnp.where(chosen, mask_vector, target.astype(F32)).astype(BF)
    factor = (STEPS + 1 - timesteps).astype(F32) / STEPS
    grad3 = (
        cotangent.astype(F32) * (factor[:, None] * loss_mask.astype(F32))[:, :, None]
    ).astype(BF)
    x, y0, g3 = swap_halves((source, start_y, grad3))
    length = lax.dynamic_slice_in_dim(lengths, t, 1)
    dec, sg, gy, genc, gdec, ng = compute_all(length, norm_gains, norm_shifts, x, y0, g3, weights)
    decoded = return_halves(dec)
    grad_y = return_halves(gy)
    target_grad = jnp.where(chosen, jnp.zeros((), BF), grad_y)
    mask_part = jnp.sum(jnp.where(chosen, grad_y.astype(F32), 0.0), axis=(0, 1))
    source_grad = return_halves(sg)
    vec = jnp.concatenate([ng[:6], ng[8:14], mask_part[None], jnp.zeros((3, ng.shape[1]), F32)], axis=0)
    summed, vec = call_sum(genc, gdec, vec)
    grads, offset = [], 0
    for i, m in enumerate(matrices):
        n = m.shape[0] if i in turned else m.shape[1]
        part = summed[:, offset : offset + n]
        offset += n
        grads.append(part.T if i in turned else part)
    return (decoded, source_grad, target_grad, *grads, vec[:6], vec[6:12], vec[12])


def solution(mesh):
    whole_pairs = dict(mesh.shape) == {"dp": 16, "tensor": 2}
    return jax.shard_map(
        pair_body if whole_pairs else body,
        mesh=mesh,
        in_specs=(
            P("dp", "tensor", None),
            P("dp", "tensor", None),
            P("dp", "tensor", None),
            P("dp"),
            P("dp"),
            P("dp", "tensor"),
            P("dp", "tensor"),
            P("dp", "tensor"),
            P("dp", "tensor"),
            P("dp", "tensor"),
            P("tensor", "dp"),
            P("dp", "tensor"),
            P("tensor", "dp"),
            P("dp", "tensor"),
            P("dp", "tensor"),
            P("dp", "tensor"),
            P("tensor", "dp"),
            P("dp", "tensor"),
            P("dp", "tensor"),
            P("dp", "tensor"),
            P("tensor", "dp"),
            P("dp", "tensor"),
            P("tensor", "dp"),
            P(),
            P(),
            P(),
        ),
        out_specs=(
            P("dp", "tensor", None),
            P("dp", "tensor", None),
            P("dp", "tensor", None),
            P("dp", "tensor"),
            P("dp", "tensor"),
            P("dp", "tensor"),
            P("tensor", "dp"),
            P("dp", "tensor"),
            P("tensor", "dp"),
            P("dp", "tensor"),
            P("dp", "tensor"),
            P("dp", "tensor"),
            P("tensor", "dp"),
            P("dp", "tensor"),
            P("dp", "tensor"),
            P("dp", "tensor"),
            P("tensor", "dp"),
            P("dp", "tensor"),
            P("tensor", "dp"),
            P(),
            P(),
            P(),
        ),
        check_vma=False,
    )
```

```python
import jax
import jax.numpy as jnp
from jax import lax
from jax.experimental import pallas as pl
from jax.experimental.pallas import tpu as pltpu
from jax.sharding import PartitionSpec as P

HD = 64
MICRO = 2
STEPS = 50


eps = 1e-05
floor_score = -1e30


def norm_rows(inputs, gain, shift):
    average = jnp.mean(inputs, axis=-1, keepdims=True)
    centred = inputs - average
    second = jnp.mean(centred * centred, axis=-1, keepdims=True)
    return centred * lax.rsqrt(second + eps) * gain + shift


def norm_back(inputs, gain, shift, gradient):
    unused, pullback = jax.vjp(norm_rows, inputs, gain, shift)
    return pullback(gradient)


def smooth(values):
    return jax.nn.gelu(values, approximate=False)


def spread(inputs):
    return lax.all_gather(inputs.astype(jnp.bfloat16), "tensor", axis=1, tiled=True)


def collect(partial_value):
    return lax.psum_scatter(partial_value, "tensor", scatter_dimension=1, tiled=True)


def spread_grad(gradient):
    return lax.all_gather(gradient.astype(jnp.bfloat16), "tensor", axis=1, tiled=True)


def collect_grad(partial_value):
    return lax.psum_scatter(partial_value, "tensor", scatter_dimension=1, tiled=True)


def project(inputs, weight):
    return jnp.einsum("bsk,kn->bsn", inputs, weight, preferred_element_type=jnp.float32)


def weight_grad(inputs, gradient):
    return jnp.einsum("bsk,bsn->kn", inputs, gradient, preferred_element_type=jnp.float32)


def back_project(gradient, weight):
    return jnp.einsum("bsn,kn->bsk", gradient, weight, preferred_element_type=jnp.float32)


def masked_scores(query_part, key_rows, live):
    scores = jnp.einsum(
        "bqhd,bkhd->bhqk", query_part, key_rows, preferred_element_type=jnp.float32
    ) * HD ** (-0.5)
    return jnp.where(live[:, None, None, :], scores, floor_score)


def attend_forward(query_in, keys_in, w_query, w_key, w_value, live):
    pair_count, length = (query_in.shape[0], query_in.shape[1])
    head_count = w_query.shape[1] // HD
    queries = (
        project(query_in, w_query).astype(jnp.bfloat16).reshape(pair_count, length, head_count, HD)
    )
    key_rows = (
        project(keys_in, w_key).astype(jnp.bfloat16).reshape(pair_count, length, head_count, HD)
    )
    value_rows = (
        project(keys_in, w_value).astype(jnp.bfloat16).reshape(pair_count, length, head_count, HD)
    )
    block_rows = min(512, length)
    pieces = []
    totals = []
    for offset in range(0, length, block_rows):
        scores = masked_scores(queries[:, offset : offset + block_rows], key_rows, live)
        highest = jnp.max(scores, axis=-1, keepdims=True)
        exponent = jnp.exp(scores - highest)
        summed = jnp.sum(exponent, axis=-1, keepdims=True)
        softmax = (exponent / summed).astype(jnp.bfloat16)
        pieces.append(
            jnp.einsum("bhqk,bkhd->bqhd", softmax, value_rows, preferred_element_type=jnp.float32)
        )
        totals.append(highest + jnp.log(summed))
    attended = (
        jnp.concatenate(pieces, axis=1)
        .astype(jnp.bfloat16)
        .reshape(pair_count, length, head_count * HD)
    )
    return (queries, key_rows, value_rows, attended, jnp.concatenate(totals, axis=2))


def attend_backward(whole_grad, query_in, keys_in, w_query, w_key, w_value, w_out, saved, live):
    queries, key_rows, value_rows, attended, totals = saved
    pair_count, length, head_count = (queries.shape[0], queries.shape[1], queries.shape[2])
    scale_score = HD ** (-0.5)
    out_grad = weight_grad(attended, whole_grad)
    head_grad = (
        back_project(whole_grad, w_out)
        .astype(jnp.bfloat16)
        .reshape(pair_count, length, head_count, HD)
    )
    block_rows = min(512, length)
    key_total = jnp.zeros(key_rows.shape, jnp.float32)
    value_total = jnp.zeros(value_rows.shape, jnp.float32)
    query_parts = []
    for offset in range(0, length, block_rows):
        query_part = queries[:, offset : offset + block_rows]
        grad_part = head_grad[:, offset : offset + block_rows]
        scores = masked_scores(query_part, key_rows, live)
        softmax = jnp.exp(scores - totals[:, :, offset : offset + block_rows])
        value_total = value_total + jnp.einsum(
            "bhqk,bqhd->bkhd",
            softmax.astype(jnp.bfloat16),
            grad_part,
            preferred_element_type=jnp.float32,
        )
        soft_grad = jnp.einsum(
            "bqhd,bkhd->bhqk", grad_part, value_rows, preferred_element_type=jnp.float32
        )
        inner = jnp.sum(softmax * soft_grad, axis=-1, keepdims=True)
        score_grad = (softmax * (soft_grad - inner)).astype(jnp.bfloat16)
        query_parts.append(
            jnp.einsum("bhqk,bkhd->bqhd", score_grad, key_rows, preferred_element_type=jnp.float32)
            * scale_score
        )
        key_total = (
            key_total
            + jnp.einsum(
                "bhqk,bqhd->bkhd", score_grad, query_part, preferred_element_type=jnp.float32
            )
            * scale_score
        )
    query_grad = (
        jnp.concatenate(query_parts, axis=1)
        .astype(jnp.bfloat16)
        .reshape(pair_count, length, head_count * HD)
    )
    key_grad = key_total.astype(jnp.bfloat16).reshape(
        pair_count, key_rows.shape[1], head_count * HD
    )
    value_grad = value_total.astype(jnp.bfloat16).reshape(
        pair_count, value_rows.shape[1], head_count * HD
    )
    grads = (
        weight_grad(query_in, query_grad),
        weight_grad(keys_in, key_grad),
        weight_grad(keys_in, value_grad),
        out_grad,
    )
    into_keys = back_project(key_grad, w_key) + back_project(value_grad, w_value)
    return (grads, back_project(query_grad, w_query), into_keys)


def feed_forward(inputs, w_up, w_down):
    lifted = project(inputs, w_up)
    active = smooth(lifted).astype(jnp.bfloat16)
    return (lifted, active, project(active, w_down))


def feed_backward(gradient, inputs, w_up, w_down, lifted, active):
    down_grad = weight_grad(active, gradient)
    active_grad = back_project(gradient, w_down)
    unused, smooth_back = jax.vjp(smooth, lifted)
    lifted_grad = smooth_back(active_grad)[0].astype(jnp.bfloat16)
    return ((weight_grad(inputs, lifted_grad), down_grad), back_project(lifted_grad, w_up))


def body(
    source,
    target,
    cotangent,
    lengths,
    timesteps,
    masked,
    loss_mask,
    enc_query,
    enc_key,
    enc_value,
    enc_out,
    enc_up,
    enc_down,
    self_query,
    self_key,
    self_value,
    self_out,
    cross_query,
    cross_key,
    cross_value,
    cross_out,
    dec_up,
    dec_down,
    norm_gains,
    norm_shifts,
    mask_vector,
):
    pairs_dev, rows_dev = (source.shape[0], source.shape[1])
    per_micro = pairs_dev // MICRO
    seq_len = rows_dev * lax.axis_size("tensor")
    positions = jnp.arange(seq_len)
    gains, shifts = (norm_gains, norm_shifts)
    gain_total = jnp.zeros(norm_gains.shape, jnp.float32)
    shift_total = jnp.zeros(norm_shifts.shape, jnp.float32)
    mask_total = jnp.zeros(mask_vector.shape, jnp.float32)
    decoded_parts = []
    source_parts = []
    target_parts = []
    running = None
    for micro in range(MICRO):
        weights = (
            lax.all_gather(enc_query, "dp", axis=0, tiled=True),
            lax.all_gather(enc_key, "dp", axis=0, tiled=True),
            lax.all_gather(enc_value, "dp", axis=0, tiled=True),
            lax.all_gather(enc_out, "dp", axis=1, tiled=True),
            lax.all_gather(enc_up, "dp", axis=0, tiled=True),
            lax.all_gather(enc_down, "dp", axis=1, tiled=True),
            lax.all_gather(self_query, "dp", axis=0, tiled=True),
            lax.all_gather(self_key, "dp", axis=0, tiled=True),
            lax.all_gather(self_value, "dp", axis=0, tiled=True),
            lax.all_gather(self_out, "dp", axis=1, tiled=True),
            lax.all_gather(cross_query, "dp", axis=0, tiled=True),
            lax.all_gather(cross_key, "dp", axis=0, tiled=True),
            lax.all_gather(cross_value, "dp", axis=0, tiled=True),
            lax.all_gather(cross_out, "dp", axis=1, tiled=True),
            lax.all_gather(dec_up, "dp", axis=0, tiled=True),
            lax.all_gather(dec_down, "dp", axis=1, tiled=True),
        )
        wide = (
            lax.all_gather(weights[4], "tensor", axis=1, tiled=True),
            lax.all_gather(weights[5], "tensor", axis=0, tiled=True),
            lax.all_gather(weights[14], "tensor", axis=1, tiled=True),
            lax.all_gather(weights[15], "tensor", axis=0, tiled=True),
        )
        lower = micro * per_micro
        upper = lower + per_micro
        live = positions[None, :] < lengths[lower:upper][:, None]
        every = jnp.ones((per_micro, seq_len), bool)
        inputs_x = source[lower:upper].astype(jnp.float32)
        rows0 = spread(norm_rows(inputs_x, gains[0], shifts[0]))
        saved0 = attend_forward(rows0, rows0, weights[0], weights[1], weights[2], live)
        stream1 = inputs_x + collect(project(saved0[3], weights[3]))
        normed1 = norm_rows(stream1, gains[1], shifts[1])
        rows1 = normed1.astype(jnp.bfloat16)
        lifted1, active1, partial1 = feed_forward(rows1, wide[0], wide[1])
        stream2 = stream1 + partial1
        memory_rows = spread(norm_rows(stream2, gains[2], shifts[2]))
        chosen = masked[lower:upper][:, :, None] == 1
        start_y = jnp.where(chosen, mask_vector, target[lower:upper].astype(jnp.float32))
        rows3 = spread(norm_rows(start_y, gains[3], shifts[3]))
        saved3 = attend_forward(rows3, rows3, weights[6], weights[7], weights[8], every)
        stream4 = start_y + collect(project(saved3[3], weights[9]))
        rows4 = spread(norm_rows(stream4, gains[4], shifts[4]))
        saved4 = attend_forward(rows4, memory_rows, weights[10], weights[11], weights[12], live)
        stream5 = stream4 + collect(project(saved4[3], weights[13]))
        normed5 = norm_rows(stream5, gains[5], shifts[5])
        rows5 = normed5.astype(jnp.bfloat16)
        lifted5, active5, partial5 = feed_forward(rows5, wide[2], wide[3])
        stream6 = stream5 + partial5
        decoded_parts.append(stream6.astype(jnp.bfloat16))
        factor = (STEPS + 1 - timesteps[lower:upper]).astype(jnp.float32) / STEPS
        grad6 = (
            cotangent[lower:upper].astype(jnp.float32)
            * (factor[:, None] * loss_mask[lower:upper].astype(jnp.float32))[:, :, None]
        )
        (up5, down5), into5 = feed_backward(
            grad6.astype(jnp.bfloat16), rows5, wide[2], wide[3], lifted5, active5
        )
        back5 = norm_back(stream5, gains[5], shifts[5], into5)
        grad5 = grad6 + back5[0]
        grads4, query_term4, memory_term = attend_backward(
            spread_grad(grad5),
            rows4,
            memory_rows,
            weights[10],
            weights[11],
            weights[12],
            weights[13],
            saved4,
            live,
        )
        back4 = norm_back(stream4, gains[4], shifts[4], collect_grad(query_term4))
        grad4 = grad5 + back4[0]
        memory_grad = collect_grad(memory_term)
        grads3, query_term3, keys_term3 = attend_backward(
            spread_grad(grad4),
            rows3,
            rows3,
            weights[6],
            weights[7],
            weights[8],
            weights[9],
            saved3,
            every,
        )
        back3 = norm_back(start_y, gains[3], shifts[3], collect_grad(query_term3 + keys_term3))
        grad_y = grad4 + back3[0]
        target_parts.append(jnp.where(chosen, 0.0, grad_y).astype(jnp.bfloat16))
        mask_total = mask_total + jnp.sum(jnp.where(chosen, grad_y, 0.0), axis=(0, 1))
        back2 = norm_back(stream2, gains[2], shifts[2], memory_grad)
        grad2 = back2[0]
        (up1, down1), into1 = feed_backward(
            grad2.astype(jnp.bfloat16), rows1, wide[0], wide[1], lifted1, active1
        )
        back1 = norm_back(stream1, gains[1], shifts[1], into1)
        grad1 = grad2 + back1[0]
        grads0, query_term0, keys_term0 = attend_backward(
            spread_grad(grad1),
            rows0,
            rows0,
            weights[0],
            weights[1],
            weights[2],
            weights[3],
            saved0,
            live,
        )
        back0 = norm_back(inputs_x, gains[0], shifts[0], collect_grad(query_term0 + keys_term0))
        source_parts.append((grad1 + back0[0]).astype(jnp.bfloat16))
        gain_total = gain_total + jnp.stack(
            [back0[1], back1[1], back2[1], back3[1], back4[1], back5[1]]
        )
        shift_total = shift_total + jnp.stack(
            [back0[2], back1[2], back2[2], back3[2], back4[2], back5[2]]
        )
        up1, down1, up5, down5 = (
            lax.psum_scatter(
                up1.astype(jnp.bfloat16), "tensor", scatter_dimension=1, tiled=True
            ).astype(jnp.float32),
            lax.psum_scatter(
                down1.astype(jnp.bfloat16), "tensor", scatter_dimension=0, tiled=True
            ).astype(jnp.float32),
            lax.psum_scatter(
                up5.astype(jnp.bfloat16), "tensor", scatter_dimension=1, tiled=True
            ).astype(jnp.float32),
            lax.psum_scatter(
                down5.astype(jnp.bfloat16), "tensor", scatter_dimension=0, tiled=True
            ).astype(jnp.float32),
        )
        fresh = (
            grads0[0],
            grads0[1],
            grads0[2],
            grads0[3],
            up1,
            down1,
            grads3[0],
            grads3[1],
            grads3[2],
            grads3[3],
            grads4[0],
            grads4[1],
            grads4[2],
            grads4[3],
            up5,
            down5,
        )
        running = fresh if micro == 0 else jax.tree.map(jnp.add, running, tuple(fresh))
    running = (
        lax.psum_scatter(
            running[0].astype(jnp.bfloat16), "dp", scatter_dimension=0, tiled=True
        ).astype(jnp.float32),
        lax.psum_scatter(
            running[1].astype(jnp.bfloat16), "dp", scatter_dimension=0, tiled=True
        ).astype(jnp.float32),
        lax.psum_scatter(
            running[2].astype(jnp.bfloat16), "dp", scatter_dimension=0, tiled=True
        ).astype(jnp.float32),
        lax.psum_scatter(
            running[3].astype(jnp.bfloat16), "dp", scatter_dimension=1, tiled=True
        ).astype(jnp.float32),
        lax.psum_scatter(
            running[4].astype(jnp.bfloat16), "dp", scatter_dimension=0, tiled=True
        ).astype(jnp.float32),
        lax.psum_scatter(
            running[5].astype(jnp.bfloat16), "dp", scatter_dimension=1, tiled=True
        ).astype(jnp.float32),
        lax.psum_scatter(
            running[6].astype(jnp.bfloat16), "dp", scatter_dimension=0, tiled=True
        ).astype(jnp.float32),
        lax.psum_scatter(
            running[7].astype(jnp.bfloat16), "dp", scatter_dimension=0, tiled=True
        ).astype(jnp.float32),
        lax.psum_scatter(
            running[8].astype(jnp.bfloat16), "dp", scatter_dimension=0, tiled=True
        ).astype(jnp.float32),
        lax.psum_scatter(
            running[9].astype(jnp.bfloat16), "dp", scatter_dimension=1, tiled=True
        ).astype(jnp.float32),
        lax.psum_scatter(
            running[10].astype(jnp.bfloat16), "dp", scatter_dimension=0, tiled=True
        ).astype(jnp.float32),
        lax.psum_scatter(
            running[11].astype(jnp.bfloat16), "dp", scatter_dimension=0, tiled=True
        ).astype(jnp.float32),
        lax.psum_scatter(
            running[12].astype(jnp.bfloat16), "dp", scatter_dimension=0, tiled=True
        ).astype(jnp.float32),
        lax.psum_scatter(
            running[13].astype(jnp.bfloat16), "dp", scatter_dimension=1, tiled=True
        ).astype(jnp.float32),
        lax.psum_scatter(
            running[14].astype(jnp.bfloat16), "dp", scatter_dimension=0, tiled=True
        ).astype(jnp.float32),
        lax.psum_scatter(
            running[15].astype(jnp.bfloat16), "dp", scatter_dimension=1, tiled=True
        ).astype(jnp.float32),
    )
    vectors = lax.psum((gain_total, shift_total, mask_total), ("dp", "tensor"))
    return (
        jnp.concatenate(decoded_parts, axis=0),
        jnp.concatenate(source_parts, axis=0),
        jnp.concatenate(target_parts, axis=0),
        running[0],
        running[1],
        running[2],
        running[3],
        running[4],
        running[5],
        running[6],
        running[7],
        running[8],
        running[9],
        running[10],
        running[11],
        running[12],
        running[13],
        running[14],
        running[15],
        vectors[0],
        vectors[1],
        vectors[2],
    )


F32 = jnp.float32
BF = jnp.bfloat16
LOG2E = 1.4426950408889634
LN2 = 0.6931471805599453
NN = (((1,), (0,)), ((), ()))
NT = (((1,), (1,)), ((), ()))
MESH = pl.DeviceIdType.MESH
RB = 256
VMEM_LIMIT = 62 * 2**20


def dg(left, right, dims=NN):
    return lax.dot_general(left, right, dims, preferred_element_type=F32)


def ln_hat(x):
    centred = x - jnp.mean(x, axis=-1, keepdims=True)
    rstd = lax.rsqrt(jnp.mean(centred * centred, axis=-1, keepdims=True) + eps)
    return centred * rstd, rstd


def ln_back(x, gain, gradient):
    hat, rstd = ln_hat(x)
    scaled = gradient * gain
    first = jnp.mean(scaled, axis=-1, keepdims=True)
    second = jnp.mean(scaled * hat, axis=-1, keepdims=True)
    dx = rstd * (scaled - first - hat * second)
    dgain = jnp.sum(gradient * hat, axis=0, keepdims=True)
    dshift = jnp.sum(gradient, axis=0, keepdims=True)
    return dx, dgain, dshift


def gelu_both(u):
    size = jnp.abs(u)
    t = 1.0 / (1.0 + (0.3275911 * 0.7071067811865476) * size)
    ex = jnp.exp2(u * u * (-0.5 * LOG2E))
    poly = t * (
        0.127414796
        + t * (-0.142248368 + t * (0.7107068705 + t * (-0.7265760135 + t * 0.5307027145)))
    )
    tail = poly * ex
    phi = jnp.where(u > 0, 1.0 - tail, tail)
    return u * phi, phi + u * ex * 0.3989422804014327


def rows_loop(total, step, run):
    def once(i, carry):
        run(pl.ds(pl.multiple_of(i * step, step), step))
        return carry

    lax.fori_loop(0, total // step, once, 0)


def load_weight(w_hbm, offset, width, dst, sems, base):
    copies = []
    for t in range(2):
        src = pl.ds(offset, width)
        to = pl.ds(t * width, width)
        cp = pltpu.make_async_copy(
            w_hbm.at[t, :, src] if len(w_hbm.shape) == 3 else w_hbm.at[t, :, :, :, :, src],
            dst.at[:, to] if len(dst.shape) == 2 else dst.at[:, :, :, :, to],
            sems.at[base + t],
        )
        cp.start()
        copies.append(cp)
    return copies


def wait_all(copies):
    for cp in copies:
        cp.wait()


def whole(ref):
    value = ref[...]
    return value if value.ndim == 2 else value.reshape(-1, value.shape[-1])


def normalize(x, gain, shift, a):
    def run(sl):
        hat, unused = ln_hat(x[sl, :].astype(F32))
        a[sl, :] = (hat * gain + shift).astype(BF)

    rows_loop(x.shape[0], 2 * RB, run)


def attn_project(a, kv, wq, wk, wv, q, k, v):
    def run(sl):
        q[sl, :] = (dg(a[sl, :], whole(wq)) * (LOG2E * HD**-0.5)).astype(BF)
        k[sl, :] = dg(kv[sl, :], whole(wk)).astype(BF)
        v[sl, :] = dg(kv[sl, :], whole(wv)).astype(BF)

    rows_loop(a.shape[0], 2 * RB, run)


def attn_core(length, q, k, v, o, ol, r, e_hbm, ebuf, esem):
    seq = q.shape[0]
    pairs = q.shape[1] // 128
    block = 512
    lane = lax.broadcasted_iota(jnp.int32, (1, 128), 1)
    low = lane < 64
    one = jnp.ones((), BF)
    key = lax.broadcasted_iota(jnp.int32, (seq, 1), 0)
    bias = jnp.where(key < length, 0.0, floor_score).astype(F32)

    def out(p, h):
        slot = lax.rem(p, 2) * 2 + h
        return pltpu.make_async_copy(ebuf.at[slot], e_hbm.at[2 * p + h], esem.at[slot])

    def pair(p, carry):
        @pl.when(p > 1)
        def unused_wait():
            out(p - 2, 0).wait()
            out(p - 2, 1).wait()

        base = lax.rem(p, 2) * 2
        cols = pl.ds(pl.multiple_of(p * 128, 128), 128)
        kp = k[:, cols].astype(F32)
        vp = v[:, cols]
        ka = (
            jnp.where(low, kp, jnp.where(lane == 64, bias, 0.0)).astype(BF),
            jnp.where(low, jnp.where(lane == 0, bias, 0.0), kp).astype(BF),
        )
        va = jnp.where(low, vp, one), jnp.where(low, one, vp)
        for b in range(seq // block):
            sl = pl.ds(b * block, block)
            qp = q[sl, cols]
            parts = []
            for h in range(2):
                qm = jnp.where(low, qp, one) if h == 0 else jnp.where(low, one, qp)
                s = dg(qm, ka[h], NT)
                e = jnp.exp2(s - jnp.max(s, axis=-1, keepdims=True)).astype(BF)
                ebuf[base + h, sl, :] = e
                parts.append(dg(e, va[h]))
            un = jnp.where(low, parts[0], parts[1])
            inverse = 1.0 / pltpu.roll(jnp.where(low, parts[1], parts[0]), 64, 1)
            r[sl, cols] = inverse.astype(BF)
            joined = un * inverse
            rounded = joined.astype(BF)
            o[sl, cols] = rounded
            ol[sl, cols] = (joined - rounded.astype(F32)).astype(BF)
        out(p, 0).start()
        out(p, 1).start()
        return carry

    lax.fori_loop(0, pairs, pair, 0)
    for p in (pairs - 2, pairs - 1):
        out(p, 0).wait()
        out(p, 1).wait()


def attn_join(x, o, wo, y):
    def run(sl):
        y[sl, :] = x[sl, :].astype(F32) + dg(o[sl, :], whole(wo), NT)

    rows_loop(x.shape[0], 2 * RB, run)


def attn_back_core(q, k, v, do, o, ol, e_hbm, ebuf, esem, ds, dq, dk, dv):
    seq = q.shape[0]
    heads = e_hbm.shape[0]
    block = 512
    lane = lax.broadcasted_iota(jnp.int32, (1, 128), 1)
    low = lane < 64
    zero = jnp.zeros((), BF)
    one = jnp.ones((), BF)
    row2 = lax.broadcasted_iota(jnp.int32, (256, 128), 0)
    col2 = lax.broadcasted_iota(jnp.int32, (256, 128), 1)
    swap = jnp.where(((row2 // 64) % 2) != (col2 // 64), 1.0, 0.0).astype(BF)

    def fetch(p, h):
        slot = lax.rem(p, 2) * 2 + h
        return pltpu.make_async_copy(e_hbm.at[2 * p + h], ebuf.at[slot], esem.at[slot])

    fetch(0, 0).start()
    fetch(0, 1).start()

    def pair(p, carry):
        cols = pl.ds(pl.multiple_of(p * 128, 128), 128)
        fetch(p, 0).wait()
        fetch(p, 1).wait()

        @pl.when(p + 1 < heads // 2)
        def unused_fetch():
            fetch(p + 1, 0).start()
            fetch(p + 1, 1).start()

        base = lax.rem(p, 2) * 2
        qp, kp, vp, dop = q[:, cols], k[:, cols], v[:, cols], do[:, cols]
        product = dop.astype(F32) * (o[:, cols].astype(F32) + ol[:, cols].astype(F32))
        high = product.astype(BF)
        rest = (product - high.astype(F32)).astype(BF)
        inner = -dg(jnp.concatenate([high, rest], axis=1), swap)
        inner_high = inner.astype(BF)
        inner_rest = (inner - inner_high.astype(F32)).astype(BF)
        do_t, q_t = dop.T, qp.T
        dq_sum = None
        dks, dvs = [], []
        for h in range(2):
            if h == 0:
                lhs = jnp.where(low, dop, jnp.where(lane == 64, inner_high, inner_rest))
                va = jnp.where(low, vp, jnp.where(lane < 66, one, zero))
                km = jnp.where(low, kp, zero)
            else:
                lhs = jnp.where(low, jnp.where(lane == 0, inner_high, inner_rest), dop)
                va = jnp.where(low, jnp.where(lane < 2, one, zero), vp)
                km = jnp.where(low, zero, kp)
            for b in range(seq // block):
                sl = pl.ds(b * block, block)
                t = dg(lhs[b * block : (b + 1) * block], va, NT)
                ds[h, sl, :] = ebuf[base + h, sl, :] * t.astype(BF)
            part = dg(ds[h], km)
            dq_sum = part if dq_sum is None else dq_sum + part
            dks.append(dg(q_t[64 * h : 64 * h + 64], ds[h]))
            dvs.append(dg(do_t[64 * h : 64 * h + 64], ebuf[base + h]))
        dq[:, cols] = (dq_sum * HD**-0.5).astype(BF)
        dk[:, cols] = (jnp.concatenate(dks, axis=0) * LN2).astype(BF).T
        dv[:, cols] = jnp.concatenate(dvs, axis=0).astype(BF).T
        return carry

    lax.fori_loop(0, heads // 2, pair, 0)


class Gather:
    def __init__(self, own, out, send, recv):
        self.own, self.out, self.send, self.recv = own, out, send, recv
        self.spot = places()
        self.chunks = own.shape[1] // CHUNK
        self.sends, self.pending = [], {}

    def push(self, src, dst, k, i, device):
        copy = pltpu.make_async_remote_copy(
            src_ref=src, dst_ref=dst, send_sem=self.send.at[k, i], recv_sem=self.recv.at[k, i],
            device_id=device, device_id_type=MESH,
        )
        copy.start()
        self.sends.append(copy)
        self.pending.setdefault(k, []).append(copy)

    def stage(self, k, s):
        t, z, y, c = self.spot
        own, out = self.own, self.out
        half = CHUNK // 2
        full = pl.ds(k * CHUNK, CHUNK)
        left = pl.ds(k * CHUNK, half)
        right = pl.ds(k * CHUNK + half, half)
        for copy in self.pending.pop(k, ()):
            copy.wait_recv()
        if s == 0:
            for j in range(1, 4):
                self.push(own.at[:, full], out.at[t, z, y, c, :, full], k, j - 1, at(t, lax.rem(z + j, 4), y, c))
        elif s == 1:
            a = out.at[t, :, y, c, :, left]
            b = out.at[t, :, y, c, :, right]
            self.push(a, a, k, 3, at(1 - t, z, y, c))
            self.push(b, b, k, 4, at(t, z, 1 - y, c))
        elif s == 2:
            a = out.at[:, :, y, c, :, left]
            b = out.at[t, :, :, c, :, right]
            self.push(a, a, k, 5, at(t, z, 1 - y, c))
            self.push(b, b, k, 6, at(1 - t, z, y, c))
        elif s == 3:
            a = out.at[:, :, :, c, :, full]
            self.push(a, a, k, 7, at(t, z, y, 1 - c))

    def tick(self, i):
        for s in (4, 3, 2, 1, 0):
            if 0 <= i - s < self.chunks:
                self.stage(i - s, s)

    def finish(self):
        for copy in self.sends:
            copy.wait_send()


class Exchange:
    def __init__(self, send, recv, local):
        self.send, self.recv, self.local = send, recv, local
        self.open = []

    def start(self, i, halves, dst):
        t, z, y, c = places()
        rows = halves.shape[1]
        mine = dst.at[pl.ds(pl.multiple_of(t * rows, rows), rows), :]
        far = pltpu.make_async_remote_copy(
            src_ref=halves.at[1 - t], dst_ref=mine, send_sem=self.send.at[i], recv_sem=self.recv.at[i],
            device_id=at(1 - t, z, y, c), device_id_type=MESH,
        )
        near = pltpu.make_async_copy(halves.at[t], mine, self.local.at[i])
        far.start()
        near.start()
        self.open.append(far)
        return far, near

    def finish(self):
        for far in self.open:
            far.wait_send()


def forward(
    len_ref, gains, shifts, own, src_hbm, y0_hbm, g3_hbm,
    w_hbm, x_o, y0_o, g3_o,
    a0_o, q0_o, k0_o, v0_o, o0_o, ol0_o, r0_o, e0_o, x1_o, a1_o, h1_o, gp1_o, x2_o, mem_o,
    a3_o, q3_o, k3_o, v3_o, o3_o, ol3_o, r3_o, e3_o, y1_o,
    a4_o, q4_o, k4_o, v4_o, o4_o, ol4_o, r4_o, e4_o, y2_o,
    x, y0, wq, wk, wv, wo, sq, sk, sv, so, wu, wd, a, q, k, v, o, ol, r, a3, q3, k3, v3, o3, ol3, r3,
    x1, a1, h, gp, x2, mem, y1, y2, ebuf,
    gsend, grecv, xsend, xrecv, local, wsem, esem, osem,
):
    t, z, y, c = places()
    seq, width = x.shape
    n1, n2 = width // 2, h.shape[1] // 2
    greet(all_partners(t, z, y, c))
    halves = Exchange(xsend, xrecv, local)
    gather = Gather(own, w_hbm, gsend, grecv)
    mine = pltpu.make_async_copy(own, w_hbm.at[t, z, y, c], local.at[3])
    mine.start()
    gather.tick(0)
    x_far, x_near = halves.start(0, src_hbm, x)
    save = Saver(osem)
    x_near.wait()
    x_far.wait_recv()
    normalize(x, gains[0:1, :], shifts[0:1, :], a)
    save(x, x_o)
    save(a, a0_o, "A")
    mine.wait()
    for i in range(1, 5):
        gather.tick(i)
    loads = {}

    def load(name, offset, refs, n, base):
        loads[name] = []
        for i, ref in enumerate(refs):
            loads[name] += load_weight(w_hbm, offset + i * n, n, ref, wsem, base + 2 * i)

    load("enc", 0, (wq, wk, wv, wo), n1, 0)
    y0_far, y0_near = halves.start(1, y0_hbm, y0)
    gather.tick(5)
    load("self", 4 * n1, (sq, sk, sv, so), n1, 8)
    wait_all(loads["enc"])
    attn_project(a, a, wq, wk, wv, q, k, v)
    for src, dst in ((q, q0_o), (k, k0_o), (v, v0_o)):
        save(src, dst, "A")
    gather.tick(6)
    g3_far, g3_near = halves.start(2, g3_hbm, g3_o)
    attn_core(len_ref[0], q, k, v, o, ol, r, e0_o, ebuf, esem)
    for src, dst in ((o, o0_o), (ol, ol0_o), (r, r0_o)):
        save(src, dst, "A")
    gather.tick(7)
    load("feed", 8 * n1, (wu, wd), n2, 16)
    attn_join(x, o, wo, x1)
    save(x1, x1_o)
    y0_near.wait()
    y0_far.wait_recv()
    save(y0, y0_o)
    normalize(y0, gains[3:4, :], shifts[3:4, :], a3)
    wait_all(loads["self"])
    attn_project(a3, a3, sq, sk, sv, q3, k3, v3)
    for src, dst in ((a3, a3_o), (q3, q3_o), (k3, k3_o), (v3, v3_o)):
        save(src, dst)
    gather.tick(8)
    load("cross", 8 * n1 + 2 * n2, (wq, wk, wv, wo), n1, 0)
    attn_core(seq, q3, k3, v3, o3, ol3, r3, e3_o, ebuf, esem)
    for src, dst in ((o3, o3_o), (ol3, ol3_o), (r3, r3_o)):
        save(src, dst)
    gather.tick(9)
    attn_join(y0, o3, so, y1)
    save(y1, y1_o)
    save.free("A")
    normalize(y1, gains[4:5, :], shifts[4:5, :], a)
    wait_all(loads["feed"])

    def feed(sl):
        stream = x1[sl, :]
        hat, unused = ln_hat(stream)
        rows = (hat * gains[1:2, :] + shifts[1:2, :]).astype(BF)
        a1[sl, :] = rows
        active, slope = gelu_both(dg(rows, whole(wu)))
        active = active.astype(BF)
        h[sl, :] = active
        gp[sl, :] = slope.astype(BF)
        out = stream + dg(active, whole(wd), NT)
        x2[sl, :] = out
        hat, unused = ln_hat(out)
        mem[sl, :] = (hat * gains[2:3, :] + shifts[2:3, :]).astype(BF)

    rows_loop(seq, RB, feed)
    for src, dst in ((a1, a1_o), (h, h1_o), (gp, gp1_o), (x2, x2_o), (mem, mem_o)):
        save(src, dst)
    gather.tick(10)
    wait_all(loads["cross"])
    attn_project(a, mem, wq, wk, wv, q, k, v)
    for src, dst in ((a, a4_o), (q, q4_o), (k, k4_o), (v, v4_o)):
        save(src, dst)
    attn_core(len_ref[0], q, k, v, o, ol, r, e4_o, ebuf, esem)
    for src, dst in ((o, o4_o), (ol, ol4_o), (r, r4_o)):
        save(src, dst)
    attn_join(y1, o, wo, y2)
    save(y2, y2_o)
    g3_near.wait()
    g3_far.wait_recv()
    halves.finish()
    gather.finish()
    save.finish()


def attn_backward(
    g, x, gain, ng, index, a_t, kv_t, g_t, wq, wk, wv, wo, q, k, v, o, ol, r, e_hbm, ebuf, esem, ds,
    do, dq, dk, dv, stage, slot, free, emit, into_keys, finish,
):
    seq = x.shape[0]

    def before(sl):
        rows = g[sl, :].astype(BF)
        g_t[:, sl] = rows.T
        do[sl, :] = (dg(rows, wo[...]) * r[sl, :].astype(F32)).astype(BF)

    rows_loop(seq, 2 * RB, before)
    free(slot + 3)
    stage[slot + 3] = dg(g_t[...], o[...]).astype(BF)
    emit(slot + 3)
    attn_back_core(q, k, v, do, o, ol, e_hbm, ebuf, esem, ds, dq, dk, dv)
    free(slot)
    stage[slot] = dg(a_t[...], dq[...]).astype(BF)
    emit(slot)
    free(slot + 1)
    stage[slot + 1] = dg(kv_t[...], dk[...]).astype(BF)
    emit(slot + 1)
    free(slot + 2)
    stage[slot + 2] = dg(kv_t[...], dv[...]).astype(BF)
    emit(slot + 2)

    def after(sl):
        into = dg(dq[sl, :], wq[...], NT)
        keys = dg(dk[sl, :], wk[...], NT) + dg(dv[sl, :], wv[...], NT)
        if into_keys is None:
            into = into + keys
        else:
            into_keys[sl, :] = keys
        dx, dgain, dshift = ln_back(x[sl, :].astype(F32), gain, into)
        ng[index : index + 1, :] += dgain
        ng[8 + index : 9 + index, :] += dshift
        finish(sl, g[sl, :] + dx)

    rows_loop(seq, 2 * RB, after)


def dec_backward(
    gains, shifts, y2_hbm, g3_hbm, y1_hbm, y0_hbm, mem_hbm, a4_hbm, q4_hbm, k4_hbm, v4_hbm, o4_hbm, ol4_hbm, r4_hbm,
    a3_hbm, q3_hbm, k3_hbm, v3_hbm, o3_hbm, ol3_hbm, r3_hbm, e4_o, e3_o, w_hbm,
    dec_o, gy_o, ge_o, grad_o, ng,
    y2, g3, y1, y0, mem, a, q, k, v, o, ol, r, sq, sk, sv, so, cq, ck, cv, co, wu, wd,
    big, gs, do, a_t, kv_t, g_t, dec, stage, ebuf,
    xsem, wsem, esem, osem,
):
    seq, width = y0.shape
    n1, n2 = sq.shape[1] // 2, wu.shape[1] // 2
    ins = []

    def fetch(src, dst):
        cp = pltpu.make_async_copy(src, dst, xsem.at[len(ins)])
        cp.start()
        ins.append(cp)
        return cp

    loads = {}

    def load(name, offset, refs, n, base):
        loads[name] = []
        for i, ref in enumerate(refs):
            loads[name] += load_weight(w_hbm, offset + i * n, n, ref, wsem, base + 2 * i)

    first = [fetch(y2_hbm, y2), fetch(g3_hbm, g3)]
    load("feed", 12 * n1 + 2 * n2, (wu, wd), n2, 0)
    cross = [
        fetch(src, dst)
        for src, dst in ((o4_hbm, o), (r4_hbm, r), (a4_hbm, a), (mem_hbm, mem), (q4_hbm, q), (k4_hbm, k),
                         (v4_hbm, v), (ol4_hbm, ol), (y1_hbm, y1))
    ]
    load("cross", 8 * n1 + 2 * n2, (cq, ck, cv, co), n1, 4)
    load("self", 4 * n1, (sq, sk, sv, so), n1, 12)
    ng[...] = jnp.zeros_like(ng)
    wait_all(first)
    wait_all(loads["feed"])
    save = Saver(osem)
    h, du = big.at[0], big.at[1]

    def feed(sl):
        stream = y2[sl, :]
        hat, unused = ln_hat(stream)
        rows = (hat * gains[5:6, :] + shifts[5:6, :]).astype(BF)
        a_t[:, sl] = rows.T
        active, slope = gelu_both(dg(rows, wu[...]))
        active = active.astype(BF)
        h[sl, :] = active
        dec[sl, :] = (stream + dg(active, wd[...], NT)).astype(BF)
        grad = g3[sl, :]
        g_t[:, sl] = grad.T
        lifted = (dg(grad, wd[...]) * slope).astype(BF)
        du[sl, :] = lifted
        into = dg(lifted, wu[...], NT)
        dx, dgain, dshift = ln_back(stream, gains[5:6, :], into)
        ng[5:6, :] += dgain
        ng[13:14, :] += dshift
        gs[sl, :] = grad.astype(F32) + dx

    rows_loop(seq, RB, feed)
    save(dec, dec_o, "dec")
    parts = 2 * n2 // width

    def emit_part(src_slot, offset, n, lower):
        done = 0
        while done < width:
            t = (lower + done) // n
            at = (lower + done) % n
            take = min(width - done, n - at)
            save(
                stage.at[src_slot, :, pl.ds(done, take)],
                grad_o.at[t, :, pl.ds(offset + at, take)],
                src_slot,
            )
            done += take

    ff_offset = 8 * n1
    for j in range(parts):
        cols = pl.ds(j * width, width)
        stage[j] = dg(a_t[...], du[:, cols]).astype(BF)
        emit_part(j, ff_offset, n2, j * width)
        stage[parts + j] = dg(g_t[...], h[:, cols]).astype(BF)
        emit_part(parts + j, ff_offset + n2, n2, j * width)

    def emit(slot):
        emit_part(slot, slot * n1, n1, 0)

    ds = big.at[0]
    ds_view = big.at[0]
    dq, dk, dv = (big.at[1, :, pl.ds(i * width, width)] for i in range(3))
    wait_all(cross)
    wait_all(loads["cross"])
    a_t[...] = a[...].T
    kv_t[...] = mem[...].T

    def keep(sl, gradient):
        gs[sl, :] = gradient

    attn_backward(
        gs, y1, gains[4:5, :], ng, 4, a_t, kv_t, g_t, cq, ck, cv, co, q, k, v, o, ol, r, e4_o,
        ebuf, esem, SplitColumns(ds_view, seq), do, dq, dk, dv, stage, 4, save.free, emit, y2, keep,
    )
    save(y2, ge_o)
    second = [
        fetch(src, dst)
        for src, dst in ((a3_hbm, a), (o3_hbm, o), (r3_hbm, r), (q3_hbm, q), (k3_hbm, k), (v3_hbm, v),
                         (ol3_hbm, ol), (y0_hbm, y0))
    ]
    wait_all(loads["self"])
    wait_all(second)
    a_t[...] = a[...].T

    def last(sl, gradient):
        dec[sl, :] = gradient.astype(BF)

    save.free("dec")
    attn_backward(
        gs, y0, gains[3:4, :], ng, 3, a_t, a_t, g_t, sq, sk, sv, so, q, k, v, o, ol, r, e3_o,
        ebuf, esem, SplitColumns(ds_view, seq), do, dq, dk, dv, stage, 0, save.free, emit, None, last,
    )
    save(dec, gy_o)
    save.finish()


class Saver:
    def __init__(self, sems):
        self.sems, self.count, self.live = sems, 0, []

    def __call__(self, src, dst, slot=None):
        cp = pltpu.make_async_copy(src, dst, self.sems.at[self.count])
        cp.start()
        self.count += 1
        self.live.append((slot, cp))

    def free(self, slot):
        for name, cp in self.live:
            if name == slot:
                cp.wait()
        self.live = [entry for entry in self.live if entry[0] != slot]

    def finish(self):
        for name, cp in self.live:
            cp.wait()
        self.live = []


class SplitColumns:
    def __init__(self, ref, n):
        self.ref, self.n = ref, n

    def cols(self, h):
        return pl.ds(h * self.n, self.n)

    def __getitem__(self, h):
        return self.ref[:, self.cols(h)]

    def __setitem__(self, key, value):
        h, sl, unused = key
        self.ref[sl, self.cols(h)] = value


def enc_backward(
    gains, shifts, ge_hbm, x_hbm, x1_hbm, x2_hbm, a0_hbm, q0_hbm, k0_hbm, v0_hbm, o0_hbm, ol0_hbm, r0_hbm,
    a1_hbm, h1_hbm, gp1_hbm, e0_hbm, w_hbm,
    sg_o, grad_o, ng,
    ge, x, x1, x2, a0, q, k, v, o, ol, r, a1, big, wq, wk, wv, wo, wu, wd, gs, do, a_t, g_t, sg, stage, ebuf,
    xsem, wsem, esem, osem,
):
    seq, width = x.shape
    n1, n2 = wq.shape[1] // 2, wu.shape[1] // 2
    ins = {}
    order = (
        ("ge", ge_hbm, ge), ("x2", x2_hbm, x2), ("gp", gp1_hbm, big.at[1]), ("x1", x1_hbm, x1),
        ("a1", a1_hbm, a1), ("h", h1_hbm, big.at[0]), ("o", o0_hbm, o), ("ol", ol0_hbm, ol), ("r", r0_hbm, r),
        ("q", q0_hbm, q), ("k", k0_hbm, k), ("v", v0_hbm, v), ("a0", a0_hbm, a0), ("x", x_hbm, x),
    )
    loads = {}

    def begin(names):
        for i, (name, src, dst) in enumerate(order):
            if name in names:
                cp = pltpu.make_async_copy(src, dst, xsem.at[i])
                cp.start()
                ins[name] = cp

    begin(("ge", "x2", "gp", "x1"))
    offsets = (0, n1, 2 * n1, 3 * n1, 8 * n1, 8 * n1 + n2)
    for i, w in ((5, wd), (4, wu)):
        loads[i] = load_weight(w_hbm, offsets[i], n2, w, wsem, 2 * i)
    begin(("a1", "h", "o", "ol", "r", "q", "k", "v", "a0", "x"))
    for i, w in ((3, wo), (0, wq), (1, wk), (2, wv)):
        loads[i] = load_weight(w_hbm, offsets[i], n1, w, wsem, 2 * i)
    ng[...] = jnp.zeros_like(ng)
    for name in ("ge", "x2", "gp", "x1"):
        ins[name].wait()
    wait_all(loads[5])
    wait_all(loads[4])
    h, du = big.at[0], big.at[1]
    save = Saver(osem)

    def feed(sl):
        dx, dgain, dshift = ln_back(x2[sl, :], gains[2:3, :], ge[sl, :])
        ng[2:3, :] += dgain
        ng[10:11, :] += dshift
        grad = dx.astype(BF)
        g_t[:, sl] = grad.T
        lifted = (dg(grad, wd[...]) * du[sl, :].astype(F32)).astype(BF)
        du[sl, :] = lifted
        into = dg(lifted, wu[...], NT)
        dx1, dgain, dshift = ln_back(x1[sl, :], gains[1:2, :], into)
        ng[1:2, :] += dgain
        ng[9:10, :] += dshift
        gs[sl, :] = dx + dx1

    rows_loop(seq, RB, feed)
    parts = 2 * n2 // width

    def emit_part(src_slot, offset, n, lower):
        done = 0
        while done < width:
            t = (lower + done) // n
            at = (lower + done) % n
            take = min(width - done, n - at)
            save(
                stage.at[src_slot, :, pl.ds(done, take)],
                grad_o.at[t, :, pl.ds(offset + at, take)],
            )
            done += take

    ins["a1"].wait()
    ins["h"].wait()
    a_t[...] = a1[...].T
    for j in range(parts):
        cols = pl.ds(j * width, width)
        stage[4 + j] = dg(a_t[...], du[:, cols]).astype(BF)
        emit_part(4 + j, 4 * n1, n2, j * width)
        stage[4 + parts + j] = dg(g_t[...], h[:, cols]).astype(BF)
        emit_part(4 + parts + j, 4 * n1 + n2, n2, j * width)
    for name in ("o", "ol", "r", "q", "k", "v", "a0", "x"):
        ins[name].wait()
    for i in range(4):
        wait_all(loads[i])
    a_t[...] = a0[...].T

    def emit(slot):
        emit_part(slot, slot * n1, n1, 0)

    def last(sl, gradient):
        sg[sl, :] = gradient.astype(BF)

    dq, dk, dv = (big.at[1, :, pl.ds(i * width, width)] for i in range(3))
    attn_backward(
        gs, x, gains[0:1, :], ng, 0, a_t, a_t, g_t, wq, wk, wv, wo, q, k, v, o, ol, r, e0_hbm,
        ebuf, esem, SplitColumns(big.at[0], seq), do, dq, dk, dv, stage, 0, save.free, emit, None, last,
    )
    save(sg, sg_o)
    save.finish()


def compute_all(length, gains, shifts, own, source, start_y, grad3):
    rows, width = source.shape[1:]
    seq = 2 * rows
    total = own.shape[1]
    n1 = width // 2
    n2 = (total - 12 * n1) // 4
    hidden = 2 * n2
    heads = width // HD
    chunks = total // CHUNK
    part = own.shape[0]
    sd = jax.ShapeDtypeStruct
    any_spec = pl.BlockSpec(memory_space=pl.ANY)
    vmem = pl.BlockSpec(memory_space=pltpu.VMEM)
    smem = pl.BlockSpec(memory_space=pltpu.SMEM)
    dma = pltpu.SemaphoreType.DMA
    row = lambda kind: sd((seq, width), kind)
    tall = lambda kind: sd((seq, hidden), kind)
    escores = sd((heads, seq, seq), BF)
    vrow = lambda kind: pltpu.VMEM((seq, width), kind)
    vsq = pltpu.VMEM((width, width), BF)
    vwide = pltpu.VMEM((width, hidden), BF)
    vtall = pltpu.VMEM((seq, hidden), BF)
    vsq5 = pltpu.VMEM((4, 2, 2, part, width), BF)
    vwide5 = pltpu.VMEM((4, 2, 2, part, hidden), BF)
    ebuf = pltpu.VMEM((4, seq, seq), BF)
    attention = [row(BF)] * 7 + [escores]
    (
        gathered, x, y0, g3,
        a0, q0, k0, v0, o0, ol0, r0, e0, x1, a1, h1, gp1, x2, mem,
        a3, q3, k3, v3, o3, ol3, r3, e3, y1,
        a4, q4, k4, v4, o4, ol4, r4, e4, y2,
    ) = pl.pallas_call(
        forward,
        in_specs=[smem, vmem, vmem] + [any_spec] * 4,
        out_specs=[any_spec] * 36,
        out_shape=[sd((2, 4, 2, 2, part, total), BF)] + [row(BF)] * 3
        + attention + [row(F32), row(BF), tall(BF), tall(BF), row(F32), row(BF)]
        + attention + [row(F32)]
        + attention + [row(F32)],
        scratch_shapes=[vrow(BF)] * 2 + [vsq5] * 8 + [vwide5] * 2 + [vrow(BF)] * 14
        + [vrow(F32), vrow(BF), vtall, vtall, vrow(F32), vrow(BF), vrow(F32), vrow(F32), ebuf]
        + [dma((chunks, 8)), dma((chunks, 8)), dma((3,)), dma((3,)), dma((4,)), dma((20,)), dma((4,)), dma((35,))],
        compiler_params=pltpu.CompilerParams(
            vmem_limit_bytes=VMEM_LIMIT, collective_id=0, has_side_effects=True
        ),
        name="forward",
    )(length, gains, shifts, own, source, start_y, grad3)
    weights = gathered.reshape(2, width, total)
    slots = max(8, 2 * (hidden // width))
    dec, gy, ge, gdec, ng_dec = pl.pallas_call(
        dec_backward,
        in_specs=[vmem, vmem] + [any_spec] * 22,
        out_specs=[any_spec] * 4 + [vmem],
        out_shape=[row(BF), row(BF), row(F32), sd((2, width, 8 * n1 + 2 * n2), BF), sd((16, width), F32)],
        scratch_shapes=[vrow(F32), vrow(BF), vrow(F32)] + [vrow(BF)] * 9
        + [vsq] * 8 + [vwide] * 2
        + [pltpu.VMEM((2, seq, hidden), BF), vrow(F32), vrow(BF)]
        + [pltpu.VMEM((width, seq), BF)] * 3 + [vrow(BF), pltpu.VMEM((slots, width, width), BF), ebuf]
        + [dma((19,)), dma((20,)), dma((4,)), dma((3 + 4 * slots,))],
        compiler_params=pltpu.CompilerParams(vmem_limit_bytes=VMEM_LIMIT),
        name="dec_backward",
    )(gains, shifts, y2, g3, y1, y0, mem, a4, q4, k4, v4, o4, ol4, r4, a3, q3, k3, v3, o3, ol3, r3, e4, e3, weights)
    slots = 4 + 2 * (hidden // width)
    sg, genc, ng_enc = pl.pallas_call(
        enc_backward,
        in_specs=[vmem, vmem] + [any_spec] * 16,
        out_specs=[any_spec] * 2 + [vmem],
        out_shape=[row(BF), sd((2, width, 4 * n1 + 2 * n2), BF), sd((16, width), F32)],
        scratch_shapes=[vrow(F32), vrow(BF), vrow(F32), vrow(F32)] + [vrow(BF)] * 8
        + [pltpu.VMEM((2, seq, hidden), BF)] + [vsq] * 4 + [vwide] * 2 + [vrow(F32), vrow(BF)]
        + [pltpu.VMEM((width, seq), BF)] * 2 + [vrow(BF), pltpu.VMEM((slots, width, width), BF), ebuf]
        + [dma((14,)), dma((12,)), dma((4,)), dma((3 + 4 * slots,))],
        compiler_params=pltpu.CompilerParams(vmem_limit_bytes=VMEM_LIMIT),
        name="enc_backward",
    )(gains, shifts, ge, x, x1, x2, a0, q0, k0, v0, o0, ol0, r0, a1, h1, gp1, e0, weights)
    return dec, sg, gy, genc, gdec, ng_enc + ng_dec


def places():
    d = lax.axis_index("dp")
    return lax.axis_index("tensor"), d // 4, (d // 2) % 2, d % 2


def at(t, z, y, c):
    return (z * 4 + y * 2 + c, t)


def greet(partners):
    barrier = pltpu.get_barrier_semaphore()
    for device in partners:
        pl.semaphore_signal(barrier, inc=1, device_id=device, device_id_type=MESH)
    pl.semaphore_wait(barrier, len(partners))


def all_partners(t, z, y, c):
    others = [at(t, lax.rem(z + j, 4), y, c) for j in range(1, 4)]
    return [at(t, z, y, 1 - c), at(1 - t, z, y, c), at(t, z, 1 - y, c)] + others


CHUNK = 1024


def sum_grads(genc, gdec, vec, out, vec_out, r1, s1, r2a, r2b, s2a, s2b, r3a, r3b, s3, r4, v1, vr, send, recv, local, vsend, vrecv):
    t, z, y, c = places()
    greet(all_partners(t, z, y, c))
    enc_chunks = genc.shape[-1] // CHUNK
    chunks = enc_chunks + gdec.shape[-1] // CHUNK
    half = CHUNK // 2
    sends = []

    def push(src, dst, ssem, rsem, device):
        copy = pltpu.make_async_remote_copy(
            src_ref=src, dst_ref=dst, send_sem=ssem, recv_sem=rsem, device_id=device, device_id_type=MESH,
        )
        copy.start()
        sends.append(copy)
        return copy

    def big(k):
        if k < enc_chunks:
            return genc, pl.ds(k * CHUNK, CHUNK)
        return gdec, pl.ds((k - enc_chunks) * CHUNK, CHUNK)

    pending, own = {}, {}
    left, right = pl.ds(0, half), pl.ds(half, half)

    def stage(k, s):
        if s == 0:
            g, cols = big(k)
            own[k] = pltpu.make_async_copy(g.at[:, :, :, c, :, cols], s1.at[k], local.at[k])
            own[k].start()
            pending[k] = [push(g.at[:, :, :, 1 - c, :, cols], r1.at[k], send.at[k, 0], recv.at[k, 0], at(t, z, y, 1 - c))]
            return
        for copy in pending[k]:
            copy.wait_recv()
        if s == 1:
            own[k].wait()
            s1[k] = (s1[k].astype(F32) + r1[k].astype(F32)).astype(BF)
            pending[k] = [
                push(s1.at[k, 1 - t, :, :, :, left], r2a.at[k], send.at[k, 1], recv.at[k, 1], at(1 - t, z, y, c)),
                push(s1.at[k, :, :, 1 - y, :, right], r2b.at[k], send.at[k, 2], recv.at[k, 2], at(t, z, 1 - y, c)),
            ]
        elif s == 2:
            s2a[k] = (s1[k, t, :, :, :, left].astype(F32) + r2a[k].astype(F32)).astype(BF)
            s2b[k] = (s1[k, :, :, y, :, right].astype(F32) + r2b[k].astype(F32)).astype(BF)
            pending[k] = [
                push(s2a.at[k, :, 1 - y], r3a.at[k], send.at[k, 3], recv.at[k, 3], at(t, z, 1 - y, c)),
                push(s2b.at[k, 1 - t], r3b.at[k], send.at[k, 4], recv.at[k, 4], at(1 - t, z, y, c)),
            ]
        elif s == 3:
            s3[k, :, :, left] = (s2a[k, :, y].astype(F32) + r3a[k].astype(F32)).astype(BF)
            s3[k, :, :, right] = (s2b[k, t].astype(F32) + r3b[k].astype(F32)).astype(BF)
            pending[k] = []
            for j in range(1, 4):
                zz = lax.rem(z + j, 4)
                pending[k].append(push(s3.at[k, zz], r4.at[k, j - 1], send.at[k, 4 + j], recv.at[k, 4 + j], at(t, zz, y, c)))
        elif s == 4:
            out[:, pl.ds(k * CHUNK, CHUNK)] = (s3[k, z].astype(F32) + r4[k, 0].astype(F32)) + (
                r4[k, 1].astype(F32) + r4[k, 2].astype(F32)
            )

    vpending = []

    def vector_stage(s):
        for copy in vpending:
            copy.wait_recv()
        vpending.clear()
        if s == 0:
            v1[0] = vec[...]
        elif s < 4:
            v1[s] = v1[s - 1] + vr[s - 1]
        if s < 3:
            device = (at(t, z, y, 1 - c), at(1 - t, z, y, c), at(t, z, 1 - y, c))[s]
            vpending.append(push(v1.at[s], vr.at[s], vsend.at[s], vrecv.at[s], device))
        elif s == 3:
            for j in range(1, 4):
                vpending.append(
                    push(v1.at[3], vr.at[2 + j], vsend.at[2 + j], vrecv.at[2 + j], at(t, lax.rem(z + j, 4), y, c))
                )
        else:
            vec_out[...] = (v1[3] + vr[3]) + (vr[4] + vr[5])

    for tick in range(chunks + 4):
        for s in (4, 3, 2, 1, 0):
            k = tick - s
            if 0 <= k < chunks:
                stage(k, s)
        if tick < 5:
            vector_stage(tick)
    for copy in sends:
        copy.wait_send()


def call_sum(genc, gdec, vec):
    rows = genc.shape[1] // 16
    split = lambda g: g.reshape(2, 4, 2, 2, rows, g.shape[2])
    n = genc.shape[2] + gdec.shape[2]
    chunks = n // CHUNK
    half = CHUNK // 2
    any_spec = pl.BlockSpec(memory_space=pl.ANY)
    vmem = pl.BlockSpec(memory_space=pltpu.VMEM)
    dma = pltpu.SemaphoreType.DMA
    buf = lambda *dims: pltpu.VMEM((chunks,) + dims, BF)
    return pl.pallas_call(
        sum_grads,
        in_specs=[any_spec, any_spec, vmem],
        out_specs=[vmem, vmem],
        out_shape=[jax.ShapeDtypeStruct((rows, n), F32), jax.ShapeDtypeStruct(vec.shape, F32)],
        scratch_shapes=[
            buf(2, 4, 2, rows, CHUNK), buf(2, 4, 2, rows, CHUNK),
            buf(4, 2, rows, half), buf(2, 4, rows, half), buf(4, 2, rows, half), buf(2, 4, rows, half),
            buf(4, rows, half), buf(4, rows, half), buf(4, rows, CHUNK), buf(3, rows, CHUNK),
            pltpu.VMEM((4,) + vec.shape, F32), pltpu.VMEM((6,) + vec.shape, F32),
            dma((chunks, 8)), dma((chunks, 8)), dma((chunks,)), dma((6,)), dma((6,)),
        ],
        compiler_params=pltpu.CompilerParams(
            collective_id=1, has_side_effects=True, vmem_limit_bytes=VMEM_LIMIT
        ),
        name="sum_grads",
    )(split(genc), split(gdec), vec)


def return_halves(whole):
    t = lax.axis_index("tensor")
    rows = whole.shape[0] // 2
    parts = whole.reshape(2, rows, whole.shape[1])
    sent = lax.dynamic_index_in_dim(parts, 1 - t, 0, keepdims=False)
    kept = lax.dynamic_index_in_dim(parts, t, 0, keepdims=False)
    got = lax.ppermute(sent, "tensor", [(0, 1), (1, 0)])
    return jnp.stack([jnp.where(t == 0, kept, got), jnp.where(t == 0, got, kept)])


def pair_body(*arguments):
    source, target, cotangent, lengths, timesteps, masked, loss_mask = arguments[:7]
    matrices = arguments[7:23]
    norm_gains, norm_shifts, mask_vector = arguments[23:]
    t = lax.axis_index("tensor")
    turned = (3, 5, 9, 13, 15)
    order = (0, 1, 2, 3, 6, 7, 8, 9, 4, 5, 10, 11, 12, 13, 14, 15)
    own = jnp.concatenate([matrices[i].T if i in turned else matrices[i] for i in order], axis=1)
    chosen = masked[:, :, None] == 1
    start_y = jnp.where(chosen, mask_vector, target.astype(F32)).astype(BF)
    factor = (STEPS + 1 - timesteps).astype(F32) / STEPS
    grad3 = (
        cotangent.astype(F32) * (factor[:, None] * loss_mask.astype(F32))[:, :, None]
    ).astype(BF)
    length = lax.dynamic_slice_in_dim(lengths, t, 1)
    dec, sg, gy, genc, gdec, ng = compute_all(
        length, norm_gains, norm_shifts, own, source, start_y, grad3
    )
    decoded = return_halves(dec)
    grad_y = return_halves(gy)
    target_grad = jnp.where(chosen, jnp.zeros((), BF), grad_y)
    mask_part = jnp.sum(jnp.where(chosen, grad_y.astype(F32), 0.0), axis=(0, 1))
    source_grad = return_halves(sg)
    vec = jnp.concatenate([ng[:6], ng[8:14], mask_part[None], jnp.zeros((3, ng.shape[1]), F32)], axis=0)
    summed, vec = call_sum(genc, gdec, vec)
    grads, offset = [], 0
    for i, m in enumerate(matrices):
        n = m.shape[0] if i in turned else m.shape[1]
        part = summed[:, offset : offset + n]
        offset += n
        grads.append(part.T if i in turned else part)
    return (decoded, source_grad, target_grad, *grads, vec[:6], vec[6:12], vec[12])


def solution(mesh):
    whole_pairs = dict(mesh.shape) == {"dp": 16, "tensor": 2}
    return jax.shard_map(
        pair_body if whole_pairs else body,
        mesh=mesh,
        in_specs=(
            P("dp", "tensor", None),
            P("dp", "tensor", None),
            P("dp", "tensor", None),
            P("dp"),
            P("dp"),
            P("dp", "tensor"),
            P("dp", "tensor"),
            P("dp", "tensor"),
            P("dp", "tensor"),
            P("dp", "tensor"),
            P("tensor", "dp"),
            P("dp", "tensor"),
            P("tensor", "dp"),
            P("dp", "tensor"),
            P("dp", "tensor"),
            P("dp", "tensor"),
            P("tensor", "dp"),
            P("dp", "tensor"),
            P("dp", "tensor"),
            P("dp", "tensor"),
            P("tensor", "dp"),
            P("dp", "tensor"),
            P("tensor", "dp"),
            P(),
            P(),
            P(),
        ),
        out_specs=(
            P("dp", "tensor", None),
            P("dp", "tensor", None),
            P("dp", "tensor", None),
            P("dp", "tensor"),
            P("dp", "tensor"),
            P("dp", "tensor"),
            P("tensor", "dp"),
            P("dp", "tensor"),
            P("tensor", "dp"),
            P("dp", "tensor"),
            P("dp", "tensor"),
            P("dp", "tensor"),
            P("tensor", "dp"),
            P("dp", "tensor"),
            P("dp", "tensor"),
            P("dp", "tensor"),
            P("tensor", "dp"),
            P("dp", "tensor"),
            P("tensor", "dp"),
            P(),
            P(),
            P(),
        ),
        check_vma=False,
    )
```

```python
import jax
import jax.numpy as jnp
from jax import lax
from jax.experimental import pallas as pl
from jax.experimental.pallas import tpu as pltpu
from jax.sharding import PartitionSpec as P

HD = 64
MICRO = 2
STEPS = 50


eps = 1e-05
floor_score = -1e30


def norm_rows(inputs, gain, shift):
    average = jnp.mean(inputs, axis=-1, keepdims=True)
    centred = inputs - average
    second = jnp.mean(centred * centred, axis=-1, keepdims=True)
    return centred * lax.rsqrt(second + eps) * gain + shift


def norm_back(inputs, gain, shift, gradient):
    unused, pullback = jax.vjp(norm_rows, inputs, gain, shift)
    return pullback(gradient)


def smooth(values):
    return jax.nn.gelu(values, approximate=False)


def spread(inputs):
    return lax.all_gather(inputs.astype(jnp.bfloat16), "tensor", axis=1, tiled=True)


def collect(partial_value):
    return lax.psum_scatter(partial_value, "tensor", scatter_dimension=1, tiled=True)


def spread_grad(gradient):
    return lax.all_gather(gradient.astype(jnp.bfloat16), "tensor", axis=1, tiled=True)


def collect_grad(partial_value):
    return lax.psum_scatter(partial_value, "tensor", scatter_dimension=1, tiled=True)


def project(inputs, weight):
    return jnp.einsum("bsk,kn->bsn", inputs, weight, preferred_element_type=jnp.float32)


def weight_grad(inputs, gradient):
    return jnp.einsum("bsk,bsn->kn", inputs, gradient, preferred_element_type=jnp.float32)


def back_project(gradient, weight):
    return jnp.einsum("bsn,kn->bsk", gradient, weight, preferred_element_type=jnp.float32)


def masked_scores(query_part, key_rows, live):
    scores = jnp.einsum(
        "bqhd,bkhd->bhqk", query_part, key_rows, preferred_element_type=jnp.float32
    ) * HD ** (-0.5)
    return jnp.where(live[:, None, None, :], scores, floor_score)


def attend_forward(query_in, keys_in, w_query, w_key, w_value, live):
    pair_count, length = (query_in.shape[0], query_in.shape[1])
    head_count = w_query.shape[1] // HD
    queries = (
        project(query_in, w_query).astype(jnp.bfloat16).reshape(pair_count, length, head_count, HD)
    )
    key_rows = (
        project(keys_in, w_key).astype(jnp.bfloat16).reshape(pair_count, length, head_count, HD)
    )
    value_rows = (
        project(keys_in, w_value).astype(jnp.bfloat16).reshape(pair_count, length, head_count, HD)
    )
    block_rows = min(512, length)
    pieces = []
    totals = []
    for offset in range(0, length, block_rows):
        scores = masked_scores(queries[:, offset : offset + block_rows], key_rows, live)
        highest = jnp.max(scores, axis=-1, keepdims=True)
        exponent = jnp.exp(scores - highest)
        summed = jnp.sum(exponent, axis=-1, keepdims=True)
        softmax = (exponent / summed).astype(jnp.bfloat16)
        pieces.append(
            jnp.einsum("bhqk,bkhd->bqhd", softmax, value_rows, preferred_element_type=jnp.float32)
        )
        totals.append(highest + jnp.log(summed))
    attended = (
        jnp.concatenate(pieces, axis=1)
        .astype(jnp.bfloat16)
        .reshape(pair_count, length, head_count * HD)
    )
    return (queries, key_rows, value_rows, attended, jnp.concatenate(totals, axis=2))


def attend_backward(whole_grad, query_in, keys_in, w_query, w_key, w_value, w_out, saved, live):
    queries, key_rows, value_rows, attended, totals = saved
    pair_count, length, head_count = (queries.shape[0], queries.shape[1], queries.shape[2])
    scale_score = HD ** (-0.5)
    out_grad = weight_grad(attended, whole_grad)
    head_grad = (
        back_project(whole_grad, w_out)
        .astype(jnp.bfloat16)
        .reshape(pair_count, length, head_count, HD)
    )
    block_rows = min(512, length)
    key_total = jnp.zeros(key_rows.shape, jnp.float32)
    value_total = jnp.zeros(value_rows.shape, jnp.float32)
    query_parts = []
    for offset in range(0, length, block_rows):
        query_part = queries[:, offset : offset + block_rows]
        grad_part = head_grad[:, offset : offset + block_rows]
        scores = masked_scores(query_part, key_rows, live)
        softmax = jnp.exp(scores - totals[:, :, offset : offset + block_rows])
        value_total = value_total + jnp.einsum(
            "bhqk,bqhd->bkhd",
            softmax.astype(jnp.bfloat16),
            grad_part,
            preferred_element_type=jnp.float32,
        )
        soft_grad = jnp.einsum(
            "bqhd,bkhd->bhqk", grad_part, value_rows, preferred_element_type=jnp.float32
        )
        inner = jnp.sum(softmax * soft_grad, axis=-1, keepdims=True)
        score_grad = (softmax * (soft_grad - inner)).astype(jnp.bfloat16)
        query_parts.append(
            jnp.einsum("bhqk,bkhd->bqhd", score_grad, key_rows, preferred_element_type=jnp.float32)
            * scale_score
        )
        key_total = (
            key_total
            + jnp.einsum(
                "bhqk,bqhd->bkhd", score_grad, query_part, preferred_element_type=jnp.float32
            )
            * scale_score
        )
    query_grad = (
        jnp.concatenate(query_parts, axis=1)
        .astype(jnp.bfloat16)
        .reshape(pair_count, length, head_count * HD)
    )
    key_grad = key_total.astype(jnp.bfloat16).reshape(
        pair_count, key_rows.shape[1], head_count * HD
    )
    value_grad = value_total.astype(jnp.bfloat16).reshape(
        pair_count, value_rows.shape[1], head_count * HD
    )
    grads = (
        weight_grad(query_in, query_grad),
        weight_grad(keys_in, key_grad),
        weight_grad(keys_in, value_grad),
        out_grad,
    )
    into_keys = back_project(key_grad, w_key) + back_project(value_grad, w_value)
    return (grads, back_project(query_grad, w_query), into_keys)


def feed_forward(inputs, w_up, w_down):
    lifted = project(inputs, w_up)
    active = smooth(lifted).astype(jnp.bfloat16)
    return (lifted, active, project(active, w_down))


def feed_backward(gradient, inputs, w_up, w_down, lifted, active):
    down_grad = weight_grad(active, gradient)
    active_grad = back_project(gradient, w_down)
    unused, smooth_back = jax.vjp(smooth, lifted)
    lifted_grad = smooth_back(active_grad)[0].astype(jnp.bfloat16)
    return ((weight_grad(inputs, lifted_grad), down_grad), back_project(lifted_grad, w_up))


def body(
    source,
    target,
    cotangent,
    lengths,
    timesteps,
    masked,
    loss_mask,
    enc_query,
    enc_key,
    enc_value,
    enc_out,
    enc_up,
    enc_down,
    self_query,
    self_key,
    self_value,
    self_out,
    cross_query,
    cross_key,
    cross_value,
    cross_out,
    dec_up,
    dec_down,
    norm_gains,
    norm_shifts,
    mask_vector,
):
    pairs_dev, rows_dev = (source.shape[0], source.shape[1])
    per_micro = pairs_dev // MICRO
    seq_len = rows_dev * lax.axis_size("tensor")
    positions = jnp.arange(seq_len)
    gains, shifts = (norm_gains, norm_shifts)
    gain_total = jnp.zeros(norm_gains.shape, jnp.float32)
    shift_total = jnp.zeros(norm_shifts.shape, jnp.float32)
    mask_total = jnp.zeros(mask_vector.shape, jnp.float32)
    decoded_parts = []
    source_parts = []
    target_parts = []
    running = None
    for micro in range(MICRO):
        weights = (
            lax.all_gather(enc_query, "dp", axis=0, tiled=True),
            lax.all_gather(enc_key, "dp", axis=0, tiled=True),
            lax.all_gather(enc_value, "dp", axis=0, tiled=True),
            lax.all_gather(enc_out, "dp", axis=1, tiled=True),
            lax.all_gather(enc_up, "dp", axis=0, tiled=True),
            lax.all_gather(enc_down, "dp", axis=1, tiled=True),
            lax.all_gather(self_query, "dp", axis=0, tiled=True),
            lax.all_gather(self_key, "dp", axis=0, tiled=True),
            lax.all_gather(self_value, "dp", axis=0, tiled=True),
            lax.all_gather(self_out, "dp", axis=1, tiled=True),
            lax.all_gather(cross_query, "dp", axis=0, tiled=True),
            lax.all_gather(cross_key, "dp", axis=0, tiled=True),
            lax.all_gather(cross_value, "dp", axis=0, tiled=True),
            lax.all_gather(cross_out, "dp", axis=1, tiled=True),
            lax.all_gather(dec_up, "dp", axis=0, tiled=True),
            lax.all_gather(dec_down, "dp", axis=1, tiled=True),
        )
        wide = (
            lax.all_gather(weights[4], "tensor", axis=1, tiled=True),
            lax.all_gather(weights[5], "tensor", axis=0, tiled=True),
            lax.all_gather(weights[14], "tensor", axis=1, tiled=True),
            lax.all_gather(weights[15], "tensor", axis=0, tiled=True),
        )
        lower = micro * per_micro
        upper = lower + per_micro
        live = positions[None, :] < lengths[lower:upper][:, None]
        every = jnp.ones((per_micro, seq_len), bool)
        inputs_x = source[lower:upper].astype(jnp.float32)
        rows0 = spread(norm_rows(inputs_x, gains[0], shifts[0]))
        saved0 = attend_forward(rows0, rows0, weights[0], weights[1], weights[2], live)
        stream1 = inputs_x + collect(project(saved0[3], weights[3]))
        normed1 = norm_rows(stream1, gains[1], shifts[1])
        rows1 = normed1.astype(jnp.bfloat16)
        lifted1, active1, partial1 = feed_forward(rows1, wide[0], wide[1])
        stream2 = stream1 + partial1
        memory_rows = spread(norm_rows(stream2, gains[2], shifts[2]))
        chosen = masked[lower:upper][:, :, None] == 1
        start_y = jnp.where(chosen, mask_vector, target[lower:upper].astype(jnp.float32))
        rows3 = spread(norm_rows(start_y, gains[3], shifts[3]))
        saved3 = attend_forward(rows3, rows3, weights[6], weights[7], weights[8], every)
        stream4 = start_y + collect(project(saved3[3], weights[9]))
        rows4 = spread(norm_rows(stream4, gains[4], shifts[4]))
        saved4 = attend_forward(rows4, memory_rows, weights[10], weights[11], weights[12], live)
        stream5 = stream4 + collect(project(saved4[3], weights[13]))
        normed5 = norm_rows(stream5, gains[5], shifts[5])
        rows5 = normed5.astype(jnp.bfloat16)
        lifted5, active5, partial5 = feed_forward(rows5, wide[2], wide[3])
        stream6 = stream5 + partial5
        decoded_parts.append(stream6.astype(jnp.bfloat16))
        factor = (STEPS + 1 - timesteps[lower:upper]).astype(jnp.float32) / STEPS
        grad6 = (
            cotangent[lower:upper].astype(jnp.float32)
            * (factor[:, None] * loss_mask[lower:upper].astype(jnp.float32))[:, :, None]
        )
        (up5, down5), into5 = feed_backward(
            grad6.astype(jnp.bfloat16), rows5, wide[2], wide[3], lifted5, active5
        )
        back5 = norm_back(stream5, gains[5], shifts[5], into5)
        grad5 = grad6 + back5[0]
        grads4, query_term4, memory_term = attend_backward(
            spread_grad(grad5),
            rows4,
            memory_rows,
            weights[10],
            weights[11],
            weights[12],
            weights[13],
            saved4,
            live,
        )
        back4 = norm_back(stream4, gains[4], shifts[4], collect_grad(query_term4))
        grad4 = grad5 + back4[0]
        memory_grad = collect_grad(memory_term)
        grads3, query_term3, keys_term3 = attend_backward(
            spread_grad(grad4),
            rows3,
            rows3,
            weights[6],
            weights[7],
            weights[8],
            weights[9],
            saved3,
            every,
        )
        back3 = norm_back(start_y, gains[3], shifts[3], collect_grad(query_term3 + keys_term3))
        grad_y = grad4 + back3[0]
        target_parts.append(jnp.where(chosen, 0.0, grad_y).astype(jnp.bfloat16))
        mask_total = mask_total + jnp.sum(jnp.where(chosen, grad_y, 0.0), axis=(0, 1))
        back2 = norm_back(stream2, gains[2], shifts[2], memory_grad)
        grad2 = back2[0]
        (up1, down1), into1 = feed_backward(
            grad2.astype(jnp.bfloat16), rows1, wide[0], wide[1], lifted1, active1
        )
        back1 = norm_back(stream1, gains[1], shifts[1], into1)
        grad1 = grad2 + back1[0]
        grads0, query_term0, keys_term0 = attend_backward(
            spread_grad(grad1),
            rows0,
            rows0,
            weights[0],
            weights[1],
            weights[2],
            weights[3],
            saved0,
            live,
        )
        back0 = norm_back(inputs_x, gains[0], shifts[0], collect_grad(query_term0 + keys_term0))
        source_parts.append((grad1 + back0[0]).astype(jnp.bfloat16))
        gain_total = gain_total + jnp.stack(
            [back0[1], back1[1], back2[1], back3[1], back4[1], back5[1]]
        )
        shift_total = shift_total + jnp.stack(
            [back0[2], back1[2], back2[2], back3[2], back4[2], back5[2]]
        )
        up1, down1, up5, down5 = (
            lax.psum_scatter(
                up1.astype(jnp.bfloat16), "tensor", scatter_dimension=1, tiled=True
            ).astype(jnp.float32),
            lax.psum_scatter(
                down1.astype(jnp.bfloat16), "tensor", scatter_dimension=0, tiled=True
            ).astype(jnp.float32),
            lax.psum_scatter(
                up5.astype(jnp.bfloat16), "tensor", scatter_dimension=1, tiled=True
            ).astype(jnp.float32),
            lax.psum_scatter(
                down5.astype(jnp.bfloat16), "tensor", scatter_dimension=0, tiled=True
            ).astype(jnp.float32),
        )
        fresh = (
            grads0[0],
            grads0[1],
            grads0[2],
            grads0[3],
            up1,
            down1,
            grads3[0],
            grads3[1],
            grads3[2],
            grads3[3],
            grads4[0],
            grads4[1],
            grads4[2],
            grads4[3],
            up5,
            down5,
        )
        running = fresh if micro == 0 else jax.tree.map(jnp.add, running, tuple(fresh))
    running = (
        lax.psum_scatter(
            running[0].astype(jnp.bfloat16), "dp", scatter_dimension=0, tiled=True
        ).astype(jnp.float32),
        lax.psum_scatter(
            running[1].astype(jnp.bfloat16), "dp", scatter_dimension=0, tiled=True
        ).astype(jnp.float32),
        lax.psum_scatter(
            running[2].astype(jnp.bfloat16), "dp", scatter_dimension=0, tiled=True
        ).astype(jnp.float32),
        lax.psum_scatter(
            running[3].astype(jnp.bfloat16), "dp", scatter_dimension=1, tiled=True
        ).astype(jnp.float32),
        lax.psum_scatter(
            running[4].astype(jnp.bfloat16), "dp", scatter_dimension=0, tiled=True
        ).astype(jnp.float32),
        lax.psum_scatter(
            running[5].astype(jnp.bfloat16), "dp", scatter_dimension=1, tiled=True
        ).astype(jnp.float32),
        lax.psum_scatter(
            running[6].astype(jnp.bfloat16), "dp", scatter_dimension=0, tiled=True
        ).astype(jnp.float32),
        lax.psum_scatter(
            running[7].astype(jnp.bfloat16), "dp", scatter_dimension=0, tiled=True
        ).astype(jnp.float32),
        lax.psum_scatter(
            running[8].astype(jnp.bfloat16), "dp", scatter_dimension=0, tiled=True
        ).astype(jnp.float32),
        lax.psum_scatter(
            running[9].astype(jnp.bfloat16), "dp", scatter_dimension=1, tiled=True
        ).astype(jnp.float32),
        lax.psum_scatter(
            running[10].astype(jnp.bfloat16), "dp", scatter_dimension=0, tiled=True
        ).astype(jnp.float32),
        lax.psum_scatter(
            running[11].astype(jnp.bfloat16), "dp", scatter_dimension=0, tiled=True
        ).astype(jnp.float32),
        lax.psum_scatter(
            running[12].astype(jnp.bfloat16), "dp", scatter_dimension=0, tiled=True
        ).astype(jnp.float32),
        lax.psum_scatter(
            running[13].astype(jnp.bfloat16), "dp", scatter_dimension=1, tiled=True
        ).astype(jnp.float32),
        lax.psum_scatter(
            running[14].astype(jnp.bfloat16), "dp", scatter_dimension=0, tiled=True
        ).astype(jnp.float32),
        lax.psum_scatter(
            running[15].astype(jnp.bfloat16), "dp", scatter_dimension=1, tiled=True
        ).astype(jnp.float32),
    )
    vectors = lax.psum((gain_total, shift_total, mask_total), ("dp", "tensor"))
    return (
        jnp.concatenate(decoded_parts, axis=0),
        jnp.concatenate(source_parts, axis=0),
        jnp.concatenate(target_parts, axis=0),
        running[0],
        running[1],
        running[2],
        running[3],
        running[4],
        running[5],
        running[6],
        running[7],
        running[8],
        running[9],
        running[10],
        running[11],
        running[12],
        running[13],
        running[14],
        running[15],
        vectors[0],
        vectors[1],
        vectors[2],
    )


F32 = jnp.float32
BF = jnp.bfloat16
LOG2E = 1.4426950408889634
LN2 = 0.6931471805599453
NN = (((1,), (0,)), ((), ()))
NT = (((1,), (1,)), ((), ()))
MESH = pl.DeviceIdType.MESH
RB = 256
VMEM_LIMIT = 63 * 2**20


def dg(left, right, dims=NN):
    return lax.dot_general(left, right, dims, preferred_element_type=F32)


def ln_hat(x):
    centred = x - jnp.mean(x, axis=-1, keepdims=True)
    rstd = lax.rsqrt(jnp.mean(centred * centred, axis=-1, keepdims=True) + eps)
    return centred * rstd, rstd


def ln_back(x, gain, gradient):
    hat, rstd = ln_hat(x)
    scaled = gradient * gain
    first = jnp.mean(scaled, axis=-1, keepdims=True)
    second = jnp.mean(scaled * hat, axis=-1, keepdims=True)
    dx = rstd * (scaled - first - hat * second)
    dgain = jnp.sum(gradient * hat, axis=0, keepdims=True)
    dshift = jnp.sum(gradient, axis=0, keepdims=True)
    return dx, dgain, dshift


def gelu_both(u):
    size = jnp.abs(u)
    t = 1.0 / (1.0 + (0.3275911 * 0.7071067811865476) * size)
    ex = jnp.exp2(u * u * (-0.5 * LOG2E))
    poly = t * (
        0.127414796
        + t * (-0.142248368 + t * (0.7107068705 + t * (-0.7265760135 + t * 0.5307027145)))
    )
    tail = poly * ex
    phi = jnp.where(u > 0, 1.0 - tail, tail)
    return u * phi, phi + u * ex * 0.3989422804014327


def rows_loop(total, step, run):
    def once(i, carry):
        run(pl.ds(pl.multiple_of(i * step, step), step))
        return carry

    lax.fori_loop(0, total // step, once, 0)


def load_weight(w_hbm, offset, width, dst, sems, base):
    copies = []
    for t in range(2):
        src = pl.ds(offset, width)
        to = pl.ds(t * width, width)
        cp = pltpu.make_async_copy(
            w_hbm.at[t, :, src] if len(w_hbm.shape) == 3 else w_hbm.at[t, :, :, :, :, src],
            dst.at[:, to] if len(dst.shape) == 2 else dst.at[:, :, :, :, to],
            sems.at[base + t],
        )
        cp.start()
        copies.append(cp)
    return copies


def wait_all(copies):
    for cp in copies:
        cp.wait()


def whole(ref):
    value = ref[...]
    return value if value.ndim == 2 else value.reshape(-1, value.shape[-1])


def normalize(x, gain, shift, a):
    def run(sl):
        hat, unused = ln_hat(x[sl, :].astype(F32))
        a[sl, :] = (hat * gain + shift).astype(BF)

    rows_loop(x.shape[0], 2 * RB, run)


def attn_project(a, kv, wq, wk, wv, q, k, v):
    def run(sl):
        q[sl, :] = (dg(a[sl, :], whole(wq)) * (LOG2E * HD**-0.5)).astype(BF)
        k[sl, :] = dg(kv[sl, :], whole(wk)).astype(BF)
        v[sl, :] = dg(kv[sl, :], whole(wv)).astype(BF)

    rows_loop(a.shape[0], 2 * RB, run)


def attn_core(length, q, k, v, o, ol, r, e_hbm, ebuf, esem, between):
    seq = q.shape[0]
    pairs = q.shape[1] // 128
    block = 512
    lane = lax.broadcasted_iota(jnp.int32, (1, 128), 1)
    low = lane < 64
    one = jnp.ones((), BF)
    key = lax.broadcasted_iota(jnp.int32, (seq, 1), 0)
    bias = jnp.where(key < length, 0.0, floor_score).astype(F32)

    def out(p, h):
        slot = lax.rem(p, 2) * 2 + h
        return pltpu.make_async_copy(ebuf.at[slot], e_hbm.at[2 * p + h], esem.at[slot])

    def pair(p, carry):
        @pl.when(p > 1)
        def unused_wait():
            out(p - 2, 0).wait()
            out(p - 2, 1).wait()

        base = lax.rem(p, 2) * 2
        cols = pl.ds(pl.multiple_of(p * 128, 128), 128)
        kp = k[:, cols].astype(F32)
        vp = v[:, cols]
        ka = (
            jnp.where(low, kp, jnp.where(lane == 64, bias, 0.0)).astype(BF),
            jnp.where(low, jnp.where(lane == 0, bias, 0.0), kp).astype(BF),
        )
        va = jnp.where(low, vp, one), jnp.where(low, one, vp)
        for b in range(seq // block):
            sl = pl.ds(b * block, block)
            qp = q[sl, cols]
            parts = []
            for h in range(2):
                qm = jnp.where(low, qp, one) if h == 0 else jnp.where(low, one, qp)
                s = dg(qm, ka[h], NT)
                e = jnp.exp2(s - jnp.max(s, axis=-1, keepdims=True)).astype(BF)
                ebuf[base + h, sl, :] = e
                parts.append(dg(e, va[h]))
            un = jnp.where(low, parts[0], parts[1])
            inverse = 1.0 / pltpu.roll(jnp.where(low, parts[1], parts[0]), 64, 1)
            r[sl, cols] = inverse.astype(BF)
            joined = un * inverse
            rounded = joined.astype(BF)
            o[sl, cols] = rounded
            ol[sl, cols] = (joined - rounded.astype(F32)).astype(BF)
        out(p, 0).start()
        out(p, 1).start()
        return carry

    lax.fori_loop(0, pairs // 2, pair, 0)
    between()
    lax.fori_loop(pairs // 2, pairs, pair, 0)
    for p in (pairs - 2, pairs - 1):
        out(p, 0).wait()
        out(p, 1).wait()


def attn_join(x, o, wo, y):
    def run(sl):
        y[sl, :] = x[sl, :].astype(F32) + dg(o[sl, :], whole(wo), NT)

    rows_loop(x.shape[0], 2 * RB, run)


def attn_back_core(q, k, v, do, o, ol, e_hbm, ebuf, esem, ds, dq, dk, dv, between):
    seq = q.shape[0]
    heads = e_hbm.shape[0]
    block = 512
    lane = lax.broadcasted_iota(jnp.int32, (1, 128), 1)
    low = lane < 64
    zero = jnp.zeros((), BF)
    one = jnp.ones((), BF)
    row2 = lax.broadcasted_iota(jnp.int32, (256, 128), 0)
    col2 = lax.broadcasted_iota(jnp.int32, (256, 128), 1)
    swap = jnp.where(((row2 // 64) % 2) != (col2 // 64), 1.0, 0.0).astype(BF)

    def fetch(p, h):
        slot = lax.rem(p, 2) * 2 + h
        return pltpu.make_async_copy(e_hbm.at[2 * p + h], ebuf.at[slot], esem.at[slot])

    for h in range(2):
        fetch(0, h).start()

    def pair(p, carry):
        cols = pl.ds(pl.multiple_of(p * 128, 128), 128)
        fetch(p, 0).wait()
        fetch(p, 1).wait()

        @pl.when(p + 1 < heads // 2)
        def unused_fetch():
            fetch(p + 1, 0).start()
            fetch(p + 1, 1).start()

        base = lax.rem(p, 2) * 2
        qp, kp, vp, dop = q[:, cols], k[:, cols], v[:, cols], do[:, cols]
        product = dop.astype(F32) * (o[:, cols].astype(F32) + ol[:, cols].astype(F32))
        high = product.astype(BF)
        rest = (product - high.astype(F32)).astype(BF)
        inner = -dg(jnp.concatenate([high, rest], axis=1), swap)
        inner_high = inner.astype(BF)
        inner_rest = (inner - inner_high.astype(F32)).astype(BF)
        do_t, q_t = dop.T, qp.T
        dq_sum = None
        dks, dvs = [], []
        for h in range(2):
            if h == 0:
                lhs = jnp.where(low, dop, jnp.where(lane == 64, inner_high, inner_rest))
                va = jnp.where(low, vp, jnp.where(lane < 66, one, zero))
                km = jnp.where(low, kp, zero)
            else:
                lhs = jnp.where(low, jnp.where(lane == 0, inner_high, inner_rest), dop)
                va = jnp.where(low, jnp.where(lane < 2, one, zero), vp)
                km = jnp.where(low, zero, kp)
            for b in range(seq // block):
                sl = pl.ds(b * block, block)
                t = dg(lhs[b * block : (b + 1) * block], va, NT)
                ds[h, sl, :] = ebuf[base + h, sl, :] * t.astype(BF)
            part = dg(ds[h], km)
            dq_sum = part if dq_sum is None else dq_sum + part
            dks.append(dg(q_t[64 * h : 64 * h + 64], ds[h]))
            dvs.append(dg(do_t[64 * h : 64 * h + 64], ebuf[base + h]))
        dq[:, cols] = (dq_sum * HD**-0.5).astype(BF)
        dk[:, cols] = (jnp.concatenate(dks, axis=0) * LN2).astype(BF).T
        dv[:, cols] = jnp.concatenate(dvs, axis=0).astype(BF).T
        return carry

    lax.fori_loop(0, heads // 4, pair, 0)
    between()
    lax.fori_loop(heads // 4, heads // 2, pair, 0)


def places():
    d = lax.axis_index("dp")
    return lax.axis_index("tensor"), d // 4, (d // 2) % 2, d % 2


def at(t, z, y, c):
    return (z * 4 + y * 2 + c, t)


def greet(partners):
    barrier = pltpu.get_barrier_semaphore()
    for device in partners:
        pl.semaphore_signal(barrier, inc=1, device_id=device, device_id_type=MESH)
    pl.semaphore_wait(barrier, len(partners))


def all_partners(t, z, y, c):
    others = [at(t, lax.rem(z + j, 4), y, c) for j in range(1, 4)]
    return [at(t, z, y, 1 - c), at(1 - t, z, y, c), at(t, z, 1 - y, c)] + others


class Saver:
    def __init__(self, sems):
        self.sems, self.count, self.live = sems, 0, []

    def __call__(self, src, dst, slot=None):
        cp = pltpu.make_async_copy(src, dst, self.sems.at[self.count])
        cp.start()
        self.count += 1
        self.live.append((slot, cp))

    def free(self, slot):
        for name, cp in self.live:
            if name == slot:
                cp.wait()
        self.live = [entry for entry in self.live if entry[0] != slot]

    def finish(self):
        for name, cp in self.live:
            cp.wait()
        self.live = []


class SplitColumns:
    def __init__(self, ref, n):
        self.ref, self.n = ref, n

    def cols(self, h):
        return pl.ds(h * self.n, self.n)

    def __getitem__(self, h):
        return self.ref[:, self.cols(h)]

    def __setitem__(self, key, value):
        h, sl, unused = key
        self.ref[sl, self.cols(h)] = value


class Gather:
    def __init__(self, own, out, send, recv, chunks):
        self.own, self.out, self.send, self.recv, self.chunks = own, out, send, recv, chunks
        self.spot = places()
        self.sends, self.pending = [], {}

    def push(self, src, dst, k, i, device):
        copy = pltpu.make_async_remote_copy(
            src_ref=src, dst_ref=dst, send_sem=self.send.at[k, i], recv_sem=self.recv.at[k, i],
            device_id=device, device_id_type=MESH,
        )
        copy.start()
        self.sends.append(copy)
        self.pending.setdefault(k, []).append(copy)

    def move(self, *steps):
        for k, s in steps:
            self.stage(k, s)

    def stage(self, k, s):
        t, z, y, c = self.spot
        own, out = self.own, self.out
        start, width, split = self.chunks[k]
        full = pl.ds(start, width)
        half = width // 2 if split else width
        left = pl.ds(start, half)
        right = pl.ds(start + half, half)
        by_x, by_y = at(1 - t, z, y, c), at(t, z, 1 - y, c)
        for copy in self.pending.pop(k, ()):
            copy.wait_recv()
        if s == 0:
            for j in range(1, 4):
                self.push(own.at[:, full], out.at[t, z, y, c, :, full], k, j - 1, at(t, lax.rem(z + j, 4), y, c))
        elif s == 1:
            a = out.at[t, :, y, c, :, left]
            self.push(a, a, k, 3, by_x)
            if split:
                b = out.at[t, :, y, c, :, right]
                self.push(b, b, k, 4, by_y)
        elif s == 2:
            a = out.at[:, :, y, c, :, left]
            self.push(a, a, k, 5, by_y)
            if split:
                b = out.at[t, :, :, c, :, right]
                self.push(b, b, k, 6, by_x)
        elif s == 3:
            a = out.at[:, :, :, c, :, full]
            self.push(a, a, k, 7, at(t, z, y, 1 - c))

    def finish(self):
        for copy in self.sends:
            copy.wait_send()


class Exchange:
    def __init__(self, send, recv, local):
        self.send, self.recv, self.local = send, recv, local
        self.open = []

    def start(self, i, src, kept, dst):
        t, z, y, c = places()
        far = pltpu.make_async_remote_copy(
            src_ref=src, dst_ref=dst, send_sem=self.send.at[i], recv_sem=self.recv.at[i],
            device_id=at(1 - t, z, y, c), device_id_type=MESH,
        )
        near = pltpu.make_async_copy(kept, dst, self.local.at[i])
        far.start()
        near.start()
        self.open.append(far)
        return far, near

    def give(self, i, halves, dst):
        t = lax.axis_index("tensor")
        rows = halves.shape[1]
        mine = dst.at[pl.ds(pl.multiple_of(t * rows, rows), rows), :]
        return self.start(i, halves.at[1 - t], halves.at[t], mine)

    def back(self, i, pair, dst):
        t = lax.axis_index("tensor")
        rows = dst.shape[1]
        kept = pair.at[pl.ds(pl.multiple_of(t * rows, rows), rows), :]
        sent = pair.at[pl.ds(pl.multiple_of((1 - t) * rows, rows), rows), :]
        return self.start(i, sent, kept, dst.at[t])

    def finish(self):
        for far in self.open:
            far.wait_send()


def arrived(copies):
    far, near = copies
    near.wait()
    far.wait_recv()


def column(values):
    return jnp.broadcast_to(values, (128, values.shape[1])).T[:, :1]


def weight_loader(w_hbm, sems):
    loads = {}

    def load(name, offset, refs, n, base):
        loads[name] = []
        for i, ref in enumerate(refs):
            loads[name] += load_weight(w_hbm, offset + i * n, n, ref, sems, base + 2 * i)

    def ready(name):
        wait_all(loads[name])

    return load, ready


TURNED = (3, 5, 9, 13, 15)
PACKED = (0, 1, 2, 3, 6, 7, 8, 9, 4, 5, 10, 11, 12, 13, 14, 15)


def forward(
    lengths, timesteps, gains, shifts, mask_row, masked, loss_mask, *refs,
):
    matrices, refs = refs[:16], refs[16:]
    (
        src_hbm, target_hbm, cot_hbm,
        w_hbm, x_o, y0_o, g3_o,
        a0_o, q0_o, k0_o, v0_o, o0_o, ol0_o, r0_o, e0_o, x1_o, a1_o, h1_o, gp1_o, x2_o, mem_o,
        a3_o, q3_o, k3_o, v3_o, o3_o, ol3_o, r3_o, e3_o, y1_o,
        a4_o, q4_o, k4_o, v4_o, o4_o, ol4_o, r4_o, e4_o, y2_o,
        own, tgt, cot, x, y0, wq, wk, wv, wo, sq, sk, sv, so, wu, wd,
        a, q, k, v, o, ol, r, a3, q3, k3, v3, o3, ol3, r3,
        x1, a1, h, gp, x2, mem, y1, y2, ebuf,
        gsend, grecv, xsend, xrecv, local, wsem, esem, osem,
    ) = refs
    t, z, y, c = places()
    seq, width = x.shape
    n1, n2 = width // 2, h.shape[1] // 2
    in_tgt = pltpu.make_async_copy(target_hbm, tgt, local.at[4])
    in_cot = pltpu.make_async_copy(cot_hbm, cot, local.at[5])
    in_tgt.start()
    in_cot.start()
    offset = 0
    for i in PACKED:
        part = matrices[i][...].T if i in TURNED else matrices[i][...]
        own[:, pl.ds(offset, part.shape[1])] = part
        offset += part.shape[1]
    greet(all_partners(t, z, y, c))
    halves = Exchange(xsend, xrecv, local)
    first = 3 * n1
    gather = Gather(
        own, w_hbm, gsend, grecv,
        (
            (0, first, True), (first, 8 * n1 - first, True), (8 * n1, n2, False), (8 * n1 + n2, n2, False),
            (8 * n1 + 2 * n2, 4 * n1, False), (12 * n1 + 2 * n2, n2, False), (12 * n1 + 3 * n2, n2, False),
        ),
    )
    mine = pltpu.make_async_copy(own, w_hbm.at[t, z, y, c], local.at[3])
    mine.start()
    gather.move((0, 0))
    x_in = halves.give(0, src_hbm, x)
    save = Saver(osem)
    in_tgt.wait()
    for i in range(2):
        chosen = column(masked[i : i + 1, :].astype(F32)) == 1.0
        tgt[i] = jnp.where(chosen, mask_row[...], tgt[i].astype(F32)).astype(BF)
    mine.wait()
    gather.move((0, 1), (1, 0))
    in_cot.wait()
    for i in range(2):
        factor = (STEPS + 1 - timesteps[i]).astype(F32) / STEPS
        weight = column(loss_mask[i : i + 1, :].astype(F32)) * factor
        cot[i] = (cot[i].astype(F32) * weight).astype(BF)
    gather.move((0, 2), (2, 0))
    arrived(x_in)
    normalize(x, gains[0:1, :], shifts[0:1, :], a)
    save(x, x_o)
    save(a, a0_o, "A")
    gather.move((0, 3), (1, 1))
    y0_in = halves.give(1, tgt, y0)
    gather.move((0, 4))
    load, ready = weight_loader(w_hbm, wsem)
    load("enc", 0, (wq, wk, wv), n1, 0)
    gather.move((1, 2), (3, 0))
    ready("enc")
    attn_project(a, a, wq, wk, wv, q, k, v)
    for src, dst in ((q, q0_o), (k, k0_o), (v, v0_o)):
        save(src, dst, "A")
    gather.move((1, 3), (2, 1), (4, 0))
    length = lengths[t]

    def between0():
        gather.move((1, 4), (2, 2), (3, 1))

    attn_core(length, q, k, v, o, ol, r, e0_o, ebuf, esem, between0)
    load("out", 3 * n1, (wo,), n1, 6)
    load("self", 4 * n1, (sq, sk, sv, so), n1, 8)
    for src, dst in ((o, o0_o), (ol, ol0_o), (r, r0_o)):
        save(src, dst, "A")
    arrived(y0_in)
    save(y0, y0_o)
    normalize(y0, gains[3:4, :], shifts[3:4, :], a3)
    gather.move((2, 3), (3, 2), (4, 1), (5, 0))
    ready("out")
    attn_join(x, o, wo, x1)
    save(x1, x1_o)
    ready("self")
    attn_project(a3, a3, sq, sk, sv, q3, k3, v3)
    for src, dst in ((a3, a3_o), (q3, q3_o), (k3, k3_o), (v3, v3_o)):
        save(src, dst)
    gather.move((2, 4), (3, 3), (4, 2), (5, 1))
    g3_in = halves.give(2, cot, g3_o)

    def between3():
        gather.move((3, 4), (4, 3), (5, 2), (6, 0))

    attn_core(seq, q3, k3, v3, o3, ol3, r3, e3_o, ebuf, esem, between3)
    load("feed", 8 * n1, (wu, wd), n2, 16)
    for src, dst in ((o3, o3_o), (ol3, ol3_o), (r3, r3_o)):
        save(src, dst)
    gather.move((4, 4), (5, 3), (6, 1))
    load("cross", 8 * n1 + 2 * n2, (wq, wk, wv, wo), n1, 0)
    attn_join(y0, o3, so, y1)
    save(y1, y1_o)
    save.free("A")
    normalize(y1, gains[4:5, :], shifts[4:5, :], a)
    ready("feed")

    def feed(sl):
        stream = x1[sl, :]
        hat, unused = ln_hat(stream)
        rows = (hat * gains[1:2, :] + shifts[1:2, :]).astype(BF)
        a1[sl, :] = rows
        active, slope = gelu_both(dg(rows, whole(wu)))
        active = active.astype(BF)
        h[sl, :] = active
        gp[sl, :] = slope.astype(BF)
        out = stream + dg(active, whole(wd), NT)
        x2[sl, :] = out
        hat, unused = ln_hat(out)
        mem[sl, :] = (hat * gains[2:3, :] + shifts[2:3, :]).astype(BF)

    rows_loop(seq, RB, feed)
    for src, dst in ((a1, a1_o), (h, h1_o), (gp, gp1_o), (x2, x2_o), (mem, mem_o)):
        save(src, dst)
    gather.move((5, 4), (6, 2))
    ready("cross")
    attn_project(a, mem, wq, wk, wv, q, k, v)
    for src, dst in ((a, a4_o), (q, q4_o), (k, k4_o), (v, v4_o)):
        save(src, dst)

    def between4():
        gather.move((6, 3))

    attn_core(length, q, k, v, o, ol, r, e4_o, ebuf, esem, between4)
    for src, dst in ((o, o4_o), (ol, ol4_o), (r, r4_o)):
        save(src, dst)
    gather.move((6, 4))
    attn_join(y1, o, wo, y2)
    save(y2, y2_o)
    arrived(g3_in)
    halves.finish()
    gather.finish()
    save.finish()


class Reduce:
    def __init__(self, out, chunks):
        self.out, self.chunks = out, chunks
        self.spot = places()
        self.sends, self.pending = [], {}

    def push(self, name, i, src, dst, device):
        send, recv = self.chunks[name][5:7]
        copy = pltpu.make_async_remote_copy(
            src_ref=src, dst_ref=dst, send_sem=send.at[i], recv_sem=recv.at[i],
            device_id=device, device_id_type=MESH,
        )
        copy.start()
        self.sends.append((name, copy))
        self.pending.setdefault(name, []).append(copy)

    def move(self, *steps):
        for name, s in steps:
            self.stage(name, s)

    def stage(self, name, s):
        t, z, y, c = self.spot
        g, r1, r2, r3, r4, send, recv, start, split = self.chunks[name]
        width = g.shape[-1]
        half = width // 2 if split else width
        left = pl.ds(0, half)
        right = pl.ds(half, half)
        by_x, by_y = at(1 - t, z, y, c), at(t, z, 1 - y, c)

        def add(mine, theirs):
            mine[...] = (mine[...].astype(F32) + theirs[...].astype(F32)).astype(BF)

        for copy in self.pending.pop(name, ()):
            copy.wait_recv()
        if s == 0:
            self.push(name, 0, g.at[:, :, :, 1 - c], r1, at(t, z, y, 1 - c))
        elif s == 1:
            add(g.at[:, :, 1 - y, c], r1.at[:, :, 1 - y])
            self.push(name, 1, g.at[:, :, 1 - y, c, :, left], r2.at[:, :, :, left], by_y)
            add(g.at[:, :, y, c], r1.at[:, :, y])
            if split:
                self.push(name, 2, g.at[1 - t, :, :, c, :, right], r3.at[0], by_x)
        elif s == 2:
            rows = g.at[:, :, y, c, :, left]
            add(rows, r2.at[:, :, :, left])
            if not split:
                self.push(name, 2, g.at[1 - t, :, y, c], r3, by_x)
            else:
                self.push(name, 3, g.at[1 - t, :, y, c, :, left], r3.at[1, :, 0], by_x)
                add(g.at[t, :, :, c, :, right], r3.at[0])
                self.push(name, 4, g.at[t, :, 1 - y, c, :, right], r3.at[1, :, 1], by_y)
        elif s == 3:
            if not split:
                add(g.at[t, :, y, c], r3)
            else:
                add(g.at[t, :, y, c, :, left], r3.at[1, :, 0])
                add(g.at[t, :, y, c, :, right], r3.at[1, :, 1])
            for j in range(1, 4):
                zz = lax.rem(z + j, 4)
                self.push(name, 4 + j, g.at[t, zz, y, c], r4.at[j - 1], at(t, zz, y, c))
        elif s == 4:
            self.out[:, pl.ds(start, width)] = (g[t, z, y, c].astype(F32) + r4[0].astype(F32)) + (
                r4[1].astype(F32) + r4[2].astype(F32)
            )

    def release(self, name):
        for owner, copy in self.sends:
            if owner == name:
                copy.wait_send()
        self.sends = [entry for entry in self.sends if entry[0] != name]

    def finish(self):
        for owner, copy in self.sends:
            copy.wait_send()
        self.sends = []


def put(g, first, n, value, lower=0):
    done = 0
    while done < value.shape[1]:
        t, offset = (lower + done) // n, (lower + done) % n
        take = min(value.shape[1] - done, n - offset)
        block = value[:, done : done + take].astype(BF)
        g[t, :, :, :, :, pl.ds(first + offset, take)] = block.reshape(g.shape[1:5] + (take,))
        done += take


def add_norm(ng, index, dgain, dshift):
    ng[index : index + 1, :] += dgain
    ng[6 + index : 7 + index, :] += dshift


def attn_backward(
    g, x, gain, ng, index, a_t, kv_t, g_t, wq, wk, wv, wo, q, k, v, o, ol, r, e_hbm, ebuf, esem, ds,
    do, dq, dk, dv, grads, n1, before_core, between, after_core, after_grads, into_keys, finish,
):
    seq = x.shape[0]

    def before(sl):
        rows = g[sl, :].astype(BF)
        g_t[:, sl] = rows.T
        do[sl, :] = (dg(rows, wo[...]) * r[sl, :].astype(F32)).astype(BF)

    rows_loop(seq, 2 * RB, before)
    put(grads, 3 * n1, n1, dg(g_t[...], o[...]))
    before_core()
    attn_back_core(q, k, v, do, o, ol, e_hbm, ebuf, esem, ds, dq, dk, dv, between)
    after_core()
    put(grads, 0, n1, dg(a_t[...], dq[...]))
    put(grads, n1, n1, dg(kv_t[...], dk[...]))
    put(grads, 2 * n1, n1, dg(kv_t[...], dv[...]))
    after_grads()

    def after(sl):
        into = dg(dq[sl, :], wq[...], NT)
        keys = dg(dk[sl, :], wk[...], NT) + dg(dv[sl, :], wv[...], NT)
        if into_keys is None:
            into = into + keys
        else:
            into_keys[sl, :] = keys
        dx, dgain, dshift = ln_back(x[sl, :].astype(F32), gain, into)
        add_norm(ng, index, dgain, dshift)
        finish(sl, g[sl, :] + dx)

    rows_loop(seq, 2 * RB, after)


def fetcher(sems):
    count = [0]

    def fetch(*pairs):
        copies = []
        for src, dst in pairs:
            cp = pltpu.make_async_copy(src, dst, sems.at[count[0]])
            count[0] += 1
            cp.start()
            copies.append(cp)
        return copies

    return fetch


def nothing():
    return None


def dec_backward(
    gains, shifts, y2_hbm, g3_hbm, y1_hbm, mem_hbm, a4_hbm, q4_hbm, k4_hbm, v4_hbm, o4_hbm, ol4_hbm, r4_hbm, e4_hbm,
    x2_hbm, x1_hbm, a1_hbm, h1_hbm, gp1_hbm, w_hbm,
    dec_o, g4_o, g1_o, up_o, down_o, sums, ng,
    y2, g3, y1, a, q, k, v, o, ol, r, x2, cq, ck, cv, co, wu, wd,
    big, gs, do, a_t, g_t, g_up, g_down, g_cross, ebuf,
    ru1, ru2, ru3, ru4, rd1, rd2, rd3, rd4, rc1, rc2, rc3, rc4,
    rsend, rrecv, xsend, xrecv, local, isem, wsem, esem, osem,
):
    t, z, y, c = places()
    seq, width = y1.shape
    n1, n2 = cq.shape[1] // 2, wu.shape[1] // 2
    fetch = fetcher(isem)
    load, ready = weight_loader(w_hbm, wsem)
    first = fetch((y2_hbm, y2), (g3_hbm, g3))
    load("feed", 12 * n1 + 2 * n2, (wu, wd), n2, 0)
    load("cross", 8 * n1 + 2 * n2, (cq, ck, cv, co), n1, 4)
    cross = fetch(
        (o4_hbm, o), (r4_hbm, r), (a4_hbm, a), (q4_hbm, q), (k4_hbm, k),
        (v4_hbm, v), (ol4_hbm, ol), (y1_hbm, y1), (x2_hbm, x2),
    )
    greet(all_partners(t, z, y, c))
    halves = Exchange(xsend, xrecv, local)
    reduce = Reduce(
        sums,
        {
            "up": (g_up, ru1, ru2, ru3, ru4, rsend.at[0], rrecv.at[0], 0, False),
            "down": (g_down, rd1, rd2, rd3, rd4, rsend.at[1], rrecv.at[1], n2, False),
            "cross": (g_cross, rc1, rc2, rc3, rc4, rsend.at[2], rrecv.at[2], 2 * n2, False),
        },
    )
    ng[...] = jnp.zeros_like(ng)
    save = Saver(osem)
    wait_all(first)
    ready("feed")
    h, du = big.at[0], big.at[1]

    def feed(sl):
        stream = y2[sl, :]
        hat, unused = ln_hat(stream)
        rows = (hat * gains[5:6, :] + shifts[5:6, :]).astype(BF)
        a_t[:, sl] = rows.T
        active, slope = gelu_both(dg(rows, wu[...]))
        active = active.astype(BF)
        h[sl, :] = active
        grad = g3[sl, :]
        g3[sl, :] = (stream + dg(active, wd[...], NT)).astype(BF)
        g_t[:, sl] = grad.T
        lifted = (dg(grad, wd[...]) * slope).astype(BF)
        du[sl, :] = lifted
        dx, dgain, dshift = ln_back(stream, gains[5:6, :], dg(lifted, wu[...], NT))
        add_norm(ng, 5, dgain, dshift)
        gs[sl, :] = grad.astype(F32) + dx

    rows_loop(seq, RB, feed)
    dec_back = halves.back(0, g3, dec_o)
    block = width
    for j in range(2 * n2 // block):
        put(g_up, 0, n2, dg(a_t[...], du[:, pl.ds(j * block, block)]), j * block)
    reduce.move(("up", 0))
    for j in range(2 * n2 // block):
        put(g_down, 0, n2, dg(g_t[...], h[:, pl.ds(j * block, block)]), j * block)
    load("enc", 8 * n1, (wu, wd), n2, 12)
    reduce.move(("up", 1), ("down", 0))
    wait_all(cross)
    ready("cross")
    a_t[...] = a[...].T
    memory = big.at[1, :, pl.ds(3 * width, width)]
    late = fetch((mem_hbm, memory))
    dq, dk, dv = (big.at[1, :, pl.ds(i * width, width)] for i in range(3))

    def before_core():
        reduce.move(("down", 1))

    def between():
        reduce.move(("up", 2))

    def after_core():
        wait_all(late)
        late.clear()
        g_t[...] = memory[...].T
        late.extend(
            fetch(
                (gp1_hbm.at[:, pl.ds(0, n2)], ebuf.at[2]), (gp1_hbm.at[:, pl.ds(n2, n2)], ebuf.at[3]),
                (h1_hbm.at[:, pl.ds(0, n2)], ebuf.at[0]), (h1_hbm.at[:, pl.ds(n2, n2)], ebuf.at[1]),
            )
        )
        reduce.move(("up", 3), ("down", 2))

    def after_grads():
        late.extend(fetch((a1_hbm, a)))
        reduce.move(("cross", 0), ("up", 4), ("down", 3))

    def keep(sl, gradient):
        gs[sl, :] = gradient

    attn_backward(
        gs, y1, gains[4:5, :], ng, 4, a_t, g_t, g_t, cq, ck, cv, co, q, k, v, o, ol, r, e4_hbm,
        ebuf, esem, SplitColumns(big.at[0], seq), do, dq, dk, dv, g_cross, n1,
        before_core, between, after_core, after_grads, y2, keep,
    )
    save(gs, g4_o)
    late.extend(fetch((x1_hbm, y1)))
    reduce.move(("cross", 1), ("down", 4))
    reduce.release("up")
    reduce.release("down")
    wait_all(late)
    ready("enc")
    save.finish()

    def feed_back(sl):
        dx, dgain, dshift = ln_back(x2[sl, :], gains[2:3, :], y2[sl, :])
        add_norm(ng, 2, dgain, dshift)
        grad = dx.astype(BF)
        g_t[:, sl] = grad.T
        a_t[:, sl] = a[sl, :].T
        into = None
        for i in range(2):
            cols = pl.ds(i * n2, n2)
            lifted = (dg(grad, wd[:, cols]) * ebuf[2 + i, sl, :].astype(F32)).astype(BF)
            ebuf[2 + i, sl, :] = lifted
            part = dg(lifted, wu[:, cols], NT)
            into = part if into is None else into + part
        dx1, dgain, dshift = ln_back(y1[sl, :], gains[1:2, :], into)
        add_norm(ng, 1, dgain, dshift)
        gs[sl, :] = dx + dx1

    rows_loop(seq, RB, feed_back)
    save(gs, g1_o)
    reduce.move(("cross", 2))
    for i in range(2):
        for j in range(n2 // block):
            cols = pl.ds(j * block, block)
            put(g_up, 0, n2, dg(a_t[...], ebuf[2 + i, :, cols]), i * n2 + j * block)
    save(g_up, up_o)
    for i in range(2):
        for j in range(n2 // block):
            cols = pl.ds(j * block, block)
            put(g_down, 0, n2, dg(g_t[...], ebuf[i, :, cols]), i * n2 + j * block)
    save(g_down, down_o)
    reduce.move(("cross", 3))
    reduce.move(("cross", 4))
    arrived(dec_back)
    halves.finish()
    reduce.finish()
    save.finish()


def last_backward(
    gains, ng2, masked, g4_hbm, g1_hbm, y0_hbm, a3_hbm, q3_hbm, k3_hbm, v3_hbm, o3_hbm, ol3_hbm, r3_hbm, e3_hbm,
    x_hbm, a0_hbm, q0_hbm, k0_hbm, v0_hbm, o0_hbm, ol0_hbm, r0_hbm, e0_hbm, up_hbm, down_hbm, w_hbm,
    sg_o, target_o, sums, vec,
    gs, x, a, q, k, v, o, ol, r, wq, wk, wv, wo, vq, vk, vv, vo, big, do, a_t, g_t, gy, sg, back, ng,
    g_up, g_down, g_self, g_enc, ebuf,
    ru1, ru2, ru3, ru4, rd1, rd2, rd3, rd4, rs1, rs2, rs3, rs4, re1, re2, re3, re4, v1, vr,
    rsend, rrecv, xsend, xrecv, local, vsend, vrecv, isem, wsem, esem,
):
    t, z, y, c = places()
    seq, width = x.shape
    n1 = wq.shape[1] // 2
    n2 = g_up.shape[-1]
    fetch = fetcher(isem)
    load, ready = weight_loader(w_hbm, wsem)
    ups = fetch((up_hbm, g_up), (down_hbm, g_down))
    first = fetch(
        (g4_hbm, gs), (o3_hbm, o), (r3_hbm, r), (a3_hbm, a), (q3_hbm, q), (k3_hbm, k), (v3_hbm, v), (ol3_hbm, ol),
        (y0_hbm, x),
    )
    load("self", 4 * n1, (wq, wk, wv, wo), n1, 0)
    load("enc", 0, (vq, vk, vv, vo), n1, 8)
    greet(all_partners(t, z, y, c))
    halves = Exchange(xsend, xrecv, local)
    reduce = Reduce(
        sums,
        {
            "up": (g_up, ru1, ru2, ru3, ru4, rsend.at[0], rrecv.at[0], 0, False),
            "down": (g_down, rd1, rd2, rd3, rd4, rsend.at[1], rrecv.at[1], n2, False),
            "self": (g_self, rs1, rs2, rs3, rs4, rsend.at[2], rrecv.at[2], 2 * n2, False),
            "enc": (g_enc, re1, re2, re3, re4, rsend.at[3], rrecv.at[3], 2 * n2 + 4 * n1, True),
        },
    )
    ng[...] = ng2[...]
    wait_all(ups)
    reduce.move(("up", 0), ("down", 0))
    wait_all(first)
    ready("self")
    a_t[...] = a[...].T
    dq, dk, dv = (big.at[1, :, pl.ds(i * width, width)] for i in range(3))
    ds = SplitColumns(big.at[0], seq)
    reduce.move(("up", 1))

    def before_core3():
        reduce.move(("down", 1))

    def between3():
        reduce.move(("up", 2))

    late = []

    def after_core3():
        late.extend(fetch((q0_hbm, q), (k0_hbm, k), (v0_hbm, v), (o0_hbm, o), (ol0_hbm, ol), (r0_hbm, r), (a0_hbm, a)))
        reduce.move(("up", 3), ("down", 2))

    def after_grads3():
        reduce.move(("self", 0), ("up", 4))

    def last3(sl, gradient):
        gy[sl, :] = gradient.astype(BF)

    attn_backward(
        gs, x, gains[3:4, :], ng, 3, a_t, a_t, g_t, wq, wk, wv, wo, q, k, v, o, ol, r, e3_hbm,
        ebuf, esem, ds, do, dq, dk, dv, g_self, n1,
        before_core3, between3, after_core3, after_grads3, None, last3,
    )
    gy_back = halves.back(0, gy, back)
    late.extend(fetch((x_hbm, x), (g1_hbm, gs)))
    reduce.move(("self", 1), ("down", 3))
    wait_all(late)
    ready("enc")
    a_t[...] = a[...].T

    def before_core0():
        reduce.move(("down", 4))

    def between0():
        reduce.move(("self", 2))

    def after_core0():
        reduce.move(("self", 3))
        arrived(gy_back)
        total = jnp.zeros((1, width), F32)
        for i in range(2):
            chosen = column(masked[i : i + 1, :].astype(F32)) == 1.0
            rows = back[i].astype(F32)
            total = total + jnp.sum(jnp.where(chosen, rows, 0.0), axis=0, keepdims=True)
            target_o[i] = jnp.where(chosen, 0.0, rows).astype(BF)
        ng[12:13, :] = total

    def after_grads0():
        reduce.move(("enc", 0), ("self", 4), ("enc", 1))

    def last0(sl, gradient):
        sg[sl, :] = gradient.astype(BF)

    attn_backward(
        gs, x, gains[0:1, :], ng, 0, a_t, a_t, g_t, vq, vk, vv, vo, q, k, v, o, ol, r, e0_hbm,
        ebuf, esem, ds, do, dq, dk, dv, g_enc, n1,
        before_core0, between0, after_core0, after_grads0, None, last0,
    )
    sg_back = halves.back(1, sg, sg_o)
    waiting = []

    def vector(s):
        for copy in waiting:
            copy.wait_recv()
        waiting.clear()
        if s == 0:
            v1[0] = ng[...]
        elif s < 4:
            v1[s] = v1[s - 1] + vr[s - 1]
        if s < 3:
            targets = ((s, (at(t, z, y, 1 - c), at(t, z, 1 - y, c), at(1 - t, z, y, c))[s]),)
        elif s == 3:
            targets = tuple((2 + j, at(t, lax.rem(z + j, 4), y, c)) for j in range(1, 4))
        else:
            targets = ()
            vec[...] = (v1[3] + vr[3]) + (vr[4] + vr[5])
        for slot, device in targets:
            copy = pltpu.make_async_remote_copy(
                src_ref=v1.at[s], dst_ref=vr.at[slot], send_sem=vsend.at[slot], recv_sem=vrecv.at[slot],
                device_id=device, device_id_type=MESH,
            )
            copy.start()
            reduce.sends.append(("vector", copy))
            waiting.append(copy)

    vector(0)
    vector(1)
    reduce.move(("enc", 2))
    vector(2)
    vector(3)
    reduce.move(("enc", 3))
    vector(4)
    reduce.move(("enc", 4))
    arrived(sg_back)
    halves.finish()
    reduce.finish()


def compute_all(lengths, timesteps, gains, shifts, mask_vector, masked, loss_mask, matrices, source, target, cotangent):
    rows, width = source.shape[1:]
    seq = 2 * rows
    n1 = width // 2
    part = matrices[0].shape[0]
    n2 = matrices[4].shape[1]
    total = 12 * n1 + 4 * n2
    hidden = 2 * n2
    heads = width // HD
    sd = jax.ShapeDtypeStruct
    any_spec = pl.BlockSpec(memory_space=pl.ANY)
    vmem = pl.BlockSpec(memory_space=pltpu.VMEM)
    smem = pl.BlockSpec(memory_space=pltpu.SMEM)
    dma = pltpu.SemaphoreType.DMA
    row = lambda kind: sd((seq, width), kind)
    tall = lambda kind: sd((seq, hidden), kind)
    halves = sd((2, rows, width), BF)
    escores = sd((heads, seq, seq), BF)
    vrow = lambda kind: pltpu.VMEM((seq, width), kind)
    vhalves = pltpu.VMEM((2, rows, width), BF)
    vsq = pltpu.VMEM((width, width), BF)
    vwide = pltpu.VMEM((width, hidden), BF)
    vtall = pltpu.VMEM((seq, hidden), BF)
    vsq5 = pltpu.VMEM((4, 2, 2, part, width), BF)
    vwide5 = pltpu.VMEM((4, 2, 2, part, hidden), BF)
    turned = pltpu.VMEM((width, seq), BF)
    big = pltpu.VMEM((2, seq, hidden), BF)
    ebuf = pltpu.VMEM((4, seq, seq), BF)
    grads = lambda n: pltpu.VMEM((2, 4, 2, 2, part, n), BF)

    def landing(n, split=False):
        r3 = (2, 4, 2, part, n // 2) if split else (4, part, n)
        return [
            pltpu.VMEM(dims, BF) for dims in ((2, 4, 2, part, n), (2, 4, part, n), r3, (3, part, n))
        ]

    def params(number):
        return pltpu.CompilerParams(
            vmem_limit_bytes=VMEM_LIMIT, collective_id=number, has_side_effects=True
        )

    attention = [row(BF)] * 7 + [escores]
    (
        gathered, x, y0, g3,
        a0, q0, k0, v0, o0, ol0, r0, e0, x1, a1, h1, gp1, x2, mem,
        a3, q3, k3, v3, o3, ol3, r3, e3, y1,
        a4, q4, k4, v4, o4, ol4, r4, e4, y2,
    ) = pl.pallas_call(
        forward,
        in_specs=[smem, smem] + [vmem] * 21 + [any_spec] * 3,
        out_specs=[any_spec] * 36,
        out_shape=[sd((2, 4, 2, 2, part, total), BF)] + [row(BF)] * 3
        + attention + [row(F32), row(BF), tall(BF), tall(BF), row(F32), row(BF)]
        + attention + [row(F32)]
        + attention + [row(F32)],
        scratch_shapes=[pltpu.VMEM((part, total), BF), vhalves, vhalves]
        + [vrow(BF)] * 2 + [vsq5] * 8 + [vwide5] * 2 + [vrow(BF)] * 14
        + [vrow(F32), vrow(BF), vtall, vtall, vrow(F32), vrow(BF), vrow(F32), vrow(F32), ebuf]
        + [dma((7, 8)), dma((7, 8)), dma((3,)), dma((3,)), dma((6,)), dma((20,)), dma((4,)), dma((35,))],
        compiler_params=params(0),
        name="forward",
    )(lengths, timesteps, gains, shifts, mask_vector[None], masked, loss_mask, *matrices, source, target, cotangent)
    weights = gathered.reshape(2, width, total)
    decoded, g4, g1, up, down, sums2, ng = pl.pallas_call(
        dec_backward,
        in_specs=[vmem, vmem] + [any_spec] * 18,
        out_specs=[any_spec] * 5 + [vmem] * 2,
        out_shape=[halves, row(F32), row(F32)] + [sd((2, 4, 2, 2, part, n2), BF)] * 2
        + [sd((part, 2 * n2 + 4 * n1), F32), sd((16, width), F32)],
        scratch_shapes=[vrow(F32), vrow(BF), vrow(F32)] + [vrow(BF)] * 7 + [vrow(F32)]
        + [vsq] * 4 + [vwide] * 2 + [big, vrow(F32), vrow(BF)] + [turned] * 2
        + [grads(n2), grads(n2), grads(4 * n1), ebuf]
        + landing(n2) + landing(n2) + landing(4 * n1)
        + [dma((3, 8)), dma((3, 8)), dma((1,)), dma((1,)), dma((1,)), dma((18,)), dma((16,)), dma((4,)), dma((4,))],
        compiler_params=params(1),
        name="dec_backward",
    )(gains, shifts, y2, g3, y1, mem, a4, q4, k4, v4, o4, ol4, r4, e4, x2, x1, a1, h1, gp1, weights)
    source_grad, target_grad, sums3, vec = pl.pallas_call(
        last_backward,
        in_specs=[vmem] * 3 + [any_spec] * 23,
        out_specs=[any_spec, vmem, vmem, vmem],
        out_shape=[halves, halves, sd((part, 2 * n2 + 8 * n1), F32), sd((16, width), F32)],
        scratch_shapes=[vrow(F32)] + [vrow(BF)] * 8 + [vsq] * 8 + [big, vrow(BF)] + [turned] * 2
        + [vrow(BF), vrow(BF), vhalves, pltpu.VMEM((16, width), F32)]
        + [grads(n2), grads(n2), grads(4 * n1), grads(4 * n1), ebuf]
        + landing(n2) + landing(n2) + landing(4 * n1) + landing(4 * n1, True)
        + [pltpu.VMEM((4, 16, width), F32), pltpu.VMEM((6, 16, width), F32)]
        + [dma((4, 8)), dma((4, 8)), dma((2,)), dma((2,)), dma((2,)), dma((6,)), dma((6,)), dma((20,)), dma((16,)), dma((4,))],
        compiler_params=params(2),
        name="last_backward",
    )(
        gains, ng, masked, g4, g1, y0, a3, q3, k3, v3, o3, ol3, r3, e3,
        x, a0, q0, k0, v0, o0, ol0, r0, e0, up, down, weights,
    )
    return decoded, source_grad, target_grad, sums2, sums3, vec


def pair_body(*arguments):
    source, target, cotangent, lengths, timesteps, masked, loss_mask = arguments[:7]
    matrices = arguments[7:23]
    norm_gains, norm_shifts, mask_vector = arguments[23:]
    decoded, source_grad, target_grad, sums2, sums3, vec = compute_all(
        lengths, timesteps, norm_gains, norm_shifts, mask_vector, masked, loss_mask, matrices, source, target, cotangent
    )
    grads = {}
    for summed, held in ((sums2, (14, 15, 10, 11, 12, 13)), (sums3, (4, 5, 6, 7, 8, 9, 0, 1, 2, 3))):
        offset = 0
        for i in held:
            n = matrices[i].shape[0] if i in TURNED else matrices[i].shape[1]
            part = summed[:, offset : offset + n]
            offset += n
            grads[i] = part.T if i in TURNED else part
    return (
        decoded, source_grad, target_grad, *(grads[i] for i in range(16)), vec[:6], vec[6:12], vec[12],
    )


def solution(mesh):
    whole_pairs = dict(mesh.shape) == {"dp": 16, "tensor": 2}
    return jax.shard_map(
        pair_body if whole_pairs else body,
        mesh=mesh,
        in_specs=(
            P("dp", "tensor", None),
            P("dp", "tensor", None),
            P("dp", "tensor", None),
            P("dp"),
            P("dp"),
            P("dp", "tensor"),
            P("dp", "tensor"),
            P("dp", "tensor"),
            P("dp", "tensor"),
            P("dp", "tensor"),
            P("tensor", "dp"),
            P("dp", "tensor"),
            P("tensor", "dp"),
            P("dp", "tensor"),
            P("dp", "tensor"),
            P("dp", "tensor"),
            P("tensor", "dp"),
            P("dp", "tensor"),
            P("dp", "tensor"),
            P("dp", "tensor"),
            P("tensor", "dp"),
            P("dp", "tensor"),
            P("tensor", "dp"),
            P(),
            P(),
            P(),
        ),
        out_specs=(
            P("dp", "tensor", None),
            P("dp", "tensor", None),
            P("dp", "tensor", None),
            P("dp", "tensor"),
            P("dp", "tensor"),
            P("dp", "tensor"),
            P("tensor", "dp"),
            P("dp", "tensor"),
            P("tensor", "dp"),
            P("dp", "tensor"),
            P("dp", "tensor"),
            P("dp", "tensor"),
            P("tensor", "dp"),
            P("dp", "tensor"),
            P("dp", "tensor"),
            P("dp", "tensor"),
            P("tensor", "dp"),
            P("dp", "tensor"),
            P("tensor", "dp"),
            P(),
            P(),
            P(),
        ),
        check_vma=False,
    )
```

```python
import jax
import jax.numpy as jnp
from jax import lax
from jax.experimental import pallas as pl
from jax.experimental.pallas import tpu as pltpu
from jax.sharding import PartitionSpec as P

HD = 64
MICRO = 2
STEPS = 50


eps = 1e-05
floor_score = -1e30


def norm_rows(inputs, gain, shift):
    average = jnp.mean(inputs, axis=-1, keepdims=True)
    centred = inputs - average
    second = jnp.mean(centred * centred, axis=-1, keepdims=True)
    return centred * lax.rsqrt(second + eps) * gain + shift


def norm_back(inputs, gain, shift, gradient):
    unused, pullback = jax.vjp(norm_rows, inputs, gain, shift)
    return pullback(gradient)


def smooth(values):
    return jax.nn.gelu(values, approximate=False)


def spread(inputs):
    return lax.all_gather(inputs.astype(jnp.bfloat16), "tensor", axis=1, tiled=True)


def collect(partial_value):
    return lax.psum_scatter(partial_value, "tensor", scatter_dimension=1, tiled=True)


def spread_grad(gradient):
    return lax.all_gather(gradient.astype(jnp.bfloat16), "tensor", axis=1, tiled=True)


def collect_grad(partial_value):
    return lax.psum_scatter(partial_value, "tensor", scatter_dimension=1, tiled=True)


def project(inputs, weight):
    return jnp.einsum("bsk,kn->bsn", inputs, weight, preferred_element_type=jnp.float32)


def weight_grad(inputs, gradient):
    return jnp.einsum("bsk,bsn->kn", inputs, gradient, preferred_element_type=jnp.float32)


def back_project(gradient, weight):
    return jnp.einsum("bsn,kn->bsk", gradient, weight, preferred_element_type=jnp.float32)


def masked_scores(query_part, key_rows, live):
    scores = jnp.einsum(
        "bqhd,bkhd->bhqk", query_part, key_rows, preferred_element_type=jnp.float32
    ) * HD ** (-0.5)
    return jnp.where(live[:, None, None, :], scores, floor_score)


def attend_forward(query_in, keys_in, w_query, w_key, w_value, live):
    pair_count, length = (query_in.shape[0], query_in.shape[1])
    head_count = w_query.shape[1] // HD
    queries = (
        project(query_in, w_query).astype(jnp.bfloat16).reshape(pair_count, length, head_count, HD)
    )
    key_rows = (
        project(keys_in, w_key).astype(jnp.bfloat16).reshape(pair_count, length, head_count, HD)
    )
    value_rows = (
        project(keys_in, w_value).astype(jnp.bfloat16).reshape(pair_count, length, head_count, HD)
    )
    block_rows = min(512, length)
    pieces = []
    totals = []
    for offset in range(0, length, block_rows):
        scores = masked_scores(queries[:, offset : offset + block_rows], key_rows, live)
        highest = jnp.max(scores, axis=-1, keepdims=True)
        exponent = jnp.exp(scores - highest)
        summed = jnp.sum(exponent, axis=-1, keepdims=True)
        softmax = (exponent / summed).astype(jnp.bfloat16)
        pieces.append(
            jnp.einsum("bhqk,bkhd->bqhd", softmax, value_rows, preferred_element_type=jnp.float32)
        )
        totals.append(highest + jnp.log(summed))
    attended = (
        jnp.concatenate(pieces, axis=1)
        .astype(jnp.bfloat16)
        .reshape(pair_count, length, head_count * HD)
    )
    return (queries, key_rows, value_rows, attended, jnp.concatenate(totals, axis=2))


def attend_backward(whole_grad, query_in, keys_in, w_query, w_key, w_value, w_out, saved, live):
    queries, key_rows, value_rows, attended, totals = saved
    pair_count, length, head_count = (queries.shape[0], queries.shape[1], queries.shape[2])
    scale_score = HD ** (-0.5)
    out_grad = weight_grad(attended, whole_grad)
    head_grad = (
        back_project(whole_grad, w_out)
        .astype(jnp.bfloat16)
        .reshape(pair_count, length, head_count, HD)
    )
    block_rows = min(512, length)
    key_total = jnp.zeros(key_rows.shape, jnp.float32)
    value_total = jnp.zeros(value_rows.shape, jnp.float32)
    query_parts = []
    for offset in range(0, length, block_rows):
        query_part = queries[:, offset : offset + block_rows]
        grad_part = head_grad[:, offset : offset + block_rows]
        scores = masked_scores(query_part, key_rows, live)
        softmax = jnp.exp(scores - totals[:, :, offset : offset + block_rows])
        value_total = value_total + jnp.einsum(
            "bhqk,bqhd->bkhd",
            softmax.astype(jnp.bfloat16),
            grad_part,
            preferred_element_type=jnp.float32,
        )
        soft_grad = jnp.einsum(
            "bqhd,bkhd->bhqk", grad_part, value_rows, preferred_element_type=jnp.float32
        )
        inner = jnp.sum(softmax * soft_grad, axis=-1, keepdims=True)
        score_grad = (softmax * (soft_grad - inner)).astype(jnp.bfloat16)
        query_parts.append(
            jnp.einsum("bhqk,bkhd->bqhd", score_grad, key_rows, preferred_element_type=jnp.float32)
            * scale_score
        )
        key_total = (
            key_total
            + jnp.einsum(
                "bhqk,bqhd->bkhd", score_grad, query_part, preferred_element_type=jnp.float32
            )
            * scale_score
        )
    query_grad = (
        jnp.concatenate(query_parts, axis=1)
        .astype(jnp.bfloat16)
        .reshape(pair_count, length, head_count * HD)
    )
    key_grad = key_total.astype(jnp.bfloat16).reshape(
        pair_count, key_rows.shape[1], head_count * HD
    )
    value_grad = value_total.astype(jnp.bfloat16).reshape(
        pair_count, value_rows.shape[1], head_count * HD
    )
    grads = (
        weight_grad(query_in, query_grad),
        weight_grad(keys_in, key_grad),
        weight_grad(keys_in, value_grad),
        out_grad,
    )
    into_keys = back_project(key_grad, w_key) + back_project(value_grad, w_value)
    return (grads, back_project(query_grad, w_query), into_keys)


def feed_forward(inputs, w_up, w_down):
    lifted = project(inputs, w_up)
    active = smooth(lifted).astype(jnp.bfloat16)
    return (lifted, active, project(active, w_down))


def feed_backward(gradient, inputs, w_up, w_down, lifted, active):
    down_grad = weight_grad(active, gradient)
    active_grad = back_project(gradient, w_down)
    unused, smooth_back = jax.vjp(smooth, lifted)
    lifted_grad = smooth_back(active_grad)[0].astype(jnp.bfloat16)
    return ((weight_grad(inputs, lifted_grad), down_grad), back_project(lifted_grad, w_up))


def body(
    source,
    target,
    cotangent,
    lengths,
    timesteps,
    masked,
    loss_mask,
    enc_query,
    enc_key,
    enc_value,
    enc_out,
    enc_up,
    enc_down,
    self_query,
    self_key,
    self_value,
    self_out,
    cross_query,
    cross_key,
    cross_value,
    cross_out,
    dec_up,
    dec_down,
    norm_gains,
    norm_shifts,
    mask_vector,
):
    pairs_dev, rows_dev = (source.shape[0], source.shape[1])
    per_micro = pairs_dev // MICRO
    seq_len = rows_dev * lax.axis_size("tensor")
    positions = jnp.arange(seq_len)
    gains, shifts = (norm_gains, norm_shifts)
    gain_total = jnp.zeros(norm_gains.shape, jnp.float32)
    shift_total = jnp.zeros(norm_shifts.shape, jnp.float32)
    mask_total = jnp.zeros(mask_vector.shape, jnp.float32)
    decoded_parts = []
    source_parts = []
    target_parts = []
    running = None
    for micro in range(MICRO):
        weights = (
            lax.all_gather(enc_query, "dp", axis=0, tiled=True),
            lax.all_gather(enc_key, "dp", axis=0, tiled=True),
            lax.all_gather(enc_value, "dp", axis=0, tiled=True),
            lax.all_gather(enc_out, "dp", axis=1, tiled=True),
            lax.all_gather(enc_up, "dp", axis=0, tiled=True),
            lax.all_gather(enc_down, "dp", axis=1, tiled=True),
            lax.all_gather(self_query, "dp", axis=0, tiled=True),
            lax.all_gather(self_key, "dp", axis=0, tiled=True),
            lax.all_gather(self_value, "dp", axis=0, tiled=True),
            lax.all_gather(self_out, "dp", axis=1, tiled=True),
            lax.all_gather(cross_query, "dp", axis=0, tiled=True),
            lax.all_gather(cross_key, "dp", axis=0, tiled=True),
            lax.all_gather(cross_value, "dp", axis=0, tiled=True),
            lax.all_gather(cross_out, "dp", axis=1, tiled=True),
            lax.all_gather(dec_up, "dp", axis=0, tiled=True),
            lax.all_gather(dec_down, "dp", axis=1, tiled=True),
        )
        wide = (
            lax.all_gather(weights[4], "tensor", axis=1, tiled=True),
            lax.all_gather(weights[5], "tensor", axis=0, tiled=True),
            lax.all_gather(weights[14], "tensor", axis=1, tiled=True),
            lax.all_gather(weights[15], "tensor", axis=0, tiled=True),
        )
        lower = micro * per_micro
        upper = lower + per_micro
        live = positions[None, :] < lengths[lower:upper][:, None]
        every = jnp.ones((per_micro, seq_len), bool)
        inputs_x = source[lower:upper].astype(jnp.float32)
        rows0 = spread(norm_rows(inputs_x, gains[0], shifts[0]))
        saved0 = attend_forward(rows0, rows0, weights[0], weights[1], weights[2], live)
        stream1 = inputs_x + collect(project(saved0[3], weights[3]))
        normed1 = norm_rows(stream1, gains[1], shifts[1])
        rows1 = normed1.astype(jnp.bfloat16)
        lifted1, active1, partial1 = feed_forward(rows1, wide[0], wide[1])
        stream2 = stream1 + partial1
        memory_rows = spread(norm_rows(stream2, gains[2], shifts[2]))
        chosen = masked[lower:upper][:, :, None] == 1
        start_y = jnp.where(chosen, mask_vector, target[lower:upper].astype(jnp.float32))
        rows3 = spread(norm_rows(start_y, gains[3], shifts[3]))
        saved3 = attend_forward(rows3, rows3, weights[6], weights[7], weights[8], every)
        stream4 = start_y + collect(project(saved3[3], weights[9]))
        rows4 = spread(norm_rows(stream4, gains[4], shifts[4]))
        saved4 = attend_forward(rows4, memory_rows, weights[10], weights[11], weights[12], live)
        stream5 = stream4 + collect(project(saved4[3], weights[13]))
        normed5 = norm_rows(stream5, gains[5], shifts[5])
        rows5 = normed5.astype(jnp.bfloat16)
        lifted5, active5, partial5 = feed_forward(rows5, wide[2], wide[3])
        stream6 = stream5 + partial5
        decoded_parts.append(stream6.astype(jnp.bfloat16))
        factor = (STEPS + 1 - timesteps[lower:upper]).astype(jnp.float32) / STEPS
        grad6 = (
            cotangent[lower:upper].astype(jnp.float32)
            * (factor[:, None] * loss_mask[lower:upper].astype(jnp.float32))[:, :, None]
        )
        (up5, down5), into5 = feed_backward(
            grad6.astype(jnp.bfloat16), rows5, wide[2], wide[3], lifted5, active5
        )
        back5 = norm_back(stream5, gains[5], shifts[5], into5)
        grad5 = grad6 + back5[0]
        grads4, query_term4, memory_term = attend_backward(
            spread_grad(grad5),
            rows4,
            memory_rows,
            weights[10],
            weights[11],
            weights[12],
            weights[13],
            saved4,
            live,
        )
        back4 = norm_back(stream4, gains[4], shifts[4], collect_grad(query_term4))
        grad4 = grad5 + back4[0]
        memory_grad = collect_grad(memory_term)
        grads3, query_term3, keys_term3 = attend_backward(
            spread_grad(grad4),
            rows3,
            rows3,
            weights[6],
            weights[7],
            weights[8],
            weights[9],
            saved3,
            every,
        )
        back3 = norm_back(start_y, gains[3], shifts[3], collect_grad(query_term3 + keys_term3))
        grad_y = grad4 + back3[0]
        target_parts.append(jnp.where(chosen, 0.0, grad_y).astype(jnp.bfloat16))
        mask_total = mask_total + jnp.sum(jnp.where(chosen, grad_y, 0.0), axis=(0, 1))
        back2 = norm_back(stream2, gains[2], shifts[2], memory_grad)
        grad2 = back2[0]
        (up1, down1), into1 = feed_backward(
            grad2.astype(jnp.bfloat16), rows1, wide[0], wide[1], lifted1, active1
        )
        back1 = norm_back(stream1, gains[1], shifts[1], into1)
        grad1 = grad2 + back1[0]
        grads0, query_term0, keys_term0 = attend_backward(
            spread_grad(grad1),
            rows0,
            rows0,
            weights[0],
            weights[1],
            weights[2],
            weights[3],
            saved0,
            live,
        )
        back0 = norm_back(inputs_x, gains[0], shifts[0], collect_grad(query_term0 + keys_term0))
        source_parts.append((grad1 + back0[0]).astype(jnp.bfloat16))
        gain_total = gain_total + jnp.stack(
            [back0[1], back1[1], back2[1], back3[1], back4[1], back5[1]]
        )
        shift_total = shift_total + jnp.stack(
            [back0[2], back1[2], back2[2], back3[2], back4[2], back5[2]]
        )
        up1, down1, up5, down5 = (
            lax.psum_scatter(
                up1.astype(jnp.bfloat16), "tensor", scatter_dimension=1, tiled=True
            ).astype(jnp.float32),
            lax.psum_scatter(
                down1.astype(jnp.bfloat16), "tensor", scatter_dimension=0, tiled=True
            ).astype(jnp.float32),
            lax.psum_scatter(
                up5.astype(jnp.bfloat16), "tensor", scatter_dimension=1, tiled=True
            ).astype(jnp.float32),
            lax.psum_scatter(
                down5.astype(jnp.bfloat16), "tensor", scatter_dimension=0, tiled=True
            ).astype(jnp.float32),
        )
        fresh = (
            grads0[0],
            grads0[1],
            grads0[2],
            grads0[3],
            up1,
            down1,
            grads3[0],
            grads3[1],
            grads3[2],
            grads3[3],
            grads4[0],
            grads4[1],
            grads4[2],
            grads4[3],
            up5,
            down5,
        )
        running = fresh if micro == 0 else jax.tree.map(jnp.add, running, tuple(fresh))
    running = (
        lax.psum_scatter(
            running[0].astype(jnp.bfloat16), "dp", scatter_dimension=0, tiled=True
        ).astype(jnp.float32),
        lax.psum_scatter(
            running[1].astype(jnp.bfloat16), "dp", scatter_dimension=0, tiled=True
        ).astype(jnp.float32),
        lax.psum_scatter(
            running[2].astype(jnp.bfloat16), "dp", scatter_dimension=0, tiled=True
        ).astype(jnp.float32),
        lax.psum_scatter(
            running[3].astype(jnp.bfloat16), "dp", scatter_dimension=1, tiled=True
        ).astype(jnp.float32),
        lax.psum_scatter(
            running[4].astype(jnp.bfloat16), "dp", scatter_dimension=0, tiled=True
        ).astype(jnp.float32),
        lax.psum_scatter(
            running[5].astype(jnp.bfloat16), "dp", scatter_dimension=1, tiled=True
        ).astype(jnp.float32),
        lax.psum_scatter(
            running[6].astype(jnp.bfloat16), "dp", scatter_dimension=0, tiled=True
        ).astype(jnp.float32),
        lax.psum_scatter(
            running[7].astype(jnp.bfloat16), "dp", scatter_dimension=0, tiled=True
        ).astype(jnp.float32),
        lax.psum_scatter(
            running[8].astype(jnp.bfloat16), "dp", scatter_dimension=0, tiled=True
        ).astype(jnp.float32),
        lax.psum_scatter(
            running[9].astype(jnp.bfloat16), "dp", scatter_dimension=1, tiled=True
        ).astype(jnp.float32),
        lax.psum_scatter(
            running[10].astype(jnp.bfloat16), "dp", scatter_dimension=0, tiled=True
        ).astype(jnp.float32),
        lax.psum_scatter(
            running[11].astype(jnp.bfloat16), "dp", scatter_dimension=0, tiled=True
        ).astype(jnp.float32),
        lax.psum_scatter(
            running[12].astype(jnp.bfloat16), "dp", scatter_dimension=0, tiled=True
        ).astype(jnp.float32),
        lax.psum_scatter(
            running[13].astype(jnp.bfloat16), "dp", scatter_dimension=1, tiled=True
        ).astype(jnp.float32),
        lax.psum_scatter(
            running[14].astype(jnp.bfloat16), "dp", scatter_dimension=0, tiled=True
        ).astype(jnp.float32),
        lax.psum_scatter(
            running[15].astype(jnp.bfloat16), "dp", scatter_dimension=1, tiled=True
        ).astype(jnp.float32),
    )
    vectors = lax.psum((gain_total, shift_total, mask_total), ("dp", "tensor"))
    return (
        jnp.concatenate(decoded_parts, axis=0),
        jnp.concatenate(source_parts, axis=0),
        jnp.concatenate(target_parts, axis=0),
        running[0],
        running[1],
        running[2],
        running[3],
        running[4],
        running[5],
        running[6],
        running[7],
        running[8],
        running[9],
        running[10],
        running[11],
        running[12],
        running[13],
        running[14],
        running[15],
        vectors[0],
        vectors[1],
        vectors[2],
    )


F32 = jnp.float32
BF = jnp.bfloat16
LOG2E = 1.4426950408889634
LN2 = 0.6931471805599453
NN = (((1,), (0,)), ((), ()))
NT = (((1,), (1,)), ((), ()))
MESH = pl.DeviceIdType.MESH
RB = 256
VMEM_LIMIT = 63 * 2**20


def dg(left, right, dims=NN):
    return lax.dot_general(left, right, dims, preferred_element_type=F32)


def ln_hat(x):
    centred = x - jnp.mean(x, axis=-1, keepdims=True)
    rstd = lax.rsqrt(jnp.mean(centred * centred, axis=-1, keepdims=True) + eps)
    return centred * rstd, rstd


def ln_back(x, gain, gradient):
    hat, rstd = ln_hat(x)
    scaled = gradient * gain
    first = jnp.mean(scaled, axis=-1, keepdims=True)
    second = jnp.mean(scaled * hat, axis=-1, keepdims=True)
    dx = rstd * (scaled - first - hat * second)
    dgain = jnp.sum(gradient * hat, axis=0, keepdims=True)
    dshift = jnp.sum(gradient, axis=0, keepdims=True)
    return dx, dgain, dshift


def gelu_both(u):
    size = jnp.abs(u)
    t = 1.0 / (1.0 + (0.3275911 * 0.7071067811865476) * size)
    ex = jnp.exp2(u * u * (-0.5 * LOG2E))
    poly = t * (
        0.127414796
        + t * (-0.142248368 + t * (0.7107068705 + t * (-0.7265760135 + t * 0.5307027145)))
    )
    tail = poly * ex
    phi = jnp.where(u > 0, 1.0 - tail, tail)
    return u * phi, phi + u * ex * 0.3989422804014327


def rows_loop(total, step, run):
    def once(i, carry):
        run(pl.ds(pl.multiple_of(i * step, step), step))
        return carry

    lax.fori_loop(0, total // step, once, 0)


def load_weight(w_hbm, offset, width, dst, sems, base):
    copies = []
    for t in range(2):
        src = pl.ds(offset, width)
        to = pl.ds(t * width, width)
        cp = pltpu.make_async_copy(
            w_hbm.at[t, :, src] if len(w_hbm.shape) == 3 else w_hbm.at[t, :, :, :, :, src],
            dst.at[:, to] if len(dst.shape) == 2 else dst.at[:, :, :, :, to],
            sems.at[base + t],
        )
        cp.start()
        copies.append(cp)
    return copies


def wait_all(copies):
    for cp in copies:
        cp.wait()


def whole(ref):
    value = ref[...]
    return value if value.ndim == 2 else value.reshape(-1, value.shape[-1])


def normalize(x, gain, shift, a):
    def run(sl):
        hat, unused = ln_hat(x[sl, :].astype(F32))
        a[sl, :] = (hat * gain + shift).astype(BF)

    rows_loop(x.shape[0], 2 * RB, run)


def attn_project(a, kv, wq, wk, wv, q, k, v):
    def run(sl):
        q[sl, :] = (dg(a[sl, :], whole(wq)) * (LOG2E * HD**-0.5)).astype(BF)
        k[sl, :] = dg(kv[sl, :], whole(wk)).astype(BF)
        v[sl, :] = dg(kv[sl, :], whole(wv)).astype(BF)

    rows_loop(a.shape[0], 2 * RB, run)


def attn_core(length, q, k, v, o, ol, r, e_hbm, ebuf, esem, between):
    seq = q.shape[0]
    pairs = q.shape[1] // 128
    block = 512
    lane = lax.broadcasted_iota(jnp.int32, (1, 128), 1)
    low = lane < 64
    one = jnp.ones((), BF)
    key = lax.broadcasted_iota(jnp.int32, (seq, 1), 0)
    bias = jnp.where(key < length, 0.0, floor_score).astype(F32)

    def out(p, h):
        slot = lax.rem(p, 2) * 2 + h
        return pltpu.make_async_copy(ebuf.at[slot], e_hbm.at[2 * p + h], esem.at[slot])

    def pair(p, carry):
        @pl.when(p > 1)
        def unused_wait():
            out(p - 2, 0).wait()
            out(p - 2, 1).wait()

        base = lax.rem(p, 2) * 2
        cols = pl.ds(pl.multiple_of(p * 128, 128), 128)
        kp = k[:, cols].astype(F32)
        vp = v[:, cols]
        ka = (
            jnp.where(low, kp, jnp.where(lane == 64, bias, 0.0)).astype(BF),
            jnp.where(low, jnp.where(lane == 0, bias, 0.0), kp).astype(BF),
        )
        va = jnp.where(low, vp, one), jnp.where(low, one, vp)
        for b in range(seq // block):
            sl = pl.ds(b * block, block)
            qp = q[sl, cols]
            parts = []
            for h in range(2):
                qm = jnp.where(low, qp, one) if h == 0 else jnp.where(low, one, qp)
                s = dg(qm, ka[h], NT)
                e = jnp.exp2(s - jnp.max(s, axis=-1, keepdims=True)).astype(BF)
                ebuf[base + h, sl, :] = e
                parts.append(dg(e, va[h]))
            un = jnp.where(low, parts[0], parts[1])
            inverse = 1.0 / pltpu.roll(jnp.where(low, parts[1], parts[0]), 64, 1)
            r[sl, cols] = inverse.astype(BF)
            joined = un * inverse
            rounded = joined.astype(BF)
            o[sl, cols] = rounded
            ol[sl, cols] = (joined - rounded.astype(F32)).astype(BF)
        out(p, 0).start()
        out(p, 1).start()
        return carry

    lax.fori_loop(0, pairs // 2, pair, 0)
    between()
    lax.fori_loop(pairs // 2, pairs, pair, 0)
    for p in (pairs - 2, pairs - 1):
        out(p, 0).wait()
        out(p, 1).wait()


def attn_join(x, o, wo, y):
    def run(sl):
        y[sl, :] = x[sl, :].astype(F32) + dg(o[sl, :], whole(wo), NT)

    rows_loop(x.shape[0], 2 * RB, run)


def first_scores(e_hbm, ebuf, esem):
    for h in range(2):
        pltpu.make_async_copy(e_hbm.at[h], ebuf.at[h], esem.at[h]).start()


def attn_back_core(q, k, v, do, o, ol, e_hbm, ebuf, esem, ds, dq, dk, dv, between):
    seq = q.shape[0]
    heads = e_hbm.shape[0]
    block = 512
    lane = lax.broadcasted_iota(jnp.int32, (1, 128), 1)
    low = lane < 64
    zero = jnp.zeros((), BF)
    one = jnp.ones((), BF)
    row2 = lax.broadcasted_iota(jnp.int32, (256, 128), 0)
    col2 = lax.broadcasted_iota(jnp.int32, (256, 128), 1)
    swap = jnp.where(((row2 // 64) % 2) != (col2 // 64), 1.0, 0.0).astype(BF)

    def fetch(p, h):
        slot = lax.rem(p, 2) * 2 + h
        return pltpu.make_async_copy(e_hbm.at[2 * p + h], ebuf.at[slot], esem.at[slot])

    def pair(p, carry):
        cols = pl.ds(pl.multiple_of(p * 128, 128), 128)
        fetch(p, 0).wait()
        fetch(p, 1).wait()

        @pl.when(p + 1 < heads // 2)
        def unused_fetch():
            fetch(p + 1, 0).start()
            fetch(p + 1, 1).start()

        base = lax.rem(p, 2) * 2
        qp, kp, vp, dop = q[:, cols], k[:, cols], v[:, cols], do[:, cols]
        product = dop.astype(F32) * (o[:, cols].astype(F32) + ol[:, cols].astype(F32))
        high = product.astype(BF)
        rest = (product - high.astype(F32)).astype(BF)
        inner = -dg(jnp.concatenate([high, rest], axis=1), swap)
        inner_high = inner.astype(BF)
        inner_rest = (inner - inner_high.astype(F32)).astype(BF)
        do_t, q_t = dop.T, qp.T
        dq_sum = None
        dks, dvs = [], []
        for h in range(2):
            if h == 0:
                lhs = jnp.where(low, dop, jnp.where(lane == 64, inner_high, inner_rest))
                va = jnp.where(low, vp, jnp.where(lane < 66, one, zero))
                km = jnp.where(low, kp, zero)
            else:
                lhs = jnp.where(low, jnp.where(lane == 0, inner_high, inner_rest), dop)
                va = jnp.where(low, jnp.where(lane < 2, one, zero), vp)
                km = jnp.where(low, zero, kp)
            for b in range(seq // block):
                sl = pl.ds(b * block, block)
                t = dg(lhs[b * block : (b + 1) * block], va, NT)
                ds[h, sl, :] = ebuf[base + h, sl, :] * t.astype(BF)
            part = dg(ds[h], km)
            dq_sum = part if dq_sum is None else dq_sum + part
            dks.append(dg(q_t[64 * h : 64 * h + 64], ds[h]))
            dvs.append(dg(do_t[64 * h : 64 * h + 64], ebuf[base + h]))
        dq[:, cols] = (dq_sum * HD**-0.5).astype(BF)
        dk[:, cols] = (jnp.concatenate(dks, axis=0) * LN2).astype(BF).T
        dv[:, cols] = jnp.concatenate(dvs, axis=0).astype(BF).T
        return carry

    lax.fori_loop(0, heads // 4, pair, 0)
    between()
    lax.fori_loop(heads // 4, heads // 2, pair, 0)


def places():
    d = lax.axis_index("dp")
    return lax.axis_index("tensor"), d // 4, (d // 2) % 2, d % 2


def at(t, z, y, c):
    return (z * 4 + y * 2 + c, t)


def greet(partners):
    barrier = pltpu.get_barrier_semaphore()
    for device in partners:
        pl.semaphore_signal(barrier, inc=1, device_id=device, device_id_type=MESH)
    pl.semaphore_wait(barrier, len(partners))


def all_partners(t, z, y, c):
    others = [at(t, lax.rem(z + j, 4), y, c) for j in range(1, 4)]
    return [at(t, z, y, 1 - c), at(1 - t, z, y, c), at(t, z, 1 - y, c)] + others


class Saver:
    def __init__(self, sems):
        self.sems, self.count, self.live = sems, 0, []

    def __call__(self, src, dst, slot=None):
        cp = pltpu.make_async_copy(src, dst, self.sems.at[self.count])
        cp.start()
        self.count += 1
        self.live.append((slot, cp))

    def free(self, slot):
        for name, cp in self.live:
            if name == slot:
                cp.wait()
        self.live = [entry for entry in self.live if entry[0] != slot]

    def finish(self):
        for name, cp in self.live:
            cp.wait()
        self.live = []


class SplitColumns:
    def __init__(self, ref, n):
        self.ref, self.n = ref, n

    def cols(self, h):
        return pl.ds(h * self.n, self.n)

    def __getitem__(self, h):
        return self.ref[:, self.cols(h)]

    def __setitem__(self, key, value):
        h, sl, unused = key
        self.ref[sl, self.cols(h)] = value


GATHER_PLAN = (
    ((0, 0), (1, 0), (3, 0), (4, 0)),
    ((0, 1),),
    ((1, 1),),
    ((0, 2), (3, 1)),
    ((0, 3), (0, 4), (1, 2)),
    ((2, 0), (3, 2)),
    ((1, 3), (5, 0)),
    ((1, 4), (2, 1), (4, 1)),
    ((3, 3),),
    (),
    ((2, 2), (6, 0), (6, 1)),
    ((2, 3), (4, 2), (5, 1)),
    ((2, 4), (3, 4)),
    ((4, 3), (6, 2)),
    ((4, 4), (5, 2)),
    (),
    ((6, 3),),
    ((5, 3),),
    (),
    ((5, 4), (6, 4)),
)


class Gather:
    def __init__(self, own, out, send, recv, chunks):
        self.own, self.out, self.send, self.recv, self.chunks = own, out, send, recv, chunks
        self.spot = places()
        self.sends, self.pending = [], {}

    def push(self, src, dst, k, i, device):
        copy = pltpu.make_async_remote_copy(
            src_ref=src, dst_ref=dst, send_sem=self.send.at[k, i], recv_sem=self.recv.at[k, i],
            device_id=device, device_id_type=MESH,
        )
        copy.start()
        self.sends.append(copy)
        self.pending.setdefault(k, []).append(copy)

    def move(self, point):
        for k, s in GATHER_PLAN[point]:
            self.stage(k, s)

    def stage(self, k, s):
        t, z, y, c = self.spot
        own, out = self.own, self.out
        start, width, split = self.chunks[k]
        full = pl.ds(start, width)
        half = width // 2 if split else width
        left = pl.ds(start, half)
        right = pl.ds(start + half, half)
        by_x, by_y = at(1 - t, z, y, c), at(t, z, 1 - y, c)
        for copy in self.pending.pop(k, ()):
            copy.wait_recv()
        if s == 0:
            for j in range(1, 4):
                self.push(own.at[:, full], out.at[t, z, y, c, :, full], k, j - 1, at(t, lax.rem(z + j, 4), y, c))
        elif s == 1:
            a = out.at[t, :, y, c, :, left]
            self.push(a, a, k, 3, by_x)
            if split:
                b = out.at[t, :, y, c, :, right]
                self.push(b, b, k, 4, by_y)
        elif s == 2:
            a = out.at[:, :, y, c, :, left]
            self.push(a, a, k, 5, by_y)
            if split:
                b = out.at[t, :, :, c, :, right]
                self.push(b, b, k, 6, by_x)
        elif s == 3:
            a = out.at[:, :, :, c, :, full]
            self.push(a, a, k, 7, at(t, z, y, 1 - c))

    def finish(self):
        for copy in self.sends:
            copy.wait_send()


class Exchange:
    def __init__(self, send, recv, local):
        self.send, self.recv, self.local = send, recv, local
        self.open = []

    def start(self, i, src, kept, dst):
        t, z, y, c = places()
        far = pltpu.make_async_remote_copy(
            src_ref=src, dst_ref=dst, send_sem=self.send.at[i], recv_sem=self.recv.at[i],
            device_id=at(1 - t, z, y, c), device_id_type=MESH,
        )
        near = pltpu.make_async_copy(kept, dst, self.local.at[i])
        far.start()
        near.start()
        self.open.append(far)
        return far, near

    def give(self, i, halves, dst):
        t = lax.axis_index("tensor")
        rows = halves.shape[1]
        mine = dst.at[pl.ds(pl.multiple_of(t * rows, rows), rows), :]
        return self.start(i, halves.at[1 - t], halves.at[t], mine)

    def back(self, i, pair, dst):
        t = lax.axis_index("tensor")
        rows = dst.shape[1]
        kept = pair.at[pl.ds(pl.multiple_of(t * rows, rows), rows), :]
        sent = pair.at[pl.ds(pl.multiple_of((1 - t) * rows, rows), rows), :]
        return self.start(i, sent, kept, dst.at[t])

    def finish(self):
        for far in self.open:
            far.wait_send()


def arrived(copies):
    far, near = copies
    near.wait()
    far.wait_recv()


def column(values):
    return jnp.broadcast_to(values, (128, values.shape[1])).T[:, :1]


def weight_loader(w_hbm, sems):
    loads = {}

    def load(name, offset, refs, n, base):
        loads[name] = []
        for i, ref in enumerate(refs):
            loads[name] += load_weight(w_hbm, offset + i * n, n, ref, sems, base + 2 * i)

    def ready(name):
        wait_all(loads[name])

    return load, ready


TURNED = (3, 5, 9, 13, 15)
PACKED = (0, 1, 2, 3, 6, 7, 8, 9, 4, 5, 10, 11, 12, 13, 14, 15)


def forward(
    lengths, timesteps, gains, shifts, mask_row, masked, loss_mask, *refs,
):
    matrices, refs = refs[:16], refs[16:]
    (
        src_hbm, target_hbm, cot_hbm,
        w_hbm, x_o, y0_o, g3_o,
        a0_o, q0_o, k0_o, v0_o, o0_o, ol0_o, r0_o, e0_o, x1_o, a1_o, h1_o, gp1_o, x2_o, mem_o,
        a3_o, q3_o, k3_o, v3_o, o3_o, ol3_o, r3_o, e3_o, y1_o,
        a4_o, q4_o, k4_o, v4_o, o4_o, ol4_o, r4_o, e4_o, y2_o,
        own, tgt, cot, x, y0, wq, wk, wv, wo, sq, sk, sv, so, wu, wd,
        a, q, k, v, o, ol, r, a3, q3, k3, v3, o3, ol3, r3,
        x1, a1, h, gp, x2, mem, y1, y2, ebuf,
        gsend, grecv, xsend, xrecv, local, wsem, esem, osem,
    ) = refs
    t, z, y, c = places()
    seq, width = x.shape
    n1, n2 = width // 2, h.shape[1] // 2
    in_tgt = pltpu.make_async_copy(target_hbm, tgt, local.at[4])
    in_cot = pltpu.make_async_copy(cot_hbm, cot, local.at[5])
    in_tgt.start()
    in_cot.start()
    offset = 0
    for i in PACKED:
        part = matrices[i][...]
        own[:, pl.ds(offset, part.shape[1])] = part
        offset += part.shape[1]
    greet(all_partners(t, z, y, c))
    halves = Exchange(xsend, xrecv, local)
    first = 3 * n1
    widths = (first, 8 * n1 - first, n2, n2, 4 * n1, n2, n2)
    splits = (True, True, True, False, True, True, True)
    gather = Gather(
        own, w_hbm, gsend, grecv,
        tuple((sum(widths[:i]), widths[i], splits[i]) for i in range(len(widths))),
    )
    mine = pltpu.make_async_copy(own, w_hbm.at[t, z, y, c], local.at[3])
    mine.start()
    gather.move(0)
    x_in = halves.give(0, src_hbm, x)
    save = Saver(osem)
    in_tgt.wait()
    for i in range(2):
        chosen = column(masked[i : i + 1, :].astype(F32)) == 1.0
        tgt[i] = jnp.where(chosen, mask_row[...], tgt[i].astype(F32)).astype(BF)
    mine.wait()
    gather.move(1)
    in_cot.wait()
    for i in range(2):
        factor = (STEPS + 1 - timesteps[i]).astype(F32) / STEPS
        weight = column(loss_mask[i : i + 1, :].astype(F32)) * factor
        cot[i] = (cot[i].astype(F32) * weight).astype(BF)
    gather.move(2)
    arrived(x_in)
    normalize(x, gains[0:1, :], shifts[0:1, :], a)
    save(x, x_o)
    save(a, a0_o, "A")
    gather.move(3)
    gather.move(4)
    load, ready = weight_loader(w_hbm, wsem)
    load("enc", 0, (wq, wk, wv), n1, 0)
    y0_in = halves.give(1, tgt, y0)
    ready("enc")
    attn_project(a, a, wq, wk, wv, q, k, v)
    for src, dst in ((q, q0_o), (k, k0_o), (v, v0_o)):
        save(src, dst, "A")
    gather.move(5)
    length = lengths[t]

    def between0():
        gather.move(6)

    attn_core(length, q, k, v, o, ol, r, e0_o, ebuf, esem, between0)
    gather.move(7)
    load("out", 3 * n1, (wo,), n1, 6)
    load("self", 4 * n1, (sq, sk, sv, so), n1, 8)
    for src, dst in ((o, o0_o), (ol, ol0_o), (r, r0_o)):
        save(src, dst, "A")
    arrived(y0_in)
    save(y0, y0_o)
    normalize(y0, gains[3:4, :], shifts[3:4, :], a3)
    gather.move(8)
    ready("self")
    attn_project(a3, a3, sq, sk, sv, q3, k3, v3)
    for src, dst in ((a3, a3_o), (q3, q3_o), (k3, k3_o), (v3, v3_o)):
        save(src, dst)
    ready("out")
    attn_join(x, o, wo, x1)
    save(x1, x1_o)
    gather.move(9)
    gather.move(10)

    def between3():
        gather.move(11)

    attn_core(seq, q3, k3, v3, o3, ol3, r3, e3_o, ebuf, esem, between3)
    gather.move(12)
    load("feed", 8 * n1, (wu, wd), n2, 16)
    for src, dst in ((o3, o3_o), (ol3, ol3_o), (r3, r3_o)):
        save(src, dst)
    attn_join(y0, o3, so, y1)
    save(y1, y1_o)
    save.free("A")
    normalize(y1, gains[4:5, :], shifts[4:5, :], a)
    gather.move(13)
    ready("feed")

    def feed(sl):
        stream = x1[sl, :]
        hat, unused = ln_hat(stream)
        rows = (hat * gains[1:2, :] + shifts[1:2, :]).astype(BF)
        a1[sl, :] = rows
        active, slope = gelu_both(dg(rows, whole(wu)))
        active = active.astype(BF)
        h[sl, :] = active
        gp[sl, :] = slope.astype(BF)
        out = stream + dg(active, whole(wd), NT)
        x2[sl, :] = out.astype(BF)
        hat, unused = ln_hat(out)
        mem[sl, :] = (hat * gains[2:3, :] + shifts[2:3, :]).astype(BF)

    rows_loop(seq // 2, RB, feed)
    gather.move(14)
    load("cross", 8 * n1 + 2 * n2, (wq, wk, wv, wo), n1, 0)
    rows_loop(seq // 2, RB, lambda sl: feed(pl.ds(pl.multiple_of(seq // 2 + sl.start, RB), RB)))
    g3_in = halves.give(2, cot, g3_o)
    for src, dst in ((a1, a1_o), (h, h1_o), (gp, gp1_o), (x2, x2_o), (mem, mem_o)):
        save(src, dst)
    gather.move(15)
    ready("cross")
    attn_project(a, mem, wq, wk, wv, q, k, v)
    for src, dst in ((a, a4_o), (q, q4_o), (k, k4_o), (v, v4_o)):
        save(src, dst)
    gather.move(16)

    def between4():
        gather.move(17)

    attn_core(length, q, k, v, o, ol, r, e4_o, ebuf, esem, between4)
    for src, dst in ((o, o4_o), (ol, ol4_o), (r, r4_o)):
        save(src, dst)
    gather.move(18)
    attn_join(y1, o, wo, y2)
    save(y2, y2_o)
    gather.move(19)
    arrived(g3_in)
    halves.finish()
    gather.finish()
    save.finish()


class Reduce:
    def __init__(self, out, chunks):
        self.out, self.chunks = out, chunks
        self.spot = places()
        self.sends, self.pending = [], {}

    def push(self, name, i, src, dst, device):
        send, recv = self.chunks[name][5:7]
        copy = pltpu.make_async_remote_copy(
            src_ref=src, dst_ref=dst, send_sem=send.at[i], recv_sem=recv.at[i],
            device_id=device, device_id_type=MESH,
        )
        copy.start()
        self.sends.append((name, copy))
        self.pending.setdefault(name, []).append(copy)

    def move(self, *steps):
        for name, s in steps:
            self.stage(name, s)

    def stage(self, name, s):
        t, z, y, c = self.spot
        g, r1, r2, r3, r4, send, recv, start, split = self.chunks[name]
        width = g.shape[-1]
        half = width // 2 if split else width
        left = pl.ds(0, half)
        right = pl.ds(half, half)
        by_x, by_y = at(1 - t, z, y, c), at(t, z, 1 - y, c)

        def add(mine, theirs):
            mine[...] = (mine[...].astype(F32) + theirs[...].astype(F32)).astype(BF)

        for copy in self.pending.pop(name, ()):
            copy.wait_recv()
        if s == 0:
            self.push(name, 0, g.at[:, :, :, 1 - c], r1, at(t, z, y, 1 - c))
        elif s == 1:
            add(g.at[:, :, 1 - y, c], r1.at[:, :, 1 - y])
            self.push(name, 1, g.at[:, :, 1 - y, c, :, left], r2.at[:, :, :, left], by_y)
            add(g.at[:, :, y, c], r1.at[:, :, y])
            if split:
                self.push(name, 2, g.at[1 - t, :, :, c, :, right], r3.at[0], by_x)
        elif s == 2:
            rows = g.at[:, :, y, c, :, left]
            add(rows, r2.at[:, :, :, left])
            if not split:
                self.push(name, 2, g.at[1 - t, :, y, c], r3, by_x)
            else:
                self.push(name, 3, g.at[1 - t, :, y, c, :, left], r3.at[1, :, 0], by_x)
                add(g.at[t, :, :, c, :, right], r3.at[0])
                self.push(name, 4, g.at[t, :, 1 - y, c, :, right], r3.at[1, :, 1], by_y)
        elif s == 3:
            if not split:
                add(g.at[t, :, y, c], r3)
            else:
                add(g.at[t, :, y, c, :, left], r3.at[1, :, 0])
                add(g.at[t, :, y, c, :, right], r3.at[1, :, 1])
            for j in range(1, 4):
                zz = lax.rem(z + j, 4)
                self.push(name, 4 + j, g.at[t, zz, y, c], r4.at[j - 1], at(t, zz, y, c))
        elif s == 4:
            self.out[:, pl.ds(start, width)] = (g[t, z, y, c].astype(F32) + r4[0].astype(F32)) + (
                r4[1].astype(F32) + r4[2].astype(F32)
            )

    def release(self, name):
        for owner, copy in self.sends:
            if owner == name:
                copy.wait_send()
        self.sends = [entry for entry in self.sends if entry[0] != name]

    def finish(self):
        for owner, copy in self.sends:
            copy.wait_send()
        self.sends = []


def put(g, first, n, value, lower=0):
    done = 0
    while done < value.shape[1]:
        t, offset = (lower + done) // n, (lower + done) % n
        take = min(value.shape[1] - done, n - offset)
        block = value[:, done : done + take].astype(BF)
        g[t, :, :, :, :, pl.ds(first + offset, take)] = block.reshape(g.shape[1:5] + (take,))
        done += take


def add_norm(ng, index, dgain, dshift):
    ng[index : index + 1, :] += dgain
    ng[6 + index : 7 + index, :] += dshift


def attn_backward(
    g, x, gain, ng, index, a_t, kv_t, g_t, wq, wk, wv, wo, q, k, v, o, ol, r, e_hbm, ebuf, esem, ds,
    do, dq, dk, dv, grads, n1, before_core, between, after_core, after_grads, into_keys, finish,
):
    seq = x.shape[0]

    def before(sl):
        rows = g[sl, :].astype(BF)
        g_t[:, sl] = rows.T
        do[sl, :] = (dg(rows, wo[...]) * r[sl, :].astype(F32)).astype(BF)

    rows_loop(seq, 2 * RB, before)
    put(grads, 3 * n1, n1, dg(g_t[...], o[...]))
    before_core()
    attn_back_core(q, k, v, do, o, ol, e_hbm, ebuf, esem, ds, dq, dk, dv, between)
    after_core()
    put(grads, 0, n1, dg(a_t[...], dq[...]))
    put(grads, n1, n1, dg(kv_t[...], dk[...]))
    put(grads, 2 * n1, n1, dg(kv_t[...], dv[...]))
    after_grads()

    def after(sl):
        into = dg(dq[sl, :], wq[...], NT)
        keys = dg(dk[sl, :], wk[...], NT) + dg(dv[sl, :], wv[...], NT)
        if into_keys is None:
            into = into + keys
        else:
            into_keys[sl, :] = keys
        dx, dgain, dshift = ln_back(x[sl, :].astype(F32), gain, into)
        add_norm(ng, index, dgain, dshift)
        finish(sl, g[sl, :] + dx)

    rows_loop(seq, 2 * RB, after)


def fetcher(sems):
    count = [0]

    def fetch(*pairs):
        copies = []
        for src, dst in pairs:
            cp = pltpu.make_async_copy(src, dst, sems.at[count[0]])
            count[0] += 1
            cp.start()
            copies.append(cp)
        return copies

    return fetch


def nothing():
    return None


def dec_backward(
    gains, shifts, y2_hbm, g3_hbm, y1_hbm, mem_hbm, a4_hbm, q4_hbm, k4_hbm, v4_hbm, o4_hbm, ol4_hbm, r4_hbm, e4_hbm,
    x2_hbm, x1_hbm, a1_hbm, h1_hbm, gp1_hbm, w_hbm,
    dec_o, g4_o, g1_o, up_o, down_o, sums, ng,
    y2, g3, y1, a, q, k, v, o, ol, r, cq, ck, cv, co, wu, wd,
    big, gs, do, a_t, g_t, g_up, g_down, g_cross, ebuf,
    ru1, ru2, ru3, ru4, rd1, rd2, rd3, rd4, rc1, rc2, rc3, rc4,
    rsend, rrecv, xsend, xrecv, local, isem, wsem, esem, osem,
):
    t, z, y, c = places()
    seq, width = y1.shape
    n1, n2 = cq.shape[1] // 2, wu.shape[1] // 2
    fetch = fetcher(isem)
    load, ready = weight_loader(w_hbm, wsem)
    first = fetch((y2_hbm, y2), (g3_hbm, g3))
    load("feed", 12 * n1 + 2 * n2, (wu, wd), n2, 0)
    greet(all_partners(t, z, y, c))
    halves = Exchange(xsend, xrecv, local)
    reduce = Reduce(
        sums,
        {
            "up": (g_up, ru1, ru2, ru3, ru4, rsend.at[0], rrecv.at[0], 0, True),
            "down": (g_down, rd1, rd2, rd3, rd4, rsend.at[1], rrecv.at[1], n2, True),
            "cross": (g_cross, rc1, rc2, rc3, rc4, rsend.at[2], rrecv.at[2], 2 * n2, True),
        },
    )
    ng[...] = jnp.zeros_like(ng)
    save = Saver(osem)
    wait_all(first)
    ready("feed")
    load("cross", 8 * n1 + 2 * n2, (cq, ck, cv, co), n1, 4)
    cross = fetch(
        (o4_hbm, o), (r4_hbm, r), (a4_hbm, a), (q4_hbm, q), (k4_hbm, k),
        (v4_hbm, v), (ol4_hbm, ol), (y1_hbm, y1),
    )
    first_scores(e4_hbm, ebuf, esem)
    h, du = big.at[0], big.at[1]

    def feed(sl):
        stream = y2[sl, :]
        hat, unused = ln_hat(stream)
        rows = (hat * gains[5:6, :] + shifts[5:6, :]).astype(BF)
        a_t[:, sl] = rows.T
        active, slope = gelu_both(dg(rows, wu[...]))
        active = active.astype(BF)
        h[sl, :] = active
        grad = g3[sl, :]
        g3[sl, :] = (stream + dg(active, wd[...], NT)).astype(BF)
        g_t[:, sl] = grad.T
        lifted = (dg(grad, wd[...]) * slope).astype(BF)
        du[sl, :] = lifted
        dx, dgain, dshift = ln_back(stream, gains[5:6, :], dg(lifted, wu[...], NT))
        add_norm(ng, 5, dgain, dshift)
        gs[sl, :] = grad.astype(F32) + dx

    rows_loop(seq, RB, feed)
    dec_back = halves.back(0, g3, dec_o)
    block = width
    for j in range(2 * n2 // block):
        put(g_up, 0, n2, dg(a_t[...], du[:, pl.ds(j * block, block)]), j * block)
    reduce.move(("up", 0))
    for j in range(2 * n2 // block):
        put(g_down, 0, n2, dg(g_t[...], h[:, pl.ds(j * block, block)]), j * block)
    load("enc", 8 * n1, (wu, wd), n2, 12)
    reduce.move(("up", 1))
    wait_all(cross)
    ready("cross")
    a_t[...] = a[...].T
    memory = big.at[1, :, pl.ds(3 * width, width)]
    late = fetch((mem_hbm, memory))
    dq, dk, dv = (big.at[1, :, pl.ds(i * width, width)] for i in range(3))

    def before_core():
        reduce.move(("down", 0))

    def between():
        reduce.move(("down", 1))

    def after_core():
        wait_all(late)
        late.clear()
        late.extend(fetch((x2_hbm, r)))
        g_t[...] = memory[...].T
        late.extend(
            fetch(
                (gp1_hbm.at[:, pl.ds(0, n2)], ebuf.at[2]), (gp1_hbm.at[:, pl.ds(n2, n2)], ebuf.at[3]),
                (h1_hbm.at[:, pl.ds(0, n2)], ebuf.at[0]), (h1_hbm.at[:, pl.ds(n2, n2)], ebuf.at[1]),
            )
        )
        reduce.move(("up", 2))

    def after_grads():
        late.extend(fetch((a1_hbm, a)))
        reduce.move(("cross", 0), ("down", 2))

    def keep(sl, gradient):
        gs[sl, :] = gradient

    attn_backward(
        gs, y1, gains[4:5, :], ng, 4, a_t, g_t, g_t, cq, ck, cv, co, q, k, v, o, ol, r, e4_hbm,
        ebuf, esem, SplitColumns(big.at[0], seq), do, dq, dk, dv, g_cross, n1,
        before_core, between, after_core, after_grads, y2, keep,
    )
    save(gs, g4_o)
    late.extend(fetch((x1_hbm, y1)))
    reduce.move(("up", 3), ("cross", 1))
    wait_all(late)
    ready("enc")
    save.finish()

    def feed_back(sl):
        dx, dgain, dshift = ln_back(r[sl, :].astype(F32), gains[2:3, :], y2[sl, :])
        add_norm(ng, 2, dgain, dshift)
        grad = dx.astype(BF)
        g_t[:, sl] = grad.T
        a_t[:, sl] = a[sl, :].T
        into = None
        for i in range(2):
            cols = pl.ds(i * n2, n2)
            lifted = (dg(grad, wd[:, cols]) * ebuf[2 + i, sl, :].astype(F32)).astype(BF)
            ebuf[2 + i, sl, :] = lifted
            part = dg(lifted, wu[:, cols], NT)
            into = part if into is None else into + part
        dx1, dgain, dshift = ln_back(y1[sl, :], gains[1:2, :], into)
        add_norm(ng, 1, dgain, dshift)
        gs[sl, :] = dx + dx1

    rows_loop(seq // 2, RB, feed_back)
    reduce.move(("down", 3))
    rows_loop(seq // 2, RB, lambda sl: feed_back(pl.ds(pl.multiple_of(seq // 2 + sl.start, RB), RB)))
    save(gs, g1_o)
    reduce.move(("cross", 2), ("up", 4))
    reduce.release("up")
    for i in range(2):
        for j in range(n2 // block):
            cols = pl.ds(j * block, block)
            put(g_up, 0, n2, dg(a_t[...], ebuf[2 + i, :, cols]), i * n2 + j * block)
    save(g_up, up_o)
    reduce.move(("cross", 3), ("down", 4))
    reduce.release("down")
    for i in range(2):
        for j in range(n2 // block):
            cols = pl.ds(j * block, block)
            put(g_down, 0, n2, dg(g_t[...], ebuf[i, :, cols]), i * n2 + j * block)
    save(g_down, down_o)
    reduce.move(("cross", 4))
    arrived(dec_back)
    halves.finish()
    reduce.finish()
    save.finish()


def last_backward(
    gains, ng2, masked, g4_hbm, g1_hbm, y0_hbm, a3_hbm, q3_hbm, k3_hbm, v3_hbm, o3_hbm, ol3_hbm, r3_hbm, e3_hbm,
    x_hbm, a0_hbm, q0_hbm, k0_hbm, v0_hbm, o0_hbm, ol0_hbm, r0_hbm, e0_hbm, up_hbm, down_hbm, w_hbm,
    sg_o, target_o, sums, vec,
    gs, gs1, x, x0, a, q, k, v, o, ol, r, wq, wk, wv, wo, vo, big, do, a_t, g_t, gy, ng,
    g_up, g_down, g_self, g_enc, ebuf,
    ru1, ru2, ru3, ru4, rd1, rd2, rd3, rd4, rs1, rs2, rs3, rs4, re1, re2, re3, re4, ro1, ro2, ro3, ro4, v1, vr,
    rsend, rrecv, xsend, xrecv, local, vsend, vrecv, isem, wsem, esem,
):
    t, z, y, c = places()
    seq, width = x.shape
    n1 = wq.shape[1] // 2
    n2 = g_up.shape[-1]
    fetch = fetcher(isem)
    load, ready = weight_loader(w_hbm, wsem)
    load("self out", 7 * n1, (wo,), n1, 0)
    first = fetch((g4_hbm, gs), (o3_hbm, o), (r3_hbm, r))
    ups = fetch((up_hbm, g_up), (down_hbm, g_down))
    first_scores(e3_hbm, ebuf, esem)
    second = fetch((q3_hbm, q), (k3_hbm, k), (v3_hbm, v), (ol3_hbm, ol), (a3_hbm, a), (y0_hbm, x))
    load("self", 4 * n1, (wq, wk, wv), n1, 2)
    load("enc out", 3 * n1, (vo,), n1, 8)
    late = fetch((g1_hbm, gs1), (x_hbm, x0))
    greet(all_partners(t, z, y, c))
    halves = Exchange(xsend, xrecv, local)
    reduce = Reduce(
        sums,
        {
            "up": (g_up, ru1, ru2, ru3, ru4, rsend.at[0], rrecv.at[0], 0, False),
            "down": (g_down, rd1, rd2, rd3, rd4, rsend.at[1], rrecv.at[1], n2, True),
            "self": (g_self, rs1, rs2, rs3, rs4, rsend.at[2], rrecv.at[2], 2 * n2, True),
            "enc": (
                g_enc.at[:, :, :, :, :, pl.ds(0, 3 * n1)], re1, re2, re3, re4, rsend.at[3], rrecv.at[3],
                2 * n2 + 4 * n1, True,
            ),
            "out": (
                g_enc.at[:, :, :, :, :, pl.ds(3 * n1, n1)], ro1, ro2, ro3, ro4, rsend.at[4], rrecv.at[4],
                2 * n2 + 7 * n1, True,
            ),
        },
    )
    ng[...] = ng2[...]
    wait_all(ups)
    reduce.move(("up", 0))
    wait_all(first)
    ready("self out")
    dq, dk, dv = (big.at[1, :, pl.ds(i * width, width)] for i in range(3))
    ds = SplitColumns(big.at[0], seq)

    def before_core3():
        wait_all(second)
        a_t[...] = a[...].T
        ready("self")
        reduce.move(("up", 1), ("down", 0))

    def between3():
        reduce.move(("down", 1))

    def after_core3():
        late.extend(fetch((o0_hbm, o), (r0_hbm, r), (q0_hbm, q), (k0_hbm, k), (v0_hbm, v), (ol0_hbm, ol), (a0_hbm, a)))
        first_scores(e0_hbm, ebuf, esem)
        reduce.move(("up", 2), ("down", 2))

    def after_grads3():
        reduce.move(("self", 0))

    def last3(sl, gradient):
        gy[sl, :] = gradient.astype(BF)

    attn_backward(
        gs, x, gains[3:4, :], ng, 3, a_t, a_t, g_t, wq, wk, wv, wo, q, k, v, o, ol, r, e3_hbm,
        ebuf, esem, ds, do, dq, dk, dv, g_self, n1,
        before_core3, between3, after_core3, after_grads3, None, last3,
    )
    load("enc", 0, (wq, wk, wv), n1, 10)
    gy_back = halves.back(0, gy, target_o)
    reduce.move(("self", 1), ("up", 3))
    wait_all(late)
    ready("enc out")
    a_t[...] = a[...].T

    def before_core0():
        reduce.move(("out", 0), ("down", 3))

    def between0():
        reduce.move(("self", 2), ("out", 1))

    def after_core0():
        reduce.move(("out", 2), ("up", 4))
        arrived(gy_back)
        total = jnp.zeros((1, width), F32)
        for i in range(2):
            chosen = column(masked[i : i + 1, :].astype(F32)) == 1.0
            rows = target_o[i].astype(F32)
            total = total + jnp.sum(jnp.where(chosen, rows, 0.0), axis=0, keepdims=True)
            target_o[i] = jnp.where(chosen, 0.0, rows).astype(BF)
        ng[12:13, :] = total

    def after_grads0():
        ready("enc")
        gy_back[0].wait_send()
        reduce.move(("enc", 0), ("self", 3), ("out", 3), ("enc", 1))

    def last0(sl, gradient):
        gy[sl, :] = gradient.astype(BF)

    attn_backward(
        gs1, x0, gains[0:1, :], ng, 0, a_t, a_t, g_t, wq, wk, wv, vo, q, k, v, o, ol, r, e0_hbm,
        ebuf, esem, ds, do, dq, dk, dv, g_enc, n1,
        before_core0, between0, after_core0, after_grads0, None, last0,
    )
    sg_back = halves.back(1, gy, sg_o)
    waiting = []

    def vector(s):
        for copy in waiting:
            copy.wait_recv()
        waiting.clear()
        if s == 0:
            v1[0] = ng[...]
        elif s < 4:
            v1[s] = v1[s - 1] + vr[s - 1]
        if s < 3:
            targets = ((s, (at(t, z, y, 1 - c), at(t, z, 1 - y, c), at(1 - t, z, y, c))[s]),)
        elif s == 3:
            targets = tuple((2 + j, at(t, lax.rem(z + j, 4), y, c)) for j in range(1, 4))
        else:
            targets = ()
            vec[...] = (v1[3] + vr[3]) + (vr[4] + vr[5])
        for slot, device in targets:
            copy = pltpu.make_async_remote_copy(
                src_ref=v1.at[s], dst_ref=vr.at[slot], send_sem=vsend.at[slot], recv_sem=vrecv.at[slot],
                device_id=device, device_id_type=MESH,
            )
            copy.start()
            reduce.sends.append(("vector", copy))
            waiting.append(copy)

    vector(0)
    reduce.move(("down", 4), ("self", 4), ("out", 4))
    vector(1)
    reduce.move(("enc", 2))
    vector(2)
    vector(3)
    reduce.move(("enc", 3))
    vector(4)
    reduce.move(("enc", 4))
    arrived(sg_back)
    sg_back[0].wait_send()
    reduce.finish()


def unpack(sums2, sums3, vec, *refs):
    grads, (gains_o, shifts_o, mask_o) = refs[:16], refs[16:]
    for summed, held in ((sums2, (14, 15, 10, 11, 12, 13)), (sums3, (4, 5, 6, 7, 8, 9, 0, 1, 2, 3))):
        offset = 0
        for i in held:
            n = grads[i].shape[1]
            grads[i][...] = summed[:, pl.ds(offset, n)]
            offset += n
    gains_o[...] = vec[0:6, :]
    shifts_o[...] = vec[6:12, :]
    mask_o[...] = vec[12:13, :]


def compute_all(lengths, timesteps, gains, shifts, mask_vector, masked, loss_mask, matrices, source, target, cotangent):
    rows, width = source.shape[1:]
    seq = 2 * rows
    n1 = width // 2
    part = matrices[0].shape[0]
    n2 = matrices[4].shape[1]
    total = 12 * n1 + 4 * n2
    hidden = 2 * n2
    heads = width // HD
    sd = jax.ShapeDtypeStruct
    any_spec = pl.BlockSpec(memory_space=pl.ANY)
    vmem = pl.BlockSpec(memory_space=pltpu.VMEM)
    smem = pl.BlockSpec(memory_space=pltpu.SMEM)
    dma = pltpu.SemaphoreType.DMA
    row = lambda kind: sd((seq, width), kind)
    tall = lambda kind: sd((seq, hidden), kind)
    halves = sd((2, rows, width), BF)
    escores = sd((heads, seq, seq), BF)
    vrow = lambda kind: pltpu.VMEM((seq, width), kind)
    vhalves = pltpu.VMEM((2, rows, width), BF)
    vsq = pltpu.VMEM((width, width), BF)
    vwide = pltpu.VMEM((width, hidden), BF)
    vtall = pltpu.VMEM((seq, hidden), BF)
    vsq5 = pltpu.VMEM((4, 2, 2, part, width), BF)
    vwide5 = pltpu.VMEM((4, 2, 2, part, hidden), BF)
    turned = pltpu.VMEM((width, seq), BF)
    big = pltpu.VMEM((2, seq, hidden), BF)
    ebuf = pltpu.VMEM((4, seq, seq), BF)
    grads = lambda n: pltpu.VMEM((2, 4, 2, 2, part, n), BF)

    def landing(n, split=False):
        r3 = (2, 4, 2, part, n // 2) if split else (4, part, n)
        return [
            pltpu.VMEM(dims, BF) for dims in ((2, 4, 2, part, n), (2, 4, part, n), r3, (3, part, n))
        ]

    def params(number):
        return pltpu.CompilerParams(
            vmem_limit_bytes=VMEM_LIMIT, collective_id=number, has_side_effects=True
        )

    attention = [row(BF)] * 7 + [escores]
    (
        gathered, x, y0, g3,
        a0, q0, k0, v0, o0, ol0, r0, e0, x1, a1, h1, gp1, x2, mem,
        a3, q3, k3, v3, o3, ol3, r3, e3, y1,
        a4, q4, k4, v4, o4, ol4, r4, e4, y2,
    ) = pl.pallas_call(
        forward,
        in_specs=[smem, smem] + [vmem] * 21 + [any_spec] * 3,
        out_specs=[any_spec] * 36,
        out_shape=[sd((2, 4, 2, 2, part, total), BF)] + [row(BF)] * 3
        + attention + [row(F32), row(BF), tall(BF), tall(BF), row(BF), row(BF)]
        + attention + [row(F32)]
        + attention + [row(F32)],
        scratch_shapes=[pltpu.VMEM((part, total), BF), vhalves, vhalves]
        + [vrow(BF)] * 2 + [vsq5] * 8 + [vwide5] * 2 + [vrow(BF)] * 14
        + [vrow(F32), vrow(BF), vtall, vtall, vrow(BF), vrow(BF), vrow(F32), vrow(F32), ebuf]
        + [dma((7, 8)), dma((7, 8)), dma((3,)), dma((3,)), dma((6,)), dma((20,)), dma((4,)), dma((35,))],
        compiler_params=params(0),
        name="forward",
    )(lengths, timesteps, gains, shifts, mask_vector[None], masked, loss_mask, *matrices, source, target, cotangent)
    weights = gathered.reshape(2, width, total)
    decoded, g4, g1, up, down, sums2, ng = pl.pallas_call(
        dec_backward,
        in_specs=[vmem, vmem] + [any_spec] * 18,
        out_specs=[any_spec] * 5 + [vmem] * 2,
        out_shape=[halves, row(F32), row(F32)] + [sd((2, 4, 2, 2, part, n2), BF)] * 2
        + [sd((part, 2 * n2 + 4 * n1), F32), sd((16, width), F32)],
        scratch_shapes=[vrow(F32), vrow(BF), vrow(F32)] + [vrow(BF)] * 7
        + [vsq] * 4 + [vwide] * 2 + [big, vrow(F32), vrow(BF)] + [turned] * 2
        + [grads(n2), grads(n2), grads(4 * n1), ebuf]
        + landing(n2, True) + landing(n2, True) + landing(4 * n1, True)
        + [dma((3, 8)), dma((3, 8)), dma((1,)), dma((1,)), dma((1,)), dma((18,)), dma((16,)), dma((4,)), dma((4,))],
        compiler_params=params(1),
        name="dec_backward",
    )(gains, shifts, y2, g3, y1, mem, a4, q4, k4, v4, o4, ol4, r4, e4, x2, x1, a1, h1, gp1, weights)
    source_grad, target_grad, sums3, vec = pl.pallas_call(
        last_backward,
        in_specs=[vmem] * 3 + [any_spec] * 23,
        out_specs=[any_spec, vmem, vmem, vmem],
        out_shape=[halves, halves, sd((part, 2 * n2 + 8 * n1), F32), sd((16, width), F32)],
        scratch_shapes=[vrow(F32)] * 2 + [vrow(BF)] * 9 + [vsq] * 5 + [big, vrow(BF)] + [turned] * 2
        + [vrow(BF), pltpu.VMEM((16, width), F32)]
        + [grads(n2), grads(n2), grads(4 * n1), grads(4 * n1), ebuf]
        + landing(n2) + landing(n2, True) + landing(4 * n1, True) + landing(3 * n1, True) + landing(n1, True)
        + [pltpu.VMEM((4, 16, width), F32), pltpu.VMEM((6, 16, width), F32)]
        + [dma((5, 8)), dma((5, 8)), dma((2,)), dma((2,)), dma((2,)), dma((6,)), dma((6,)), dma((20,)), dma((16,)), dma((4,))],
        compiler_params=params(2),
        name="last_backward",
    )(
        gains, ng, masked, g4, g1, y0, a3, q3, k3, v3, o3, ol3, r3, e3,
        x, a0, q0, k0, v0, o0, ol0, r0, e0, up, down, weights,
    )
    square, tall_square = sd((part, n1), F32), sd((part, n2), F32)
    small = pl.pallas_call(
        unpack,
        in_specs=[vmem] * 3,
        out_specs=[vmem] * 19,
        out_shape=[tall_square if i in (4, 5, 14, 15) else square for i in range(16)]
        + [sd((6, width), F32)] * 2 + [sd((1, width), F32)],
        name="unpack",
    )(sums2, sums3, vec)
    return (decoded, source_grad, target_grad, *small)


def pair_body(*arguments):
    source, target, cotangent, lengths, timesteps, masked, loss_mask = arguments[:7]
    matrices = [m.T if i in TURNED else m for i, m in enumerate(arguments[7:23])]
    norm_gains, norm_shifts, mask_vector = arguments[23:]
    outs = compute_all(
        lengths, timesteps, norm_gains, norm_shifts, mask_vector, masked, loss_mask, matrices, source, target, cotangent
    )
    grads = [g.T if i in TURNED else g for i, g in enumerate(outs[3:19])]
    return (*outs[:3], *grads, outs[19], outs[20], outs[21][0])


def solution(mesh):
    whole_pairs = dict(mesh.shape) == {"dp": 16, "tensor": 2}
    return jax.shard_map(
        pair_body if whole_pairs else body,
        mesh=mesh,
        in_specs=(
            P("dp", "tensor", None),
            P("dp", "tensor", None),
            P("dp", "tensor", None),
            P("dp"),
            P("dp"),
            P("dp", "tensor"),
            P("dp", "tensor"),
            P("dp", "tensor"),
            P("dp", "tensor"),
            P("dp", "tensor"),
            P("tensor", "dp"),
            P("dp", "tensor"),
            P("tensor", "dp"),
            P("dp", "tensor"),
            P("dp", "tensor"),
            P("dp", "tensor"),
            P("tensor", "dp"),
            P("dp", "tensor"),
            P("dp", "tensor"),
            P("dp", "tensor"),
            P("tensor", "dp"),
            P("dp", "tensor"),
            P("tensor", "dp"),
            P(),
            P(),
            P(),
        ),
        out_specs=(
            P("dp", "tensor", None),
            P("dp", "tensor", None),
            P("dp", "tensor", None),
            P("dp", "tensor"),
            P("dp", "tensor"),
            P("dp", "tensor"),
            P("tensor", "dp"),
            P("dp", "tensor"),
            P("tensor", "dp"),
            P("dp", "tensor"),
            P("dp", "tensor"),
            P("dp", "tensor"),
            P("tensor", "dp"),
            P("dp", "tensor"),
            P("dp", "tensor"),
            P("dp", "tensor"),
            P("tensor", "dp"),
            P("dp", "tensor"),
            P("tensor", "dp"),
            P(),
            P(),
            P(),
        ),
        check_vma=False,
    )
```

```python
import jax
import jax.numpy as jnp
from jax import lax
from jax.experimental import pallas as pl
from jax.experimental.pallas import tpu as pltpu
from jax.sharding import PartitionSpec as P

HD = 64
MICRO = 2
STEPS = 50


eps = 1e-05
floor_score = -1e30


def norm_rows(inputs, gain, shift):
    average = jnp.mean(inputs, axis=-1, keepdims=True)
    centred = inputs - average
    second = jnp.mean(centred * centred, axis=-1, keepdims=True)
    return centred * lax.rsqrt(second + eps) * gain + shift


def norm_back(inputs, gain, shift, gradient):
    unused, pullback = jax.vjp(norm_rows, inputs, gain, shift)
    return pullback(gradient)


def smooth(values):
    return jax.nn.gelu(values, approximate=False)


def spread(inputs):
    return lax.all_gather(inputs.astype(jnp.bfloat16), "tensor", axis=1, tiled=True)


def collect(partial_value):
    return lax.psum_scatter(partial_value, "tensor", scatter_dimension=1, tiled=True)


def spread_grad(gradient):
    return lax.all_gather(gradient.astype(jnp.bfloat16), "tensor", axis=1, tiled=True)


def collect_grad(partial_value):
    return lax.psum_scatter(partial_value, "tensor", scatter_dimension=1, tiled=True)


def project(inputs, weight):
    return jnp.einsum("bsk,kn->bsn", inputs, weight, preferred_element_type=jnp.float32)


def weight_grad(inputs, gradient):
    return jnp.einsum("bsk,bsn->kn", inputs, gradient, preferred_element_type=jnp.float32)


def back_project(gradient, weight):
    return jnp.einsum("bsn,kn->bsk", gradient, weight, preferred_element_type=jnp.float32)


def masked_scores(query_part, key_rows, live):
    scores = jnp.einsum(
        "bqhd,bkhd->bhqk", query_part, key_rows, preferred_element_type=jnp.float32
    ) * HD ** (-0.5)
    return jnp.where(live[:, None, None, :], scores, floor_score)


def attend_forward(query_in, keys_in, w_query, w_key, w_value, live):
    pair_count, length = (query_in.shape[0], query_in.shape[1])
    head_count = w_query.shape[1] // HD
    queries = (
        project(query_in, w_query).astype(jnp.bfloat16).reshape(pair_count, length, head_count, HD)
    )
    key_rows = (
        project(keys_in, w_key).astype(jnp.bfloat16).reshape(pair_count, length, head_count, HD)
    )
    value_rows = (
        project(keys_in, w_value).astype(jnp.bfloat16).reshape(pair_count, length, head_count, HD)
    )
    block_rows = min(512, length)
    pieces = []
    totals = []
    for offset in range(0, length, block_rows):
        scores = masked_scores(queries[:, offset : offset + block_rows], key_rows, live)
        highest = jnp.max(scores, axis=-1, keepdims=True)
        exponent = jnp.exp(scores - highest)
        summed = jnp.sum(exponent, axis=-1, keepdims=True)
        softmax = (exponent / summed).astype(jnp.bfloat16)
        pieces.append(
            jnp.einsum("bhqk,bkhd->bqhd", softmax, value_rows, preferred_element_type=jnp.float32)
        )
        totals.append(highest + jnp.log(summed))
    attended = (
        jnp.concatenate(pieces, axis=1)
        .astype(jnp.bfloat16)
        .reshape(pair_count, length, head_count * HD)
    )
    return (queries, key_rows, value_rows, attended, jnp.concatenate(totals, axis=2))


def attend_backward(whole_grad, query_in, keys_in, w_query, w_key, w_value, w_out, saved, live):
    queries, key_rows, value_rows, attended, totals = saved
    pair_count, length, head_count = (queries.shape[0], queries.shape[1], queries.shape[2])
    scale_score = HD ** (-0.5)
    out_grad = weight_grad(attended, whole_grad)
    head_grad = (
        back_project(whole_grad, w_out)
        .astype(jnp.bfloat16)
        .reshape(pair_count, length, head_count, HD)
    )
    block_rows = min(512, length)
    key_total = jnp.zeros(key_rows.shape, jnp.float32)
    value_total = jnp.zeros(value_rows.shape, jnp.float32)
    query_parts = []
    for offset in range(0, length, block_rows):
        query_part = queries[:, offset : offset + block_rows]
        grad_part = head_grad[:, offset : offset + block_rows]
        scores = masked_scores(query_part, key_rows, live)
        softmax = jnp.exp(scores - totals[:, :, offset : offset + block_rows])
        value_total = value_total + jnp.einsum(
            "bhqk,bqhd->bkhd",
            softmax.astype(jnp.bfloat16),
            grad_part,
            preferred_element_type=jnp.float32,
        )
        soft_grad = jnp.einsum(
            "bqhd,bkhd->bhqk", grad_part, value_rows, preferred_element_type=jnp.float32
        )
        inner = jnp.sum(softmax * soft_grad, axis=-1, keepdims=True)
        score_grad = (softmax * (soft_grad - inner)).astype(jnp.bfloat16)
        query_parts.append(
            jnp.einsum("bhqk,bkhd->bqhd", score_grad, key_rows, preferred_element_type=jnp.float32)
            * scale_score
        )
        key_total = (
            key_total
            + jnp.einsum(
                "bhqk,bqhd->bkhd", score_grad, query_part, preferred_element_type=jnp.float32
            )
            * scale_score
        )
    query_grad = (
        jnp.concatenate(query_parts, axis=1)
        .astype(jnp.bfloat16)
        .reshape(pair_count, length, head_count * HD)
    )
    key_grad = key_total.astype(jnp.bfloat16).reshape(
        pair_count, key_rows.shape[1], head_count * HD
    )
    value_grad = value_total.astype(jnp.bfloat16).reshape(
        pair_count, value_rows.shape[1], head_count * HD
    )
    grads = (
        weight_grad(query_in, query_grad),
        weight_grad(keys_in, key_grad),
        weight_grad(keys_in, value_grad),
        out_grad,
    )
    into_keys = back_project(key_grad, w_key) + back_project(value_grad, w_value)
    return (grads, back_project(query_grad, w_query), into_keys)


def feed_forward(inputs, w_up, w_down):
    lifted = project(inputs, w_up)
    active = smooth(lifted).astype(jnp.bfloat16)
    return (lifted, active, project(active, w_down))


def feed_backward(gradient, inputs, w_up, w_down, lifted, active):
    down_grad = weight_grad(active, gradient)
    active_grad = back_project(gradient, w_down)
    unused, smooth_back = jax.vjp(smooth, lifted)
    lifted_grad = smooth_back(active_grad)[0].astype(jnp.bfloat16)
    return ((weight_grad(inputs, lifted_grad), down_grad), back_project(lifted_grad, w_up))


def body(
    source,
    target,
    cotangent,
    lengths,
    timesteps,
    masked,
    loss_mask,
    enc_query,
    enc_key,
    enc_value,
    enc_out,
    enc_up,
    enc_down,
    self_query,
    self_key,
    self_value,
    self_out,
    cross_query,
    cross_key,
    cross_value,
    cross_out,
    dec_up,
    dec_down,
    norm_gains,
    norm_shifts,
    mask_vector,
):
    pairs_dev, rows_dev = (source.shape[0], source.shape[1])
    per_micro = pairs_dev // MICRO
    seq_len = rows_dev * lax.axis_size("tensor")
    positions = jnp.arange(seq_len)
    gains, shifts = (norm_gains, norm_shifts)
    gain_total = jnp.zeros(norm_gains.shape, jnp.float32)
    shift_total = jnp.zeros(norm_shifts.shape, jnp.float32)
    mask_total = jnp.zeros(mask_vector.shape, jnp.float32)
    decoded_parts = []
    source_parts = []
    target_parts = []
    running = None
    for micro in range(MICRO):
        weights = (
            lax.all_gather(enc_query, "dp", axis=0, tiled=True),
            lax.all_gather(enc_key, "dp", axis=0, tiled=True),
            lax.all_gather(enc_value, "dp", axis=0, tiled=True),
            lax.all_gather(enc_out, "dp", axis=1, tiled=True),
            lax.all_gather(enc_up, "dp", axis=0, tiled=True),
            lax.all_gather(enc_down, "dp", axis=1, tiled=True),
            lax.all_gather(self_query, "dp", axis=0, tiled=True),
            lax.all_gather(self_key, "dp", axis=0, tiled=True),
            lax.all_gather(self_value, "dp", axis=0, tiled=True),
            lax.all_gather(self_out, "dp", axis=1, tiled=True),
            lax.all_gather(cross_query, "dp", axis=0, tiled=True),
            lax.all_gather(cross_key, "dp", axis=0, tiled=True),
            lax.all_gather(cross_value, "dp", axis=0, tiled=True),
            lax.all_gather(cross_out, "dp", axis=1, tiled=True),
            lax.all_gather(dec_up, "dp", axis=0, tiled=True),
            lax.all_gather(dec_down, "dp", axis=1, tiled=True),
        )
        wide = (
            lax.all_gather(weights[4], "tensor", axis=1, tiled=True),
            lax.all_gather(weights[5], "tensor", axis=0, tiled=True),
            lax.all_gather(weights[14], "tensor", axis=1, tiled=True),
            lax.all_gather(weights[15], "tensor", axis=0, tiled=True),
        )
        lower = micro * per_micro
        upper = lower + per_micro
        live = positions[None, :] < lengths[lower:upper][:, None]
        every = jnp.ones((per_micro, seq_len), bool)
        inputs_x = source[lower:upper].astype(jnp.float32)
        rows0 = spread(norm_rows(inputs_x, gains[0], shifts[0]))
        saved0 = attend_forward(rows0, rows0, weights[0], weights[1], weights[2], live)
        stream1 = inputs_x + collect(project(saved0[3], weights[3]))
        normed1 = norm_rows(stream1, gains[1], shifts[1])
        rows1 = normed1.astype(jnp.bfloat16)
        lifted1, active1, partial1 = feed_forward(rows1, wide[0], wide[1])
        stream2 = stream1 + partial1
        memory_rows = spread(norm_rows(stream2, gains[2], shifts[2]))
        chosen = masked[lower:upper][:, :, None] == 1
        start_y = jnp.where(chosen, mask_vector, target[lower:upper].astype(jnp.float32))
        rows3 = spread(norm_rows(start_y, gains[3], shifts[3]))
        saved3 = attend_forward(rows3, rows3, weights[6], weights[7], weights[8], every)
        stream4 = start_y + collect(project(saved3[3], weights[9]))
        rows4 = spread(norm_rows(stream4, gains[4], shifts[4]))
        saved4 = attend_forward(rows4, memory_rows, weights[10], weights[11], weights[12], live)
        stream5 = stream4 + collect(project(saved4[3], weights[13]))
        normed5 = norm_rows(stream5, gains[5], shifts[5])
        rows5 = normed5.astype(jnp.bfloat16)
        lifted5, active5, partial5 = feed_forward(rows5, wide[2], wide[3])
        stream6 = stream5 + partial5
        decoded_parts.append(stream6.astype(jnp.bfloat16))
        factor = (STEPS + 1 - timesteps[lower:upper]).astype(jnp.float32) / STEPS
        grad6 = (
            cotangent[lower:upper].astype(jnp.float32)
            * (factor[:, None] * loss_mask[lower:upper].astype(jnp.float32))[:, :, None]
        )
        (up5, down5), into5 = feed_backward(
            grad6.astype(jnp.bfloat16), rows5, wide[2], wide[3], lifted5, active5
        )
        back5 = norm_back(stream5, gains[5], shifts[5], into5)
        grad5 = grad6 + back5[0]
        grads4, query_term4, memory_term = attend_backward(
            spread_grad(grad5),
            rows4,
            memory_rows,
            weights[10],
            weights[11],
            weights[12],
            weights[13],
            saved4,
            live,
        )
        back4 = norm_back(stream4, gains[4], shifts[4], collect_grad(query_term4))
        grad4 = grad5 + back4[0]
        memory_grad = collect_grad(memory_term)
        grads3, query_term3, keys_term3 = attend_backward(
            spread_grad(grad4),
            rows3,
            rows3,
            weights[6],
            weights[7],
            weights[8],
            weights[9],
            saved3,
            every,
        )
        back3 = norm_back(start_y, gains[3], shifts[3], collect_grad(query_term3 + keys_term3))
        grad_y = grad4 + back3[0]
        target_parts.append(jnp.where(chosen, 0.0, grad_y).astype(jnp.bfloat16))
        mask_total = mask_total + jnp.sum(jnp.where(chosen, grad_y, 0.0), axis=(0, 1))
        back2 = norm_back(stream2, gains[2], shifts[2], memory_grad)
        grad2 = back2[0]
        (up1, down1), into1 = feed_backward(
            grad2.astype(jnp.bfloat16), rows1, wide[0], wide[1], lifted1, active1
        )
        back1 = norm_back(stream1, gains[1], shifts[1], into1)
        grad1 = grad2 + back1[0]
        grads0, query_term0, keys_term0 = attend_backward(
            spread_grad(grad1),
            rows0,
            rows0,
            weights[0],
            weights[1],
            weights[2],
            weights[3],
            saved0,
            live,
        )
        back0 = norm_back(inputs_x, gains[0], shifts[0], collect_grad(query_term0 + keys_term0))
        source_parts.append((grad1 + back0[0]).astype(jnp.bfloat16))
        gain_total = gain_total + jnp.stack(
            [back0[1], back1[1], back2[1], back3[1], back4[1], back5[1]]
        )
        shift_total = shift_total + jnp.stack(
            [back0[2], back1[2], back2[2], back3[2], back4[2], back5[2]]
        )
        up1, down1, up5, down5 = (
            lax.psum_scatter(
                up1.astype(jnp.bfloat16), "tensor", scatter_dimension=1, tiled=True
            ).astype(jnp.float32),
            lax.psum_scatter(
                down1.astype(jnp.bfloat16), "tensor", scatter_dimension=0, tiled=True
            ).astype(jnp.float32),
            lax.psum_scatter(
                up5.astype(jnp.bfloat16), "tensor", scatter_dimension=1, tiled=True
            ).astype(jnp.float32),
            lax.psum_scatter(
                down5.astype(jnp.bfloat16), "tensor", scatter_dimension=0, tiled=True
            ).astype(jnp.float32),
        )
        fresh = (
            grads0[0],
            grads0[1],
            grads0[2],
            grads0[3],
            up1,
            down1,
            grads3[0],
            grads3[1],
            grads3[2],
            grads3[3],
            grads4[0],
            grads4[1],
            grads4[2],
            grads4[3],
            up5,
            down5,
        )
        running = fresh if micro == 0 else jax.tree.map(jnp.add, running, tuple(fresh))
    running = (
        lax.psum_scatter(
            running[0].astype(jnp.bfloat16), "dp", scatter_dimension=0, tiled=True
        ).astype(jnp.float32),
        lax.psum_scatter(
            running[1].astype(jnp.bfloat16), "dp", scatter_dimension=0, tiled=True
        ).astype(jnp.float32),
        lax.psum_scatter(
            running[2].astype(jnp.bfloat16), "dp", scatter_dimension=0, tiled=True
        ).astype(jnp.float32),
        lax.psum_scatter(
            running[3].astype(jnp.bfloat16), "dp", scatter_dimension=1, tiled=True
        ).astype(jnp.float32),
        lax.psum_scatter(
            running[4].astype(jnp.bfloat16), "dp", scatter_dimension=0, tiled=True
        ).astype(jnp.float32),
        lax.psum_scatter(
            running[5].astype(jnp.bfloat16), "dp", scatter_dimension=1, tiled=True
        ).astype(jnp.float32),
        lax.psum_scatter(
            running[6].astype(jnp.bfloat16), "dp", scatter_dimension=0, tiled=True
        ).astype(jnp.float32),
        lax.psum_scatter(
            running[7].astype(jnp.bfloat16), "dp", scatter_dimension=0, tiled=True
        ).astype(jnp.float32),
        lax.psum_scatter(
            running[8].astype(jnp.bfloat16), "dp", scatter_dimension=0, tiled=True
        ).astype(jnp.float32),
        lax.psum_scatter(
            running[9].astype(jnp.bfloat16), "dp", scatter_dimension=1, tiled=True
        ).astype(jnp.float32),
        lax.psum_scatter(
            running[10].astype(jnp.bfloat16), "dp", scatter_dimension=0, tiled=True
        ).astype(jnp.float32),
        lax.psum_scatter(
            running[11].astype(jnp.bfloat16), "dp", scatter_dimension=0, tiled=True
        ).astype(jnp.float32),
        lax.psum_scatter(
            running[12].astype(jnp.bfloat16), "dp", scatter_dimension=0, tiled=True
        ).astype(jnp.float32),
        lax.psum_scatter(
            running[13].astype(jnp.bfloat16), "dp", scatter_dimension=1, tiled=True
        ).astype(jnp.float32),
        lax.psum_scatter(
            running[14].astype(jnp.bfloat16), "dp", scatter_dimension=0, tiled=True
        ).astype(jnp.float32),
        lax.psum_scatter(
            running[15].astype(jnp.bfloat16), "dp", scatter_dimension=1, tiled=True
        ).astype(jnp.float32),
    )
    vectors = lax.psum((gain_total, shift_total, mask_total), ("dp", "tensor"))
    return (
        jnp.concatenate(decoded_parts, axis=0),
        jnp.concatenate(source_parts, axis=0),
        jnp.concatenate(target_parts, axis=0),
        running[0],
        running[1],
        running[2],
        running[3],
        running[4],
        running[5],
        running[6],
        running[7],
        running[8],
        running[9],
        running[10],
        running[11],
        running[12],
        running[13],
        running[14],
        running[15],
        vectors[0],
        vectors[1],
        vectors[2],
    )


F32 = jnp.float32
BF = jnp.bfloat16
LOG2E = 1.4426950408889634
LN2 = 0.6931471805599453
NN = (((1,), (0,)), ((), ()))
NT = (((1,), (1,)), ((), ()))
MESH = pl.DeviceIdType.MESH
RB = 512
FB = 256
VMEM_LIMIT = 63 * 2**20


def dg(left, right, dims=NN):
    return lax.dot_general(left, right, dims, preferred_element_type=F32)


def ln_hat(x):
    centred = x - jnp.mean(x, axis=-1, keepdims=True)
    rstd = lax.rsqrt(jnp.mean(centred * centred, axis=-1, keepdims=True) + eps)
    return centred * rstd, rstd


def ln_back(x, gain, gradient):
    hat, rstd = ln_hat(x)
    scaled = gradient * gain
    first = jnp.mean(scaled, axis=-1, keepdims=True)
    second = jnp.mean(scaled * hat, axis=-1, keepdims=True)
    dx = rstd * (scaled - first - hat * second)
    dgain = jnp.sum(gradient * hat, axis=0, keepdims=True)
    dshift = jnp.sum(gradient, axis=0, keepdims=True)
    return dx, dgain, dshift


def gelu_both(u):
    size = jnp.abs(u)
    t = 1.0 / (1.0 + (0.3275911 * 0.7071067811865476) * size)
    ex = jnp.exp2(u * u * (-0.5 * LOG2E))
    poly = t * (
        0.127414796
        + t * (-0.142248368 + t * (0.7107068705 + t * (-0.7265760135 + t * 0.5307027145)))
    )
    tail = poly * ex
    phi = jnp.where(u > 0, 1.0 - tail, tail)
    return u * phi, phi + u * ex * 0.3989422804014327


def rows_loop(total, step, run):
    def once(i, carry):
        run(pl.ds(pl.multiple_of(i * step, step), step))
        return carry

    lax.fori_loop(0, total // step, once, 0)


def load_weight(w_hbm, offset, width, dst, sems, base):
    copies = []
    for t in range(2):
        src = pl.ds(offset, width)
        to = pl.ds(t * width, width)
        cp = pltpu.make_async_copy(
            w_hbm.at[t, :, src] if len(w_hbm.shape) == 3 else w_hbm.at[t, :, :, :, :, src],
            dst.at[:, to] if len(dst.shape) == 2 else dst.at[:, :, :, :, to],
            sems.at[base + t],
        )
        cp.start()
        copies.append(cp)
    return copies


def wait_all(copies):
    for cp in copies:
        cp.wait()


def columns(ref, lower, width):
    value = ref[..., pl.ds(lower, width)]
    return value if value.ndim == 2 else value.reshape(-1, width)


def whole(ref):
    value = ref[...]
    return value if value.ndim == 2 else value.reshape(-1, value.shape[-1])


def normalize(x, gain, shift, a):
    def run(sl):
        hat, unused = ln_hat(x[sl, :].astype(F32))
        a[sl, :] = (hat * gain + shift).astype(BF)

    rows_loop(x.shape[0], RB, run)


def product_into(a, w, to, scale):
    def run(sl):
        value = dg(a[sl, :], whole(w))
        to[sl, :] = (value if scale is None else value * scale).astype(BF)

    rows_loop(a.shape[0], RB, run)


def attn_project(a, kv, wq, wk, wv, q, k, v):
    product_into(a, wq, q, LOG2E * HD**-0.5)
    product_into(kv, wk, k, None)
    product_into(kv, wv, v, None)


def score_copy(p, h, e_hbm, ebuf, esem):
    slot = lax.rem(p, 2) * 2 + h
    return pltpu.make_async_copy(ebuf.at[slot], e_hbm.at[2 * p + h], esem.at[slot])


def drain_scores(e_hbm, ebuf, esem):
    for p in range(2):
        for h in range(2):
            score_copy(p, h, e_hbm, ebuf, esem).wait()


def attn_core(length, q, k, v, o, ol, r, e_hbm, ebuf, esem, between, fresh):
    seq = q.shape[0]
    pairs = q.shape[1] // 128
    block = 256
    lane = lax.broadcasted_iota(jnp.int32, (1, 128), 1)
    low = lane < 64
    one = jnp.ones((), BF)
    key = lax.broadcasted_iota(jnp.int32, (seq, 1), 0)
    bias = jnp.where(key < length, 0.0, floor_score).astype(F32)
    items = [(b, h) for b in range(seq // block) for h in range(2)]

    def pair(p, carry):
        @pl.when((p > 1) if fresh else (p >= 0))
        def unused_wait():
            score_copy(p, 0, e_hbm, ebuf, esem).wait()
            score_copy(p, 1, e_hbm, ebuf, esem).wait()

        base = lax.rem(p, 2) * 2
        cols = pl.ds(pl.multiple_of(p * 128, 128), 128)
        kp = k[:, cols].astype(F32)
        vp = v[:, cols]
        ka = (
            jnp.where(low, kp, jnp.where(lane == 64, bias, 0.0)).astype(BF),
            jnp.where(low, jnp.where(lane == 0, bias, 0.0), kp).astype(BF),
        )
        va = jnp.where(low, vp, one), jnp.where(low, one, vp)

        def scores(b, h):
            qp = q[pl.ds(b * block, block), cols]
            return dg(jnp.where(low, qp, one) if h == 0 else jnp.where(low, one, qp), ka[h], NT)

        parts = []
        s = scores(*items[0])
        for n, (b, h) in enumerate(items):
            sl = pl.ds(b * block, block)
            following = scores(*items[n + 1]) if n + 1 < len(items) else None
            e = jnp.exp2(s - jnp.max(s, axis=-1, keepdims=True)).astype(BF)
            ebuf[base + h, sl, :] = e
            parts.append(dg(e, va[h]))
            s = following
            if h == 1:
                first, second = parts
                parts = []
                inverse = 1.0 / pltpu.roll(jnp.where(low, second, first), 64, 1)
                r[sl, cols] = inverse.astype(BF)
                joined = jnp.where(low, first, second) * inverse
                rounded = joined.astype(BF)
                o[sl, cols] = rounded
                ol[sl, cols] = (joined - rounded.astype(F32)).astype(BF)
        score_copy(p, 0, e_hbm, ebuf, esem).start()
        score_copy(p, 1, e_hbm, ebuf, esem).start()
        return carry

    lax.fori_loop(0, pairs // 2, pair, 0)
    between()
    lax.fori_loop(pairs // 2, pairs, pair, 0)


def attn_join(x, o, wo, y, lowered):
    def run(sl):
        joined = x[sl, :].astype(F32) + dg(o[sl, :], whole(wo), NT)
        y[sl, :] = joined
        if lowered is not None:
            lowered[sl, :] = joined.astype(BF)

    rows_loop(x.shape[0], RB, run)


def first_scores(e_hbm, ebuf, esem):
    for h in range(2):
        pltpu.make_async_copy(e_hbm.at[h], ebuf.at[h], esem.at[h]).start()


def attn_back_core(q, k, v, do, o, ol, e_hbm, ebuf, esem, ds, dq, dk, dv, between):
    seq = q.shape[0]
    heads = e_hbm.shape[0]
    block = 512
    lane = lax.broadcasted_iota(jnp.int32, (1, 128), 1)
    low = lane < 64
    zero = jnp.zeros((), BF)
    one = jnp.ones((), BF)
    row2 = lax.broadcasted_iota(jnp.int32, (256, 128), 0)
    col2 = lax.broadcasted_iota(jnp.int32, (256, 128), 1)
    swap = jnp.where(((row2 // 64) % 2) != (col2 // 64), 1.0, 0.0).astype(BF)

    def fetch(p, h):
        slot = lax.rem(p, 2) * 2 + h
        return pltpu.make_async_copy(e_hbm.at[2 * p + h], ebuf.at[slot], esem.at[slot])

    def pair(p, carry):
        cols = pl.ds(pl.multiple_of(p * 128, 128), 128)
        fetch(p, 0).wait()
        fetch(p, 1).wait()

        @pl.when(p + 1 < heads // 2)
        def unused_fetch():
            fetch(p + 1, 0).start()
            fetch(p + 1, 1).start()

        base = lax.rem(p, 2) * 2
        qp, kp, vp, dop = q[:, cols], k[:, cols], v[:, cols], do[:, cols]
        product = dop.astype(F32) * (o[:, cols].astype(F32) + ol[:, cols].astype(F32))
        high = product.astype(BF)
        rest = (product - high.astype(F32)).astype(BF)
        inner = -dg(jnp.concatenate([high, rest], axis=1), swap)
        inner_high = inner.astype(BF)
        inner_rest = (inner - inner_high.astype(F32)).astype(BF)
        do_t, q_t = dop.T, qp.T
        lhs = (
            jnp.where(low, dop, jnp.where(lane == 64, inner_high, inner_rest)),
            jnp.where(low, jnp.where(lane == 0, inner_high, inner_rest), dop),
        )
        va = (
            jnp.where(low, vp, jnp.where(lane < 66, one, zero)),
            jnp.where(low, jnp.where(lane < 2, one, zero), vp),
        )
        km = jnp.concatenate([jnp.where(low, kp, zero), jnp.where(low, zero, kp)], axis=0)
        dvs = [dg(do_t, ebuf[base + h])[64 * h : 64 * h + 64] for h in range(2)]
        for h in range(2):
            for b in range(seq // block):
                sl = pl.ds(b * block, block)
                t = dg(lhs[h][b * block : (b + 1) * block], va[h], NT)
                ds[sl, pl.ds(h * seq, seq)] = ebuf[base + h, sl, :] * t.astype(BF)
        dks = [dg(q_t, ds[:, pl.ds(h * seq, seq)])[64 * h : 64 * h + 64] for h in range(2)]
        dq_sum = dg(ds[...], km)
        dq[:, cols] = (dq_sum * HD**-0.5).astype(BF)
        dk[:, cols] = (jnp.concatenate(dks, axis=0) * LN2).astype(BF).T
        dv[:, cols] = jnp.concatenate(dvs, axis=0).astype(BF).T
        return carry

    lax.fori_loop(0, heads // 4, pair, 0)
    between()
    lax.fori_loop(heads // 4, heads // 2, pair, 0)


def places():
    d = lax.axis_index("dp")
    return lax.axis_index("tensor"), d // 4, (d // 2) % 2, d % 2


def at(t, z, y, c):
    return (z * 4 + y * 2 + c, t)


def greet(partners):
    barrier = pltpu.get_barrier_semaphore()
    for device in partners:
        pl.semaphore_signal(barrier, inc=1, device_id=device, device_id_type=MESH)
    pl.semaphore_wait(barrier, len(partners))


def all_partners(t, z, y, c):
    others = [at(t, lax.rem(z + j, 4), y, c) for j in range(1, 4)]
    return [at(t, z, y, 1 - c), at(1 - t, z, y, c), at(t, z, 1 - y, c)] + others


class Saver:
    def __init__(self, sems):
        self.sems, self.count, self.live = sems, 0, []

    def __call__(self, src, dst, slot=None):
        cp = pltpu.make_async_copy(src, dst, self.sems.at[self.count])
        cp.start()
        self.count += 1
        self.live.append((slot, cp))

    def free(self, slot):
        for name, cp in self.live:
            if name == slot:
                cp.wait()
        self.live = [entry for entry in self.live if entry[0] != slot]

    def finish(self):
        for name, cp in self.live:
            cp.wait()
        self.live = []


GATHER_PLAN = (
    ((0, 0), (1, 0), (2, 0), (4, 0), (5, 0), (6, 0)),
    ((0, 1), (1, 1), (3, 0)),
    ((0, 2),),
    ((1, 2), (2, 1), (3, 1)),
    ((7, 0),),
    ((0, 3), (0, 4), (1, 3), (1, 4), (2, 2), (4, 1)),
    (),
    ((3, 2), (5, 1)),
    ((7, 1),),
    ((2, 3), (2, 4)),
    ((4, 2),),
    (),
    ((5, 2), (6, 1), (7, 2)),
    ((3, 3), (4, 3)),
    ((3, 4), (4, 4)),
    ((5, 3),),
    ((5, 4), (6, 2)),
    (),
    (),
    ((6, 3), (7, 3)),
    (),
    ((6, 4), (7, 4)),
)
GATHER_ORDERS = (
    ("zxy",), ("zxy",), ("zxy",), ("xyz",), ("zxy", "zyx"), ("zxy", "zyx"), ("zxy", "zyx"), ("xyz",),
)


class Gather:
    def __init__(self, own, out, send, recv, widths):
        self.own, self.out, self.send, self.recv = own, out, send, recv
        self.starts = [sum(widths[:i]) for i in range(len(widths))]
        self.widths = widths
        self.spot = places()
        self.sends, self.pending = [], {}

    def push(self, src, dst, k, i, device):
        copy = pltpu.make_async_remote_copy(
            src_ref=src, dst_ref=dst, send_sem=self.send.at[k, i], recv_sem=self.recv.at[k, i],
            device_id=device, device_id_type=MESH,
        )
        copy.start()
        self.sends.append(copy)
        self.pending.setdefault(k, []).append(copy)

    def move(self, point):
        for k, s in GATHER_PLAN[point]:
            self.stage(k, s)

    def stage(self, k, s):
        t, z, y, c = self.spot
        every = slice(None)
        for copy in self.pending.pop(k, ()):
            copy.wait_recv()
        if s == 3:
            a = self.out.at[:, :, :, c, :, pl.ds(self.starts[k], self.widths[k])]
            self.push(a, a, k, 10, at(t, z, y, 1 - c))
        if s > 2:
            return
        orders = GATHER_ORDERS[k]
        width = self.widths[k] // len(orders)
        for i, order in enumerate(orders):
            cols = pl.ds(self.starts[k] + i * width, width)
            known = order[:s]
            dst = self.out.at[
                every if "x" in known else t, every if "z" in known else z, every if "y" in known else y, c, :, cols
            ]
            src = self.own.at[:, cols] if s == 0 else dst
            if order[s] == "z":
                for j in range(1, 4):
                    self.push(src, dst, k, 5 * i + j - 1, at(t, lax.rem(z + j, 4), y, c))
            elif order[s] == "x":
                self.push(src, dst, k, 5 * i + 3, at(1 - t, z, y, c))
            else:
                self.push(src, dst, k, 5 * i + 4, at(t, z, 1 - y, c))

    def finish(self):
        for copy in self.sends:
            copy.wait_send()


class Exchange:
    def __init__(self, send, recv, local):
        self.send, self.recv, self.local = send, recv, local
        self.open = []

    def start(self, i, src, kept, dst):
        t, z, y, c = places()
        far = pltpu.make_async_remote_copy(
            src_ref=src, dst_ref=dst, send_sem=self.send.at[i], recv_sem=self.recv.at[i],
            device_id=at(1 - t, z, y, c), device_id_type=MESH,
        )
        near = pltpu.make_async_copy(kept, dst, self.local.at[i])
        far.start()
        near.start()
        self.open.append(far)
        return far, near

    def give(self, i, halves, dst, part=0, parts=1):
        t = lax.axis_index("tensor")
        rows = halves.shape[1]
        take = rows // parts
        mine = dst.at[pl.ds(pl.multiple_of(t * rows + part * take, take), take), :]
        some = pl.ds(part * take, take)
        return self.start(i, halves.at[1 - t, some, :], halves.at[t, some, :], mine)

    def back(self, i, pair, dst):
        t = lax.axis_index("tensor")
        rows = dst.shape[1]
        kept = pair.at[pl.ds(pl.multiple_of(t * rows, rows), rows), :]
        sent = pair.at[pl.ds(pl.multiple_of((1 - t) * rows, rows), rows), :]
        return self.start(i, sent, kept, dst.at[t])

    def finish(self):
        for far in self.open:
            far.wait_send()


def arrived(copies):
    far, near = copies
    near.wait()
    far.wait_recv()


def column(values):
    return jnp.broadcast_to(values, (128, values.shape[1])).T[:, :1]


def weight_loader(w_hbm, sems):
    loads = {}

    def load(name, offset, refs, n, base):
        loads[name] = []
        for i, ref in enumerate(refs):
            loads[name] += load_weight(w_hbm, offset + i * n, n, ref, sems, base + 2 * i)

    def ready(name):
        wait_all(loads[name])

    return load, ready


TURNED = (3, 5, 9, 13, 15)
PACKED = (0, 1, 2, 3, 6, 7, 8, 9, 4, 5, 10, 11, 12, 13, 14, 15)


def forward(
    lengths, timesteps, gains, shifts, mask_row, masked, loss_mask, *refs,
):
    matrices, refs = refs[:16], refs[16:]
    (
        src_hbm, target_hbm, cot_hbm,
        w_hbm, x_o, y0_o, g3_o,
        a0_o, q0_o, k0_o, v0_o, o0_o, ol0_o, r0_o, e0_o, x1_o, a1_o, h1_o, gp1_o, x2_o, mem_o,
        a3_o, q3_o, k3_o, v3_o, o3_o, ol3_o, r3_o, e3_o, y1_o,
        a4_o, q4_o, k4_o, v4_o, o4_o, ol4_o, r4_o, e4_o, y2_o,
        own, tgt, cot, x, y0, wq, wk, wv, wo, sq, sk, sv, so, wu, wd,
        a, q, k, v, o, ol, r, a3, q3, k3, v3, o3, ol3, r3,
        x1, a1, h, gp, x2, mem, y1, y2, ebuf,
        gsend, grecv, xsend, xrecv, local, wsem, esem, osem,
    ) = refs
    t, z, y, c = places()
    seq, width = x.shape
    n1, n2 = width // 2, h.shape[1] // 2
    in_tgt = pltpu.make_async_copy(target_hbm, tgt, local.at[5])
    in_cot = pltpu.make_async_copy(cot_hbm, cot, local.at[6])
    in_tgt.start()
    in_cot.start()
    offset = 0
    for i in PACKED:
        part = matrices[i][...]
        own[:, pl.ds(offset, part.shape[1])] = part
        offset += part.shape[1]
    greet(all_partners(t, z, y, c))
    halves = Exchange(xsend, xrecv, local)
    gather = Gather(own, w_hbm, gsend, grecv, (2 * n1, 2 * n1, 4 * n1, n2, n2, 4 * n1, n2, n2))
    mine = pltpu.make_async_copy(own, w_hbm.at[t, z, y, c], local.at[4])
    mine.start()
    gather.move(0)
    x_in = [halves.give(0, src_hbm, x, 0, 2)]
    save = Saver(osem)
    in_tgt.wait()
    for i in range(2):
        chosen = column(masked[i : i + 1, :].astype(F32)) == 1.0
        tgt[i] = jnp.where(chosen, mask_row[...], tgt[i].astype(F32)).astype(BF)
    mine.wait()
    gather.move(1)
    in_cot.wait()
    for i in range(2):
        factor = (STEPS + 1 - timesteps[i]).astype(F32) / STEPS
        weight = column(loss_mask[i : i + 1, :].astype(F32)) * factor
        cot[i] = (cot[i].astype(F32) * weight).astype(BF)
    gather.move(2)
    x_in.append(halves.give(3, src_hbm, x, 1, 2))
    gather.move(3)
    for copies in x_in:
        arrived(copies)
    normalize(x, gains[0:1, :], shifts[0:1, :], a)
    save(x, x_o, "x")
    save(a, a0_o, "A")
    gather.move(4)
    gather.move(5)
    load, ready = weight_loader(w_hbm, wsem)
    load("enc", 0, (wq, wk), n1, 0)
    load("out", 2 * n1, (wv, wo), n1, 4)
    ready("enc")
    product_into(a, wq, q, LOG2E * HD**-0.5)
    product_into(a, wk, k, None)
    gather.move(6)
    y0_in = halves.give(1, tgt, y0)
    ready("out")
    product_into(a, wv, v, None)
    for src, dst in ((q, q0_o), (k, k0_o), (v, v0_o)):
        save(src, dst, "A")
    gather.move(7)
    length = lengths[t]

    def between0():
        gather.move(8)

    attn_core(length, q, k, v, o, ol, r, e0_o, ebuf, esem, between0, True)
    gather.move(9)
    load("self", 4 * n1, (sq, sk, sv, so), n1, 8)
    for src, dst in ((o, o0_o), (ol, ol0_o), (r, r0_o)):
        save(src, dst, "A")
    arrived(y0_in)
    save(y0, y0_o, "y0")
    normalize(y0, gains[3:4, :], shifts[3:4, :], a3)
    gather.move(10)
    save.free("x")
    attn_join(x, o, wo, x1, x)
    save(x, x1_o)
    ready("self")
    attn_project(a3, a3, sq, sk, sv, q3, k3, v3)
    for src, dst in ((a3, a3_o), (q3, q3_o), (k3, k3_o), (v3, v3_o)):
        save(src, dst)
    gather.move(11)
    gather.move(12)
    g3_in = halves.give(2, cot, g3_o)

    def between3():
        gather.move(13)

    attn_core(seq, q3, k3, v3, o3, ol3, r3, e3_o, ebuf, esem, between3, False)
    gather.move(14)
    load("feed", 8 * n1, (wu, wd), n2, 16)
    for src, dst in ((o3, o3_o), (ol3, ol3_o), (r3, r3_o)):
        save(src, dst)
    save.free("y0")
    attn_join(y0, o3, so, y1, y0)
    save(y0, y1_o)
    save.free("A")
    normalize(y1, gains[4:5, :], shifts[4:5, :], a)
    gather.move(15)
    ready("feed")

    def feed(sl):
        stream = x1[sl, :]
        hat, unused = ln_hat(stream)
        rows = (hat * gains[1:2, :] + shifts[1:2, :]).astype(BF)
        a1[sl, :] = rows
        out = stream
        lifted = dg(rows, columns(wu, 0, FB))
        for lower in range(0, 2 * n2, FB):
            cols = pl.ds(lower, FB)
            following = dg(rows, columns(wu, lower + FB, FB)) if lower + FB < 2 * n2 else None
            active, slope = gelu_both(lifted)
            active = active.astype(BF)
            h[sl, cols] = active
            gp[sl, cols] = slope.astype(BF)
            out = out + dg(active, columns(wd, lower, FB), NT)
            lifted = following
        x2[sl, :] = out.astype(BF)
        hat, unused = ln_hat(out)
        mem[sl, :] = (hat * gains[2:3, :] + shifts[2:3, :]).astype(BF)

    rows_loop(seq // 2, RB, feed)
    gather.move(16)
    load("cross", 8 * n1 + 2 * n2, (wq, wk, wv, wo), n1, 0)
    rows_loop(seq // 2, RB, lambda sl: feed(pl.ds(pl.multiple_of(seq // 2 + sl.start, RB), RB)))
    for src, dst in ((a1, a1_o), (h, h1_o), (gp, gp1_o), (x2, x2_o), (mem, mem_o)):
        save(src, dst)
    gather.move(17)
    ready("cross")
    attn_project(a, mem, wq, wk, wv, q, k, v)
    for src, dst in ((a, a4_o), (q, q4_o), (k, k4_o), (v, v4_o)):
        save(src, dst)
    gather.move(18)

    def between4():
        gather.move(19)

    attn_core(length, q, k, v, o, ol, r, e4_o, ebuf, esem, between4, False)
    for src, dst in ((o, o4_o), (ol, ol4_o), (r, r4_o)):
        save(src, dst)
    gather.move(20)
    attn_join(y1, o, wo, y2, None)
    save(y2, y2_o)
    gather.move(21)
    drain_scores(e4_o, ebuf, esem)
    arrived(g3_in)
    halves.finish()
    gather.finish()
    save.finish()


class Reduce:
    def __init__(self, out, chunks):
        self.out, self.chunks = out, chunks
        self.spot = places()
        self.sends, self.pending = [], {}

    def push(self, name, i, src, dst, device):
        send, recv = self.chunks[name][5:7]
        copy = pltpu.make_async_remote_copy(
            src_ref=src, dst_ref=dst, send_sem=send.at[i], recv_sem=recv.at[i],
            device_id=device, device_id_type=MESH,
        )
        copy.start()
        self.sends.append((name, copy))
        self.pending.setdefault(name, []).append(copy)

    def move(self, *steps):
        for name, s in steps:
            self.stage(name, s)

    def stage(self, name, s):
        t, z, y, c = self.spot
        g, r1, r2, r3, r4, send, recv, start, split = self.chunks[name]
        width = g.shape[-1]
        half = width // 2 if split else width
        left = pl.ds(0, half)
        right = pl.ds(half, half)
        by_x, by_y = at(1 - t, z, y, c), at(t, z, 1 - y, c)

        def add(mine, theirs):
            mine[...] = (mine[...].astype(F32) + theirs[...].astype(F32)).astype(BF)

        for copy in self.pending.pop(name, ()):
            copy.wait_recv()
        if s == 0:
            self.push(name, 0, g.at[:, :, :, 1 - c], r1, at(t, z, y, 1 - c))
        elif s == 1:
            add(g.at[:, :, 1 - y, c], r1.at[:, :, 1 - y])
            self.push(name, 1, g.at[:, :, 1 - y, c, :, left], r2.at[:, :, :, left], by_y)
            add(g.at[:, :, y, c], r1.at[:, :, y])
            if split:
                self.push(name, 2, g.at[1 - t, :, :, c, :, right], r3.at[0], by_x)
        elif s == 2:
            rows = g.at[:, :, y, c, :, left]
            add(rows, r2.at[:, :, :, left])
            if not split:
                self.push(name, 2, g.at[1 - t, :, y, c], r3, by_x)
            else:
                self.push(name, 3, g.at[1 - t, :, y, c, :, left], r3.at[1, :, 0], by_x)
                add(g.at[t, :, :, c, :, right], r3.at[0])
                self.push(name, 4, g.at[t, :, 1 - y, c, :, right], r3.at[1, :, 1], by_y)
        elif s == 3:
            if not split:
                add(g.at[t, :, y, c], r3)
            else:
                add(g.at[t, :, y, c, :, left], r3.at[1, :, 0])
                add(g.at[t, :, y, c, :, right], r3.at[1, :, 1])
            for j in range(1, 4):
                zz = lax.rem(z + j, 4)
                self.push(name, 4 + j, g.at[t, zz, y, c], r4.at[j - 1], at(t, zz, y, c))
        elif s == 4:
            self.out[:, pl.ds(start, width)] = (g[t, z, y, c].astype(F32) + r4[0].astype(F32)) + (
                r4[1].astype(F32) + r4[2].astype(F32)
            )

    def release(self, name):
        for owner, copy in self.sends:
            if owner == name:
                copy.wait_send()
        self.sends = [entry for entry in self.sends if entry[0] != name]

    def finish(self):
        for owner, copy in self.sends:
            copy.wait_send()
        self.sends = []


def put(g, first, n, value, lower=0):
    done = 0
    while done < value.shape[1]:
        t, offset = (lower + done) // n, (lower + done) % n
        take = min(value.shape[1] - done, n - offset)
        block = value[:, done : done + take].astype(BF)
        g[t, :, :, :, :, pl.ds(first + offset, take)] = block.reshape(g.shape[1:5] + (take,))
        done += take


def add_norm(ng, index, dgain, dshift):
    ng[index : index + 1, :] += dgain
    ng[6 + index : 7 + index, :] += dshift


def attn_backward(
    g, x, gain, ng, index, a_t, kv_t, g_t, wq, wk, wv, wo, q, k, v, o, ol, r, e_hbm, ebuf, esem, ds,
    do, dq, dk, dv, grads, n1, before_core, between, after_core, after_grads, into_keys, finish,
):
    seq = x.shape[0]

    def before(sl):
        rows = g[sl, :].astype(BF)
        g_t[:, sl] = rows.T
        do[sl, :] = (dg(rows, wo[...]) * r[sl, :].astype(F32)).astype(BF)

    rows_loop(seq, RB, before)
    put(grads, 3 * n1, n1, dg(g_t[...], o[...]))
    before_core()
    attn_back_core(q, k, v, do, o, ol, e_hbm, ebuf, esem, ds, dq, dk, dv, between)
    after_core()
    put(grads, 0, n1, dg(a_t[...], dq[...]))
    put(grads, n1, n1, dg(kv_t[...], dk[...]))
    put(grads, 2 * n1, n1, dg(kv_t[...], dv[...]))
    after_grads()

    def after(sl):
        into = dg(dq[sl, :], wq[...], NT)
        keys = dg(dk[sl, :], wk[...], NT) + dg(dv[sl, :], wv[...], NT)
        if into_keys is None:
            into = into + keys
        else:
            into_keys[sl, :] = keys
        dx, dgain, dshift = ln_back(x[sl, :].astype(F32), gain, into)
        add_norm(ng, index, dgain, dshift)
        finish(sl, g[sl, :] + dx)

    rows_loop(seq, RB, after)


def fetcher(sems):
    count = [0]

    def fetch(*pairs):
        copies = []
        for src, dst in pairs:
            cp = pltpu.make_async_copy(src, dst, sems.at[count[0]])
            count[0] += 1
            cp.start()
            copies.append(cp)
        return copies

    return fetch


def nothing():
    return None


def dec_backward(
    gains, shifts, y2_hbm, g3_hbm, y1_hbm, mem_hbm, a4_hbm, q4_hbm, k4_hbm, v4_hbm, o4_hbm, ol4_hbm, r4_hbm, e4_hbm,
    x2_hbm, x1_hbm, a1_hbm, h1_hbm, gp1_hbm, w_hbm,
    dec_o, g4_o, g1_o, up_o, down_o, sums, ng,
    y2, g3, y1, a, q, k, v, o, ol, r, cq, ck, cv, co, wu, wd,
    big, gs, do, a_t, g_t, g_up, g_down, g_cross, ebuf,
    ru1, ru2, ru3, ru4, rd1, rd2, rd3, rd4, rc1, rc2, rc3, rc4,
    rsend, rrecv, xsend, xrecv, local, isem, wsem, esem, osem,
):
    t, z, y, c = places()
    seq, width = y1.shape
    n1, n2 = cq.shape[1] // 2, wu.shape[1] // 2
    fetch = fetcher(isem)
    load, ready = weight_loader(w_hbm, wsem)
    first = fetch((y2_hbm, y2), (g3_hbm, g3))
    load("feed", 12 * n1 + 2 * n2, (wu, wd), n2, 0)
    greet(all_partners(t, z, y, c))
    halves = Exchange(xsend, xrecv, local)
    reduce = Reduce(
        sums,
        {
            "up": (g_up, ru1, ru2, ru3, ru4, rsend.at[0], rrecv.at[0], 0, True),
            "down": (g_down, rd1, rd2, rd3, rd4, rsend.at[1], rrecv.at[1], n2, True),
            "cross": (g_cross, rc1, rc2, rc3, rc4, rsend.at[2], rrecv.at[2], 2 * n2, True),
        },
    )
    ng[...] = jnp.zeros_like(ng)
    save = Saver(osem)
    wait_all(first)
    ready("feed")
    load("cross", 8 * n1 + 2 * n2, (cq, ck, cv, co), n1, 4)
    cross = fetch(
        (o4_hbm, o), (r4_hbm, r), (a4_hbm, a), (q4_hbm, q), (k4_hbm, k),
        (v4_hbm, v), (ol4_hbm, ol), (y1_hbm, y1),
    )
    first_scores(e4_hbm, ebuf, esem)
    h, du = big.at[0], big.at[1]

    def feed(sl):
        stream = y2[sl, :]
        hat, unused = ln_hat(stream)
        rows = (hat * gains[5:6, :] + shifts[5:6, :]).astype(BF)
        a_t[:, sl] = rows.T
        grad = g3[sl, :]
        g_t[:, sl] = grad.T
        out, into = stream, None
        lifted, pulled = dg(rows, columns(wu, 0, FB)), dg(grad, columns(wd, 0, FB))
        for lower in range(0, 2 * n2, FB):
            cols = pl.ds(lower, FB)
            if lower + FB < 2 * n2:
                following = dg(rows, columns(wu, lower + FB, FB)), dg(grad, columns(wd, lower + FB, FB))
            active, slope = gelu_both(lifted)
            active = active.astype(BF)
            h[sl, cols] = active
            pushed = (pulled * slope).astype(BF)
            du[sl, cols] = pushed
            out = out + dg(active, columns(wd, lower, FB), NT)
            part = dg(pushed, columns(wu, lower, FB), NT)
            into = part if into is None else into + part
            lifted, pulled = following
        g3[sl, :] = out.astype(BF)
        dx, dgain, dshift = ln_back(stream, gains[5:6, :], into)
        add_norm(ng, 5, dgain, dshift)
        gs[sl, :] = grad.astype(F32) + dx

    rows_loop(seq, RB, feed)
    dec_back = halves.back(0, g3, dec_o)
    block = width
    for j in range(2 * n2 // block):
        put(g_up, 0, n2, dg(a_t[...], du[:, pl.ds(j * block, block)]), j * block)
    reduce.move(("up", 0))
    for j in range(2 * n2 // block):
        put(g_down, 0, n2, dg(g_t[...], h[:, pl.ds(j * block, block)]), j * block)
    load("enc", 8 * n1, (wu, wd), n2, 12)
    reduce.move(("up", 1))
    wait_all(cross)
    ready("cross")
    a_t[...] = a[...].T
    memory = big.at[1, :, pl.ds(3 * width, width)]
    late = fetch((mem_hbm, memory))
    dq, dk, dv = (big.at[1, :, pl.ds(i * width, width)] for i in range(3))

    def before_core():
        reduce.move(("down", 0))

    def between():
        reduce.move(("down", 1))

    def after_core():
        wait_all(late)
        late.clear()
        late.extend(fetch((x2_hbm, r)))
        g_t[...] = memory[...].T
        late.extend(
            fetch(
                (gp1_hbm.at[:, pl.ds(0, n2)], ebuf.at[2]), (gp1_hbm.at[:, pl.ds(n2, n2)], ebuf.at[3]),
                (h1_hbm.at[:, pl.ds(0, n2)], ebuf.at[0]), (h1_hbm.at[:, pl.ds(n2, n2)], ebuf.at[1]),
            )
        )
        reduce.move(("up", 2))

    def after_grads():
        late.extend(fetch((a1_hbm, a)))
        reduce.move(("cross", 0), ("down", 2))

    def keep(sl, gradient):
        gs[sl, :] = gradient

    attn_backward(
        gs, y1, gains[4:5, :], ng, 4, a_t, g_t, g_t, cq, ck, cv, co, q, k, v, o, ol, r, e4_hbm,
        ebuf, esem, big.at[0], do, dq, dk, dv, g_cross, n1,
        before_core, between, after_core, after_grads, y2, keep,
    )
    save(gs, g4_o)
    late.extend(fetch((x1_hbm, y1)))
    reduce.move(("up", 3), ("cross", 1))
    wait_all(late)
    ready("enc")
    save.finish()

    def feed_back(sl):
        dx, dgain, dshift = ln_back(r[sl, :].astype(F32), gains[2:3, :], y2[sl, :])
        add_norm(ng, 2, dgain, dshift)
        grad = dx.astype(BF)
        g_t[:, sl] = grad.T
        a_t[:, sl] = a[sl, :].T
        into = None
        pulled = dg(grad, columns(wd, 0, FB))
        for lower in range(0, 2 * n2, FB):
            i, cols = lower // n2, pl.ds(lower % n2, FB)
            following = dg(grad, columns(wd, lower + FB, FB)) if lower + FB < 2 * n2 else None
            pushed = (pulled * ebuf[2 + i, sl, cols].astype(F32)).astype(BF)
            ebuf[2 + i, sl, cols] = pushed
            part = dg(pushed, columns(wu, lower, FB), NT)
            into = part if into is None else into + part
            pulled = following
        dx1, dgain, dshift = ln_back(y1[sl, :].astype(F32), gains[1:2, :], into)
        add_norm(ng, 1, dgain, dshift)
        gs[sl, :] = dx + dx1

    rows_loop(seq // 2, RB, feed_back)
    reduce.move(("down", 3))
    rows_loop(seq // 2, RB, lambda sl: feed_back(pl.ds(pl.multiple_of(seq // 2 + sl.start, RB), RB)))
    save(gs, g1_o)
    reduce.move(("cross", 2), ("up", 4))
    reduce.release("up")
    for i in range(2):
        for j in range(n2 // block):
            cols = pl.ds(j * block, block)
            put(g_up, 0, n2, dg(a_t[...], ebuf[2 + i, :, cols]), i * n2 + j * block)
    save(g_up, up_o)
    reduce.move(("cross", 3), ("down", 4))
    reduce.release("down")
    for i in range(2):
        for j in range(n2 // block):
            cols = pl.ds(j * block, block)
            put(g_down, 0, n2, dg(g_t[...], ebuf[i, :, cols]), i * n2 + j * block)
    save(g_down, down_o)
    reduce.move(("cross", 4))
    arrived(dec_back)
    halves.finish()
    reduce.finish()
    save.finish()


def last_backward(
    gains, ng2, masked, g4_hbm, g1_hbm, y0_hbm, a3_hbm, q3_hbm, k3_hbm, v3_hbm, o3_hbm, ol3_hbm, r3_hbm, e3_hbm,
    x_hbm, a0_hbm, q0_hbm, k0_hbm, v0_hbm, o0_hbm, ol0_hbm, r0_hbm, e0_hbm, up_hbm, down_hbm, w_hbm,
    sg_o, target_o, sums, vec,
    gs, gs1, x, x0, a, q, k, v, o, ol, r, wq, wk, wv, wo, vo, big, do, a_t, g_t, gy, ng,
    g_up, g_down, g_self, g_enc, ebuf,
    ru1, ru2, ru3, ru4, rd1, rd2, rd3, rd4, rs1, rs2, rs3, rs4, re1, re2, re3, re4, ro1, ro2, ro3, ro4, v1, vr,
    rsend, rrecv, xsend, xrecv, local, vsend, vrecv, isem, wsem, esem,
):
    t, z, y, c = places()
    seq, width = x.shape
    n1 = wq.shape[1] // 2
    n2 = g_up.shape[-1]
    fetch = fetcher(isem)
    load, ready = weight_loader(w_hbm, wsem)
    load("self out", 7 * n1, (wo,), n1, 0)
    first = fetch((g4_hbm, gs), (o3_hbm, o), (r3_hbm, r))
    ups = fetch((up_hbm, g_up), (down_hbm, g_down))
    first_scores(e3_hbm, ebuf, esem)
    second = fetch((q3_hbm, q), (k3_hbm, k), (v3_hbm, v), (ol3_hbm, ol), (a3_hbm, a), (y0_hbm, x))
    load("self", 4 * n1, (wq, wk, wv), n1, 2)
    load("enc out", 3 * n1, (vo,), n1, 8)
    late = fetch((g1_hbm, gs1), (x_hbm, x0))
    greet(all_partners(t, z, y, c))
    halves = Exchange(xsend, xrecv, local)
    reduce = Reduce(
        sums,
        {
            "up": (g_up, ru1, ru2, ru3, ru4, rsend.at[0], rrecv.at[0], 0, False),
            "down": (g_down, rd1, rd2, rd3, rd4, rsend.at[1], rrecv.at[1], n2, True),
            "self": (g_self, rs1, rs2, rs3, rs4, rsend.at[2], rrecv.at[2], 2 * n2, True),
            "enc": (
                g_enc.at[:, :, :, :, :, pl.ds(0, 3 * n1)], re1, re2, re3, re4, rsend.at[3], rrecv.at[3],
                2 * n2 + 4 * n1, True,
            ),
            "out": (
                g_enc.at[:, :, :, :, :, pl.ds(3 * n1, n1)], ro1, ro2, ro3, ro4, rsend.at[4], rrecv.at[4],
                2 * n2 + 7 * n1, True,
            ),
        },
    )
    ng[...] = ng2[...]
    wait_all(ups)
    reduce.move(("up", 0))
    wait_all(first)
    ready("self out")
    dq, dk, dv = (big.at[1, :, pl.ds(i * width, width)] for i in range(3))
    ds = big.at[0]

    def before_core3():
        wait_all(second)
        a_t[...] = a[...].T
        ready("self")
        reduce.move(("up", 1), ("down", 0))

    def between3():
        reduce.move(("down", 1))

    def after_core3():
        late.extend(fetch((o0_hbm, o), (r0_hbm, r), (q0_hbm, q), (k0_hbm, k), (v0_hbm, v), (ol0_hbm, ol), (a0_hbm, a)))
        first_scores(e0_hbm, ebuf, esem)
        reduce.move(("up", 2), ("down", 2))

    def after_grads3():
        reduce.move(("self", 0))

    def last3(sl, gradient):
        gy[sl, :] = gradient.astype(BF)

    attn_backward(
        gs, x, gains[3:4, :], ng, 3, a_t, a_t, g_t, wq, wk, wv, wo, q, k, v, o, ol, r, e3_hbm,
        ebuf, esem, ds, do, dq, dk, dv, g_self, n1,
        before_core3, between3, after_core3, after_grads3, None, last3,
    )
    load("enc", 0, (wq, wk, wv), n1, 10)
    gy_back = halves.back(0, gy, target_o)
    reduce.move(("self", 1), ("up", 3))
    wait_all(late)
    ready("enc out")
    a_t[...] = a[...].T

    def before_core0():
        reduce.move(("out", 0), ("down", 3))

    def between0():
        reduce.move(("self", 2), ("out", 1))

    def after_core0():
        reduce.move(("out", 2), ("up", 4))
        arrived(gy_back)
        total = jnp.zeros((1, width), F32)
        for i in range(2):
            chosen = column(masked[i : i + 1, :].astype(F32)) == 1.0
            rows = target_o[i].astype(F32)
            total = total + jnp.sum(jnp.where(chosen, rows, 0.0), axis=0, keepdims=True)
            target_o[i] = jnp.where(chosen, 0.0, rows).astype(BF)
        ng[12:13, :] = total

    def after_grads0():
        ready("enc")
        gy_back[0].wait_send()
        reduce.move(("enc", 0), ("self", 3), ("out", 3), ("enc", 1))

    def last0(sl, gradient):
        gy[sl, :] = gradient.astype(BF)

    attn_backward(
        gs1, x0, gains[0:1, :], ng, 0, a_t, a_t, g_t, wq, wk, wv, vo, q, k, v, o, ol, r, e0_hbm,
        ebuf, esem, ds, do, dq, dk, dv, g_enc, n1,
        before_core0, between0, after_core0, after_grads0, None, last0,
    )
    sg_back = halves.back(1, gy, sg_o)
    waiting = []

    def vector(s):
        for copy in waiting:
            copy.wait_recv()
        waiting.clear()
        if s == 0:
            v1[0] = ng[...]
        elif s < 4:
            v1[s] = v1[s - 1] + vr[s - 1]
        if s < 3:
            targets = ((s, (at(t, z, y, 1 - c), at(t, z, 1 - y, c), at(1 - t, z, y, c))[s]),)
        elif s == 3:
            targets = tuple((2 + j, at(t, lax.rem(z + j, 4), y, c)) for j in range(1, 4))
        else:
            targets = ()
            vec[...] = (v1[3] + vr[3]) + (vr[4] + vr[5])
        for slot, device in targets:
            copy = pltpu.make_async_remote_copy(
                src_ref=v1.at[s], dst_ref=vr.at[slot], send_sem=vsend.at[slot], recv_sem=vrecv.at[slot],
                device_id=device, device_id_type=MESH,
            )
            copy.start()
            reduce.sends.append(("vector", copy))
            waiting.append(copy)

    vector(0)
    reduce.move(("down", 4), ("self", 4), ("out", 4))
    vector(1)
    reduce.move(("enc", 2))
    vector(2)
    vector(3)
    reduce.move(("enc", 3))
    vector(4)
    reduce.move(("enc", 4))
    arrived(sg_back)
    sg_back[0].wait_send()
    reduce.finish()


def unpack(sums2, sums3, vec, *refs):
    grads, (gains_o, shifts_o, mask_o) = refs[:16], refs[16:]
    for summed, held in ((sums2, (14, 15, 10, 11, 12, 13)), (sums3, (4, 5, 6, 7, 8, 9, 0, 1, 2, 3))):
        offset = 0
        for i in held:
            n = grads[i].shape[1]
            grads[i][...] = summed[:, pl.ds(offset, n)]
            offset += n
    gains_o[...] = vec[0:6, :]
    shifts_o[...] = vec[6:12, :]
    mask_o[...] = vec[12:13, :]


def compute_all(lengths, timesteps, gains, shifts, mask_vector, masked, loss_mask, matrices, source, target, cotangent):
    rows, width = source.shape[1:]
    seq = 2 * rows
    n1 = width // 2
    part = matrices[0].shape[0]
    n2 = matrices[4].shape[1]
    total = 12 * n1 + 4 * n2
    hidden = 2 * n2
    heads = width // HD
    sd = jax.ShapeDtypeStruct
    any_spec = pl.BlockSpec(memory_space=pl.ANY)
    vmem = pl.BlockSpec(memory_space=pltpu.VMEM)
    smem = pl.BlockSpec(memory_space=pltpu.SMEM)
    dma = pltpu.SemaphoreType.DMA
    row = lambda kind: sd((seq, width), kind)
    tall = lambda kind: sd((seq, hidden), kind)
    halves = sd((2, rows, width), BF)
    escores = sd((heads, seq, seq), BF)
    vrow = lambda kind: pltpu.VMEM((seq, width), kind)
    vhalves = pltpu.VMEM((2, rows, width), BF)
    vsq = pltpu.VMEM((width, width), BF)
    vwide = pltpu.VMEM((width, hidden), BF)
    vtall = pltpu.VMEM((seq, hidden), BF)
    vsq5 = pltpu.VMEM((4, 2, 2, part, width), BF)
    vwide5 = pltpu.VMEM((4, 2, 2, part, hidden), BF)
    turned = pltpu.VMEM((width, seq), BF)
    big = pltpu.VMEM((2, seq, hidden), BF)
    ebuf = pltpu.VMEM((4, seq, seq), BF)
    grads = lambda n: pltpu.VMEM((2, 4, 2, 2, part, n), BF)

    def landing(n, split=False):
        r3 = (2, 4, 2, part, n // 2) if split else (4, part, n)
        return [
            pltpu.VMEM(dims, BF) for dims in ((2, 4, 2, part, n), (2, 4, part, n), r3, (3, part, n))
        ]

    def params(number):
        return pltpu.CompilerParams(
            vmem_limit_bytes=VMEM_LIMIT, collective_id=number, has_side_effects=True
        )

    attention = [row(BF)] * 7 + [escores]
    (
        gathered, x, y0, g3,
        a0, q0, k0, v0, o0, ol0, r0, e0, x1, a1, h1, gp1, x2, mem,
        a3, q3, k3, v3, o3, ol3, r3, e3, y1,
        a4, q4, k4, v4, o4, ol4, r4, e4, y2,
    ) = pl.pallas_call(
        forward,
        in_specs=[smem, smem] + [vmem] * 21 + [any_spec] * 3,
        out_specs=[any_spec] * 36,
        out_shape=[sd((2, 4, 2, 2, part, total), BF)] + [row(BF)] * 3
        + attention + [row(BF), row(BF), tall(BF), tall(BF), row(BF), row(BF)]
        + attention + [row(BF)]
        + attention + [row(F32)],
        scratch_shapes=[pltpu.VMEM((part, total), BF), vhalves, vhalves]
        + [vrow(BF)] * 2 + [vsq5] * 8 + [vwide5] * 2 + [vrow(BF)] * 14
        + [vrow(F32), vrow(BF), vtall, vtall, vrow(BF), vrow(BF), vrow(F32), vrow(F32), ebuf]
        + [dma((8, 11)), dma((8, 11)), dma((4,)), dma((4,)), dma((7,)), dma((20,)), dma((4,)), dma((35,))],
        compiler_params=params(0),
        name="forward",
    )(lengths, timesteps, gains, shifts, mask_vector[None], masked, loss_mask, *matrices, source, target, cotangent)
    weights = gathered.reshape(2, width, total)
    decoded, g4, g1, up, down, sums2, ng = pl.pallas_call(
        dec_backward,
        in_specs=[vmem, vmem] + [any_spec] * 18,
        out_specs=[any_spec] * 5 + [vmem] * 2,
        out_shape=[halves, row(F32), row(F32)] + [sd((2, 4, 2, 2, part, n2), BF)] * 2
        + [sd((part, 2 * n2 + 4 * n1), F32), sd((16, width), F32)],
        scratch_shapes=[vrow(F32)] + [vrow(BF)] * 9
        + [vsq] * 4 + [vwide] * 2 + [big, vrow(F32), vrow(BF)] + [turned] * 2
        + [grads(n2), grads(n2), grads(4 * n1), ebuf]
        + landing(n2, True) + landing(n2, True) + landing(4 * n1, True)
        + [dma((3, 8)), dma((3, 8)), dma((1,)), dma((1,)), dma((1,)), dma((18,)), dma((16,)), dma((4,)), dma((4,))],
        compiler_params=params(1),
        name="dec_backward",
    )(gains, shifts, y2, g3, y1, mem, a4, q4, k4, v4, o4, ol4, r4, e4, x2, x1, a1, h1, gp1, weights)
    source_grad, target_grad, sums3, vec = pl.pallas_call(
        last_backward,
        in_specs=[vmem] * 3 + [any_spec] * 23,
        out_specs=[any_spec, vmem, vmem, vmem],
        out_shape=[halves, halves, sd((part, 2 * n2 + 8 * n1), F32), sd((16, width), F32)],
        scratch_shapes=[vrow(F32)] * 2 + [vrow(BF)] * 9 + [vsq] * 5 + [big, vrow(BF)] + [turned] * 2
        + [vrow(BF), pltpu.VMEM((16, width), F32)]
        + [grads(n2), grads(n2), grads(4 * n1), grads(4 * n1), ebuf]
        + landing(n2) + landing(n2, True) + landing(4 * n1, True) + landing(3 * n1, True) + landing(n1, True)
        + [pltpu.VMEM((4, 16, width), F32), pltpu.VMEM((6, 16, width), F32)]
        + [dma((5, 8)), dma((5, 8)), dma((2,)), dma((2,)), dma((2,)), dma((6,)), dma((6,)), dma((20,)), dma((16,)), dma((4,))],
        compiler_params=params(2),
        name="last_backward",
    )(
        gains, ng, masked, g4, g1, y0, a3, q3, k3, v3, o3, ol3, r3, e3,
        x, a0, q0, k0, v0, o0, ol0, r0, e0, up, down, weights,
    )
    square, tall_square = sd((part, n1), F32), sd((part, n2), F32)
    small = pl.pallas_call(
        unpack,
        in_specs=[vmem] * 3,
        out_specs=[vmem] * 19,
        out_shape=[tall_square if i in (4, 5, 14, 15) else square for i in range(16)]
        + [sd((6, width), F32)] * 2 + [sd((1, width), F32)],
        name="unpack",
    )(sums2, sums3, vec)
    return (decoded, source_grad, target_grad, *small)


def pair_body(*arguments):
    source, target, cotangent, lengths, timesteps, masked, loss_mask = arguments[:7]
    matrices = [m.T if i in TURNED else m for i, m in enumerate(arguments[7:23])]
    norm_gains, norm_shifts, mask_vector = arguments[23:]
    outs = compute_all(
        lengths, timesteps, norm_gains, norm_shifts, mask_vector, masked, loss_mask, matrices, source, target, cotangent
    )
    grads = [g.T if i in TURNED else g for i, g in enumerate(outs[3:19])]
    return (*outs[:3], *grads, outs[19], outs[20], outs[21][0])


def solution(mesh):
    whole_pairs = dict(mesh.shape) == {"dp": 16, "tensor": 2}
    return jax.shard_map(
        pair_body if whole_pairs else body,
        mesh=mesh,
        in_specs=(
            P("dp", "tensor", None),
            P("dp", "tensor", None),
            P("dp", "tensor", None),
            P("dp"),
            P("dp"),
            P("dp", "tensor"),
            P("dp", "tensor"),
            P("dp", "tensor"),
            P("dp", "tensor"),
            P("dp", "tensor"),
            P("tensor", "dp"),
            P("dp", "tensor"),
            P("tensor", "dp"),
            P("dp", "tensor"),
            P("dp", "tensor"),
            P("dp", "tensor"),
            P("tensor", "dp"),
            P("dp", "tensor"),
            P("dp", "tensor"),
            P("dp", "tensor"),
            P("tensor", "dp"),
            P("dp", "tensor"),
            P("tensor", "dp"),
            P(),
            P(),
            P(),
        ),
        out_specs=(
            P("dp", "tensor", None),
            P("dp", "tensor", None),
            P("dp", "tensor", None),
            P("dp", "tensor"),
            P("dp", "tensor"),
            P("dp", "tensor"),
            P("tensor", "dp"),
            P("dp", "tensor"),
            P("tensor", "dp"),
            P("dp", "tensor"),
            P("dp", "tensor"),
            P("dp", "tensor"),
            P("tensor", "dp"),
            P("dp", "tensor"),
            P("dp", "tensor"),
            P("dp", "tensor"),
            P("tensor", "dp"),
            P("dp", "tensor"),
            P("tensor", "dp"),
            P(),
            P(),
            P(),
        ),
        check_vma=False,
    )
```

```python
import jax
import jax.numpy as jnp
from jax import lax
from jax.experimental import pallas as pl
from jax.experimental.pallas import tpu as pltpu
from jax.sharding import PartitionSpec as P

HD = 64
MICRO = 2
STEPS = 50


eps = 1e-05
floor_score = -1e30


def norm_rows(inputs, gain, shift):
    average = jnp.mean(inputs, axis=-1, keepdims=True)
    centred = inputs - average
    second = jnp.mean(centred * centred, axis=-1, keepdims=True)
    return centred * lax.rsqrt(second + eps) * gain + shift


def norm_back(inputs, gain, shift, gradient):
    unused, pullback = jax.vjp(norm_rows, inputs, gain, shift)
    return pullback(gradient)


def smooth(values):
    return jax.nn.gelu(values, approximate=False)


def spread(inputs):
    return lax.all_gather(inputs.astype(jnp.bfloat16), "tensor", axis=1, tiled=True)


def collect(partial_value):
    return lax.psum_scatter(partial_value, "tensor", scatter_dimension=1, tiled=True)


def spread_grad(gradient):
    return lax.all_gather(gradient.astype(jnp.bfloat16), "tensor", axis=1, tiled=True)


def collect_grad(partial_value):
    return lax.psum_scatter(partial_value, "tensor", scatter_dimension=1, tiled=True)


def project(inputs, weight):
    return jnp.einsum("bsk,kn->bsn", inputs, weight, preferred_element_type=jnp.float32)


def weight_grad(inputs, gradient):
    return jnp.einsum("bsk,bsn->kn", inputs, gradient, preferred_element_type=jnp.float32)


def back_project(gradient, weight):
    return jnp.einsum("bsn,kn->bsk", gradient, weight, preferred_element_type=jnp.float32)


def masked_scores(query_part, key_rows, live):
    scores = jnp.einsum(
        "bqhd,bkhd->bhqk", query_part, key_rows, preferred_element_type=jnp.float32
    ) * HD ** (-0.5)
    return jnp.where(live[:, None, None, :], scores, floor_score)


def attend_forward(query_in, keys_in, w_query, w_key, w_value, live):
    pair_count, length = (query_in.shape[0], query_in.shape[1])
    head_count = w_query.shape[1] // HD
    queries = (
        project(query_in, w_query).astype(jnp.bfloat16).reshape(pair_count, length, head_count, HD)
    )
    key_rows = (
        project(keys_in, w_key).astype(jnp.bfloat16).reshape(pair_count, length, head_count, HD)
    )
    value_rows = (
        project(keys_in, w_value).astype(jnp.bfloat16).reshape(pair_count, length, head_count, HD)
    )
    block_rows = min(512, length)
    pieces = []
    totals = []
    for offset in range(0, length, block_rows):
        scores = masked_scores(queries[:, offset : offset + block_rows], key_rows, live)
        highest = jnp.max(scores, axis=-1, keepdims=True)
        exponent = jnp.exp(scores - highest)
        summed = jnp.sum(exponent, axis=-1, keepdims=True)
        softmax = (exponent / summed).astype(jnp.bfloat16)
        pieces.append(
            jnp.einsum("bhqk,bkhd->bqhd", softmax, value_rows, preferred_element_type=jnp.float32)
        )
        totals.append(highest + jnp.log(summed))
    attended = (
        jnp.concatenate(pieces, axis=1)
        .astype(jnp.bfloat16)
        .reshape(pair_count, length, head_count * HD)
    )
    return (queries, key_rows, value_rows, attended, jnp.concatenate(totals, axis=2))


def attend_backward(whole_grad, query_in, keys_in, w_query, w_key, w_value, w_out, saved, live):
    queries, key_rows, value_rows, attended, totals = saved
    pair_count, length, head_count = (queries.shape[0], queries.shape[1], queries.shape[2])
    scale_score = HD ** (-0.5)
    out_grad = weight_grad(attended, whole_grad)
    head_grad = (
        back_project(whole_grad, w_out)
        .astype(jnp.bfloat16)
        .reshape(pair_count, length, head_count, HD)
    )
    block_rows = min(512, length)
    key_total = jnp.zeros(key_rows.shape, jnp.float32)
    value_total = jnp.zeros(value_rows.shape, jnp.float32)
    query_parts = []
    for offset in range(0, length, block_rows):
        query_part = queries[:, offset : offset + block_rows]
        grad_part = head_grad[:, offset : offset + block_rows]
        scores = masked_scores(query_part, key_rows, live)
        softmax = jnp.exp(scores - totals[:, :, offset : offset + block_rows])
        value_total = value_total + jnp.einsum(
            "bhqk,bqhd->bkhd",
            softmax.astype(jnp.bfloat16),
            grad_part,
            preferred_element_type=jnp.float32,
        )
        soft_grad = jnp.einsum(
            "bqhd,bkhd->bhqk", grad_part, value_rows, preferred_element_type=jnp.float32
        )
        inner = jnp.sum(softmax * soft_grad, axis=-1, keepdims=True)
        score_grad = (softmax * (soft_grad - inner)).astype(jnp.bfloat16)
        query_parts.append(
            jnp.einsum("bhqk,bkhd->bqhd", score_grad, key_rows, preferred_element_type=jnp.float32)
            * scale_score
        )
        key_total = (
            key_total
            + jnp.einsum(
                "bhqk,bqhd->bkhd", score_grad, query_part, preferred_element_type=jnp.float32
            )
            * scale_score
        )
    query_grad = (
        jnp.concatenate(query_parts, axis=1)
        .astype(jnp.bfloat16)
        .reshape(pair_count, length, head_count * HD)
    )
    key_grad = key_total.astype(jnp.bfloat16).reshape(
        pair_count, key_rows.shape[1], head_count * HD
    )
    value_grad = value_total.astype(jnp.bfloat16).reshape(
        pair_count, value_rows.shape[1], head_count * HD
    )
    grads = (
        weight_grad(query_in, query_grad),
        weight_grad(keys_in, key_grad),
        weight_grad(keys_in, value_grad),
        out_grad,
    )
    into_keys = back_project(key_grad, w_key) + back_project(value_grad, w_value)
    return (grads, back_project(query_grad, w_query), into_keys)


def feed_forward(inputs, w_up, w_down):
    lifted = project(inputs, w_up)
    active = smooth(lifted).astype(jnp.bfloat16)
    return (lifted, active, project(active, w_down))


def feed_backward(gradient, inputs, w_up, w_down, lifted, active):
    down_grad = weight_grad(active, gradient)
    active_grad = back_project(gradient, w_down)
    unused, smooth_back = jax.vjp(smooth, lifted)
    lifted_grad = smooth_back(active_grad)[0].astype(jnp.bfloat16)
    return ((weight_grad(inputs, lifted_grad), down_grad), back_project(lifted_grad, w_up))


def body(
    source,
    target,
    cotangent,
    lengths,
    timesteps,
    masked,
    loss_mask,
    enc_query,
    enc_key,
    enc_value,
    enc_out,
    enc_up,
    enc_down,
    self_query,
    self_key,
    self_value,
    self_out,
    cross_query,
    cross_key,
    cross_value,
    cross_out,
    dec_up,
    dec_down,
    norm_gains,
    norm_shifts,
    mask_vector,
):
    pairs_dev, rows_dev = (source.shape[0], source.shape[1])
    per_micro = pairs_dev // MICRO
    seq_len = rows_dev * lax.axis_size("tensor")
    positions = jnp.arange(seq_len)
    gains, shifts = (norm_gains, norm_shifts)
    gain_total = jnp.zeros(norm_gains.shape, jnp.float32)
    shift_total = jnp.zeros(norm_shifts.shape, jnp.float32)
    mask_total = jnp.zeros(mask_vector.shape, jnp.float32)
    decoded_parts = []
    source_parts = []
    target_parts = []
    running = None
    for micro in range(MICRO):
        weights = (
            lax.all_gather(enc_query, "dp", axis=0, tiled=True),
            lax.all_gather(enc_key, "dp", axis=0, tiled=True),
            lax.all_gather(enc_value, "dp", axis=0, tiled=True),
            lax.all_gather(enc_out, "dp", axis=1, tiled=True),
            lax.all_gather(enc_up, "dp", axis=0, tiled=True),
            lax.all_gather(enc_down, "dp", axis=1, tiled=True),
            lax.all_gather(self_query, "dp", axis=0, tiled=True),
            lax.all_gather(self_key, "dp", axis=0, tiled=True),
            lax.all_gather(self_value, "dp", axis=0, tiled=True),
            lax.all_gather(self_out, "dp", axis=1, tiled=True),
            lax.all_gather(cross_query, "dp", axis=0, tiled=True),
            lax.all_gather(cross_key, "dp", axis=0, tiled=True),
            lax.all_gather(cross_value, "dp", axis=0, tiled=True),
            lax.all_gather(cross_out, "dp", axis=1, tiled=True),
            lax.all_gather(dec_up, "dp", axis=0, tiled=True),
            lax.all_gather(dec_down, "dp", axis=1, tiled=True),
        )
        wide = (
            lax.all_gather(weights[4], "tensor", axis=1, tiled=True),
            lax.all_gather(weights[5], "tensor", axis=0, tiled=True),
            lax.all_gather(weights[14], "tensor", axis=1, tiled=True),
            lax.all_gather(weights[15], "tensor", axis=0, tiled=True),
        )
        lower = micro * per_micro
        upper = lower + per_micro
        live = positions[None, :] < lengths[lower:upper][:, None]
        every = jnp.ones((per_micro, seq_len), bool)
        inputs_x = source[lower:upper].astype(jnp.float32)
        rows0 = spread(norm_rows(inputs_x, gains[0], shifts[0]))
        saved0 = attend_forward(rows0, rows0, weights[0], weights[1], weights[2], live)
        stream1 = inputs_x + collect(project(saved0[3], weights[3]))
        normed1 = norm_rows(stream1, gains[1], shifts[1])
        rows1 = normed1.astype(jnp.bfloat16)
        lifted1, active1, partial1 = feed_forward(rows1, wide[0], wide[1])
        stream2 = stream1 + partial1
        memory_rows = spread(norm_rows(stream2, gains[2], shifts[2]))
        chosen = masked[lower:upper][:, :, None] == 1
        start_y = jnp.where(chosen, mask_vector, target[lower:upper].astype(jnp.float32))
        rows3 = spread(norm_rows(start_y, gains[3], shifts[3]))
        saved3 = attend_forward(rows3, rows3, weights[6], weights[7], weights[8], every)
        stream4 = start_y + collect(project(saved3[3], weights[9]))
        rows4 = spread(norm_rows(stream4, gains[4], shifts[4]))
        saved4 = attend_forward(rows4, memory_rows, weights[10], weights[11], weights[12], live)
        stream5 = stream4 + collect(project(saved4[3], weights[13]))
        normed5 = norm_rows(stream5, gains[5], shifts[5])
        rows5 = normed5.astype(jnp.bfloat16)
        lifted5, active5, partial5 = feed_forward(rows5, wide[2], wide[3])
        stream6 = stream5 + partial5
        decoded_parts.append(stream6.astype(jnp.bfloat16))
        factor = (STEPS + 1 - timesteps[lower:upper]).astype(jnp.float32) / STEPS
        grad6 = (
            cotangent[lower:upper].astype(jnp.float32)
            * (factor[:, None] * loss_mask[lower:upper].astype(jnp.float32))[:, :, None]
        )
        (up5, down5), into5 = feed_backward(
            grad6.astype(jnp.bfloat16), rows5, wide[2], wide[3], lifted5, active5
        )
        back5 = norm_back(stream5, gains[5], shifts[5], into5)
        grad5 = grad6 + back5[0]
        grads4, query_term4, memory_term = attend_backward(
            spread_grad(grad5),
            rows4,
            memory_rows,
            weights[10],
            weights[11],
            weights[12],
            weights[13],
            saved4,
            live,
        )
        back4 = norm_back(stream4, gains[4], shifts[4], collect_grad(query_term4))
        grad4 = grad5 + back4[0]
        memory_grad = collect_grad(memory_term)
        grads3, query_term3, keys_term3 = attend_backward(
            spread_grad(grad4),
            rows3,
            rows3,
            weights[6],
            weights[7],
            weights[8],
            weights[9],
            saved3,
            every,
        )
        back3 = norm_back(start_y, gains[3], shifts[3], collect_grad(query_term3 + keys_term3))
        grad_y = grad4 + back3[0]
        target_parts.append(jnp.where(chosen, 0.0, grad_y).astype(jnp.bfloat16))
        mask_total = mask_total + jnp.sum(jnp.where(chosen, grad_y, 0.0), axis=(0, 1))
        back2 = norm_back(stream2, gains[2], shifts[2], memory_grad)
        grad2 = back2[0]
        (up1, down1), into1 = feed_backward(
            grad2.astype(jnp.bfloat16), rows1, wide[0], wide[1], lifted1, active1
        )
        back1 = norm_back(stream1, gains[1], shifts[1], into1)
        grad1 = grad2 + back1[0]
        grads0, query_term0, keys_term0 = attend_backward(
            spread_grad(grad1),
            rows0,
            rows0,
            weights[0],
            weights[1],
            weights[2],
            weights[3],
            saved0,
            live,
        )
        back0 = norm_back(inputs_x, gains[0], shifts[0], collect_grad(query_term0 + keys_term0))
        source_parts.append((grad1 + back0[0]).astype(jnp.bfloat16))
        gain_total = gain_total + jnp.stack(
            [back0[1], back1[1], back2[1], back3[1], back4[1], back5[1]]
        )
        shift_total = shift_total + jnp.stack(
            [back0[2], back1[2], back2[2], back3[2], back4[2], back5[2]]
        )
        up1, down1, up5, down5 = (
            lax.psum_scatter(
                up1.astype(jnp.bfloat16), "tensor", scatter_dimension=1, tiled=True
            ).astype(jnp.float32),
            lax.psum_scatter(
                down1.astype(jnp.bfloat16), "tensor", scatter_dimension=0, tiled=True
            ).astype(jnp.float32),
            lax.psum_scatter(
                up5.astype(jnp.bfloat16), "tensor", scatter_dimension=1, tiled=True
            ).astype(jnp.float32),
            lax.psum_scatter(
                down5.astype(jnp.bfloat16), "tensor", scatter_dimension=0, tiled=True
            ).astype(jnp.float32),
        )
        fresh = (
            grads0[0],
            grads0[1],
            grads0[2],
            grads0[3],
            up1,
            down1,
            grads3[0],
            grads3[1],
            grads3[2],
            grads3[3],
            grads4[0],
            grads4[1],
            grads4[2],
            grads4[3],
            up5,
            down5,
        )
        running = fresh if micro == 0 else jax.tree.map(jnp.add, running, tuple(fresh))
    running = (
        lax.psum_scatter(
            running[0].astype(jnp.bfloat16), "dp", scatter_dimension=0, tiled=True
        ).astype(jnp.float32),
        lax.psum_scatter(
            running[1].astype(jnp.bfloat16), "dp", scatter_dimension=0, tiled=True
        ).astype(jnp.float32),
        lax.psum_scatter(
            running[2].astype(jnp.bfloat16), "dp", scatter_dimension=0, tiled=True
        ).astype(jnp.float32),
        lax.psum_scatter(
            running[3].astype(jnp.bfloat16), "dp", scatter_dimension=1, tiled=True
        ).astype(jnp.float32),
        lax.psum_scatter(
            running[4].astype(jnp.bfloat16), "dp", scatter_dimension=0, tiled=True
        ).astype(jnp.float32),
        lax.psum_scatter(
            running[5].astype(jnp.bfloat16), "dp", scatter_dimension=1, tiled=True
        ).astype(jnp.float32),
        lax.psum_scatter(
            running[6].astype(jnp.bfloat16), "dp", scatter_dimension=0, tiled=True
        ).astype(jnp.float32),
        lax.psum_scatter(
            running[7].astype(jnp.bfloat16), "dp", scatter_dimension=0, tiled=True
        ).astype(jnp.float32),
        lax.psum_scatter(
            running[8].astype(jnp.bfloat16), "dp", scatter_dimension=0, tiled=True
        ).astype(jnp.float32),
        lax.psum_scatter(
            running[9].astype(jnp.bfloat16), "dp", scatter_dimension=1, tiled=True
        ).astype(jnp.float32),
        lax.psum_scatter(
            running[10].astype(jnp.bfloat16), "dp", scatter_dimension=0, tiled=True
        ).astype(jnp.float32),
        lax.psum_scatter(
            running[11].astype(jnp.bfloat16), "dp", scatter_dimension=0, tiled=True
        ).astype(jnp.float32),
        lax.psum_scatter(
            running[12].astype(jnp.bfloat16), "dp", scatter_dimension=0, tiled=True
        ).astype(jnp.float32),
        lax.psum_scatter(
            running[13].astype(jnp.bfloat16), "dp", scatter_dimension=1, tiled=True
        ).astype(jnp.float32),
        lax.psum_scatter(
            running[14].astype(jnp.bfloat16), "dp", scatter_dimension=0, tiled=True
        ).astype(jnp.float32),
        lax.psum_scatter(
            running[15].astype(jnp.bfloat16), "dp", scatter_dimension=1, tiled=True
        ).astype(jnp.float32),
    )
    vectors = lax.psum((gain_total, shift_total, mask_total), ("dp", "tensor"))
    return (
        jnp.concatenate(decoded_parts, axis=0),
        jnp.concatenate(source_parts, axis=0),
        jnp.concatenate(target_parts, axis=0),
        running[0],
        running[1],
        running[2],
        running[3],
        running[4],
        running[5],
        running[6],
        running[7],
        running[8],
        running[9],
        running[10],
        running[11],
        running[12],
        running[13],
        running[14],
        running[15],
        vectors[0],
        vectors[1],
        vectors[2],
    )


F32 = jnp.float32
BF = jnp.bfloat16
LOG2E = 1.4426950408889634
LN2 = 0.6931471805599453
NN = (((1,), (0,)), ((), ()))
NT = (((1,), (1,)), ((), ()))
MESH = pl.DeviceIdType.MESH
RB = 512
FB = 256
VMEM_LIMIT = 63 * 2**20


def dg(left, right, dims=NN):
    return lax.dot_general(left, right, dims, preferred_element_type=F32)


def ln_hat(x):
    centred = x - jnp.mean(x, axis=-1, keepdims=True)
    rstd = lax.rsqrt(jnp.mean(centred * centred, axis=-1, keepdims=True) + eps)
    return centred * rstd, rstd


def ln_back(x, gain, gradient):
    hat, rstd = ln_hat(x)
    scaled = gradient * gain
    first = jnp.mean(scaled, axis=-1, keepdims=True)
    second = jnp.mean(scaled * hat, axis=-1, keepdims=True)
    dx = rstd * (scaled - first - hat * second)
    dgain = jnp.sum(gradient * hat, axis=0, keepdims=True)
    dshift = jnp.sum(gradient, axis=0, keepdims=True)
    return dx, dgain, dshift


def gelu_both(u):
    size = jnp.abs(u)
    t = 1.0 / (1.0 + (0.3275911 * 0.7071067811865476) * size)
    ex = jnp.exp2(u * u * (-0.5 * LOG2E))
    poly = t * (
        0.127414796
        + t * (-0.142248368 + t * (0.7107068705 + t * (-0.7265760135 + t * 0.5307027145)))
    )
    tail = poly * ex
    phi = jnp.where(u > 0, 1.0 - tail, tail)
    return u * phi, phi + u * ex * 0.3989422804014327


def rows_loop(total, step, run):
    def once(i, carry):
        run(pl.ds(pl.multiple_of(i * step, step), step))
        return carry

    lax.fori_loop(0, total // step, once, 0)


def load_weight(w_hbm, offset, width, dst, sems, base):
    copies = []
    for t in range(2):
        src = pl.ds(offset, width)
        to = pl.ds(t * width, width)
        cp = pltpu.make_async_copy(
            w_hbm.at[t, :, src] if len(w_hbm.shape) == 3 else w_hbm.at[t, :, :, :, :, src],
            dst.at[:, to] if len(dst.shape) == 2 else dst.at[:, :, :, :, to],
            sems.at[base + t],
        )
        cp.start()
        copies.append(cp)
    return copies


def wait_all(copies):
    for cp in copies:
        cp.wait()


def columns(ref, lower, width):
    value = ref[..., pl.ds(lower, width)]
    return value if value.ndim == 2 else value.reshape(-1, width)


def whole(ref):
    value = ref[...]
    return value if value.ndim == 2 else value.reshape(-1, value.shape[-1])


def normalize(x, gain, shift, a):
    def run(sl):
        hat, unused = ln_hat(x[sl, :].astype(F32))
        a[sl, :] = (hat * gain + shift).astype(BF)

    rows_loop(x.shape[0], RB, run)


def product_into(a, w, to, scale):
    def run(sl):
        value = dg(a[sl, :], whole(w))
        to[sl, :] = (value if scale is None else value * scale).astype(BF)

    rows_loop(a.shape[0], RB, run)


def attn_project(a, kv, wq, wk, wv, q, k, v):
    product_into(a, wq, q, LOG2E * HD**-0.5)
    product_into(kv, wk, k, None)
    product_into(kv, wv, v, None)


def score_copy(p, h, e_hbm, ebuf, esem):
    slot = lax.rem(p, 2) * 2 + h
    return pltpu.make_async_copy(ebuf.at[slot], e_hbm.at[2 * p + h], esem.at[slot])


def drain_scores(e_hbm, ebuf, esem):
    for p in range(2):
        for h in range(2):
            score_copy(p, h, e_hbm, ebuf, esem).wait()


def attn_core(length, q, k, v, o, ol, r, e_hbm, ebuf, esem, between, fresh):
    seq = q.shape[0]
    pairs = q.shape[1] // 128
    block = 256
    lane = lax.broadcasted_iota(jnp.int32, (1, 128), 1)
    low = lane < 64
    one = jnp.ones((), BF)
    key = lax.broadcasted_iota(jnp.int32, (seq, 1), 0)
    bias = jnp.where(key < length, 0.0, floor_score).astype(F32)
    items = [(b, h) for b in range(seq // block) for h in range(2)]

    def pair(p, carry):
        @pl.when((p > 1) if fresh else (p >= 0))
        def unused_wait():
            score_copy(p, 0, e_hbm, ebuf, esem).wait()
            score_copy(p, 1, e_hbm, ebuf, esem).wait()

        base = lax.rem(p, 2) * 2
        cols = pl.ds(pl.multiple_of(p * 128, 128), 128)
        kp = k[:, cols].astype(F32)
        vp = v[:, cols]
        ka = (
            jnp.where(low, kp, jnp.where(lane == 64, bias, 0.0)).astype(BF),
            jnp.where(low, jnp.where(lane == 0, bias, 0.0), kp).astype(BF),
        )
        va = jnp.where(low, vp, one), jnp.where(low, one, vp)

        def scores(b, h):
            qp = q[pl.ds(b * block, block), cols]
            return dg(jnp.where(low, qp, one) if h == 0 else jnp.where(low, one, qp), ka[h], NT)

        parts = []
        s = scores(*items[0])
        for n, (b, h) in enumerate(items):
            sl = pl.ds(b * block, block)
            following = scores(*items[n + 1]) if n + 1 < len(items) else None
            e = jnp.exp2(s - jnp.max(s, axis=-1, keepdims=True)).astype(BF)
            ebuf[base + h, sl, :] = e
            parts.append(dg(e, va[h]))
            s = following
            if h == 1:
                first, second = parts
                parts = []
                inverse = 1.0 / pltpu.roll(jnp.where(low, second, first), 64, 1)
                r[sl, cols] = inverse.astype(BF)
                joined = jnp.where(low, first, second) * inverse
                rounded = joined.astype(BF)
                o[sl, cols] = rounded
                ol[sl, cols] = (joined - rounded.astype(F32)).astype(BF)
        score_copy(p, 0, e_hbm, ebuf, esem).start()
        score_copy(p, 1, e_hbm, ebuf, esem).start()
        return carry

    lax.fori_loop(0, pairs // 2, pair, 0)
    between()
    lax.fori_loop(pairs // 2, pairs, pair, 0)


def attn_join(x, o, wo, y, lowered):
    def run(sl):
        joined = x[sl, :].astype(F32) + dg(o[sl, :], whole(wo), NT)
        y[sl, :] = joined
        if lowered is not None:
            lowered[sl, :] = joined.astype(BF)

    rows_loop(x.shape[0], RB, run)


def first_scores(e_hbm, ebuf, esem):
    for h in range(2):
        pltpu.make_async_copy(e_hbm.at[h], ebuf.at[h], esem.at[h]).start()


def attn_back_core(q, k, v, do, o, ol, e_hbm, ebuf, esem, ds, dq, dk, dv, between):
    seq = q.shape[0]
    heads = e_hbm.shape[0]
    block = 512
    lane = lax.broadcasted_iota(jnp.int32, (1, 128), 1)
    low = lane < 64
    zero = jnp.zeros((), BF)
    one = jnp.ones((), BF)
    row2 = lax.broadcasted_iota(jnp.int32, (256, 128), 0)
    col2 = lax.broadcasted_iota(jnp.int32, (256, 128), 1)
    swap = jnp.where(((row2 // 64) % 2) != (col2 // 64), 1.0, 0.0).astype(BF)

    def fetch(p, h):
        slot = lax.rem(p, 2) * 2 + h
        return pltpu.make_async_copy(e_hbm.at[2 * p + h], ebuf.at[slot], esem.at[slot])

    def pair(p, carry):
        cols = pl.ds(pl.multiple_of(p * 128, 128), 128)
        fetch(p, 0).wait()
        fetch(p, 1).wait()

        @pl.when(p + 1 < heads // 2)
        def unused_fetch():
            fetch(p + 1, 0).start()
            fetch(p + 1, 1).start()

        base = lax.rem(p, 2) * 2
        qp, kp, vp, dop = q[:, cols], k[:, cols], v[:, cols], do[:, cols]
        product = dop.astype(F32) * (o[:, cols].astype(F32) + ol[:, cols].astype(F32))
        high = product.astype(BF)
        rest = (product - high.astype(F32)).astype(BF)
        inner = -dg(jnp.concatenate([high, rest], axis=1), swap)
        inner_high = inner.astype(BF)
        inner_rest = (inner - inner_high.astype(F32)).astype(BF)
        do_t, q_t = dop.T, qp.T
        lhs = (
            jnp.where(low, dop, jnp.where(lane == 64, inner_high, inner_rest)),
            jnp.where(low, jnp.where(lane == 0, inner_high, inner_rest), dop),
        )
        va = (
            jnp.where(low, vp, jnp.where(lane < 66, one, zero)),
            jnp.where(low, jnp.where(lane < 2, one, zero), vp),
        )
        km = jnp.concatenate([jnp.where(low, kp, zero), jnp.where(low, zero, kp)], axis=0)
        dvs = [dg(do_t, ebuf[base + h])[64 * h : 64 * h + 64] for h in range(2)]
        for h in range(2):
            for b in range(seq // block):
                sl = pl.ds(b * block, block)
                t = dg(lhs[h][b * block : (b + 1) * block], va[h], NT)
                ds[sl, pl.ds(h * seq, seq)] = ebuf[base + h, sl, :] * t.astype(BF)
        dks = [dg(q_t, ds[:, pl.ds(h * seq, seq)])[64 * h : 64 * h + 64] for h in range(2)]
        dq_sum = dg(ds[...], km)
        dq[:, cols] = (dq_sum * HD**-0.5).astype(BF)
        dk[:, cols] = (jnp.concatenate(dks, axis=0) * LN2).astype(BF).T
        dv[:, cols] = jnp.concatenate(dvs, axis=0).astype(BF).T
        return carry

    lax.fori_loop(0, heads // 4, pair, 0)
    between()
    lax.fori_loop(heads // 4, heads // 2, pair, 0)


def places():
    d = lax.axis_index("dp")
    return lax.axis_index("tensor"), d // 4, (d // 2) % 2, d % 2


def at(t, z, y, c):
    return (z * 4 + y * 2 + c, t)


def greet(partners):
    barrier = pltpu.get_barrier_semaphore()
    for device in partners:
        pl.semaphore_signal(barrier, inc=1, device_id=device, device_id_type=MESH)
    pl.semaphore_wait(barrier, len(partners))


def all_partners(t, z, y, c):
    others = [at(t, lax.rem(z + j, 4), y, c) for j in range(1, 4)]
    return [at(t, z, y, 1 - c), at(1 - t, z, y, c), at(t, z, 1 - y, c)] + others


class Saver:
    def __init__(self, sems):
        self.sems, self.count, self.live = sems, 0, []

    def __call__(self, src, dst, slot=None):
        cp = pltpu.make_async_copy(src, dst, self.sems.at[self.count])
        cp.start()
        self.count += 1
        self.live.append((slot, cp))

    def free(self, slot):
        for name, cp in self.live:
            if name == slot:
                cp.wait()
        self.live = [entry for entry in self.live if entry[0] != slot]

    def finish(self):
        for name, cp in self.live:
            cp.wait()
        self.live = []


GATHER_PLAN = (
    ((0, 0), (1, 0), (2, 0), (4, 0), (5, 0), (6, 0)),
    ((0, 1), (1, 1), (3, 0)),
    ((0, 2),),
    ((1, 2), (2, 1), (3, 1)),
    ((7, 0),),
    ((0, 3), (0, 4), (1, 3), (1, 4), (2, 2), (4, 1)),
    (),
    ((3, 2), (5, 1)),
    ((7, 1),),
    ((2, 3), (2, 4)),
    ((4, 2),),
    (),
    ((5, 2), (6, 1), (7, 2)),
    ((3, 3), (4, 3)),
    ((3, 4), (4, 4)),
    ((5, 3),),
    ((5, 4), (6, 2)),
    (),
    (),
    ((6, 3), (7, 3)),
    (),
    ((6, 4), (7, 4)),
)
GATHER_ORDERS = (
    ("zxy",), ("zxy",), ("zxy",), ("xyz",), ("zxy", "zyx"), ("zxy", "zyx"), ("zxy", "zyx"), ("xyz",),
)


class Gather:
    def __init__(self, own, out, send, recv, widths):
        self.own, self.out, self.send, self.recv = own, out, send, recv
        self.starts = [sum(widths[:i]) for i in range(len(widths))]
        self.widths = widths
        self.spot = places()
        self.sends, self.pending = [], {}

    def push(self, src, dst, k, i, device):
        copy = pltpu.make_async_remote_copy(
            src_ref=src, dst_ref=dst, send_sem=self.send.at[k, i], recv_sem=self.recv.at[k, i],
            device_id=device, device_id_type=MESH,
        )
        copy.start()
        self.sends.append(copy)
        self.pending.setdefault(k, []).append(copy)

    def move(self, point):
        for k, s in GATHER_PLAN[point]:
            self.stage(k, s)

    def stage(self, k, s):
        t, z, y, c = self.spot
        every = slice(None)
        for copy in self.pending.pop(k, ()):
            copy.wait_recv()
        if s == 3:
            a = self.out.at[:, :, :, c, :, pl.ds(self.starts[k], self.widths[k])]
            self.push(a, a, k, 10, at(t, z, y, 1 - c))
        if s > 2:
            return
        orders = GATHER_ORDERS[k]
        width = self.widths[k] // len(orders)
        for i, order in enumerate(orders):
            cols = pl.ds(self.starts[k] + i * width, width)
            known = order[:s]
            dst = self.out.at[
                every if "x" in known else t, every if "z" in known else z, every if "y" in known else y, c, :, cols
            ]
            src = self.own.at[:, cols] if s == 0 else dst
            if order[s] == "z":
                for j in range(1, 4):
                    self.push(src, dst, k, 5 * i + j - 1, at(t, lax.rem(z + j, 4), y, c))
            elif order[s] == "x":
                self.push(src, dst, k, 5 * i + 3, at(1 - t, z, y, c))
            else:
                self.push(src, dst, k, 5 * i + 4, at(t, z, 1 - y, c))

    def finish(self):
        for copy in self.sends:
            copy.wait_send()


class Exchange:
    def __init__(self, send, recv, local):
        self.send, self.recv, self.local = send, recv, local
        self.open = []

    def start(self, i, src, kept, dst):
        t, z, y, c = places()
        far = pltpu.make_async_remote_copy(
            src_ref=src, dst_ref=dst, send_sem=self.send.at[i], recv_sem=self.recv.at[i],
            device_id=at(1 - t, z, y, c), device_id_type=MESH,
        )
        near = pltpu.make_async_copy(kept, dst, self.local.at[i])
        far.start()
        near.start()
        self.open.append(far)
        return far, near

    def give(self, i, halves, dst, part=0, parts=1):
        t = lax.axis_index("tensor")
        rows = halves.shape[1]
        take = rows // parts
        mine = dst.at[pl.ds(pl.multiple_of(t * rows + part * take, take), take), :]
        some = pl.ds(part * take, take)
        return self.start(i, halves.at[1 - t, some, :], halves.at[t, some, :], mine)

    def back(self, i, pair, dst):
        t = lax.axis_index("tensor")
        rows = dst.shape[1]
        kept = pair.at[pl.ds(pl.multiple_of(t * rows, rows), rows), :]
        sent = pair.at[pl.ds(pl.multiple_of((1 - t) * rows, rows), rows), :]
        return self.start(i, sent, kept, dst.at[t])

    def finish(self):
        for far in self.open:
            far.wait_send()


def arrived(copies):
    far, near = copies
    near.wait()
    far.wait_recv()


def column(values):
    return jnp.broadcast_to(values, (128, values.shape[1])).T[:, :1]


def weight_loader(w_hbm, sems):
    loads = {}

    def load(name, offset, refs, n, base):
        loads[name] = []
        for i, ref in enumerate(refs):
            loads[name] += load_weight(w_hbm, offset + i * n, n, ref, sems, base + 2 * i)

    def ready(name):
        wait_all(loads[name])

    return load, ready


TURNED = (3, 5, 9, 13, 15)
PACKED = (0, 1, 2, 3, 6, 7, 8, 9, 4, 5, 10, 11, 12, 13, 14, 15)


def forward(
    lengths, timesteps, gains, shifts, mask_row, masked, loss_mask, *refs,
):
    matrices, refs = refs[:16], refs[16:]
    (
        src_hbm, target_hbm, cot_hbm,
        w_hbm, x_o, y0_o, g3_o,
        a0_o, q0_o, k0_o, v0_o, o0_o, ol0_o, r0_o, e0_o, x1_o, a1_o, h1_o, gp1_o, x2_o, mem_o,
        a3_o, q3_o, k3_o, v3_o, o3_o, ol3_o, r3_o, e3_o, y1_o,
        a4_o, q4_o, k4_o, v4_o, o4_o, ol4_o, r4_o, e4_o, y2_o,
        own, tgt, cot, x, y0, wq, wk, wv, wo, sq, sk, sv, so, wu, wd,
        a, q, k, v, o, ol, r, a3, q3, k3, v3, o3, ol3, r3,
        x1, a1, h, gp, x2, mem, y1, y2, ebuf,
        gsend, grecv, xsend, xrecv, local, wsem, esem, osem,
    ) = refs
    t, z, y, c = places()
    seq, width = x.shape
    n1, n2 = width // 2, h.shape[1] // 2
    in_tgt = pltpu.make_async_copy(target_hbm, tgt, local.at[5])
    in_cot = pltpu.make_async_copy(cot_hbm, cot, local.at[6])
    in_tgt.start()
    in_cot.start()
    offset = 0
    for i in PACKED:
        part = matrices[i][...]
        own[:, pl.ds(offset, part.shape[1])] = part
        offset += part.shape[1]
    greet(all_partners(t, z, y, c))
    halves = Exchange(xsend, xrecv, local)
    gather = Gather(own, w_hbm, gsend, grecv, (2 * n1, 2 * n1, 4 * n1, n2, n2, 4 * n1, n2, n2))
    mine = pltpu.make_async_copy(own, w_hbm.at[t, z, y, c], local.at[4])
    mine.start()
    gather.move(0)
    x_in = [halves.give(0, src_hbm, x, 0, 2)]
    save = Saver(osem)
    in_tgt.wait()
    for i in range(2):
        chosen = column(masked[i : i + 1, :].astype(F32)) == 1.0
        tgt[i] = jnp.where(chosen, mask_row[...], tgt[i].astype(F32)).astype(BF)
    mine.wait()
    gather.move(1)
    in_cot.wait()
    for i in range(2):
        factor = (STEPS + 1 - timesteps[i]).astype(F32) / STEPS
        weight = column(loss_mask[i : i + 1, :].astype(F32)) * factor
        cot[i] = (cot[i].astype(F32) * weight).astype(BF)
    gather.move(2)
    x_in.append(halves.give(3, src_hbm, x, 1, 2))
    gather.move(3)
    for copies in x_in:
        arrived(copies)
    normalize(x, gains[0:1, :], shifts[0:1, :], a)
    save(x, x_o, "x")
    save(a, a0_o, "A")
    gather.move(4)
    gather.move(5)
    load, ready = weight_loader(w_hbm, wsem)
    load("enc", 0, (wq, wk), n1, 0)
    load("out", 2 * n1, (wv, wo), n1, 4)
    ready("enc")
    product_into(a, wq, q, LOG2E * HD**-0.5)
    product_into(a, wk, k, None)
    gather.move(6)
    y0_in = halves.give(1, tgt, y0)
    ready("out")
    product_into(a, wv, v, None)
    for src, dst in ((q, q0_o), (k, k0_o), (v, v0_o)):
        save(src, dst, "A")
    gather.move(7)
    length = lengths[t]

    def between0():
        gather.move(8)

    attn_core(length, q, k, v, o, ol, r, e0_o, ebuf, esem, between0, True)
    gather.move(9)
    load("self", 4 * n1, (sq, sk, sv, so), n1, 8)
    for src, dst in ((o, o0_o), (ol, ol0_o), (r, r0_o)):
        save(src, dst, "A")
    arrived(y0_in)
    save(y0, y0_o, "y0")
    normalize(y0, gains[3:4, :], shifts[3:4, :], a3)
    gather.move(10)
    save.free("x")
    attn_join(x, o, wo, x1, x)
    save(x, x1_o)
    ready("self")
    attn_project(a3, a3, sq, sk, sv, q3, k3, v3)
    for src, dst in ((a3, a3_o), (q3, q3_o), (k3, k3_o), (v3, v3_o)):
        save(src, dst)
    gather.move(11)
    gather.move(12)
    g3_in = halves.give(2, cot, g3_o)

    def between3():
        gather.move(13)

    attn_core(seq, q3, k3, v3, o3, ol3, r3, e3_o, ebuf, esem, between3, False)
    gather.move(14)
    load("feed", 8 * n1, (wu, wd), n2, 16)
    for src, dst in ((o3, o3_o), (ol3, ol3_o), (r3, r3_o)):
        save(src, dst)
    save.free("y0")
    attn_join(y0, o3, so, y1, y0)
    save(y0, y1_o)
    save.free("A")
    normalize(y1, gains[4:5, :], shifts[4:5, :], a)
    gather.move(15)
    ready("feed")

    def feed(sl):
        stream = x1[sl, :]
        hat, unused = ln_hat(stream)
        rows = (hat * gains[1:2, :] + shifts[1:2, :]).astype(BF)
        a1[sl, :] = rows
        out = stream
        lifted = dg(rows, columns(wu, 0, FB))
        for lower in range(0, 2 * n2, FB):
            cols = pl.ds(lower, FB)
            following = dg(rows, columns(wu, lower + FB, FB)) if lower + FB < 2 * n2 else None
            active, slope = gelu_both(lifted)
            active = active.astype(BF)
            h[sl, cols] = active
            gp[sl, cols] = slope.astype(BF)
            out = out + dg(active, columns(wd, lower, FB), NT)
            lifted = following
        x2[sl, :] = out.astype(BF)
        hat, unused = ln_hat(out)
        mem[sl, :] = (hat * gains[2:3, :] + shifts[2:3, :]).astype(BF)

    rows_loop(seq // 2, RB, feed)
    gather.move(16)
    load("cross", 8 * n1 + 2 * n2, (wq, wk, wv, wo), n1, 0)
    rows_loop(seq // 2, RB, lambda sl: feed(pl.ds(pl.multiple_of(seq // 2 + sl.start, RB), RB)))
    for src, dst in ((a1, a1_o), (h, h1_o), (gp, gp1_o), (x2, x2_o), (mem, mem_o)):
        save(src, dst)
    gather.move(17)
    ready("cross")
    attn_project(a, mem, wq, wk, wv, q, k, v)
    for src, dst in ((a, a4_o), (q, q4_o), (k, k4_o), (v, v4_o)):
        save(src, dst)
    gather.move(18)

    def between4():
        gather.move(19)

    attn_core(length, q, k, v, o, ol, r, e4_o, ebuf, esem, between4, False)
    for src, dst in ((o, o4_o), (ol, ol4_o), (r, r4_o)):
        save(src, dst)
    gather.move(20)
    attn_join(y1, o, wo, y2, None)
    save(y2, y2_o)
    gather.move(21)
    drain_scores(e4_o, ebuf, esem)
    arrived(g3_in)
    halves.finish()
    gather.finish()
    save.finish()


class Reduce:
    def __init__(self, out, chunks):
        self.out, self.chunks = out, chunks
        self.spot = places()
        self.sends, self.pending = [], {}

    def push(self, name, i, src, dst, device):
        send, recv = self.chunks[name][5:7]
        copy = pltpu.make_async_remote_copy(
            src_ref=src, dst_ref=dst, send_sem=send.at[i], recv_sem=recv.at[i],
            device_id=device, device_id_type=MESH,
        )
        copy.start()
        self.sends.append((name, copy))
        self.pending.setdefault(name, []).append(copy)

    def move(self, *steps):
        for name, s in steps:
            self.stage(name, s)

    def stage(self, name, s):
        t, z, y, c = self.spot
        g, r1, r2, r3, r4, send, recv, start, split = self.chunks[name]
        width = g.shape[-1]
        half = width // 2 if split else width
        left = pl.ds(0, half)
        right = pl.ds(half, half)
        by_x, by_y = at(1 - t, z, y, c), at(t, z, 1 - y, c)

        def add(mine, theirs):
            mine[...] = (mine[...].astype(F32) + theirs[...].astype(F32)).astype(BF)

        for copy in self.pending.pop(name, ()):
            copy.wait_recv()
        if s == 0:
            self.push(name, 0, g.at[:, :, :, 1 - c], r1, at(t, z, y, 1 - c))
        elif s == 1:
            add(g.at[:, :, 1 - y, c], r1.at[:, :, 1 - y])
            self.push(name, 1, g.at[:, :, 1 - y, c, :, left], r2.at[:, :, :, left], by_y)
            add(g.at[:, :, y, c], r1.at[:, :, y])
            if split:
                self.push(name, 2, g.at[1 - t, :, :, c, :, right], r3.at[0], by_x)
        elif s == 2:
            rows = g.at[:, :, y, c, :, left]
            add(rows, r2.at[:, :, :, left])
            if not split:
                self.push(name, 2, g.at[1 - t, :, y, c], r3, by_x)
            else:
                self.push(name, 3, g.at[1 - t, :, y, c, :, left], r3.at[1, :, 0], by_x)
                add(g.at[t, :, :, c, :, right], r3.at[0])
                self.push(name, 4, g.at[t, :, 1 - y, c, :, right], r3.at[1, :, 1], by_y)
        elif s == 3:
            if not split:
                add(g.at[t, :, y, c], r3)
            else:
                add(g.at[t, :, y, c, :, left], r3.at[1, :, 0])
                add(g.at[t, :, y, c, :, right], r3.at[1, :, 1])
            for j in range(1, 4):
                zz = lax.rem(z + j, 4)
                self.push(name, 4 + j, g.at[t, zz, y, c], r4.at[j - 1], at(t, zz, y, c))
        elif s == 4:
            self.out[:, pl.ds(start, width)] = (g[t, z, y, c].astype(F32) + r4[0].astype(F32)) + (
                r4[1].astype(F32) + r4[2].astype(F32)
            )

    def release(self, name):
        for owner, copy in self.sends:
            if owner == name:
                copy.wait_send()
        self.sends = [entry for entry in self.sends if entry[0] != name]

    def finish(self):
        for owner, copy in self.sends:
            copy.wait_send()
        self.sends = []


def put(g, first, n, value, lower=0):
    done = 0
    while done < value.shape[1]:
        t, offset = (lower + done) // n, (lower + done) % n
        take = min(value.shape[1] - done, n - offset)
        block = value[:, done : done + take].astype(BF)
        g[t, :, :, :, :, pl.ds(first + offset, take)] = block.reshape(g.shape[1:5] + (take,))
        done += take


def add_norm(ng, index, dgain, dshift):
    ng[index : index + 1, :] += dgain
    ng[6 + index : 7 + index, :] += dshift


def attn_backward(
    g, x, gain, ng, index, a_t, kv_t, g_t, wq, wk, wv, wo, q, k, v, o, ol, r, e_hbm, ebuf, esem, ds,
    do, dq, dk, dv, grads, n1, before_core, between, after_core, after_grads, into_keys, finish,
):
    seq = x.shape[0]

    def before(sl):
        rows = g[sl, :].astype(BF)
        g_t[:, sl] = rows.T
        do[sl, :] = (dg(rows, wo[...]) * r[sl, :].astype(F32)).astype(BF)

    rows_loop(seq, RB, before)
    put(grads, 3 * n1, n1, dg(g_t[...], o[...]))
    before_core()
    attn_back_core(q, k, v, do, o, ol, e_hbm, ebuf, esem, ds, dq, dk, dv, between)
    after_core()
    put(grads, 0, n1, dg(a_t[...], dq[...]))
    put(grads, n1, n1, dg(kv_t[...], dk[...]))
    put(grads, 2 * n1, n1, dg(kv_t[...], dv[...]))
    after_grads()

    def after(sl):
        into = dg(dq[sl, :], wq[...], NT)
        keys = dg(dk[sl, :], wk[...], NT) + dg(dv[sl, :], wv[...], NT)
        if into_keys is None:
            into = into + keys
        else:
            into_keys[sl, :] = keys
        dx, dgain, dshift = ln_back(x[sl, :].astype(F32), gain, into)
        add_norm(ng, index, dgain, dshift)
        finish(sl, g[sl, :] + dx)

    rows_loop(seq, RB, after)


def fetcher(sems):
    count = [0]

    def fetch(*pairs):
        copies = []
        for src, dst in pairs:
            cp = pltpu.make_async_copy(src, dst, sems.at[count[0]])
            count[0] += 1
            cp.start()
            copies.append(cp)
        return copies

    return fetch


def nothing():
    return None


def dec_backward(
    gains, shifts, y2_hbm, g3_hbm, y1_hbm, mem_hbm, a4_hbm, q4_hbm, k4_hbm, v4_hbm, o4_hbm, ol4_hbm, r4_hbm, e4_hbm,
    x2_hbm, x1_hbm, a1_hbm, h1_hbm, gp1_hbm, w_hbm,
    dec_o, g4_o, g1_o, up_o, down_o, sums, ng,
    y2, g3, y1, a, q, k, v, o, ol, r, cq, ck, cv, co, wu, wd,
    big, gs, do, a_t, g_t, g_up, g_down, g_cross, ebuf,
    ru1, ru2, ru3, ru4, rd1, rd2, rd3, rd4, rc1, rc2, rc3, rc4,
    rsend, rrecv, xsend, xrecv, local, isem, wsem, esem, osem,
):
    t, z, y, c = places()
    seq, width = y1.shape
    n1, n2 = cq.shape[1] // 2, wu.shape[1] // 2
    fetch = fetcher(isem)
    load, ready = weight_loader(w_hbm, wsem)
    first = fetch((y2_hbm, y2), (g3_hbm, g3))
    load("feed", 12 * n1 + 2 * n2, (wu, wd), n2, 0)
    greet(all_partners(t, z, y, c))
    halves = Exchange(xsend, xrecv, local)
    reduce = Reduce(
        sums,
        {
            "up": (g_up, ru1, ru2, ru3, ru4, rsend.at[0], rrecv.at[0], 0, True),
            "down": (g_down, rd1, rd2, rd3, rd4, rsend.at[1], rrecv.at[1], n2, True),
            "cross": (g_cross, rc1, rc2, rc3, rc4, rsend.at[2], rrecv.at[2], 2 * n2, True),
        },
    )
    ng[...] = jnp.zeros_like(ng)
    save = Saver(osem)
    wait_all(first)
    ready("feed")
    load("cross", 8 * n1 + 2 * n2, (cq, ck, cv, co), n1, 4)
    cross = fetch(
        (o4_hbm, o), (r4_hbm, r), (a4_hbm, a), (q4_hbm, q), (k4_hbm, k),
        (v4_hbm, v), (ol4_hbm, ol), (y1_hbm, y1),
    )
    first_scores(e4_hbm, ebuf, esem)
    h, du = big.at[0], big.at[1]

    def feed(sl):
        stream = y2[sl, :]
        hat, unused = ln_hat(stream)
        rows = (hat * gains[5:6, :] + shifts[5:6, :]).astype(BF)
        a_t[:, sl] = rows.T
        grad = g3[sl, :]
        g_t[:, sl] = grad.T
        out, into = stream, None
        lifted, pulled = dg(rows, columns(wu, 0, FB)), dg(grad, columns(wd, 0, FB))
        for lower in range(0, 2 * n2, FB):
            cols = pl.ds(lower, FB)
            if lower + FB < 2 * n2:
                following = dg(rows, columns(wu, lower + FB, FB)), dg(grad, columns(wd, lower + FB, FB))
            active, slope = gelu_both(lifted)
            active = active.astype(BF)
            h[sl, cols] = active
            pushed = (pulled * slope).astype(BF)
            du[sl, cols] = pushed
            out = out + dg(active, columns(wd, lower, FB), NT)
            part = dg(pushed, columns(wu, lower, FB), NT)
            into = part if into is None else into + part
            lifted, pulled = following
        g3[sl, :] = out.astype(BF)
        dx, dgain, dshift = ln_back(stream, gains[5:6, :], into)
        add_norm(ng, 5, dgain, dshift)
        gs[sl, :] = grad.astype(F32) + dx

    rows_loop(seq, RB, feed)
    dec_back = halves.back(0, g3, dec_o)
    block = width
    for j in range(2 * n2 // block):
        put(g_up, 0, n2, dg(a_t[...], du[:, pl.ds(j * block, block)]), j * block)
    reduce.move(("up", 0))
    for j in range(2 * n2 // block):
        put(g_down, 0, n2, dg(g_t[...], h[:, pl.ds(j * block, block)]), j * block)
    load("enc", 8 * n1, (wu, wd), n2, 12)
    reduce.move(("down", 0))
    wait_all(cross)
    ready("cross")
    a_t[...] = a[...].T
    memory = big.at[1, :, pl.ds(3 * width, width)]
    late = fetch((mem_hbm, memory))
    dq, dk, dv = (big.at[1, :, pl.ds(i * width, width)] for i in range(3))

    def before_core():
        reduce.move(("up", 1))

    def between():
        reduce.move(("down", 1))

    def after_core():
        wait_all(late)
        late.clear()
        late.extend(fetch((x2_hbm, r)))
        g_t[...] = memory[...].T
        late.extend(
            fetch(
                (gp1_hbm.at[:, pl.ds(0, n2)], ebuf.at[2]), (gp1_hbm.at[:, pl.ds(n2, n2)], ebuf.at[3]),
                (h1_hbm.at[:, pl.ds(0, n2)], ebuf.at[0]), (h1_hbm.at[:, pl.ds(n2, n2)], ebuf.at[1]),
            )
        )
        reduce.move(("up", 2))

    def after_grads():
        late.extend(fetch((a1_hbm, a)))
        reduce.move(("cross", 0), ("down", 2))

    def keep(sl, gradient):
        gs[sl, :] = gradient

    attn_backward(
        gs, y1, gains[4:5, :], ng, 4, a_t, g_t, g_t, cq, ck, cv, co, q, k, v, o, ol, r, e4_hbm,
        ebuf, esem, big.at[0], do, dq, dk, dv, g_cross, n1,
        before_core, between, after_core, after_grads, y2, keep,
    )
    save(gs, g4_o)
    late.extend(fetch((x1_hbm, y1)))
    reduce.move(("up", 3), ("cross", 1))
    wait_all(late)
    ready("enc")
    save.finish()

    def feed_back(sl):
        dx, dgain, dshift = ln_back(r[sl, :].astype(F32), gains[2:3, :], y2[sl, :])
        add_norm(ng, 2, dgain, dshift)
        grad = dx.astype(BF)
        g_t[:, sl] = grad.T
        a_t[:, sl] = a[sl, :].T
        into = None
        pulled = dg(grad, columns(wd, 0, FB))
        for lower in range(0, 2 * n2, FB):
            i, cols = lower // n2, pl.ds(lower % n2, FB)
            following = dg(grad, columns(wd, lower + FB, FB)) if lower + FB < 2 * n2 else None
            pushed = (pulled * ebuf[2 + i, sl, cols].astype(F32)).astype(BF)
            ebuf[2 + i, sl, cols] = pushed
            part = dg(pushed, columns(wu, lower, FB), NT)
            into = part if into is None else into + part
            pulled = following
        dx1, dgain, dshift = ln_back(y1[sl, :].astype(F32), gains[1:2, :], into)
        add_norm(ng, 1, dgain, dshift)
        gs[sl, :] = dx + dx1

    rows_loop(seq // 2, RB, feed_back)
    reduce.move(("down", 3))
    rows_loop(seq // 2, RB, lambda sl: feed_back(pl.ds(pl.multiple_of(seq // 2 + sl.start, RB), RB)))
    save(gs, g1_o)
    reduce.move(("cross", 2), ("up", 4))
    reduce.release("up")
    for i in range(2):
        for j in range(n2 // block):
            cols = pl.ds(j * block, block)
            put(g_up, 0, n2, dg(a_t[...], ebuf[2 + i, :, cols]), i * n2 + j * block)
    save(g_up, up_o)
    reduce.move(("cross", 3), ("down", 4))
    reduce.release("down")
    for i in range(2):
        for j in range(n2 // block):
            cols = pl.ds(j * block, block)
            put(g_down, 0, n2, dg(g_t[...], ebuf[i, :, cols]), i * n2 + j * block)
    save(g_down, down_o)
    reduce.move(("cross", 4))
    arrived(dec_back)
    halves.finish()
    reduce.finish()
    save.finish()


def last_backward(
    gains, ng2, masked, g4_hbm, g1_hbm, y0_hbm, a3_hbm, q3_hbm, k3_hbm, v3_hbm, o3_hbm, ol3_hbm, r3_hbm, e3_hbm,
    x_hbm, a0_hbm, q0_hbm, k0_hbm, v0_hbm, o0_hbm, ol0_hbm, r0_hbm, e0_hbm, up_hbm, down_hbm, w_hbm,
    sg_o, target_o, sums, vec,
    gs, gs1, x, x0, a, q, k, v, o, ol, r, wq, wk, wv, wo, vo, big, do, a_t, g_t, gy, ng,
    g_up, g_down, g_self, g_enc, ebuf,
    ru1, ru2, ru3, ru4, rd1, rd2, rd3, rd4, rs1, rs2, rs3, rs4, re1, re2, re3, re4, ro1, ro2, ro3, ro4, v1, vr,
    rsend, rrecv, xsend, xrecv, local, vsend, vrecv, isem, wsem, esem,
):
    t, z, y, c = places()
    seq, width = x.shape
    n1 = wq.shape[1] // 2
    n2 = g_up.shape[-1]
    fetch = fetcher(isem)
    load, ready = weight_loader(w_hbm, wsem)
    load("self out", 7 * n1, (wo,), n1, 0)
    first = fetch((g4_hbm, gs), (o3_hbm, o), (r3_hbm, r))
    ups = fetch((up_hbm, g_up), (down_hbm, g_down))
    first_scores(e3_hbm, ebuf, esem)
    second = fetch((q3_hbm, q), (k3_hbm, k), (v3_hbm, v), (ol3_hbm, ol), (a3_hbm, a), (y0_hbm, x))
    load("self", 4 * n1, (wq, wk, wv), n1, 2)
    load("enc out", 3 * n1, (vo,), n1, 8)
    late = fetch((g1_hbm, gs1), (x_hbm, x0))
    greet(all_partners(t, z, y, c))
    halves = Exchange(xsend, xrecv, local)
    reduce = Reduce(
        sums,
        {
            "up": (g_up, ru1, ru2, ru3, ru4, rsend.at[0], rrecv.at[0], 0, True),
            "down": (g_down, rd1, rd2, rd3, rd4, rsend.at[1], rrecv.at[1], n2, True),
            "self": (g_self, rs1, rs2, rs3, rs4, rsend.at[2], rrecv.at[2], 2 * n2, True),
            "enc": (
                g_enc.at[:, :, :, :, :, pl.ds(0, 3 * n1)], re1, re2, re3, re4, rsend.at[3], rrecv.at[3],
                2 * n2 + 4 * n1, True,
            ),
            "out": (
                g_enc.at[:, :, :, :, :, pl.ds(3 * n1, n1)], ro1, ro2, ro3, ro4, rsend.at[4], rrecv.at[4],
                2 * n2 + 7 * n1, False,
            ),
        },
    )
    ng[...] = ng2[...]
    wait_all(ups)
    reduce.move(("up", 0), ("down", 0))
    wait_all(first)
    ready("self out")
    dq, dk, dv = (big.at[1, :, pl.ds(i * width, width)] for i in range(3))
    ds = big.at[0]

    def before_core3():
        wait_all(second)
        a_t[...] = a[...].T
        ready("self")

    def between3():
        reduce.move(("up", 1), ("down", 1))

    def after_core3():
        late.extend(fetch((o0_hbm, o), (r0_hbm, r), (q0_hbm, q), (k0_hbm, k), (v0_hbm, v), (ol0_hbm, ol), (a0_hbm, a)))
        first_scores(e0_hbm, ebuf, esem)

    def after_grads3():
        reduce.move(("self", 0), ("up", 2))

    def last3(sl, gradient):
        gy[sl, :] = gradient.astype(BF)

    attn_backward(
        gs, x, gains[3:4, :], ng, 3, a_t, a_t, g_t, wq, wk, wv, wo, q, k, v, o, ol, r, e3_hbm,
        ebuf, esem, ds, do, dq, dk, dv, g_self, n1,
        before_core3, between3, after_core3, after_grads3, None, last3,
    )
    load("enc", 0, (wq, wk, wv), n1, 10)
    reduce.move(("down", 2), ("self", 1))
    gy_back = halves.back(0, gy, target_o)
    wait_all(late)
    ready("enc out")
    a_t[...] = a[...].T

    def before_core0():
        reduce.move(("out", 0), ("up", 3))

    def between0():
        reduce.move(("out", 1))

    def after_core0():
        reduce.move(("out", 2), ("self", 2), ("down", 3), ("up", 4))
        arrived(gy_back)
        total = jnp.zeros((1, width), F32)
        for i in range(2):
            chosen = column(masked[i : i + 1, :].astype(F32)) == 1.0
            rows = target_o[i].astype(F32)
            total = total + jnp.sum(jnp.where(chosen, rows, 0.0), axis=0, keepdims=True)
            target_o[i] = jnp.where(chosen, 0.0, rows).astype(BF)
        ng[12:13, :] = total

    def after_grads0():
        ready("enc")
        gy_back[0].wait_send()
        reduce.move(("enc", 0))

    def last0(sl, gradient):
        gy[sl, :] = gradient.astype(BF)

    attn_backward(
        gs1, x0, gains[0:1, :], ng, 0, a_t, a_t, g_t, wq, wk, wv, vo, q, k, v, o, ol, r, e0_hbm,
        ebuf, esem, ds, do, dq, dk, dv, g_enc, n1,
        before_core0, between0, after_core0, after_grads0, None, last0,
    )
    waiting = []

    def vector(s):
        for copy in waiting:
            copy.wait_recv()
        waiting.clear()
        if s == 0:
            v1[0] = ng[...]
        elif s < 4:
            v1[s] = v1[s - 1] + vr[s - 1]
        if s < 3:
            targets = ((s, (at(1 - t, z, y, c), at(t, z, y, 1 - c), at(t, z, 1 - y, c))[s]),)
        elif s == 3:
            targets = tuple((2 + j, at(t, lax.rem(z + j, 4), y, c)) for j in range(1, 4))
        else:
            targets = ()
            vec[...] = (v1[3] + vr[3]) + (vr[4] + vr[5])
        for slot, device in targets:
            copy = pltpu.make_async_remote_copy(
                src_ref=v1.at[s], dst_ref=vr.at[slot], send_sem=vsend.at[slot], recv_sem=vrecv.at[slot],
                device_id=device, device_id_type=MESH,
            )
            copy.start()
            reduce.sends.append(("vector", copy))
            waiting.append(copy)

    vector(0)
    reduce.move(("enc", 1), ("self", 3), ("out", 3))
    vector(1)
    reduce.move(("enc", 2))
    sg_back = halves.back(1, gy, sg_o)
    vector(2)
    vector(3)
    reduce.move(("down", 4), ("enc", 3))
    vector(4)
    reduce.move(("self", 4), ("out", 4), ("enc", 4))
    arrived(sg_back)
    sg_back[0].wait_send()
    reduce.finish()


def unpack(sums2, sums3, vec, *refs):
    grads, (gains_o, shifts_o, mask_o) = refs[:16], refs[16:]
    for summed, held in ((sums2, (14, 15, 10, 11, 12, 13)), (sums3, (4, 5, 6, 7, 8, 9, 0, 1, 2, 3))):
        offset = 0
        for i in held:
            n = grads[i].shape[1]
            grads[i][...] = summed[:, pl.ds(offset, n)]
            offset += n
    gains_o[...] = vec[0:6, :]
    shifts_o[...] = vec[6:12, :]
    mask_o[...] = vec[12:13, :]


def compute_all(lengths, timesteps, gains, shifts, mask_vector, masked, loss_mask, matrices, source, target, cotangent):
    rows, width = source.shape[1:]
    seq = 2 * rows
    n1 = width // 2
    part = matrices[0].shape[0]
    n2 = matrices[4].shape[1]
    total = 12 * n1 + 4 * n2
    hidden = 2 * n2
    heads = width // HD
    sd = jax.ShapeDtypeStruct
    any_spec = pl.BlockSpec(memory_space=pl.ANY)
    vmem = pl.BlockSpec(memory_space=pltpu.VMEM)
    smem = pl.BlockSpec(memory_space=pltpu.SMEM)
    dma = pltpu.SemaphoreType.DMA
    row = lambda kind: sd((seq, width), kind)
    tall = lambda kind: sd((seq, hidden), kind)
    halves = sd((2, rows, width), BF)
    escores = sd((heads, seq, seq), BF)
    vrow = lambda kind: pltpu.VMEM((seq, width), kind)
    vhalves = pltpu.VMEM((2, rows, width), BF)
    vsq = pltpu.VMEM((width, width), BF)
    vwide = pltpu.VMEM((width, hidden), BF)
    vtall = pltpu.VMEM((seq, hidden), BF)
    vsq5 = pltpu.VMEM((4, 2, 2, part, width), BF)
    vwide5 = pltpu.VMEM((4, 2, 2, part, hidden), BF)
    turned = pltpu.VMEM((width, seq), BF)
    big = pltpu.VMEM((2, seq, hidden), BF)
    ebuf = pltpu.VMEM((4, seq, seq), BF)
    grads = lambda n: pltpu.VMEM((2, 4, 2, 2, part, n), BF)

    def landing(n, split=False):
        r3 = (2, 4, 2, part, n // 2) if split else (4, part, n)
        return [
            pltpu.VMEM(dims, BF) for dims in ((2, 4, 2, part, n), (2, 4, part, n), r3, (3, part, n))
        ]

    def params(number):
        return pltpu.CompilerParams(
            vmem_limit_bytes=VMEM_LIMIT, collective_id=number, has_side_effects=True
        )

    attention = [row(BF)] * 7 + [escores]
    (
        gathered, x, y0, g3,
        a0, q0, k0, v0, o0, ol0, r0, e0, x1, a1, h1, gp1, x2, mem,
        a3, q3, k3, v3, o3, ol3, r3, e3, y1,
        a4, q4, k4, v4, o4, ol4, r4, e4, y2,
    ) = pl.pallas_call(
        forward,
        in_specs=[smem, smem] + [vmem] * 21 + [any_spec] * 3,
        out_specs=[any_spec] * 36,
        out_shape=[sd((2, 4, 2, 2, part, total), BF)] + [row(BF)] * 3
        + attention + [row(BF), row(BF), tall(BF), tall(BF), row(BF), row(BF)]
        + attention + [row(BF)]
        + attention + [row(F32)],
        scratch_shapes=[pltpu.VMEM((part, total), BF), vhalves, vhalves]
        + [vrow(BF)] * 2 + [vsq5] * 8 + [vwide5] * 2 + [vrow(BF)] * 14
        + [vrow(F32), vrow(BF), vtall, vtall, vrow(BF), vrow(BF), vrow(F32), vrow(F32), ebuf]
        + [dma((8, 11)), dma((8, 11)), dma((4,)), dma((4,)), dma((7,)), dma((20,)), dma((4,)), dma((35,))],
        compiler_params=params(0),
        name="forward",
    )(lengths, timesteps, gains, shifts, mask_vector[None], masked, loss_mask, *matrices, source, target, cotangent)
    weights = gathered.reshape(2, width, total)
    decoded, g4, g1, up, down, sums2, ng = pl.pallas_call(
        dec_backward,
        in_specs=[vmem, vmem] + [any_spec] * 18,
        out_specs=[any_spec] * 5 + [vmem] * 2,
        out_shape=[halves, row(F32), row(F32)] + [sd((2, 4, 2, 2, part, n2), BF)] * 2
        + [sd((part, 2 * n2 + 4 * n1), F32), sd((16, width), F32)],
        scratch_shapes=[vrow(F32)] + [vrow(BF)] * 9
        + [vsq] * 4 + [vwide] * 2 + [big, vrow(F32), vrow(BF)] + [turned] * 2
        + [grads(n2), grads(n2), grads(4 * n1), ebuf]
        + landing(n2, True) + landing(n2, True) + landing(4 * n1, True)
        + [dma((3, 8)), dma((3, 8)), dma((1,)), dma((1,)), dma((1,)), dma((18,)), dma((16,)), dma((4,)), dma((4,))],
        compiler_params=params(1),
        name="dec_backward",
    )(gains, shifts, y2, g3, y1, mem, a4, q4, k4, v4, o4, ol4, r4, e4, x2, x1, a1, h1, gp1, weights)
    source_grad, target_grad, sums3, vec = pl.pallas_call(
        last_backward,
        in_specs=[vmem] * 3 + [any_spec] * 23,
        out_specs=[any_spec, vmem, vmem, vmem],
        out_shape=[halves, halves, sd((part, 2 * n2 + 8 * n1), F32), sd((16, width), F32)],
        scratch_shapes=[vrow(F32)] * 2 + [vrow(BF)] * 9 + [vsq] * 5 + [big, vrow(BF)] + [turned] * 2
        + [vrow(BF), pltpu.VMEM((16, width), F32)]
        + [grads(n2), grads(n2), grads(4 * n1), grads(4 * n1), ebuf]
        + landing(n2, True) + landing(n2, True) + landing(4 * n1, True) + landing(3 * n1, True) + landing(n1)
        + [pltpu.VMEM((4, 16, width), F32), pltpu.VMEM((6, 16, width), F32)]
        + [dma((5, 8)), dma((5, 8)), dma((2,)), dma((2,)), dma((2,)), dma((6,)), dma((6,)), dma((20,)), dma((16,)), dma((4,))],
        compiler_params=params(2),
        name="last_backward",
    )(
        gains, ng, masked, g4, g1, y0, a3, q3, k3, v3, o3, ol3, r3, e3,
        x, a0, q0, k0, v0, o0, ol0, r0, e0, up, down, weights,
    )
    square, tall_square = sd((part, n1), F32), sd((part, n2), F32)
    small = pl.pallas_call(
        unpack,
        in_specs=[vmem] * 3,
        out_specs=[vmem] * 19,
        out_shape=[tall_square if i in (4, 5, 14, 15) else square for i in range(16)]
        + [sd((6, width), F32)] * 2 + [sd((1, width), F32)],
        name="unpack",
    )(sums2, sums3, vec)
    return (decoded, source_grad, target_grad, *small)


def pair_body(*arguments):
    source, target, cotangent, lengths, timesteps, masked, loss_mask = arguments[:7]
    matrices = [m.T if i in TURNED else m for i, m in enumerate(arguments[7:23])]
    norm_gains, norm_shifts, mask_vector = arguments[23:]
    outs = compute_all(
        lengths, timesteps, norm_gains, norm_shifts, mask_vector, masked, loss_mask, matrices, source, target, cotangent
    )
    grads = [g.T if i in TURNED else g for i, g in enumerate(outs[3:19])]
    return (*outs[:3], *grads, outs[19], outs[20], outs[21][0])


def solution(mesh):
    whole_pairs = dict(mesh.shape) == {"dp": 16, "tensor": 2}
    return jax.shard_map(
        pair_body if whole_pairs else body,
        mesh=mesh,
        in_specs=(
            P("dp", "tensor", None),
            P("dp", "tensor", None),
            P("dp", "tensor", None),
            P("dp"),
            P("dp"),
            P("dp", "tensor"),
            P("dp", "tensor"),
            P("dp", "tensor"),
            P("dp", "tensor"),
            P("dp", "tensor"),
            P("tensor", "dp"),
            P("dp", "tensor"),
            P("tensor", "dp"),
            P("dp", "tensor"),
            P("dp", "tensor"),
            P("dp", "tensor"),
            P("tensor", "dp"),
            P("dp", "tensor"),
            P("dp", "tensor"),
            P("dp", "tensor"),
            P("tensor", "dp"),
            P("dp", "tensor"),
            P("tensor", "dp"),
            P(),
            P(),
            P(),
        ),
        out_specs=(
            P("dp", "tensor", None),
            P("dp", "tensor", None),
            P("dp", "tensor", None),
            P("dp", "tensor"),
            P("dp", "tensor"),
            P("dp", "tensor"),
            P("tensor", "dp"),
            P("dp", "tensor"),
            P("tensor", "dp"),
            P("dp", "tensor"),
            P("dp", "tensor"),
            P("dp", "tensor"),
            P("tensor", "dp"),
            P("dp", "tensor"),
            P("dp", "tensor"),
            P("dp", "tensor"),
            P("tensor", "dp"),
            P("dp", "tensor"),
            P("tensor", "dp"),
            P(),
            P(),
            P(),
        ),
        check_vma=False,
    )
```

```python
import jax
import jax.numpy as jnp
from jax import lax
from jax.experimental import pallas as pl
from jax.experimental.pallas import tpu as pltpu
from jax.sharding import PartitionSpec as P

HD = 64
MICRO = 2
STEPS = 50


eps = 1e-05
floor_score = -1e30


def norm_rows(inputs, gain, shift):
    average = jnp.mean(inputs, axis=-1, keepdims=True)
    centred = inputs - average
    second = jnp.mean(centred * centred, axis=-1, keepdims=True)
    return centred * lax.rsqrt(second + eps) * gain + shift


def norm_back(inputs, gain, shift, gradient):
    unused, pullback = jax.vjp(norm_rows, inputs, gain, shift)
    return pullback(gradient)


def smooth(values):
    return jax.nn.gelu(values, approximate=False)


def spread(inputs):
    return lax.all_gather(inputs.astype(jnp.bfloat16), "tensor", axis=1, tiled=True)


def collect(partial_value):
    return lax.psum_scatter(partial_value, "tensor", scatter_dimension=1, tiled=True)


def spread_grad(gradient):
    return lax.all_gather(gradient.astype(jnp.bfloat16), "tensor", axis=1, tiled=True)


def collect_grad(partial_value):
    return lax.psum_scatter(partial_value, "tensor", scatter_dimension=1, tiled=True)


def project(inputs, weight):
    return jnp.einsum("bsk,kn->bsn", inputs, weight, preferred_element_type=jnp.float32)


def weight_grad(inputs, gradient):
    return jnp.einsum("bsk,bsn->kn", inputs, gradient, preferred_element_type=jnp.float32)


def back_project(gradient, weight):
    return jnp.einsum("bsn,kn->bsk", gradient, weight, preferred_element_type=jnp.float32)


def masked_scores(query_part, key_rows, live):
    scores = jnp.einsum(
        "bqhd,bkhd->bhqk", query_part, key_rows, preferred_element_type=jnp.float32
    ) * HD ** (-0.5)
    return jnp.where(live[:, None, None, :], scores, floor_score)


def attend_forward(query_in, keys_in, w_query, w_key, w_value, live):
    pair_count, length = (query_in.shape[0], query_in.shape[1])
    head_count = w_query.shape[1] // HD
    queries = (
        project(query_in, w_query).astype(jnp.bfloat16).reshape(pair_count, length, head_count, HD)
    )
    key_rows = (
        project(keys_in, w_key).astype(jnp.bfloat16).reshape(pair_count, length, head_count, HD)
    )
    value_rows = (
        project(keys_in, w_value).astype(jnp.bfloat16).reshape(pair_count, length, head_count, HD)
    )
    block_rows = min(512, length)
    pieces = []
    totals = []
    for offset in range(0, length, block_rows):
        scores = masked_scores(queries[:, offset : offset + block_rows], key_rows, live)
        highest = jnp.max(scores, axis=-1, keepdims=True)
        exponent = jnp.exp(scores - highest)
        summed = jnp.sum(exponent, axis=-1, keepdims=True)
        softmax = (exponent / summed).astype(jnp.bfloat16)
        pieces.append(
            jnp.einsum("bhqk,bkhd->bqhd", softmax, value_rows, preferred_element_type=jnp.float32)
        )
        totals.append(highest + jnp.log(summed))
    attended = (
        jnp.concatenate(pieces, axis=1)
        .astype(jnp.bfloat16)
        .reshape(pair_count, length, head_count * HD)
    )
    return (queries, key_rows, value_rows, attended, jnp.concatenate(totals, axis=2))


def attend_backward(whole_grad, query_in, keys_in, w_query, w_key, w_value, w_out, saved, live):
    queries, key_rows, value_rows, attended, totals = saved
    pair_count, length, head_count = (queries.shape[0], queries.shape[1], queries.shape[2])
    scale_score = HD ** (-0.5)
    out_grad = weight_grad(attended, whole_grad)
    head_grad = (
        back_project(whole_grad, w_out)
        .astype(jnp.bfloat16)
        .reshape(pair_count, length, head_count, HD)
    )
    block_rows = min(512, length)
    key_total = jnp.zeros(key_rows.shape, jnp.float32)
    value_total = jnp.zeros(value_rows.shape, jnp.float32)
    query_parts = []
    for offset in range(0, length, block_rows):
        query_part = queries[:, offset : offset + block_rows]
        grad_part = head_grad[:, offset : offset + block_rows]
        scores = masked_scores(query_part, key_rows, live)
        softmax = jnp.exp(scores - totals[:, :, offset : offset + block_rows])
        value_total = value_total + jnp.einsum(
            "bhqk,bqhd->bkhd",
            softmax.astype(jnp.bfloat16),
            grad_part,
            preferred_element_type=jnp.float32,
        )
        soft_grad = jnp.einsum(
            "bqhd,bkhd->bhqk", grad_part, value_rows, preferred_element_type=jnp.float32
        )
        inner = jnp.sum(softmax * soft_grad, axis=-1, keepdims=True)
        score_grad = (softmax * (soft_grad - inner)).astype(jnp.bfloat16)
        query_parts.append(
            jnp.einsum("bhqk,bkhd->bqhd", score_grad, key_rows, preferred_element_type=jnp.float32)
            * scale_score
        )
        key_total = (
            key_total
            + jnp.einsum(
                "bhqk,bqhd->bkhd", score_grad, query_part, preferred_element_type=jnp.float32
            )
            * scale_score
        )
    query_grad = (
        jnp.concatenate(query_parts, axis=1)
        .astype(jnp.bfloat16)
        .reshape(pair_count, length, head_count * HD)
    )
    key_grad = key_total.astype(jnp.bfloat16).reshape(
        pair_count, key_rows.shape[1], head_count * HD
    )
    value_grad = value_total.astype(jnp.bfloat16).reshape(
        pair_count, value_rows.shape[1], head_count * HD
    )
    grads = (
        weight_grad(query_in, query_grad),
        weight_grad(keys_in, key_grad),
        weight_grad(keys_in, value_grad),
        out_grad,
    )
    into_keys = back_project(key_grad, w_key) + back_project(value_grad, w_value)
    return (grads, back_project(query_grad, w_query), into_keys)


def feed_forward(inputs, w_up, w_down):
    lifted = project(inputs, w_up)
    active = smooth(lifted).astype(jnp.bfloat16)
    return (lifted, active, project(active, w_down))


def feed_backward(gradient, inputs, w_up, w_down, lifted, active):
    down_grad = weight_grad(active, gradient)
    active_grad = back_project(gradient, w_down)
    unused, smooth_back = jax.vjp(smooth, lifted)
    lifted_grad = smooth_back(active_grad)[0].astype(jnp.bfloat16)
    return ((weight_grad(inputs, lifted_grad), down_grad), back_project(lifted_grad, w_up))


def body(
    source,
    target,
    cotangent,
    lengths,
    timesteps,
    masked,
    loss_mask,
    enc_query,
    enc_key,
    enc_value,
    enc_out,
    enc_up,
    enc_down,
    self_query,
    self_key,
    self_value,
    self_out,
    cross_query,
    cross_key,
    cross_value,
    cross_out,
    dec_up,
    dec_down,
    norm_gains,
    norm_shifts,
    mask_vector,
):
    pairs_dev, rows_dev = (source.shape[0], source.shape[1])
    per_micro = pairs_dev // MICRO
    seq_len = rows_dev * lax.axis_size("tensor")
    positions = jnp.arange(seq_len)
    gains, shifts = (norm_gains, norm_shifts)
    gain_total = jnp.zeros(norm_gains.shape, jnp.float32)
    shift_total = jnp.zeros(norm_shifts.shape, jnp.float32)
    mask_total = jnp.zeros(mask_vector.shape, jnp.float32)
    decoded_parts = []
    source_parts = []
    target_parts = []
    running = None
    for micro in range(MICRO):
        weights = (
            lax.all_gather(enc_query, "dp", axis=0, tiled=True),
            lax.all_gather(enc_key, "dp", axis=0, tiled=True),
            lax.all_gather(enc_value, "dp", axis=0, tiled=True),
            lax.all_gather(enc_out, "dp", axis=1, tiled=True),
            lax.all_gather(enc_up, "dp", axis=0, tiled=True),
            lax.all_gather(enc_down, "dp", axis=1, tiled=True),
            lax.all_gather(self_query, "dp", axis=0, tiled=True),
            lax.all_gather(self_key, "dp", axis=0, tiled=True),
            lax.all_gather(self_value, "dp", axis=0, tiled=True),
            lax.all_gather(self_out, "dp", axis=1, tiled=True),
            lax.all_gather(cross_query, "dp", axis=0, tiled=True),
            lax.all_gather(cross_key, "dp", axis=0, tiled=True),
            lax.all_gather(cross_value, "dp", axis=0, tiled=True),
            lax.all_gather(cross_out, "dp", axis=1, tiled=True),
            lax.all_gather(dec_up, "dp", axis=0, tiled=True),
            lax.all_gather(dec_down, "dp", axis=1, tiled=True),
        )
        wide = (
            lax.all_gather(weights[4], "tensor", axis=1, tiled=True),
            lax.all_gather(weights[5], "tensor", axis=0, tiled=True),
            lax.all_gather(weights[14], "tensor", axis=1, tiled=True),
            lax.all_gather(weights[15], "tensor", axis=0, tiled=True),
        )
        lower = micro * per_micro
        upper = lower + per_micro
        live = positions[None, :] < lengths[lower:upper][:, None]
        every = jnp.ones((per_micro, seq_len), bool)
        inputs_x = source[lower:upper].astype(jnp.float32)
        rows0 = spread(norm_rows(inputs_x, gains[0], shifts[0]))
        saved0 = attend_forward(rows0, rows0, weights[0], weights[1], weights[2], live)
        stream1 = inputs_x + collect(project(saved0[3], weights[3]))
        normed1 = norm_rows(stream1, gains[1], shifts[1])
        rows1 = normed1.astype(jnp.bfloat16)
        lifted1, active1, partial1 = feed_forward(rows1, wide[0], wide[1])
        stream2 = stream1 + partial1
        memory_rows = spread(norm_rows(stream2, gains[2], shifts[2]))
        chosen = masked[lower:upper][:, :, None] == 1
        start_y = jnp.where(chosen, mask_vector, target[lower:upper].astype(jnp.float32))
        rows3 = spread(norm_rows(start_y, gains[3], shifts[3]))
        saved3 = attend_forward(rows3, rows3, weights[6], weights[7], weights[8], every)
        stream4 = start_y + collect(project(saved3[3], weights[9]))
        rows4 = spread(norm_rows(stream4, gains[4], shifts[4]))
        saved4 = attend_forward(rows4, memory_rows, weights[10], weights[11], weights[12], live)
        stream5 = stream4 + collect(project(saved4[3], weights[13]))
        normed5 = norm_rows(stream5, gains[5], shifts[5])
        rows5 = normed5.astype(jnp.bfloat16)
        lifted5, active5, partial5 = feed_forward(rows5, wide[2], wide[3])
        stream6 = stream5 + partial5
        decoded_parts.append(stream6.astype(jnp.bfloat16))
        factor = (STEPS + 1 - timesteps[lower:upper]).astype(jnp.float32) / STEPS
        grad6 = (
            cotangent[lower:upper].astype(jnp.float32)
            * (factor[:, None] * loss_mask[lower:upper].astype(jnp.float32))[:, :, None]
        )
        (up5, down5), into5 = feed_backward(
            grad6.astype(jnp.bfloat16), rows5, wide[2], wide[3], lifted5, active5
        )
        back5 = norm_back(stream5, gains[5], shifts[5], into5)
        grad5 = grad6 + back5[0]
        grads4, query_term4, memory_term = attend_backward(
            spread_grad(grad5),
            rows4,
            memory_rows,
            weights[10],
            weights[11],
            weights[12],
            weights[13],
            saved4,
            live,
        )
        back4 = norm_back(stream4, gains[4], shifts[4], collect_grad(query_term4))
        grad4 = grad5 + back4[0]
        memory_grad = collect_grad(memory_term)
        grads3, query_term3, keys_term3 = attend_backward(
            spread_grad(grad4),
            rows3,
            rows3,
            weights[6],
            weights[7],
            weights[8],
            weights[9],
            saved3,
            every,
        )
        back3 = norm_back(start_y, gains[3], shifts[3], collect_grad(query_term3 + keys_term3))
        grad_y = grad4 + back3[0]
        target_parts.append(jnp.where(chosen, 0.0, grad_y).astype(jnp.bfloat16))
        mask_total = mask_total + jnp.sum(jnp.where(chosen, grad_y, 0.0), axis=(0, 1))
        back2 = norm_back(stream2, gains[2], shifts[2], memory_grad)
        grad2 = back2[0]
        (up1, down1), into1 = feed_backward(
            grad2.astype(jnp.bfloat16), rows1, wide[0], wide[1], lifted1, active1
        )
        back1 = norm_back(stream1, gains[1], shifts[1], into1)
        grad1 = grad2 + back1[0]
        grads0, query_term0, keys_term0 = attend_backward(
            spread_grad(grad1),
            rows0,
            rows0,
            weights[0],
            weights[1],
            weights[2],
            weights[3],
            saved0,
            live,
        )
        back0 = norm_back(inputs_x, gains[0], shifts[0], collect_grad(query_term0 + keys_term0))
        source_parts.append((grad1 + back0[0]).astype(jnp.bfloat16))
        gain_total = gain_total + jnp.stack(
            [back0[1], back1[1], back2[1], back3[1], back4[1], back5[1]]
        )
        shift_total = shift_total + jnp.stack(
            [back0[2], back1[2], back2[2], back3[2], back4[2], back5[2]]
        )
        up1, down1, up5, down5 = (
            lax.psum_scatter(
                up1.astype(jnp.bfloat16), "tensor", scatter_dimension=1, tiled=True
            ).astype(jnp.float32),
            lax.psum_scatter(
                down1.astype(jnp.bfloat16), "tensor", scatter_dimension=0, tiled=True
            ).astype(jnp.float32),
            lax.psum_scatter(
                up5.astype(jnp.bfloat16), "tensor", scatter_dimension=1, tiled=True
            ).astype(jnp.float32),
            lax.psum_scatter(
                down5.astype(jnp.bfloat16), "tensor", scatter_dimension=0, tiled=True
            ).astype(jnp.float32),
        )
        fresh = (
            grads0[0],
            grads0[1],
            grads0[2],
            grads0[3],
            up1,
            down1,
            grads3[0],
            grads3[1],
            grads3[2],
            grads3[3],
            grads4[0],
            grads4[1],
            grads4[2],
            grads4[3],
            up5,
            down5,
        )
        running = fresh if micro == 0 else jax.tree.map(jnp.add, running, tuple(fresh))
    running = (
        lax.psum_scatter(
            running[0].astype(jnp.bfloat16), "dp", scatter_dimension=0, tiled=True
        ).astype(jnp.float32),
        lax.psum_scatter(
            running[1].astype(jnp.bfloat16), "dp", scatter_dimension=0, tiled=True
        ).astype(jnp.float32),
        lax.psum_scatter(
            running[2].astype(jnp.bfloat16), "dp", scatter_dimension=0, tiled=True
        ).astype(jnp.float32),
        lax.psum_scatter(
            running[3].astype(jnp.bfloat16), "dp", scatter_dimension=1, tiled=True
        ).astype(jnp.float32),
        lax.psum_scatter(
            running[4].astype(jnp.bfloat16), "dp", scatter_dimension=0, tiled=True
        ).astype(jnp.float32),
        lax.psum_scatter(
            running[5].astype(jnp.bfloat16), "dp", scatter_dimension=1, tiled=True
        ).astype(jnp.float32),
        lax.psum_scatter(
            running[6].astype(jnp.bfloat16), "dp", scatter_dimension=0, tiled=True
        ).astype(jnp.float32),
        lax.psum_scatter(
            running[7].astype(jnp.bfloat16), "dp", scatter_dimension=0, tiled=True
        ).astype(jnp.float32),
        lax.psum_scatter(
            running[8].astype(jnp.bfloat16), "dp", scatter_dimension=0, tiled=True
        ).astype(jnp.float32),
        lax.psum_scatter(
            running[9].astype(jnp.bfloat16), "dp", scatter_dimension=1, tiled=True
        ).astype(jnp.float32),
        lax.psum_scatter(
            running[10].astype(jnp.bfloat16), "dp", scatter_dimension=0, tiled=True
        ).astype(jnp.float32),
        lax.psum_scatter(
            running[11].astype(jnp.bfloat16), "dp", scatter_dimension=0, tiled=True
        ).astype(jnp.float32),
        lax.psum_scatter(
            running[12].astype(jnp.bfloat16), "dp", scatter_dimension=0, tiled=True
        ).astype(jnp.float32),
        lax.psum_scatter(
            running[13].astype(jnp.bfloat16), "dp", scatter_dimension=1, tiled=True
        ).astype(jnp.float32),
        lax.psum_scatter(
            running[14].astype(jnp.bfloat16), "dp", scatter_dimension=0, tiled=True
        ).astype(jnp.float32),
        lax.psum_scatter(
            running[15].astype(jnp.bfloat16), "dp", scatter_dimension=1, tiled=True
        ).astype(jnp.float32),
    )
    vectors = lax.psum((gain_total, shift_total, mask_total), ("dp", "tensor"))
    return (
        jnp.concatenate(decoded_parts, axis=0),
        jnp.concatenate(source_parts, axis=0),
        jnp.concatenate(target_parts, axis=0),
        running[0],
        running[1],
        running[2],
        running[3],
        running[4],
        running[5],
        running[6],
        running[7],
        running[8],
        running[9],
        running[10],
        running[11],
        running[12],
        running[13],
        running[14],
        running[15],
        vectors[0],
        vectors[1],
        vectors[2],
    )


F32 = jnp.float32
BF = jnp.bfloat16
LOG2E = 1.4426950408889634
LN2 = 0.6931471805599453
NN = (((1,), (0,)), ((), ()))
NT = (((1,), (1,)), ((), ()))
MESH = pl.DeviceIdType.MESH
RB = 512
FB = 256
VMEM_LIMIT = 63 * 2**20


def dg(left, right, dims=NN):
    return lax.dot_general(left, right, dims, preferred_element_type=F32)


def ln_hat(x):
    centred = x - jnp.mean(x, axis=-1, keepdims=True)
    rstd = lax.rsqrt(jnp.mean(centred * centred, axis=-1, keepdims=True) + eps)
    return centred * rstd, rstd


def ln_back(x, gain, gradient):
    hat, rstd = ln_hat(x)
    scaled = gradient * gain
    first = jnp.mean(scaled, axis=-1, keepdims=True)
    second = jnp.mean(scaled * hat, axis=-1, keepdims=True)
    dx = rstd * (scaled - first - hat * second)
    dgain = jnp.sum(gradient * hat, axis=0, keepdims=True)
    dshift = jnp.sum(gradient, axis=0, keepdims=True)
    return dx, dgain, dshift


def gelu_both(u):
    size = jnp.abs(u)
    t = 1.0 / (1.0 + (0.3275911 * 0.7071067811865476) * size)
    ex = jnp.exp2(u * u * (-0.5 * LOG2E))
    poly = t * (
        0.127414796
        + t * (-0.142248368 + t * (0.7107068705 + t * (-0.7265760135 + t * 0.5307027145)))
    )
    tail = poly * ex
    phi = jnp.where(u > 0, 1.0 - tail, tail)
    return u * phi, phi + u * ex * 0.3989422804014327


def rows_loop(total, step, run):
    def once(i, carry):
        run(pl.ds(pl.multiple_of(i * step, step), step))
        return carry

    lax.fori_loop(0, total // step, once, 0)


def load_weight(w_hbm, offset, width, dst, sems, base):
    copies = []
    for t in range(2):
        src = pl.ds(offset, width)
        to = pl.ds(t * width, width)
        cp = pltpu.make_async_copy(
            w_hbm.at[t, :, src] if len(w_hbm.shape) == 3 else w_hbm.at[t, :, :, :, :, src],
            dst.at[:, to] if len(dst.shape) == 2 else dst.at[:, :, :, :, to],
            sems.at[base + t],
        )
        cp.start()
        copies.append(cp)
    return copies


def wait_all(copies):
    for cp in copies:
        cp.wait()


def columns(ref, lower, width):
    value = ref[..., pl.ds(lower, width)]
    return value if value.ndim == 2 else value.reshape(-1, width)


def whole(ref):
    value = ref[...]
    return value if value.ndim == 2 else value.reshape(-1, value.shape[-1])


def normalize(x, gain, shift, a):
    def run(sl):
        hat, unused = ln_hat(x[sl, :].astype(F32))
        a[sl, :] = (hat * gain + shift).astype(BF)

    rows_loop(x.shape[0], RB, run)


def product_into(a, w, to, scale):
    def run(sl):
        value = dg(a[sl, :], whole(w))
        to[sl, :] = (value if scale is None else value * scale).astype(BF)

    rows_loop(a.shape[0], RB, run)


def attn_project(a, kv, wq, wk, wv, q, k, v):
    product_into(a, wq, q, LOG2E * HD**-0.5)
    product_into(kv, wk, k, None)
    product_into(kv, wv, v, None)


def score_copy(p, h, e_hbm, ebuf, esem):
    slot = lax.rem(p, 2) * 2 + h
    return pltpu.make_async_copy(ebuf.at[slot], e_hbm.at[2 * p + h], esem.at[slot])


def drain_scores(e_hbm, ebuf, esem):
    for p in range(2):
        for h in range(2):
            score_copy(p, h, e_hbm, ebuf, esem).wait()


def attn_core(length, q, k, v, o, ol, r, e_hbm, ebuf, esem, between, fresh):
    seq = q.shape[0]
    pairs = q.shape[1] // 128
    block = 256
    lane = lax.broadcasted_iota(jnp.int32, (1, 128), 1)
    low = lane < 64
    one = jnp.ones((), BF)
    key = lax.broadcasted_iota(jnp.int32, (seq, 1), 0)
    bias = jnp.where(key < length, 0.0, floor_score).astype(F32)
    items = [(b, h) for b in range(seq // block) for h in range(2)]

    def pair(p, carry):
        @pl.when((p > 1) if fresh else (p >= 0))
        def unused_wait():
            score_copy(p, 0, e_hbm, ebuf, esem).wait()
            score_copy(p, 1, e_hbm, ebuf, esem).wait()

        base = lax.rem(p, 2) * 2
        cols = pl.ds(pl.multiple_of(p * 128, 128), 128)
        kp = k[:, cols].astype(F32)
        vp = v[:, cols]
        ka = (
            jnp.where(low, kp, jnp.where(lane == 64, bias, 0.0)).astype(BF),
            jnp.where(low, jnp.where(lane == 0, bias, 0.0), kp).astype(BF),
        )
        va = jnp.where(low, vp, one), jnp.where(low, one, vp)

        def scores(b, h):
            qp = q[pl.ds(b * block, block), cols]
            return dg(jnp.where(low, qp, one) if h == 0 else jnp.where(low, one, qp), ka[h], NT)

        parts = []
        s = scores(*items[0])
        for n, (b, h) in enumerate(items):
            sl = pl.ds(b * block, block)
            following = scores(*items[n + 1]) if n + 1 < len(items) else None
            e = jnp.exp2(s - jnp.max(s, axis=-1, keepdims=True)).astype(BF)
            ebuf[base + h, sl, :] = e
            parts.append(dg(e, va[h]))
            s = following
            if h == 1:
                first, second = parts
                parts = []
                inverse = 1.0 / pltpu.roll(jnp.where(low, second, first), 64, 1)
                r[sl, cols] = inverse.astype(BF)
                joined = jnp.where(low, first, second) * inverse
                rounded = joined.astype(BF)
                o[sl, cols] = rounded
                ol[sl, cols] = (joined - rounded.astype(F32)).astype(BF)
        score_copy(p, 0, e_hbm, ebuf, esem).start()
        score_copy(p, 1, e_hbm, ebuf, esem).start()
        return carry

    lax.fori_loop(0, pairs // 2, pair, 0)
    between()
    lax.fori_loop(pairs // 2, pairs, pair, 0)


def attn_join(x, o, wo, y, lowered):
    def run(sl):
        joined = x[sl, :].astype(F32) + dg(o[sl, :], whole(wo), NT)
        y[sl, :] = joined
        if lowered is not None:
            lowered[sl, :] = joined.astype(BF)

    rows_loop(x.shape[0], RB, run)


def first_scores(e_hbm, ebuf, esem):
    for h in range(2):
        pltpu.make_async_copy(e_hbm.at[h], ebuf.at[h], esem.at[h]).start()


def attn_back_core(q, k, v, do, o, ol, e_hbm, ebuf, esem, ds, dq, dk, dv, between):
    seq = q.shape[0]
    heads = e_hbm.shape[0]
    block = 512
    lane = lax.broadcasted_iota(jnp.int32, (1, 128), 1)
    low = lane < 64
    zero = jnp.zeros((), BF)
    one = jnp.ones((), BF)
    row2 = lax.broadcasted_iota(jnp.int32, (256, 128), 0)
    col2 = lax.broadcasted_iota(jnp.int32, (256, 128), 1)
    swap = jnp.where(((row2 // 64) % 2) != (col2 // 64), 1.0, 0.0).astype(BF)

    def fetch(p, h):
        slot = lax.rem(p, 2) * 2 + h
        return pltpu.make_async_copy(e_hbm.at[2 * p + h], ebuf.at[slot], esem.at[slot])

    def pair(p, carry):
        cols = pl.ds(pl.multiple_of(p * 128, 128), 128)
        fetch(p, 0).wait()
        fetch(p, 1).wait()

        @pl.when(p + 1 < heads // 2)
        def unused_fetch():
            fetch(p + 1, 0).start()
            fetch(p + 1, 1).start()

        base = lax.rem(p, 2) * 2
        qp, kp, vp, dop = q[:, cols], k[:, cols], v[:, cols], do[:, cols]
        product = dop.astype(F32) * (o[:, cols].astype(F32) + ol[:, cols].astype(F32))
        high = product.astype(BF)
        rest = (product - high.astype(F32)).astype(BF)
        inner = -dg(jnp.concatenate([high, rest], axis=1), swap)
        inner_high = inner.astype(BF)
        inner_rest = (inner - inner_high.astype(F32)).astype(BF)
        do_t, q_t = dop.T, qp.T
        lhs = (
            jnp.where(low, dop, jnp.where(lane == 64, inner_high, inner_rest)),
            jnp.where(low, jnp.where(lane == 0, inner_high, inner_rest), dop),
        )
        va = (
            jnp.where(low, vp, jnp.where(lane < 66, one, zero)),
            jnp.where(low, jnp.where(lane < 2, one, zero), vp),
        )
        km = jnp.concatenate([jnp.where(low, kp, zero), jnp.where(low, zero, kp)], axis=0)
        dvs = [dg(do_t, ebuf[base + h])[64 * h : 64 * h + 64] for h in range(2)]
        for h in range(2):
            for b in range(seq // block):
                sl = pl.ds(b * block, block)
                t = dg(lhs[h][b * block : (b + 1) * block], va[h], NT)
                ds[sl, pl.ds(h * seq, seq)] = ebuf[base + h, sl, :] * t.astype(BF)
        dks = [dg(q_t, ds[:, pl.ds(h * seq, seq)])[64 * h : 64 * h + 64] for h in range(2)]
        dq_sum = dg(ds[...], km)
        dq[:, cols] = (dq_sum * HD**-0.5).astype(BF)
        dk[:, cols] = (jnp.concatenate(dks, axis=0) * LN2).astype(BF).T
        dv[:, cols] = jnp.concatenate(dvs, axis=0).astype(BF).T
        return carry

    lax.fori_loop(0, heads // 4, pair, 0)
    between()
    lax.fori_loop(heads // 4, heads // 2, pair, 0)


def places():
    d = lax.axis_index("dp")
    return lax.axis_index("tensor"), d // 4, (d // 2) % 2, d % 2


def at(t, z, y, c):
    return (z * 4 + y * 2 + c, t)


def greet(partners):
    barrier = pltpu.get_barrier_semaphore()
    for device in partners:
        pl.semaphore_signal(barrier, inc=1, device_id=device, device_id_type=MESH)
    pl.semaphore_wait(barrier, len(partners))


def all_partners(t, z, y, c):
    others = [at(t, lax.rem(z + j, 4), y, c) for j in range(1, 4)]
    return [at(t, z, y, 1 - c), at(1 - t, z, y, c), at(t, z, 1 - y, c)] + others


class Saver:
    def __init__(self, sems):
        self.sems, self.count, self.live = sems, 0, []

    def __call__(self, src, dst, slot=None):
        cp = pltpu.make_async_copy(src, dst, self.sems.at[self.count])
        cp.start()
        self.count += 1
        self.live.append((slot, cp))

    def free(self, slot):
        for name, cp in self.live:
            if name == slot:
                cp.wait()
        self.live = [entry for entry in self.live if entry[0] != slot]

    def finish(self):
        for name, cp in self.live:
            cp.wait()
        self.live = []


GATHER_PLAN = (
    ((0, 0), (1, 0), (2, 0), (4, 0), (5, 0), (6, 0)),
    ((0, 1), (1, 1), (3, 0)),
    ((0, 2),),
    ((1, 2), (2, 1), (3, 1)),
    ((7, 0),),
    ((0, 3), (0, 4), (1, 3), (1, 4), (2, 2), (4, 1)),
    (),
    ((3, 2), (5, 1)),
    ((7, 1),),
    ((2, 3), (2, 4)),
    ((4, 2),),
    (),
    ((5, 2), (6, 1), (7, 2)),
    ((3, 3), (4, 3)),
    ((3, 4), (4, 4)),
    ((5, 3),),
    ((5, 4), (6, 2)),
    (),
    (),
    ((6, 3), (7, 3)),
    (),
    ((6, 4), (7, 4)),
)
GATHER_ORDERS = (
    ("zxy",), ("zxy",), ("zxy",), ("xyz",), ("zxy", "zyx"), ("zxy", "zyx"), ("zxy", "zyx"), ("xyz",),
)


class Gather:
    def __init__(self, own, out, send, recv, widths):
        self.own, self.out, self.send, self.recv = own, out, send, recv
        self.starts = [sum(widths[:i]) for i in range(len(widths))]
        self.widths = widths
        self.spot = places()
        self.sends, self.pending = [], {}

    def push(self, src, dst, k, i, device):
        copy = pltpu.make_async_remote_copy(
            src_ref=src, dst_ref=dst, send_sem=self.send.at[k, i], recv_sem=self.recv.at[k, i],
            device_id=device, device_id_type=MESH,
        )
        copy.start()
        self.sends.append(copy)
        self.pending.setdefault(k, []).append(copy)

    def move(self, point):
        for k, s in GATHER_PLAN[point]:
            self.stage(k, s)

    def stage(self, k, s):
        t, z, y, c = self.spot
        every = slice(None)
        for copy in self.pending.pop(k, ()):
            copy.wait_recv()
        if s == 3:
            a = self.out.at[:, :, :, c, :, pl.ds(self.starts[k], self.widths[k])]
            self.push(a, a, k, 10, at(t, z, y, 1 - c))
        if s > 2:
            return
        orders = GATHER_ORDERS[k]
        width = self.widths[k] // len(orders)
        for i, order in enumerate(orders):
            cols = pl.ds(self.starts[k] + i * width, width)
            known = order[:s]
            dst = self.out.at[
                every if "x" in known else t, every if "z" in known else z, every if "y" in known else y, c, :, cols
            ]
            src = self.own.at[:, cols] if s == 0 else dst
            if order[s] == "z":
                for j in range(1, 4):
                    self.push(src, dst, k, 5 * i + j - 1, at(t, lax.rem(z + j, 4), y, c))
            elif order[s] == "x":
                self.push(src, dst, k, 5 * i + 3, at(1 - t, z, y, c))
            else:
                self.push(src, dst, k, 5 * i + 4, at(t, z, 1 - y, c))

    def finish(self):
        for copy in self.sends:
            copy.wait_send()


class Exchange:
    def __init__(self, send, recv, local):
        self.send, self.recv, self.local = send, recv, local
        self.open = []

    def start(self, i, src, kept, dst):
        t, z, y, c = places()
        far = pltpu.make_async_remote_copy(
            src_ref=src, dst_ref=dst, send_sem=self.send.at[i], recv_sem=self.recv.at[i],
            device_id=at(1 - t, z, y, c), device_id_type=MESH,
        )
        near = pltpu.make_async_copy(kept, dst, self.local.at[i])
        far.start()
        near.start()
        self.open.append(far)
        return far, near

    def give(self, i, halves, dst, part=0, parts=1):
        t = lax.axis_index("tensor")
        rows = halves.shape[1]
        take = rows // parts
        mine = dst.at[pl.ds(pl.multiple_of(t * rows + part * take, take), take), :]
        some = pl.ds(part * take, take)
        return self.start(i, halves.at[1 - t, some, :], halves.at[t, some, :], mine)

    def back(self, i, pair, dst):
        t = lax.axis_index("tensor")
        rows = dst.shape[1]
        kept = pair.at[pl.ds(pl.multiple_of(t * rows, rows), rows), :]
        sent = pair.at[pl.ds(pl.multiple_of((1 - t) * rows, rows), rows), :]
        return self.start(i, sent, kept, dst.at[t])

    def finish(self):
        for far in self.open:
            far.wait_send()


def arrived(copies):
    far, near = copies
    near.wait()
    far.wait_recv()


def column(values):
    return jnp.broadcast_to(values, (128, values.shape[1])).T[:, :1]


def weight_loader(w_hbm, sems):
    loads = {}

    def load(name, offset, refs, n, base):
        loads[name] = []
        for i, ref in enumerate(refs):
            loads[name] += load_weight(w_hbm, offset + i * n, n, ref, sems, base + 2 * i)

    def ready(name):
        wait_all(loads[name])

    return load, ready


TURNED = (3, 5, 9, 13, 15)
PACKED = (0, 1, 2, 3, 6, 7, 8, 9, 4, 5, 10, 11, 12, 13, 14, 15)


def forward(
    lengths, timesteps, gains, shifts, mask_row, masked, loss_mask, *refs,
):
    matrices, refs = refs[:16], refs[16:]
    (
        src_hbm, target_hbm, cot_hbm,
        w_hbm, x_o, y0_o, g3_o,
        a0_o, q0_o, k0_o, v0_o, o0_o, ol0_o, r0_o, e0_o, x1_o, a1_o, h1_o, gp1_o, x2_o, mem_o,
        a3_o, q3_o, k3_o, v3_o, o3_o, ol3_o, r3_o, e3_o, y1_o,
        a4_o, q4_o, k4_o, v4_o, o4_o, ol4_o, r4_o, e4_o, y2_o,
        own, tgt, cot, x, y0, wq, wk, wv, wo, sq, sk, sv, so, wu, wd,
        a, q, k, v, o, ol, r, a3, q3, k3, v3, o3, ol3, r3,
        x1, a1, h, gp, x2, mem, y1, y2, ebuf,
        gsend, grecv, xsend, xrecv, local, wsem, esem, osem,
    ) = refs
    t, z, y, c = places()
    seq, width = x.shape
    n1, n2 = width // 2, h.shape[1] // 2
    in_tgt = pltpu.make_async_copy(target_hbm, tgt, local.at[5])
    in_cot = pltpu.make_async_copy(cot_hbm, cot, local.at[6])
    in_tgt.start()
    in_cot.start()
    offset = 0
    for i in PACKED:
        part = matrices[i][...]
        own[:, pl.ds(offset, part.shape[1])] = part
        offset += part.shape[1]
    greet(all_partners(t, z, y, c))
    halves = Exchange(xsend, xrecv, local)
    gather = Gather(own, w_hbm, gsend, grecv, (2 * n1, 2 * n1, 4 * n1, n2, n2, 4 * n1, n2, n2))
    mine = pltpu.make_async_copy(own, w_hbm.at[t, z, y, c], local.at[4])
    mine.start()
    gather.move(0)
    x_in = [halves.give(0, src_hbm, x, 0, 2)]
    save = Saver(osem)
    in_tgt.wait()
    for i in range(2):
        chosen = column(masked[i : i + 1, :].astype(F32)) == 1.0
        tgt[i] = jnp.where(chosen, mask_row[...], tgt[i].astype(F32)).astype(BF)
    mine.wait()
    gather.move(1)
    in_cot.wait()
    for i in range(2):
        factor = (STEPS + 1 - timesteps[i]).astype(F32) / STEPS
        weight = column(loss_mask[i : i + 1, :].astype(F32)) * factor
        cot[i] = (cot[i].astype(F32) * weight).astype(BF)
    gather.move(2)
    x_in.append(halves.give(3, src_hbm, x, 1, 2))
    gather.move(3)
    for copies in x_in:
        arrived(copies)
    normalize(x, gains[0:1, :], shifts[0:1, :], a)
    save(x, x_o, "x")
    save(a, a0_o, "A")
    gather.move(4)
    gather.move(5)
    load, ready = weight_loader(w_hbm, wsem)
    load("enc", 0, (wq, wk), n1, 0)
    load("out", 2 * n1, (wv, wo), n1, 4)
    ready("enc")
    product_into(a, wq, q, LOG2E * HD**-0.5)
    product_into(a, wk, k, None)
    gather.move(6)
    y0_in = halves.give(1, tgt, y0)
    ready("out")
    product_into(a, wv, v, None)
    for src, dst in ((q, q0_o), (k, k0_o), (v, v0_o)):
        save(src, dst, "A")
    gather.move(7)
    length = lengths[t]

    def between0():
        gather.move(8)

    attn_core(length, q, k, v, o, ol, r, e0_o, ebuf, esem, between0, True)
    gather.move(9)
    load("self", 4 * n1, (sq, sk, sv, so), n1, 8)
    for src, dst in ((o, o0_o), (ol, ol0_o), (r, r0_o)):
        save(src, dst, "A")
    arrived(y0_in)
    save(y0, y0_o, "y0")
    normalize(y0, gains[3:4, :], shifts[3:4, :], a3)
    gather.move(10)
    save.free("x")
    attn_join(x, o, wo, x1, x)
    save(x, x1_o)
    ready("self")
    attn_project(a3, a3, sq, sk, sv, q3, k3, v3)
    for src, dst in ((a3, a3_o), (q3, q3_o), (k3, k3_o), (v3, v3_o)):
        save(src, dst)
    gather.move(11)
    gather.move(12)
    g3_in = halves.give(2, cot, g3_o)

    def between3():
        gather.move(13)

    attn_core(seq, q3, k3, v3, o3, ol3, r3, e3_o, ebuf, esem, between3, False)
    gather.move(14)
    load("feed", 8 * n1, (wu, wd), n2, 16)
    for src, dst in ((o3, o3_o), (ol3, ol3_o), (r3, r3_o)):
        save(src, dst)
    save.free("y0")
    attn_join(y0, o3, so, y1, y0)
    save(y0, y1_o)
    save.free("A")
    normalize(y1, gains[4:5, :], shifts[4:5, :], a)
    gather.move(15)
    ready("feed")

    def feed(sl):
        stream = x1[sl, :]
        hat, unused = ln_hat(stream)
        rows = (hat * gains[1:2, :] + shifts[1:2, :]).astype(BF)
        a1[sl, :] = rows
        out = stream
        lifted = dg(rows, columns(wu, 0, FB))
        for lower in range(0, 2 * n2, FB):
            cols = pl.ds(lower, FB)
            following = dg(rows, columns(wu, lower + FB, FB)) if lower + FB < 2 * n2 else None
            active, slope = gelu_both(lifted)
            active = active.astype(BF)
            h[sl, cols] = active
            gp[sl, cols] = slope.astype(BF)
            out = out + dg(active, columns(wd, lower, FB), NT)
            lifted = following
        x2[sl, :] = out.astype(BF)
        hat, unused = ln_hat(out)
        mem[sl, :] = (hat * gains[2:3, :] + shifts[2:3, :]).astype(BF)

    rows_loop(seq // 2, RB, feed)
    gather.move(16)
    load("cross", 8 * n1 + 2 * n2, (wq, wk, wv, wo), n1, 0)
    rows_loop(seq // 2, RB, lambda sl: feed(pl.ds(pl.multiple_of(seq // 2 + sl.start, RB), RB)))
    for src, dst in ((a1, a1_o), (h, h1_o), (gp, gp1_o), (x2, x2_o), (mem, mem_o)):
        save(src, dst)
    gather.move(17)
    ready("cross")
    attn_project(a, mem, wq, wk, wv, q, k, v)
    for src, dst in ((a, a4_o), (q, q4_o), (k, k4_o), (v, v4_o)):
        save(src, dst)
    gather.move(18)

    def between4():
        gather.move(19)

    attn_core(length, q, k, v, o, ol, r, e4_o, ebuf, esem, between4, False)
    for src, dst in ((o, o4_o), (ol, ol4_o), (r, r4_o)):
        save(src, dst)
    gather.move(20)
    attn_join(y1, o, wo, y2, None)
    save(y2, y2_o)
    gather.move(21)
    drain_scores(e4_o, ebuf, esem)
    arrived(g3_in)
    halves.finish()
    gather.finish()
    save.finish()


class Reduce:
    def __init__(self, out, chunks):
        self.out, self.chunks = out, chunks
        self.spot = places()
        self.sends, self.pending = [], {}

    def push(self, name, i, src, dst, device):
        send, recv = self.chunks[name][5:7]
        copy = pltpu.make_async_remote_copy(
            src_ref=src, dst_ref=dst, send_sem=send.at[i], recv_sem=recv.at[i],
            device_id=device, device_id_type=MESH,
        )
        copy.start()
        self.sends.append((name, copy))
        self.pending.setdefault(name, []).append(copy)

    def move(self, *steps):
        for name, s in steps:
            self.stage(name, s)

    def stage(self, name, s):
        t, z, y, c = self.spot
        g, r1, r2, r3, r4, send, recv, start, split = self.chunks[name]
        width = g.shape[-1]
        half = width // 2 if split else width
        left = pl.ds(0, half)
        right = pl.ds(half, half)
        by_x, by_y = at(1 - t, z, y, c), at(t, z, 1 - y, c)

        def add(mine, theirs):
            mine[...] = (mine[...].astype(F32) + theirs[...].astype(F32)).astype(BF)

        for copy in self.pending.pop(name, ()):
            copy.wait_recv()
        if s == 0:
            self.push(name, 0, g.at[:, :, :, 1 - c], r1, at(t, z, y, 1 - c))
        elif s == 1:
            add(g.at[:, :, 1 - y, c], r1.at[:, :, 1 - y])
            self.push(name, 1, g.at[:, :, 1 - y, c, :, left], r2.at[:, :, :, left], by_y)
            add(g.at[:, :, y, c], r1.at[:, :, y])
            if split:
                self.push(name, 2, g.at[1 - t, :, :, c, :, right], r3.at[0], by_x)
        elif s == 2:
            rows = g.at[:, :, y, c, :, left]
            add(rows, r2.at[:, :, :, left])
            if not split:
                self.push(name, 2, g.at[1 - t, :, y, c], r3, by_x)
            else:
                self.push(name, 3, g.at[1 - t, :, y, c, :, left], r3.at[1, :, 0], by_x)
                add(g.at[t, :, :, c, :, right], r3.at[0])
                self.push(name, 4, g.at[t, :, 1 - y, c, :, right], r3.at[1, :, 1], by_y)
        elif s == 3:
            if not split:
                add(g.at[t, :, y, c], r3)
            else:
                add(g.at[t, :, y, c, :, left], r3.at[1, :, 0])
                add(g.at[t, :, y, c, :, right], r3.at[1, :, 1])
            for j in range(1, 4):
                zz = lax.rem(z + j, 4)
                self.push(name, 4 + j, g.at[t, zz, y, c], r4.at[j - 1], at(t, zz, y, c))
        elif s == 4:
            self.out[:, pl.ds(start, width)] = (g[t, z, y, c].astype(F32) + r4[0].astype(F32)) + (
                r4[1].astype(F32) + r4[2].astype(F32)
            )

    def release(self, name):
        for owner, copy in self.sends:
            if owner == name:
                copy.wait_send()
        self.sends = [entry for entry in self.sends if entry[0] != name]

    def finish(self):
        for owner, copy in self.sends:
            copy.wait_send()
        self.sends = []


def put(g, first, n, value, lower=0):
    done = 0
    while done < value.shape[1]:
        t, offset = (lower + done) // n, (lower + done) % n
        take = min(value.shape[1] - done, n - offset)
        block = value[:, done : done + take].astype(BF)
        g[t, :, :, :, :, pl.ds(first + offset, take)] = block.reshape(g.shape[1:5] + (take,))
        done += take


def add_norm(ng, index, dgain, dshift):
    ng[index : index + 1, :] += dgain
    ng[6 + index : 7 + index, :] += dshift


def attn_backward(
    g, x, gain, ng, index, a_t, kv_t, g_t, wq, wk, wv, wo, q, k, v, o, ol, r, e_hbm, ebuf, esem, ds,
    do, dq, dk, dv, grads, n1, before_core, between, after_core, after_grads, into_keys, finish,
):
    seq = x.shape[0]

    def before(sl):
        rows = g[sl, :].astype(BF)
        g_t[:, sl] = rows.T
        do[sl, :] = (dg(rows, wo[...]) * r[sl, :].astype(F32)).astype(BF)

    rows_loop(seq, RB, before)
    put(grads, 3 * n1, n1, dg(g_t[...], o[...]))
    before_core()
    attn_back_core(q, k, v, do, o, ol, e_hbm, ebuf, esem, ds, dq, dk, dv, between)
    after_core()
    put(grads, 0, n1, dg(a_t[...], dq[...]))
    put(grads, n1, n1, dg(kv_t[...], dk[...]))
    put(grads, 2 * n1, n1, dg(kv_t[...], dv[...]))
    after_grads()

    def after(sl):
        into = dg(dq[sl, :], wq[...], NT)
        keys = dg(dk[sl, :], wk[...], NT) + dg(dv[sl, :], wv[...], NT)
        if into_keys is None:
            into = into + keys
        else:
            into_keys[sl, :] = keys
        dx, dgain, dshift = ln_back(x[sl, :].astype(F32), gain, into)
        add_norm(ng, index, dgain, dshift)
        finish(sl, g[sl, :] + dx)

    rows_loop(seq, RB, after)


def fetcher(sems):
    count = [0]

    def fetch(*pairs):
        copies = []
        for src, dst in pairs:
            cp = pltpu.make_async_copy(src, dst, sems.at[count[0]])
            count[0] += 1
            cp.start()
            copies.append(cp)
        return copies

    return fetch


def nothing():
    return None


def dec_backward(
    gains, shifts, y2_hbm, g3_hbm, y1_hbm, mem_hbm, a4_hbm, q4_hbm, k4_hbm, v4_hbm, o4_hbm, ol4_hbm, r4_hbm, e4_hbm,
    x2_hbm, x1_hbm, a1_hbm, h1_hbm, gp1_hbm, w_hbm,
    dec_o, g4_o, g1_o, up_o, down_o, sums, ng,
    y2, g3, y1, a, q, k, v, o, ol, r, cq, ck, cv, co, wu, wd,
    big, gs, do, a_t, g_t, g_up, g_down, g_cross, ebuf,
    ru1, ru2, ru3, ru4, rd1, rd2, rd3, rd4, rc1, rc2, rc3, rc4,
    rsend, rrecv, xsend, xrecv, local, isem, wsem, esem, osem,
):
    t, z, y, c = places()
    seq, width = y1.shape
    n1, n2 = cq.shape[1] // 2, wu.shape[1] // 2
    fetch = fetcher(isem)
    load, ready = weight_loader(w_hbm, wsem)
    first = fetch((y2_hbm, y2), (g3_hbm, g3))
    load("feed", 12 * n1 + 2 * n2, (wu, wd), n2, 0)
    greet(all_partners(t, z, y, c))
    halves = Exchange(xsend, xrecv, local)
    reduce = Reduce(
        sums,
        {
            "up": (g_up, ru1, ru2, ru3, ru4, rsend.at[0], rrecv.at[0], 0, True),
            "down": (g_down, rd1, rd2, rd3, rd4, rsend.at[1], rrecv.at[1], n2, True),
            "cross": (g_cross, rc1, rc2, rc3, rc4, rsend.at[2], rrecv.at[2], 2 * n2, True),
        },
    )
    ng[...] = jnp.zeros_like(ng)
    save = Saver(osem)
    wait_all(first)
    ready("feed")
    load("cross", 8 * n1 + 2 * n2, (cq, ck, cv, co), n1, 4)
    cross = fetch(
        (o4_hbm, o), (r4_hbm, r), (a4_hbm, a), (q4_hbm, q), (k4_hbm, k),
        (v4_hbm, v), (ol4_hbm, ol), (y1_hbm, y1),
    )
    first_scores(e4_hbm, ebuf, esem)
    h, du = big.at[0], big.at[1]

    def feed(sl):
        stream = y2[sl, :]
        hat, unused = ln_hat(stream)
        rows = (hat * gains[5:6, :] + shifts[5:6, :]).astype(BF)
        a_t[:, sl] = rows.T
        grad = g3[sl, :]
        g_t[:, sl] = grad.T
        out, into = stream, None
        lifted, pulled = dg(rows, columns(wu, 0, FB)), dg(grad, columns(wd, 0, FB))
        for lower in range(0, 2 * n2, FB):
            cols = pl.ds(lower, FB)
            if lower + FB < 2 * n2:
                following = dg(rows, columns(wu, lower + FB, FB)), dg(grad, columns(wd, lower + FB, FB))
            active, slope = gelu_both(lifted)
            active = active.astype(BF)
            h[sl, cols] = active
            pushed = (pulled * slope).astype(BF)
            du[sl, cols] = pushed
            out = out + dg(active, columns(wd, lower, FB), NT)
            part = dg(pushed, columns(wu, lower, FB), NT)
            into = part if into is None else into + part
            lifted, pulled = following
        g3[sl, :] = out.astype(BF)
        dx, dgain, dshift = ln_back(stream, gains[5:6, :], into)
        add_norm(ng, 5, dgain, dshift)
        gs[sl, :] = grad.astype(F32) + dx

    rows_loop(seq, RB, feed)
    dec_back = halves.back(0, g3, dec_o)
    block = width
    for j in range(2 * n2 // block):
        put(g_up, 0, n2, dg(a_t[...], du[:, pl.ds(j * block, block)]), j * block)
    reduce.move(("up", 0))
    for j in range(2 * n2 // block):
        put(g_down, 0, n2, dg(g_t[...], h[:, pl.ds(j * block, block)]), j * block)
    load("enc", 8 * n1, (wu, wd), n2, 12)
    reduce.move(("down", 0))
    wait_all(cross)
    ready("cross")
    a_t[...] = a[...].T
    memory = big.at[1, :, pl.ds(3 * width, width)]
    late = fetch((mem_hbm, memory))
    dq, dk, dv = (big.at[1, :, pl.ds(i * width, width)] for i in range(3))

    def before_core():
        reduce.move(("up", 1))

    def between():
        reduce.move(("down", 1))

    def after_core():
        wait_all(late)
        late.clear()
        late.extend(fetch((x2_hbm, r)))
        g_t[...] = memory[...].T
        late.extend(
            fetch(
                (gp1_hbm.at[:, pl.ds(0, n2)], ebuf.at[2]), (gp1_hbm.at[:, pl.ds(n2, n2)], ebuf.at[3]),
                (h1_hbm.at[:, pl.ds(0, n2)], ebuf.at[0]), (h1_hbm.at[:, pl.ds(n2, n2)], ebuf.at[1]),
            )
        )
        reduce.move(("up", 2))

    def after_grads():
        late.extend(fetch((a1_hbm, a)))
        reduce.move(("cross", 0), ("down", 2))

    def keep(sl, gradient):
        gs[sl, :] = gradient

    attn_backward(
        gs, y1, gains[4:5, :], ng, 4, a_t, g_t, g_t, cq, ck, cv, co, q, k, v, o, ol, r, e4_hbm,
        ebuf, esem, big.at[0], do, dq, dk, dv, g_cross, n1,
        before_core, between, after_core, after_grads, y2, keep,
    )
    save(gs, g4_o)
    late.extend(fetch((x1_hbm, y1)))
    reduce.move(("up", 3), ("cross", 1))
    wait_all(late)
    ready("enc")
    save.finish()

    def feed_back(sl):
        dx, dgain, dshift = ln_back(r[sl, :].astype(F32), gains[2:3, :], y2[sl, :])
        add_norm(ng, 2, dgain, dshift)
        grad = dx.astype(BF)
        g_t[:, sl] = grad.T
        a_t[:, sl] = a[sl, :].T
        into = None
        pulled = dg(grad, columns(wd, 0, FB))
        for lower in range(0, 2 * n2, FB):
            i, cols = lower // n2, pl.ds(lower % n2, FB)
            following = dg(grad, columns(wd, lower + FB, FB)) if lower + FB < 2 * n2 else None
            pushed = (pulled * ebuf[2 + i, sl, cols].astype(F32)).astype(BF)
            ebuf[2 + i, sl, cols] = pushed
            part = dg(pushed, columns(wu, lower, FB), NT)
            into = part if into is None else into + part
            pulled = following
        dx1, dgain, dshift = ln_back(y1[sl, :].astype(F32), gains[1:2, :], into)
        add_norm(ng, 1, dgain, dshift)
        gs[sl, :] = dx + dx1

    rows_loop(seq // 2, RB, feed_back)
    reduce.move(("down", 3))
    rows_loop(seq // 2, RB, lambda sl: feed_back(pl.ds(pl.multiple_of(seq // 2 + sl.start, RB), RB)))
    save(gs, g1_o)
    reduce.move(("cross", 2), ("up", 4))
    reduce.release("up")
    for i in range(2):
        for j in range(n2 // block):
            cols = pl.ds(j * block, block)
            put(g_up, 0, n2, dg(a_t[...], ebuf[2 + i, :, cols]), i * n2 + j * block)
    save(g_up, up_o)
    reduce.move(("cross", 3), ("down", 4))
    reduce.release("down")
    for i in range(2):
        for j in range(n2 // block):
            cols = pl.ds(j * block, block)
            put(g_down, 0, n2, dg(g_t[...], ebuf[i, :, cols]), i * n2 + j * block)
    save(g_down, down_o)
    reduce.move(("cross", 4))
    arrived(dec_back)
    halves.finish()
    reduce.finish()
    save.finish()


def last_backward(
    gains, ng2, masked, g4_hbm, g1_hbm, y0_hbm, a3_hbm, q3_hbm, k3_hbm, v3_hbm, o3_hbm, ol3_hbm, r3_hbm, e3_hbm,
    x_hbm, a0_hbm, q0_hbm, k0_hbm, v0_hbm, o0_hbm, ol0_hbm, r0_hbm, e0_hbm, up_hbm, down_hbm, w_hbm,
    sg_o, target_o, sums, vec,
    gs, gs1, x, x0, a, q, k, v, o, ol, r, wq, wk, wv, wo, vo, big, do, a_t, g_t, gy, ng,
    g_up, g_down, g_self, g_enc, ebuf,
    ru1, ru2, ru3, ru4, rd1, rd2, rd3, rd4, rs1, rs2, rs3, rs4, re1, re2, re3, re4, ro1, ro2, ro3, ro4, v1, vr,
    rsend, rrecv, xsend, xrecv, local, vsend, vrecv, isem, wsem, esem,
):
    t, z, y, c = places()
    seq, width = x.shape
    n1 = wq.shape[1] // 2
    n2 = g_up.shape[-1]
    fetch = fetcher(isem)
    load, ready = weight_loader(w_hbm, wsem)
    load("self out", 7 * n1, (wo,), n1, 0)
    first = fetch((g4_hbm, gs), (o3_hbm, o), (r3_hbm, r))
    ups = fetch((up_hbm, g_up), (down_hbm, g_down))
    first_scores(e3_hbm, ebuf, esem)
    second = fetch((q3_hbm, q), (k3_hbm, k), (v3_hbm, v), (ol3_hbm, ol), (a3_hbm, a), (y0_hbm, x))
    load("self", 4 * n1, (wq, wk, wv), n1, 2)
    load("enc out", 3 * n1, (vo,), n1, 8)
    late = fetch((g1_hbm, gs1), (x_hbm, x0))
    greet(all_partners(t, z, y, c))
    halves = Exchange(xsend, xrecv, local)
    reduce = Reduce(
        sums,
        {
            "up": (g_up, ru1, ru2, ru3, ru4, rsend.at[0], rrecv.at[0], 0, True),
            "down": (g_down, rd1, rd2, rd3, rd4, rsend.at[1], rrecv.at[1], n2, True),
            "self": (g_self, rs1, rs2, rs3, rs4, rsend.at[2], rrecv.at[2], 2 * n2, True),
            "enc": (
                g_enc.at[:, :, :, :, :, pl.ds(0, 3 * n1)], re1, re2, re3, re4, rsend.at[3], rrecv.at[3],
                2 * n2 + 4 * n1, True,
            ),
            "out": (
                g_enc.at[:, :, :, :, :, pl.ds(3 * n1, n1)], ro1, ro2, ro3, ro4, rsend.at[4], rrecv.at[4],
                2 * n2 + 7 * n1, False,
            ),
        },
    )
    ng[...] = ng2[...]
    wait_all(ups)
    reduce.move(("up", 0), ("down", 0))
    wait_all(first)
    ready("self out")
    dq, dk, dv = (big.at[1, :, pl.ds(i * width, width)] for i in range(3))
    ds = big.at[0]

    def before_core3():
        wait_all(second)
        a_t[...] = a[...].T
        ready("self")

    def between3():
        reduce.move(("up", 1), ("down", 1))

    def after_core3():
        late.extend(fetch((o0_hbm, o), (r0_hbm, r), (q0_hbm, q), (k0_hbm, k), (v0_hbm, v), (ol0_hbm, ol), (a0_hbm, a)))
        first_scores(e0_hbm, ebuf, esem)

    def after_grads3():
        reduce.move(("self", 0), ("up", 2))

    def last3(sl, gradient):
        gy[sl, :] = gradient.astype(BF)

    attn_backward(
        gs, x, gains[3:4, :], ng, 3, a_t, a_t, g_t, wq, wk, wv, wo, q, k, v, o, ol, r, e3_hbm,
        ebuf, esem, ds, do, dq, dk, dv, g_self, n1,
        before_core3, between3, after_core3, after_grads3, None, last3,
    )
    load("enc", 0, (wq, wk, wv), n1, 10)
    reduce.move(("down", 2), ("self", 1))
    gy_back = halves.back(0, gy, target_o)
    wait_all(late)
    ready("enc out")
    a_t[...] = a[...].T

    def before_core0():
        reduce.move(("out", 0), ("up", 3))

    def between0():
        reduce.move(("out", 1))

    def after_core0():
        reduce.move(("out", 2), ("self", 2), ("down", 3), ("up", 4))
        arrived(gy_back)
        total = jnp.zeros((1, width), F32)
        for i in range(2):
            chosen = column(masked[i : i + 1, :].astype(F32)) == 1.0
            rows = target_o[i].astype(F32)
            total = total + jnp.sum(jnp.where(chosen, rows, 0.0), axis=0, keepdims=True)
            target_o[i] = jnp.where(chosen, 0.0, rows).astype(BF)
        ng[12:13, :] = total

    def after_grads0():
        ready("enc")
        gy_back[0].wait_send()
        reduce.move(("enc", 0))

    def last0(sl, gradient):
        gy[sl, :] = gradient.astype(BF)

    attn_backward(
        gs1, x0, gains[0:1, :], ng, 0, a_t, a_t, g_t, wq, wk, wv, vo, q, k, v, o, ol, r, e0_hbm,
        ebuf, esem, ds, do, dq, dk, dv, g_enc, n1,
        before_core0, between0, after_core0, after_grads0, None, last0,
    )
    waiting = []

    def vector(s):
        for copy in waiting:
            copy.wait_recv()
        waiting.clear()
        if s == 0:
            v1[0] = ng[...]
        elif s < 4:
            v1[s] = v1[s - 1] + vr[s - 1]
        if s < 3:
            targets = ((s, (at(1 - t, z, y, c), at(t, z, y, 1 - c), at(t, z, 1 - y, c))[s]),)
        elif s == 3:
            targets = tuple((2 + j, at(t, lax.rem(z + j, 4), y, c)) for j in range(1, 4))
        else:
            targets = ()
            vec[...] = (v1[3] + vr[3]) + (vr[4] + vr[5])
        for slot, device in targets:
            copy = pltpu.make_async_remote_copy(
                src_ref=v1.at[s], dst_ref=vr.at[slot], send_sem=vsend.at[slot], recv_sem=vrecv.at[slot],
                device_id=device, device_id_type=MESH,
            )
            copy.start()
            reduce.sends.append(("vector", copy))
            waiting.append(copy)

    vector(0)
    reduce.move(("enc", 1), ("self", 3), ("out", 3))
    vector(1)
    reduce.move(("enc", 2))
    sg_back = halves.back(1, gy, sg_o)
    vector(2)
    vector(3)
    reduce.move(("down", 4), ("enc", 3))
    vector(4)
    reduce.move(("self", 4), ("out", 4), ("enc", 4))
    arrived(sg_back)
    sg_back[0].wait_send()
    reduce.finish()


def unpack(dec, sg, tg, sums2, sums3, vec, dec_o, sg_o, tg_o, *refs):
    for src, dst in ((dec, dec_o), (sg, sg_o), (tg, tg_o)):
        dst[...] = src[...]
    grads, (gains_o, shifts_o, mask_o) = refs[:16], refs[16:]
    for summed, held in ((sums2, (14, 15, 10, 11, 12, 13)), (sums3, (4, 5, 6, 7, 8, 9, 0, 1, 2, 3))):
        offset = 0
        for i in held:
            n = grads[i].shape[1]
            grads[i][...] = summed[:, pl.ds(offset, n)]
            offset += n
    gains_o[...] = vec[0:6, :]
    shifts_o[...] = vec[6:12, :]
    mask_o[...] = vec[12:13, :]


def compute_all(lengths, timesteps, gains, shifts, mask_vector, masked, loss_mask, matrices, source, target, cotangent):
    rows, width = source.shape[1:]
    seq = 2 * rows
    n1 = width // 2
    part = matrices[0].shape[0]
    n2 = matrices[4].shape[1]
    total = 12 * n1 + 4 * n2
    hidden = 2 * n2
    heads = width // HD
    sd = jax.ShapeDtypeStruct
    any_spec = pl.BlockSpec(memory_space=pl.ANY)
    vmem = pl.BlockSpec(memory_space=pltpu.VMEM)
    smem = pl.BlockSpec(memory_space=pltpu.SMEM)
    dma = pltpu.SemaphoreType.DMA
    row = lambda kind: sd((seq, width), kind)
    tall = lambda kind: sd((seq, hidden), kind)
    halves = sd((2, rows, width), BF)
    escores = sd((heads, seq, seq), BF)
    vrow = lambda kind: pltpu.VMEM((seq, width), kind)
    vhalves = pltpu.VMEM((2, rows, width), BF)
    vsq = pltpu.VMEM((width, width), BF)
    vwide = pltpu.VMEM((width, hidden), BF)
    vtall = pltpu.VMEM((seq, hidden), BF)
    vsq5 = pltpu.VMEM((4, 2, 2, part, width), BF)
    vwide5 = pltpu.VMEM((4, 2, 2, part, hidden), BF)
    turned = pltpu.VMEM((width, seq), BF)
    big = pltpu.VMEM((2, seq, hidden), BF)
    ebuf = pltpu.VMEM((4, seq, seq), BF)
    grads = lambda n: pltpu.VMEM((2, 4, 2, 2, part, n), BF)

    def landing(n, split=False):
        r3 = (2, 4, 2, part, n // 2) if split else (4, part, n)
        return [
            pltpu.VMEM(dims, BF) for dims in ((2, 4, 2, part, n), (2, 4, part, n), r3, (3, part, n))
        ]

    def params(number):
        return pltpu.CompilerParams(
            vmem_limit_bytes=VMEM_LIMIT, collective_id=number, has_side_effects=True
        )

    attention = [row(BF)] * 7 + [escores]
    (
        gathered, x, y0, g3,
        a0, q0, k0, v0, o0, ol0, r0, e0, x1, a1, h1, gp1, x2, mem,
        a3, q3, k3, v3, o3, ol3, r3, e3, y1,
        a4, q4, k4, v4, o4, ol4, r4, e4, y2,
    ) = pl.pallas_call(
        forward,
        in_specs=[smem, smem] + [vmem] * 21 + [any_spec] * 3,
        out_specs=[any_spec] * 36,
        out_shape=[sd((2, 4, 2, 2, part, total), BF)] + [row(BF)] * 3
        + attention + [row(BF), row(BF), tall(BF), tall(BF), row(BF), row(BF)]
        + attention + [row(BF)]
        + attention + [row(F32)],
        scratch_shapes=[pltpu.VMEM((part, total), BF), vhalves, vhalves]
        + [vrow(BF)] * 2 + [vsq5] * 8 + [vwide5] * 2 + [vrow(BF)] * 14
        + [vrow(F32), vrow(BF), vtall, vtall, vrow(BF), vrow(BF), vrow(F32), vrow(F32), ebuf]
        + [dma((8, 11)), dma((8, 11)), dma((4,)), dma((4,)), dma((7,)), dma((20,)), dma((4,)), dma((35,))],
        compiler_params=params(0),
        name="forward",
    )(lengths, timesteps, gains, shifts, mask_vector[None], masked, loss_mask, *matrices, source, target, cotangent)
    weights = gathered.reshape(2, width, total)
    decoded, g4, g1, up, down, sums2, ng = pl.pallas_call(
        dec_backward,
        in_specs=[vmem, vmem] + [any_spec] * 18,
        out_specs=[any_spec] * 5 + [vmem] * 2,
        out_shape=[halves, row(F32), row(F32)] + [sd((2, 4, 2, 2, part, n2), BF)] * 2
        + [sd((part, 2 * n2 + 4 * n1), F32), sd((16, width), F32)],
        scratch_shapes=[vrow(F32)] + [vrow(BF)] * 9
        + [vsq] * 4 + [vwide] * 2 + [big, vrow(F32), vrow(BF)] + [turned] * 2
        + [grads(n2), grads(n2), grads(4 * n1), ebuf]
        + landing(n2, True) + landing(n2, True) + landing(4 * n1, True)
        + [dma((3, 8)), dma((3, 8)), dma((1,)), dma((1,)), dma((1,)), dma((18,)), dma((16,)), dma((4,)), dma((4,))],
        compiler_params=params(1),
        name="dec_backward",
    )(gains, shifts, y2, g3, y1, mem, a4, q4, k4, v4, o4, ol4, r4, e4, x2, x1, a1, h1, gp1, weights)
    source_grad, target_grad, sums3, vec = pl.pallas_call(
        last_backward,
        in_specs=[vmem] * 3 + [any_spec] * 23,
        out_specs=[any_spec, vmem, vmem, vmem],
        out_shape=[halves, halves, sd((part, 2 * n2 + 8 * n1), F32), sd((16, width), F32)],
        scratch_shapes=[vrow(F32)] * 2 + [vrow(BF)] * 9 + [vsq] * 5 + [big, vrow(BF)] + [turned] * 2
        + [vrow(BF), pltpu.VMEM((16, width), F32)]
        + [grads(n2), grads(n2), grads(4 * n1), grads(4 * n1), ebuf]
        + landing(n2, True) + landing(n2, True) + landing(4 * n1, True) + landing(3 * n1, True) + landing(n1)
        + [pltpu.VMEM((4, 16, width), F32), pltpu.VMEM((6, 16, width), F32)]
        + [dma((5, 8)), dma((5, 8)), dma((2,)), dma((2,)), dma((2,)), dma((6,)), dma((6,)), dma((20,)), dma((16,)), dma((4,))],
        compiler_params=params(2),
        name="last_backward",
    )(
        gains, ng, masked, g4, g1, y0, a3, q3, k3, v3, o3, ol3, r3, e3,
        x, a0, q0, k0, v0, o0, ol0, r0, e0, up, down, weights,
    )
    square, tall_square = sd((part, n1), F32), sd((part, n2), F32)
    small = pl.pallas_call(
        unpack,
        in_specs=[vmem] * 6,
        out_specs=[vmem] * 22,
        out_shape=[halves] * 3 + [tall_square if i in (4, 5, 14, 15) else square for i in range(16)]
        + [sd((6, width), F32)] * 2 + [sd((1, width), F32)],
        compiler_params=pltpu.CompilerParams(vmem_limit_bytes=VMEM_LIMIT),
        name="unpack",
    )(decoded, source_grad, target_grad, sums2, sums3, vec)
    return tuple(small)


def pair_body(*arguments):
    source, target, cotangent, lengths, timesteps, masked, loss_mask = arguments[:7]
    matrices = [m.T if i in TURNED else m for i, m in enumerate(arguments[7:23])]
    norm_gains, norm_shifts, mask_vector = arguments[23:]
    outs = compute_all(
        lengths, timesteps, norm_gains, norm_shifts, mask_vector, masked, loss_mask, matrices, source, target, cotangent
    )
    grads = [g.T if i in TURNED else g for i, g in enumerate(outs[3:19])]
    return (*outs[:3], *grads, outs[19], outs[20], outs[21][0])


def solution(mesh):
    whole_pairs = dict(mesh.shape) == {"dp": 16, "tensor": 2}
    return jax.shard_map(
        pair_body if whole_pairs else body,
        mesh=mesh,
        in_specs=(
            P("dp", "tensor", None),
            P("dp", "tensor", None),
            P("dp", "tensor", None),
            P("dp"),
            P("dp"),
            P("dp", "tensor"),
            P("dp", "tensor"),
            P("dp", "tensor"),
            P("dp", "tensor"),
            P("dp", "tensor"),
            P("tensor", "dp"),
            P("dp", "tensor"),
            P("tensor", "dp"),
            P("dp", "tensor"),
            P("dp", "tensor"),
            P("dp", "tensor"),
            P("tensor", "dp"),
            P("dp", "tensor"),
            P("dp", "tensor"),
            P("dp", "tensor"),
            P("tensor", "dp"),
            P("dp", "tensor"),
            P("tensor", "dp"),
            P(),
            P(),
            P(),
        ),
        out_specs=(
            P("dp", "tensor", None),
            P("dp", "tensor", None),
            P("dp", "tensor", None),
            P("dp", "tensor"),
            P("dp", "tensor"),
            P("dp", "tensor"),
            P("tensor", "dp"),
            P("dp", "tensor"),
            P("tensor", "dp"),
            P("dp", "tensor"),
            P("dp", "tensor"),
            P("dp", "tensor"),
            P("tensor", "dp"),
            P("dp", "tensor"),
            P("dp", "tensor"),
            P("dp", "tensor"),
            P("tensor", "dp"),
            P("dp", "tensor"),
            P("tensor", "dp"),
            P(),
            P(),
            P(),
        ),
        check_vma=False,
    )
```
